32 devices in a mesh: dp: 4 (over z), seq: 4 (over y, x), head: 2 (over core).
Axes of the slice: x: 2, y: 2, z: 4, core: 2. Of those that a mesh axis runs over, the one named last changes fastest.
Arguments:
- inputs: bfloat16 [32, 512, 768], P(('dp', 'head'), 'seq'), may hold values from -6 to 6
- dec_in: bfloat16 [8, 4, 768], P(('dp', 'head'), 'seq'), may hold values from -6 to 6
- cotangent: bfloat16 [8, 4, 768], P(('dp', 'head'), 'seq'), may hold values from -6 to 6
- lengths: int32 [32], P(('dp', 'head')), may hold values from 40 to 512, as said below
- bucket_table: int32 [1023], replicated, may hold values from 0 to 31, as said below
- square: float32 [10, 768, 768], P(None, ('dp', 'seq', 'head'))
- square_m: float32 [10, 768, 768], P(None, ('dp', 'seq', 'head')), may hold values from -0.0004272461 to 0.0004272461
- square_v: float32 [10, 768, 768], P(None, ('dp', 'seq', 'head')), may hold values from 6.5e-11 to 2.6e-10
- ffn_in: float32 [2, 768, 3072], P(None, ('dp', 'seq', 'head')), may hold values from -0.21875 to 0.21875
- ffn_in_m: float32 [2, 768, 3072], P(None, ('dp', 'seq', 'head')), may hold values from -0.0004272461 to 0.0004272461
- ffn_in_v: float32 [2, 768, 3072], P(None, ('dp', 'seq', 'head')), may hold values from 6.5e-11 to 2.6e-10
- ffn_out: float32 [2, 3072, 768], P(None, ('dp', 'seq', 'head')), may hold values from -0.109375 to 0.109375
- ffn_out_m: float32 [2, 3072, 768], P(None, ('dp', 'seq', 'head')), may hold values from -0.0004272461 to 0.0004272461
- ffn_out_v: float32 [2, 3072, 768], P(None, ('dp', 'seq', 'head')), may hold values from 6.5e-11 to 2.6e-10
- gains: float32 [6, 768], P(None, ('dp', 'seq', 'head'))
- gains_m: float32 [6, 768], P(None, ('dp', 'seq', 'head')), may hold values from -0.0004272461 to 0.0004272461
- gains_v: float32 [6, 768], P(None, ('dp', 'seq', 'head')), may hold values from 6.5e-11 to 2.6e-10
- rel_bias: float32 [32, 12], replicated, may hold values from -3 to 3
- rel_bias_m: float32 [32, 12], replicated, may hold values from -0.0004272461 to 0.0004272461
- rel_bias_v: float32 [32, 12], replicated, may hold values from 6.5e-11 to 2.6e-10
Outputs:
- dec_out: bfloat16 [8, 4, 768], P(('dp', 'head'), 'seq')
- input_grad: float32 [32, 512, 768], P(('dp', 'head'), 'seq')
- grad_norm: float32 [], replicated
- square_new: float32 [10, 768, 768], P(None, ('dp', 'seq', 'head'))
- square_m_new: float32 [10, 768, 768], P(None, ('dp', 'seq', 'head'))
- square_v_new: float32 [10, 768, 768], P(None, ('dp', 'seq', 'head'))
- ffn_in_new: float32 [2, 768, 3072], P(None, ('dp', 'seq', 'head'))
- ffn_in_m_new: float32 [2, 768, 3072], P(None, ('dp', 'seq', 'head'))
- ffn_in_v_new: float32 [2, 768, 3072], P(None, ('dp', 'seq', 'head'))
- ffn_out_new: float32 [2, 3072, 768], P(None, ('dp', 'seq', 'head'))
- ffn_out_m_new: float32 [2, 3072, 768], P(None, ('dp', 'seq', 'head'))
- ffn_out_v_new: float32 [2, 3072, 768], P(None, ('dp', 'seq', 'head'))
- gains_new: float32 [6, 768], P(None, ('dp', 'seq', 'head'))
- gains_m_new: float32 [6, 768], P(None, ('dp', 'seq', 'head'))
- gains_v_new: float32 [6, 768], P(None, ('dp', 'seq', 'head'))
- rel_bias_new: float32 [32, 12], replicated
- rel_bias_m_new: float32 [32, 12], replicated
- rel_bias_v_new: float32 [32, 12], replicated
The draws below stay inside these ranges and needn't reach their ends.
Inputs may be any that keep to these rules, and one draw needn't show every extreme that they name: Row n holds one document in positions 0 to lengths[n] - 1, the rest is padding; in every group of 4 consecutive rows at least one row has length 512. `bucket_table`: entry j is the bucket of relative position j - 511; buckets of offsets of one sign do not fall as the distance grows; non-positive offsets use buckets below 16, positive ones the others.
All inputs are finite; a program needn't handle non-finite values.
Results may differ from the reference program's by a relative error of at most 0.02.
The reference program's roundings to bfloat16 on the way count: a program that leaves them out, or rounds other values in their place, can miss the bound.
Values may be sent and summed in bfloat16 or wider, within the bound.
A program may use at most 320 MiB of HBM per device.

```python
import math
import jax
import jax.numpy as jnp
from jax import lax

D = 768
H = 12
HD = 64
FF = 3072
NB = 32
L = 512
ROWS_DEV = 4
STEP = 5
GROUPS = 8
DOCS = 32


def draw_lengths(key, part):
    key = jax.random.fold_in(key, 7)
    key_len, key_pick = jax.random.split(key)
    raw_draw = jax.random.randint(key_len, (DOCS,), 0, 1000)
    cubed = raw_draw * raw_draw // 1000 * raw_draw
    length = 40 + cubed * (L - 40) // 999000
    picked = jax.random.randint(key_pick, (GROUPS,), 0, ROWS_DEV)
    row_index = jnp.arange(DOCS)
    chosen = jnp.repeat(picked, ROWS_DEV)
    length = jnp.where(row_index % ROWS_DEV == chosen, L, length)
    return length.astype(jnp.int32)


def draw_bucket_table(key, part):
    key = jax.random.fold_in(key, 11)
    half_count = NB // 2
    distance = jnp.arange(L)
    rolled = jax.random.randint(key, (L,), 0, max(1, 2 * L // NB))
    rising = jnp.where(distance < NB // 4, 1, jnp.where(rolled == 0, 1, 0))
    rising = jnp.where(distance == 0, 0, rising)
    level = jnp.minimum(jnp.cumsum(rising), half_count - 1)
    level = jnp.where(distance == L - 1, half_count - 1, level)
    relative = jnp.arange(2 * L - 1) - (L - 1)
    table_out = level[jnp.abs(relative)] + jnp.where(relative > 0, half_count, 0)
    return table_out.astype(jnp.int32)


def draw_square(key, part):
    key = jax.random.fold_in(key, 3)
    which = jnp.arange(10)
    factor = jnp.where((which == 3) | (which == 9), 4.0, 1.0) * float(D) ** (-0.5)
    raw_draw = jax.random.normal(key, (10, D, D), jnp.float32)
    return (raw_draw * factor[:, None, None]).astype(jnp.float32)


def draw_gains(key, part):
    key = jax.random.fold_in(key, 5)
    spot = jnp.arange(D).astype(jnp.float32) / float(D - 1)
    rising = 0.6 * jnp.power(3.0, spot)
    jitter = jnp.clip(0.1 * jax.random.normal(key, (6, D), jnp.float32), -0.3, 0.3)
    return (rising[None, :] * (1.0 + jitter)).astype(jnp.float32)


def shard_levels(rng, shape, cuts, least, largest):
    factor_of, own = 1.0, jax.random.fold_in(rng, 6)
    for axis_at, parts in cuts:
        heights = jnp.exp(jax.random.uniform(jax.random.fold_in(own, axis_at), (parts,), jnp.float32, least / len(cuts), largest / len(cuts)))
        factor_of = factor_of * jnp.repeat(heights, shape[axis_at] // parts).reshape([-1 if axis == axis_at else 1 for axis in range(len(shape))])
    return factor_of


def scatter_about(own_key, shape, spread, most, cuts=(), held_as=jnp.bfloat16):
    array = spread * jax.random.normal(own_key, shape, jnp.float32)
    if cuts:
        array = array * shard_levels(own_key, shape, cuts, -0.22, 0.18)
    return jnp.clip(array, -most, most).astype(held_as)


def setup_inputs(seed: int = 0) -> dict:
    streams_of = jax.random.split(jax.random.key(seed), 21)
    return {
        "inputs": scatter_about(streams_of[0], (DOCS, L, D), 1.0, 6.0, ((0, 8), (1, 4))),
        "dec_in": scatter_about(streams_of[1], (GROUPS, ROWS_DEV, D), 1.0, 6.0, ((0, 8), (1, 4))),
        "cotangent": scatter_about(streams_of[2], (GROUPS, ROWS_DEV, D), 1.0, 6.0, ((0, 8), (1, 4))),
        "lengths": draw_lengths(jax.random.fold_in(streams_of[20], 71), 0),
        "bucket_table": draw_bucket_table(jax.random.fold_in(streams_of[20], 71), 0),
        "square": draw_square(jax.random.fold_in(streams_of[20], 71), 0),
        "square_m": scatter_about(streams_of[6], (10, D, D), (2.8e-05), 0.0004272461, ((1, 32),), jnp.float32),
        "square_v": jnp.clip(jnp.exp(math.log(2.5999999375692084e-10) - 1.3862944 * jax.random.uniform(streams_of[7], (10, D, D), jnp.float32) ** shard_levels(streams_of[7], (10, D, D), ((1, 32),), -0.2, 0.2)), 6.499999843923021e-11, 2.5999999375692084e-10),
        "ffn_in": scatter_about(streams_of[8], (2, D, FF), D ** -0.5, 0.21875, ((1, 32),), jnp.float32),
        "ffn_in_m": scatter_about(streams_of[9], (2, D, FF), (2.8e-05), 0.0004272461, ((1, 32),), jnp.float32),
        "ffn_in_v": jnp.clip(jnp.exp(math.log(2.5999999375692084e-10) - 1.3862944 * jax.random.uniform(streams_of[10], (2, D, FF), jnp.float32) ** shard_levels(streams_of[10], (2, D, FF), ((1, 32),), -0.2, 0.2)), 6.499999843923021e-11, 2.5999999375692084e-10),
        "ffn_out": scatter_about(streams_of[11], (2, FF, D), FF ** -0.5, 0.109375, ((1, 32),), jnp.float32),
        "ffn_out_m": scatter_about(streams_of[12], (2, FF, D), (2.8e-05), 0.0004272461, ((1, 32),), jnp.float32),
        "ffn_out_v": jnp.clip(jnp.exp(math.log(2.5999999375692084e-10) - 1.3862944 * jax.random.uniform(streams_of[13], (2, FF, D), jnp.float32) ** shard_levels(streams_of[13], (2, FF, D), ((1, 32),), -0.2, 0.2)), 6.499999843923021e-11, 2.5999999375692084e-10),
        "gains": draw_gains(jax.random.fold_in(streams_of[20], 71), 0),
        "gains_m": scatter_about(streams_of[15], (6, D), (2.8e-05), 0.0004272461, ((1, 32),), jnp.float32),
        "gains_v": jnp.clip(jnp.exp(math.log(2.5999999375692084e-10) - 1.3862944 * jax.random.uniform(streams_of[16], (6, D), jnp.float32) ** shard_levels(streams_of[16], (6, D), ((1, 32),), -0.2, 0.2)), 6.499999843923021e-11, 2.5999999375692084e-10),
        "rel_bias": scatter_about(streams_of[17], (NB, H), 0.5, 3.0, (), jnp.float32),
        "rel_bias_m": scatter_about(streams_of[18], (NB, H), (2.8e-05), 0.0004272461, (), jnp.float32),
        "rel_bias_v": jnp.clip(jnp.exp(jax.random.uniform(streams_of[19], (NB, H), jnp.float32, math.log(6.499999843923021e-11), math.log(2.5999999375692084e-10))), 6.499999843923021e-11, 2.5999999375692084e-10),
    }


@jax.custom_vjp
def low(v):
    return lax.optimization_barrier(v.astype(jnp.bfloat16)).astype(jnp.float32)

@jax.custom_vjp
def low_back(v):
    return v

def low_keep(v):
    return (low(v), None)

def low_pass(kept, grad):
    return (grad,)

def back_keep(v):
    return (v, None)

def back_low(kept, grad):
    return (low(grad),)
low.defvjp(low_keep, low_pass)
low_back.defvjp(back_keep, back_low)
norm_eps = 1e-06
neg_fill = -1e+30
beta_one = 0.9
beta_two = 0.999
adam_eps = 1e-08
decay_rate = 0.01
rate_matrix = 0.05
rate_small = 0.5
clip_bound = 1.0
highest_precision = lax.Precision.HIGHEST

def both_ways(values_in):
    return low(low_back(values_in))

def rms_gain(values_in, gain_row):
    return values_in * lax.rsqrt(lax.optimization_barrier(jnp.mean(values_in * values_in, axis=-1, keepdims=True)) + norm_eps) * gain_row

def project(left, right):
    return jnp.einsum('...d,de->...e', left, right, precision=highest_precision)

def gelu_tanh(values_in):
    return jax.nn.gelu(values_in, approximate=True)

def group_layer(params, bucket_table, enc_rows, dec_rows, lengths):
    square, ffn_in, ffn_out, gains, rel_bias = params
    doc_count = enc_rows.shape[0]
    full_span = enc_rows.shape[1]
    hidden_width = enc_rows.shape[2]
    score_scale = 1.0 / math.sqrt(HD)
    positions = jnp.arange(full_span)
    offsets = positions[None, :] - positions[:, None] + full_span - 1
    bias_table = jnp.transpose(rel_bias[bucket_table[offsets]], (2, 0, 1))
    key_valid = positions[None, :] < lengths[:, None]
    normed = low(rms_gain(enc_rows, gains[0]))
    queries = both_ways(project(normed, square[0])).reshape(doc_count, full_span, H, HD)
    keys_all = both_ways(project(normed, square[1])).reshape(doc_count, full_span, H, HD)
    values_all = both_ways(project(normed, square[2])).reshape(doc_count, full_span, H, HD)
    raw_scores = jnp.einsum('gqhd,gkhd->ghqk', queries, keys_all, precision=highest_precision)
    scores = low_back(raw_scores * score_scale) + bias_table[None]
    scores = jnp.where(key_valid[:, None, None, :], scores, neg_fill)
    attn_probs = low(jax.nn.softmax(scores, axis=-1))
    attended = both_ways(jnp.einsum('ghqk,gkhd->gqhd', attn_probs, values_all, precision=highest_precision).reshape(doc_count, full_span, hidden_width))
    hidden = enc_rows + low_back(project(attended, square[3]))
    normed_two = low(rms_gain(hidden, gains[1]))
    inner_act = low(gelu_tanh(low_back(project(normed_two, ffn_in[0]))))
    hidden_two = hidden + low_back(project(inner_act, ffn_out[0]))
    encoded = low(rms_gain(hidden_two, gains[2]))
    cross_keys = both_ways(project(encoded, square[7])).reshape(doc_count, full_span, H, HD)
    cross_values = both_ways(project(encoded, square[8])).reshape(doc_count, full_span, H, HD)
    self_norm = low(rms_gain(dec_rows, gains[3]))
    self_values = both_ways(project(self_norm, square[4]))
    dec_one = dec_rows + low_back(project(self_values, square[5]))
    cross_norm = low(rms_gain(dec_one, gains[4]))
    cross_query = both_ways(project(cross_norm, square[6])).reshape(doc_count, H, HD)
    cross_raw = jnp.einsum('ghd,gkhd->ghk', cross_query, cross_keys, precision=highest_precision)
    cross_scores = jnp.where(key_valid[:, None, :], low_back(cross_raw * score_scale), neg_fill)
    cross_probs = low(jax.nn.softmax(cross_scores, axis=-1))
    cross_att = both_ways(jnp.einsum('ghk,gkhd->ghd', cross_probs, cross_values, precision=highest_precision).reshape(doc_count, hidden_width))
    dec_two = dec_one + low_back(project(cross_att, square[9]))
    ffn_norm = low(rms_gain(dec_two, gains[5]))
    inner_dec = low(gelu_tanh(low_back(project(ffn_norm, ffn_in[1]))))
    return dec_two + low_back(project(inner_dec, ffn_out[1]))

def adam_step(weight, first, second, grad, factor, rate, decay):
    grad = grad * factor
    first = beta_one * first + (1.0 - beta_one) * grad
    second = beta_two * second + (1.0 - beta_two) * grad * grad
    first_hat = first / (1.0 - beta_one ** STEP)
    second_hat = second / (1.0 - beta_two ** STEP)
    weight = weight - rate * (first_hat / (jnp.sqrt(second_hat) + adam_eps) + decay * weight)
    return (weight, first, second)

def reference(inputs, dec_in, cotangent, lengths, bucket_table, square, square_m, square_v, ffn_in, ffn_in_m, ffn_in_v, ffn_out, ffn_out_m, ffn_out_v, gains, gains_m, gains_v, rel_bias, rel_bias_m, rel_bias_v):
    block_docs = math.gcd(DOCS, max(1, 4096 // L))
    block_count = DOCS // block_docs
    dec_flat = dec_in.reshape(DOCS, D).astype(jnp.float32)

    def rounded(weight):
        return weight.astype(jnp.bfloat16).astype(jnp.float32)

    def forward(square_r, feedforward_input_rows, ffn_out_r, gains_r, bias_r, enc_flat):
        params = (square_r, feedforward_input_rows, ffn_out_r, gains_r, bias_r)

        def one_block(pieces):
            return group_layer(params, bucket_table, pieces[0], pieces[1], pieces[2])
        stacked = (enc_flat.reshape(block_count, block_docs, L, D), dec_flat.reshape(block_count, block_docs, D), lengths.reshape(block_count, block_docs))
        return lax.map(jax.checkpoint(one_block), stacked).reshape(DOCS, D)
    dec_out, pull = jax.vjp(forward, rounded(square), rounded(ffn_in), rounded(ffn_out), rounded(gains), rel_bias, inputs.astype(jnp.float32))
    grad_square, grad_in, grad_out, grad_gain, grad_bias, input_grad = pull(cotangent.reshape(DOCS, D).astype(jnp.float32))
    total = jnp.sum(grad_square * grad_square) + jnp.sum(grad_in * grad_in) + jnp.sum(grad_out * grad_out) + jnp.sum(grad_gain * grad_gain) + jnp.sum(grad_bias * grad_bias)
    grad_norm = jnp.sqrt(total)
    factor = clip_bound / jnp.maximum(grad_norm, clip_bound)
    square_new, square_m_new, square_v_new = adam_step(square, square_m, square_v, grad_square, factor, rate_matrix, decay_rate)
    ffn_in_new, ffn_in_m_new, ffn_in_v_new = adam_step(ffn_in, ffn_in_m, ffn_in_v, grad_in, factor, rate_matrix, decay_rate)
    ffn_out_new, ffn_out_m_new, ffn_out_v_new = adam_step(ffn_out, ffn_out_m, ffn_out_v, grad_out, factor, rate_matrix, decay_rate)
    gains_new, gains_m_new, gains_v_new = adam_step(gains, gains_m, gains_v, grad_gain, factor, rate_small, 0.0)
    rel_bias_new, rel_bias_m_new, rel_bias_v_new = adam_step(rel_bias, rel_bias_m, rel_bias_v, grad_bias, factor, rate_small, 0.0)
    return (dec_out.astype(jnp.bfloat16).reshape(GROUPS, ROWS_DEV, D), input_grad, grad_norm, square_new, square_m_new, square_v_new, ffn_in_new, ffn_in_m_new, ffn_in_v_new, ffn_out_new, ffn_out_m_new, ffn_out_v_new, gains_new, gains_m_new, gains_v_new, rel_bias_new, rel_bias_m_new, rel_bias_v_new)
```

```python
import functools
import math

import jax
import jax.numpy as jnp
from jax import lax
from jax.experimental import pallas as pl
from jax.experimental.pallas import tpu as pltpu
from jax.sharding import PartitionSpec as P

H = 12
HD = 64
STEP = 5
AXES = ("dp", "seq", "head")

norm_eps = 1e-06
neg_fill = -1e30
beta_one = 0.9
beta_two = 0.999
adam_eps = 1e-08
decay_rate = 0.01
rate_matrix = 0.05
rate_small = 0.5
clip_bound = 1.0
highest_precision = lax.Precision.HIGHEST
bf16 = jnp.bfloat16
f32 = jnp.float32
BAND = 128


def rms_gain(values_in, gain_row):
    return (
        values_in
        * lax.rsqrt(jnp.mean(values_in * values_in, axis=-1, keepdims=True) + norm_eps)
        * gain_row
    )


def gelu_tanh(values_in):
    return jax.nn.gelu(values_in, approximate=True)


def matmul(left, right):
    return jnp.dot(left, right, preferred_element_type=f32)


def mm_t(left, right):
    return lax.dot_general(left, right, (((1,), (1,)), ((), ())), preferred_element_type=f32)


def mm_outer(left, right):
    return lax.dot_general(left, right, (((0,), (0,)), ((), ())), preferred_element_type=f32)


def rms_pull(values_in, gain_row, incoming):
    _, pull = jax.vjp(rms_gain, values_in, gain_row)
    return pull(incoming)


def gelu_pull(values_in, incoming):
    _, pull = jax.vjp(gelu_tanh, values_in)
    return pull(incoming)[0]


def adam_step(weight, first, second, grad, factor, rate, decay):
    grad = grad * factor
    first = beta_one * first + (1.0 - beta_one) * grad
    second = beta_two * second + (1.0 - beta_two) * grad * grad
    first_hat = first / (1.0 - beta_one**STEP)
    second_hat = second / (1.0 - beta_two**STEP)
    weight = weight - rate * (first_hat / (jnp.sqrt(second_hat) + adam_eps) + decay * weight)
    return (weight, first, second)


def bias_band(table_row, span):
    wide = jnp.broadcast_to(table_row, (BAND, 2 * span))
    shift = (2 * span - (BAND - 1)) % (2 * span)
    return pltpu.roll(wide, shift, 1, stride=1, stride_axis=0)


def band_sums(band, span):
    wide = 2 * span
    rows = BAND
    while rows > 8:
        rows //= 2
        band = band[:rows] + pltpu.roll(band[rows:], wide - rows, 1)
    row = lax.broadcasted_iota(jnp.int32, band.shape, 0)
    for step in (4, 2, 1):
        band = jnp.where((row // step) % 2 == 1, pltpu.roll(band, wide - step, 1), band)
    return pltpu.roll(jnp.sum(band, axis=0, keepdims=True), BAND - 1, 1)


def softmax_rows(q_rows, k_all, band, block, span, valid):
    start = span - BAND * (block + 1)
    scores = mm_t(q_rows, k_all) * (1.0 / math.sqrt(HD)) + band[:, start : start + span]
    scores = jnp.where(valid, scores, neg_fill)
    peak = jnp.max(scores, axis=-1, keepdims=True)
    raised = jnp.exp(scores - peak)
    return raised / jnp.sum(raised, axis=-1, keepdims=True)


def attend_fwd_kernel(len_ref, table_ref, q_ref, k_ref, v_ref, o_ref):
    span = k_ref.shape[0]
    valid = lax.broadcasted_iota(jnp.int32, (1, span), 1) < len_ref[0]
    lane = lax.broadcasted_iota(jnp.int32, (1, 2 * HD), 1)
    k_all = k_ref[...]
    v_all = v_ref[...]
    bands = [bias_band(table_ref[t], span) for t in range(2)]
    for block in range(span // BAND):
        rows = slice(block * BAND, (block + 1) * BAND)
        q_rows = q_ref[rows, :]
        parts = []
        for t in range(2):
            own = (lane // HD) == t
            probs = softmax_rows(
                jnp.where(own, q_rows, jnp.zeros_like(q_rows)), k_all, bands[t], block, span, valid
            )
            parts.append(matmul(probs.astype(bf16), v_all))
        o_ref[rows, :] = jnp.where(lane < HD, parts[0], parts[1]).astype(bf16)


def attend_bwd_kernel(
    len_ref, table_ref, q_ref, k_ref, v_ref, do_ref, dq_ref, dk_ref, dv_ref, dt_ref
):
    span = k_ref.shape[0]
    scale = 1.0 / math.sqrt(HD)
    valid = lax.broadcasted_iota(jnp.int32, (1, span), 1) < len_ref[0]
    lane = lax.broadcasted_iota(jnp.int32, (1, 2 * HD), 1)
    k_all = k_ref[...]
    v_all = v_ref[...]
    count = span // BAND
    dks, dvs = [], []
    dqs = [[None, None] for _ in range(count)]
    for t in range(2):
        own = (lane // HD) == t
        band = bias_band(table_ref[t], span)
        dk = jnp.zeros((span, 2 * HD), f32)
        dv = jnp.zeros((span, 2 * HD), f32)
        dband = jnp.zeros((BAND, 2 * span), f32)
        for block in range(count):
            rows = slice(block * BAND, (block + 1) * BAND)
            q_rows = q_ref[rows, :]
            do_rows = do_ref[rows, :]
            zero = jnp.zeros_like(q_rows)
            probs = softmax_rows(
                jnp.where(own, q_rows, zero), k_all, band, block, span, valid
            )
            dprobs = mm_t(jnp.where(own, do_rows, zero), v_all)
            dscore = probs * (dprobs - jnp.sum(dprobs * probs, axis=-1, keepdims=True))
            start = span - BAND * (block + 1)
            pieces = []
            if start:
                pieces.append(jnp.zeros((BAND, start), f32))
            pieces.append(dscore)
            if span - start:
                pieces.append(jnp.zeros((BAND, span - start), f32))
            dband = dband + jnp.concatenate(pieces, axis=1)
            dscore_b = dscore.astype(bf16)
            dv = dv + mm_outer(probs.astype(bf16), do_rows)
            dk = dk + mm_outer(dscore_b, q_rows)
            dqs[block][t] = matmul(dscore_b, k_all)
        dks.append(dk)
        dvs.append(dv)
        dt_ref[t] = band_sums(dband, span)
    dk_ref[...] = (jnp.where(lane < HD, dks[0], dks[1]) * scale).astype(bf16)
    dv_ref[...] = jnp.where(lane < HD, dvs[0], dvs[1]).astype(bf16)
    for block in range(count):
        rows = slice(block * BAND, (block + 1) * BAND)
        dq_ref[rows, :] = (jnp.where(lane < HD, dqs[block][0], dqs[block][1]) * scale).astype(bf16)


def head_specs(span, width, n):
    return [pl.BlockSpec((span, 2 * HD), lambda i: (0, i)) for _ in range(n)]


def attend_fwd(length, table, q, k, v):
    span, width = q.shape
    return pl.pallas_call(
        attend_fwd_kernel,
        grid=(width // (2 * HD),),
        out_shape=jax.ShapeDtypeStruct((span, width), bf16),
        in_specs=[
            pl.BlockSpec(memory_space=pltpu.SMEM),
            pl.BlockSpec((2, 1, 2 * span), lambda i: (i, 0, 0)),
            *head_specs(span, width, 3),
        ],
        out_specs=head_specs(span, width, 1)[0],
        compiler_params=pltpu.CompilerParams(vmem_limit_bytes=48 * 1024 * 1024),
        name="attend_fwd",
    )(length, table, q, k, v)


def attend_bwd(length, table, q, k, v, do):
    span, width = q.shape
    like = jax.ShapeDtypeStruct((span, width), bf16)
    return pl.pallas_call(
        attend_bwd_kernel,
        grid=(width // (2 * HD),),
        out_shape=(like, like, like, jax.ShapeDtypeStruct(table.shape, f32)),
        in_specs=[
            pl.BlockSpec(memory_space=pltpu.SMEM),
            pl.BlockSpec((2, 1, 2 * span), lambda i: (i, 0, 0)),
            *head_specs(span, width, 4),
        ],
        out_specs=(
            *head_specs(span, width, 3),
            pl.BlockSpec((2, 1, 2 * span), lambda i: (i, 0, 0)),
        ),
        compiler_params=pltpu.CompilerParams(vmem_limit_bytes=48 * 1024 * 1024),
        name="attend_bwd",
    )(length, table, q, k, v, do)


def on_device(
    inputs,
    dec_in,
    cotangent,
    lengths,
    bucket_table,
    square,
    square_m,
    square_v,
    ffn_in,
    ffn_in_m,
    ffn_in_v,
    ffn_out,
    ffn_out_m,
    ffn_out_v,
    gains,
    gains_m,
    gains_v,
    rel_bias,
    rel_bias_m,
    rel_bias_v,
):
    def gather_rows(x):
        return lax.all_gather(x.astype(bf16), AXES, axis=x.ndim - 2, tiled=True)

    sq_a = gather_rows(square[:4])
    w_in_e = gather_rows(ffn_in[0])
    w_out_e = gather_rows(ffn_out[0])
    sq_b = gather_rows(jnp.stack([square[i] for i in (7, 8, 4, 5, 6, 9)]))
    w_in_d = gather_rows(ffn_in[1])
    w_out_d = gather_rows(ffn_out[1])
    gain_f = lax.all_gather(gains.astype(bf16), AXES, axis=1, tiled=True).astype(f32)
    w = {0: sq_a[0], 1: sq_a[1], 2: sq_a[2], 3: sq_a[3]}
    for n, i in enumerate((7, 8, 4, 5, 6, 9)):
        w[i] = sq_b[n]

    seq_pos = lax.axis_index("seq")
    local_len, width = inputs.shape[1:]
    span = local_len * lax.axis_size("seq")
    bucket_count = rel_bias.shape[0]
    scale = 1.0 / math.sqrt(HD)
    x_b = lax.all_to_all(inputs, "seq", split_axis=0, concat_axis=1, tiled=True)[0]
    x_f = x_b.astype(f32)
    length = lax.dynamic_slice_in_dim(lengths, seq_pos, 1, 0)
    key_valid = jnp.arange(span)[None, :] < length[:, None]
    one_hot = (
        jnp.pad(bucket_table, (0, 1), constant_values=-1)[:, None]
        == jnp.arange(bucket_count)[None, :]
    ).astype(f32)
    table = jnp.einsum("ob,bh->ho", one_hot, rel_bias, precision=highest_precision)[:, None, :]

    normed = rms_gain(x_f, gain_f[0]).astype(bf16)
    q = matmul(normed, w[0]).astype(bf16)
    k = matmul(normed, w[1]).astype(bf16)
    v = matmul(normed, w[2]).astype(bf16)
    attended = attend_fwd(length, table, q, k, v)
    hidden = x_f + matmul(attended, w[3])
    normed_two = rms_gain(hidden, gain_f[1]).astype(bf16)
    pre_act = matmul(normed_two, w_in_e)
    inner_act = gelu_tanh(pre_act).astype(bf16)
    hidden_two = hidden + matmul(inner_act, w_out_e)
    encoded = rms_gain(hidden_two, gain_f[2]).astype(bf16)
    cross_k = matmul(encoded, w[7]).astype(bf16)
    cross_v = matmul(encoded, w[8]).astype(bf16)

    dec_row = dec_in.reshape(1, width).astype(f32)
    self_norm = rms_gain(dec_row, gain_f[3]).astype(bf16)
    self_values = matmul(self_norm, w[4]).astype(bf16)
    dec_one = dec_row + matmul(self_values, w[5])
    cross_norm = rms_gain(dec_one, gain_f[4]).astype(bf16)
    cross_q = matmul(cross_norm, w[6]).astype(bf16)
    head_of = (jnp.arange(width)[None, :] // HD == jnp.arange(H)[:, None]).astype(bf16)
    q_heads = head_of * cross_q
    cross_scores = jnp.where(key_valid, mm_t(q_heads, cross_k) * scale, neg_fill)
    cross_probs = jax.nn.softmax(cross_scores, axis=-1)
    cross_probs_b = cross_probs.astype(bf16)
    cross_att = jnp.sum(
        matmul(cross_probs_b, cross_v) * head_of.astype(f32), axis=0, keepdims=True
    ).astype(bf16)
    dec_two = dec_one + matmul(cross_att, w[9])
    ffn_norm = rms_gain(dec_two, gain_f[5]).astype(bf16)
    pre_dec = matmul(ffn_norm, w_in_d)
    inner_dec = gelu_tanh(pre_dec).astype(bf16)
    dec_out = dec_two + matmul(inner_dec, w_out_d)

    g_top_b = cotangent.reshape(1, width)
    g_top = g_top_b.astype(f32)
    g_pre_dec = gelu_pull(pre_dec, mm_t(g_top_b, w_out_d)).astype(bf16)
    g_two_norm, g_gain_five = rms_pull(dec_two, gain_f[5], mm_t(g_pre_dec, w_in_d))
    g_two = g_top + g_two_norm
    g_two_b = g_two.astype(bf16)
    g_att = mm_t(g_two_b, w[9]).astype(bf16)
    g_att_heads = head_of * g_att
    g_probs = mm_t(g_att_heads, cross_v)
    g_cross_v = mm_outer(cross_probs_b, g_att_heads).astype(bf16)
    g_scores = cross_probs * (g_probs - jnp.sum(g_probs * cross_probs, axis=-1, keepdims=True))
    g_scores_b = g_scores.astype(bf16)
    g_cross_q = (
        jnp.sum(matmul(g_scores_b, cross_k) * head_of.astype(f32), axis=0, keepdims=True) * scale
    ).astype(bf16)
    g_cross_k = (mm_outer(g_scores_b, q_heads) * scale).astype(bf16)
    g_one_norm, g_gain_four = rms_pull(dec_one, gain_f[4], mm_t(g_cross_q, w[6]))
    g_one_b = (g_two + g_one_norm).astype(bf16)
    g_self_values = mm_t(g_one_b, w[5]).astype(bf16)
    g_gain_three = rms_pull(dec_row, gain_f[3], mm_t(g_self_values, w[4]))[1]

    lefts = (self_norm, self_values, cross_norm, cross_att, ffn_norm, inner_dec)
    rights = (g_self_values, g_one_b, g_cross_q, g_two_b, g_pre_dec, g_top_b)
    packed = lax.all_gather(jnp.concatenate(lefts + rights, axis=1), AXES, axis=0, tiled=True)
    me = (
        lax.axis_index("dp") * lax.axis_size("seq") + seq_pos
    ) * lax.axis_size("head") + lax.axis_index("head")
    devices = packed.shape[0]
    cuts = [0]
    for piece in lefts + rights:
        cuts.append(cuts[-1] + piece.shape[1])
    dec_grads = []
    for n in range(6):
        share = lefts[n].shape[1] // devices
        left = lax.dynamic_slice_in_dim(packed, cuts[n] + me * share, share, 1)
        right = packed[:, cuts[6 + n] : cuts[7 + n]]
        dec_grads.append(mm_outer(left, right))

    g_w7 = mm_outer(encoded, g_cross_k)
    g_w8 = mm_outer(encoded, g_cross_v)
    g_encoded = mm_t(g_cross_k, w[7]) + mm_t(g_cross_v, w[8])
    g_hidden_two, g_gain_two = rms_pull(hidden_two, gain_f[2], g_encoded)
    g_hidden_two_b = g_hidden_two.astype(bf16)
    g_out_e = mm_outer(inner_act, g_hidden_two_b)
    g_pre = gelu_pull(pre_act, mm_t(g_hidden_two_b, w_out_e)).astype(bf16)
    g_in_e = mm_outer(normed_two, g_pre)
    g_hidden_norm, g_gain_one = rms_pull(hidden, gain_f[1], mm_t(g_pre, w_in_e))
    g_hidden = g_hidden_two + g_hidden_norm
    g_hidden_b = g_hidden.astype(bf16)
    g_w3 = mm_outer(attended, g_hidden_b)
    g_attended = mm_t(g_hidden_b, w[3]).astype(bf16)
    gq, gk, gv, g_table = attend_bwd(length, table, q, k, v, g_attended)
    g_bias_here = jnp.einsum("ob,ho->bh", one_hot, g_table[:, 0, :], precision=highest_precision)
    g_w0 = mm_outer(normed, gq)
    g_w1 = mm_outer(normed, gk)
    g_w2 = mm_outer(normed, gv)
    g_normed = mm_t(gq, w[0]) + mm_t(gk, w[1]) + mm_t(gv, w[2])
    g_input_norm, g_gain_zero = rms_pull(x_f, gain_f[0], g_normed)
    g_x = (g_hidden + g_input_norm).astype(bf16)
    input_grad = lax.all_to_all(g_x[None], "seq", split_axis=1, concat_axis=0, tiled=True).astype(
        f32
    )

    def scatter_rows(x):
        return lax.psum_scatter(
            x.astype(bf16), AXES, scatter_dimension=x.ndim - 2, tiled=True
        ).astype(f32)

    s_78 = scatter_rows(jnp.stack((g_w7, g_w8)))
    s_out = scatter_rows(g_out_e)
    s_in = scatter_rows(g_in_e)
    s_0123 = scatter_rows(jnp.stack((g_w0, g_w1, g_w2, g_w3)))
    summed_sq = jnp.stack(
        (
            s_0123[0],
            s_0123[1],
            s_0123[2],
            s_0123[3],
            dec_grads[0],
            dec_grads[1],
            dec_grads[2],
            s_78[0],
            s_78[1],
            dec_grads[3],
        )
    )
    summed_in = jnp.stack((s_in, dec_grads[4]))
    summed_out = jnp.stack((s_out, dec_grads[5]))
    g_gains = jnp.stack(
        (g_gain_zero, g_gain_one, g_gain_two, g_gain_three, g_gain_four, g_gain_five)
    )
    g_gains, g_bias = lax.psum((g_gains, g_bias_here), AXES)
    gain_share = gains.shape[1]
    summed_gain = lax.dynamic_slice_in_dim(g_gains, me * gain_share, gain_share, 1)
    local_squares = (
        jnp.sum(summed_sq * summed_sq)
        + jnp.sum(summed_in * summed_in)
        + jnp.sum(summed_out * summed_out)
    )
    shard_squares = lax.psum(local_squares, AXES)
    grad_norm = jnp.sqrt(shard_squares + jnp.sum(g_gains * g_gains) + jnp.sum(g_bias * g_bias))
    factor = clip_bound / jnp.maximum(grad_norm, clip_bound)
    return (
        dec_out.astype(bf16).reshape(dec_in.shape),
        input_grad,
        grad_norm,
        *adam_step(square, square_m, square_v, summed_sq, factor, rate_matrix, decay_rate),
        *adam_step(ffn_in, ffn_in_m, ffn_in_v, summed_in, factor, rate_matrix, decay_rate),
        *adam_step(ffn_out, ffn_out_m, ffn_out_v, summed_out, factor, rate_matrix, decay_rate),
        *adam_step(gains, gains_m, gains_v, summed_gain, factor, rate_small, 0.0),
        *adam_step(rel_bias, rel_bias_m, rel_bias_v, g_bias, factor, rate_small, 0.0),
    )


def solution(mesh):
    rows = P(("dp", "head"), "seq", None)
    shard = P(None, AXES, None)
    small = P(None, AXES)
    return jax.shard_map(
        on_device,
        mesh=mesh,
        in_specs=(rows, rows, rows, P(("dp", "head")), P())
        + (shard,) * 9
        + (small,) * 3
        + (P(),) * 3,
        out_specs=(rows, rows, P()) + (shard,) * 9 + (small,) * 3 + (P(),) * 3,
        check_vma=False,
    )
```

```python
import functools
import math

import jax
import jax.numpy as jnp
from jax import lax
from jax.experimental import pallas as pl
from jax.experimental.pallas import tpu as pltpu
from jax.sharding import PartitionSpec as P

H = 12
HD = 64
STEP = 5
AXES = ("dp", "seq", "head")

norm_eps = 1e-06
neg_fill = -1e30
beta_one = 0.9
beta_two = 0.999
adam_eps = 1e-08
decay_rate = 0.01
rate_matrix = 0.05
rate_small = 0.5
clip_bound = 1.0
highest_precision = lax.Precision.HIGHEST
bf16 = jnp.bfloat16
f32 = jnp.float32
BAND = 128


def rms_gain(values_in, gain_row):
    return (
        values_in
        * lax.rsqrt(jnp.mean(values_in * values_in, axis=-1, keepdims=True) + norm_eps)
        * gain_row
    )


def gelu_tanh(values_in):
    return jax.nn.gelu(values_in, approximate=True)


def matmul(left, right):
    return jnp.dot(left, right, preferred_element_type=f32)


def mm_t(left, right):
    return lax.dot_general(left, right, (((1,), (1,)), ((), ())), preferred_element_type=f32)


def mm_outer(left, right):
    return lax.dot_general(left, right, (((0,), (0,)), ((), ())), preferred_element_type=f32)


def rms_pull(values_in, gain_row, incoming):
    _, pull = jax.vjp(rms_gain, values_in, gain_row)
    return pull(incoming)


def gelu_pull(values_in, incoming):
    _, pull = jax.vjp(gelu_tanh, values_in)
    return pull(incoming)[0]


def adam_step(weight, first, second, grad, factor, rate, decay):
    grad = grad * factor
    first = beta_one * first + (1.0 - beta_one) * grad
    second = beta_two * second + (1.0 - beta_two) * grad * grad
    first_hat = first / (1.0 - beta_one**STEP)
    second_hat = second / (1.0 - beta_two**STEP)
    weight = weight - rate * (first_hat / (jnp.sqrt(second_hat) + adam_eps) + decay * weight)
    return (weight, first, second)


def bias_band(table_row, span):
    wide = jnp.broadcast_to(table_row, (BAND, 2 * span))
    shift = (2 * span - (BAND - 1)) % (2 * span)
    return pltpu.roll(wide, shift, 1, stride=1, stride_axis=0)


def band_sums(band, span):
    wide = 2 * span
    rows = BAND
    while rows > 8:
        rows //= 2
        band = band[:rows] + pltpu.roll(band[rows:], wide - rows, 1)
    row = lax.broadcasted_iota(jnp.int32, band.shape, 0)
    for step in (4, 2, 1):
        band = jnp.where((row // step) % 2 == 1, pltpu.roll(band, wide - step, 1), band)
    return pltpu.roll(jnp.sum(band, axis=0, keepdims=True), BAND - 1, 1)


def softmax_rows(q_rows, k_all, band, block, span, valid):
    start = span - BAND * (block + 1)
    scores = mm_t(q_rows, k_all) * (1.0 / math.sqrt(HD)) + band[:, start : start + span]
    scores = jnp.where(valid, scores, neg_fill)
    peak = jnp.max(scores, axis=-1, keepdims=True)
    raised = jnp.exp(scores - peak)
    return raised / jnp.sum(raised, axis=-1, keepdims=True)


def attend_fwd_kernel(len_ref, table_ref, q_ref, k_ref, v_ref, o_ref):
    span = k_ref.shape[0]
    valid = lax.broadcasted_iota(jnp.int32, (1, span), 1) < len_ref[0]
    lane = lax.broadcasted_iota(jnp.int32, (1, 2 * HD), 1)
    k_all = k_ref[...]
    v_all = v_ref[...]
    bands = [bias_band(table_ref[t], span) for t in range(2)]
    for block in range(span // BAND):
        rows = slice(block * BAND, (block + 1) * BAND)
        q_rows = q_ref[rows, :]
        parts = []
        for t in range(2):
            own = (lane // HD) == t
            probs = softmax_rows(
                jnp.where(own, q_rows, jnp.zeros_like(q_rows)), k_all, bands[t], block, span, valid
            )
            parts.append(matmul(probs.astype(bf16), v_all))
        o_ref[rows, :] = jnp.where(lane < HD, parts[0], parts[1]).astype(bf16)


def attend_bwd_kernel(
    len_ref, table_ref, q_ref, k_ref, v_ref, do_ref, dq_ref, dk_ref, dv_ref, dt_ref
):
    span = k_ref.shape[0]
    scale = 1.0 / math.sqrt(HD)
    valid = lax.broadcasted_iota(jnp.int32, (1, span), 1) < len_ref[0]
    lane = lax.broadcasted_iota(jnp.int32, (1, 2 * HD), 1)
    k_all = k_ref[...]
    v_all = v_ref[...]
    count = span // BAND
    dks, dvs = [], []
    dqs = [[None, None] for _ in range(count)]
    for t in range(2):
        own = (lane // HD) == t
        band = bias_band(table_ref[t], span)
        dk = jnp.zeros((span, 2 * HD), f32)
        dv = jnp.zeros((span, 2 * HD), f32)
        dband = jnp.zeros((BAND, 2 * span), f32)
        for block in range(count):
            rows = slice(block * BAND, (block + 1) * BAND)
            q_rows = q_ref[rows, :]
            do_rows = do_ref[rows, :]
            zero = jnp.zeros_like(q_rows)
            probs = softmax_rows(
                jnp.where(own, q_rows, zero), k_all, band, block, span, valid
            )
            dprobs = mm_t(jnp.where(own, do_rows, zero), v_all)
            dscore = probs * (dprobs - jnp.sum(dprobs * probs, axis=-1, keepdims=True))
            start = span - BAND * (block + 1)
            pieces = []
            if start:
                pieces.append(jnp.zeros((BAND, start), f32))
            pieces.append(dscore)
            if span - start:
                pieces.append(jnp.zeros((BAND, span - start), f32))
            dband = dband + jnp.concatenate(pieces, axis=1)
            dscore_b = dscore.astype(bf16)
            dv = dv + mm_outer(probs.astype(bf16), do_rows)
            dk = dk + mm_outer(dscore_b, q_rows)
            dqs[block][t] = matmul(dscore_b, k_all)
        dks.append(dk)
        dvs.append(dv)
        dt_ref[t] = band_sums(dband, span)
    dk_ref[...] = (jnp.where(lane < HD, dks[0], dks[1]) * scale).astype(bf16)
    dv_ref[...] = jnp.where(lane < HD, dvs[0], dvs[1]).astype(bf16)
    for block in range(count):
        rows = slice(block * BAND, (block + 1) * BAND)
        dq_ref[rows, :] = (jnp.where(lane < HD, dqs[block][0], dqs[block][1]) * scale).astype(bf16)


def head_specs(span, width, n):
    return [pl.BlockSpec((span, 2 * HD), lambda i: (0, i)) for _ in range(n)]


def attend_fwd(length, table, q, k, v):
    span, width = q.shape
    return pl.pallas_call(
        attend_fwd_kernel,
        grid=(width // (2 * HD),),
        out_shape=jax.ShapeDtypeStruct((span, width), bf16),
        in_specs=[
            pl.BlockSpec(memory_space=pltpu.SMEM),
            pl.BlockSpec((2, 1, 2 * span), lambda i: (i, 0, 0)),
            *head_specs(span, width, 3),
        ],
        out_specs=head_specs(span, width, 1)[0],
        compiler_params=pltpu.CompilerParams(vmem_limit_bytes=48 * 1024 * 1024),
        name="attend_fwd",
    )(length, table, q, k, v)


def attend_bwd(length, table, q, k, v, do):
    span, width = q.shape
    like = jax.ShapeDtypeStruct((span, width), bf16)
    return pl.pallas_call(
        attend_bwd_kernel,
        grid=(width // (2 * HD),),
        out_shape=(like, like, like, jax.ShapeDtypeStruct(table.shape, f32)),
        in_specs=[
            pl.BlockSpec(memory_space=pltpu.SMEM),
            pl.BlockSpec((2, 1, 2 * span), lambda i: (i, 0, 0)),
            *head_specs(span, width, 4),
        ],
        out_specs=(
            *head_specs(span, width, 3),
            pl.BlockSpec((2, 1, 2 * span), lambda i: (i, 0, 0)),
        ),
        compiler_params=pltpu.CompilerParams(vmem_limit_bytes=48 * 1024 * 1024),
        name="attend_bwd",
    )(length, table, q, k, v, do)


MESH_ID = pl.DeviceIdType.MESH
HALF = 384
ROWS = 48
MIB = 1024 * 1024


def place():
    z, s, c = lax.axis_index("dp"), lax.axis_index("seq"), lax.axis_index("head")
    near = s + 1 - 2 * (s % 2)
    far = (s + 2) % 4
    first = near + c * (far - near)
    second = far + c * (near - far)
    return z, s, c, first, second, 3 - s


def greet(z, s, c, z_count):
    barrier = pltpu.get_barrier_semaphore()
    for d in range(1, z_count):
        peer = ((z + d) % z_count, s, c)
        pl.semaphore_signal(barrier, 1, device_id=peer, device_id_type=MESH_ID)
    for d in range(1, 4):
        peer = (z, (s + d) % 4, c)
        pl.semaphore_signal(barrier, 1, device_id=peer, device_id_type=MESH_ID)
    pl.semaphore_signal(barrier, 1, device_id=(z, s, 1 - c), device_id_type=MESH_ID)
    pl.semaphore_wait(barrier, z_count + 3)


def remote(src, dst, send, recv, peer):
    return pltpu.make_async_remote_copy(
        src, dst, send, recv, device_id=peer, device_id_type=MESH_ID
    )


def cols(c, base=0):
    return pl.ds(pl.multiple_of(base + c * HALF, 128), HALF)


def unit_view(kind, n, ref, z, s, c):
    if kind == "square":
        return ref.at[n, z, s, :, cols(c)]
    if kind == "cols":
        return ref.at[n // 4, z, s, :, cols(c, (n % 4) * 2 * HALF)]
    if kind == "rows":
        return ref.at[n // 4, z, s, pl.ds((n % 4) * ROWS, ROWS), cols(c)]
    return ref.at[z, s]


class Gather:
    def __init__(self, units, refs, send, recv, z_count):
        self.units, self.refs, self.send, self.recv = units, refs, send, recv
        self.z_count = z_count
        self.where = place()
        self.started = []

    def view(self, u, z, s, c):
        kind, n = self.units[u]
        return unit_view(kind, n, self.refs[kind], z, s, c)

    def go(self, u, slot, ref, peer):
        copy = remote(ref, ref, self.send.at[u, slot], self.recv.at[u, slot], peer)
        copy.start()
        self.started.append(copy)

    def got(self, u, slot, ref):
        z, s, c = self.where[:3]
        remote(ref, ref, self.send.at[u, slot], self.recv.at[u, slot], (z, s, 1 - c)).wait_recv()

    def z_start(self, u):
        z, s, c = self.where[:3]
        for d in range(1, self.z_count):
            self.go(u, d - 1, self.view(u, z, s, c), ((z + d) % self.z_count, s, c))

    def z_wait(self, u):
        z, s, c = self.where[:3]
        for d in range(1, self.z_count):
            self.got(u, d - 1, self.view(u, (z + self.z_count - d) % self.z_count, s, c))

    def a_start(self, u):
        z, s, c, first, second, both = self.where
        self.go(u, 3, self.view(u, slice(None), s, c), (z, first, c))

    def a_wait(self, u):
        z, s, c, first, second, both = self.where
        self.got(u, 3, self.view(u, slice(None), first, c))

    def b_start(self, u):
        z, s, c, first, second, both = self.where
        self.go(u, 4, self.view(u, slice(None), s, c), (z, second, c))
        self.go(u, 5, self.view(u, slice(None), first, c), (z, second, c))

    def b_wait(self, u):
        z, s, c, first, second, both = self.where
        self.got(u, 4, self.view(u, slice(None), second, c))
        self.got(u, 5, self.view(u, slice(None), both, c))

    def s_start(self, u):
        z, s, c = self.where[:3]
        if self.units[u][0] != "gain":
            self.go(u, 6, self.view(u, slice(None), slice(None), c), (z, s, 1 - c))

    def s_wait(self, u):
        z, s, c = self.where[:3]
        if self.units[u][0] != "gain":
            self.got(u, 6, self.view(u, slice(None), slice(None), 1 - c))

    def tick(self, t, skew=2, done=None):
        steps = (
            (self.z_start,),
            (self.z_wait, self.a_start),
            (self.a_wait, self.b_start),
            (self.b_wait, self.s_start),
            (self.s_wait,) + ((done,) if done else ()),
        )
        for n, work in enumerate(steps):
            u = t - n * skew
            if 0 <= u < len(self.units):
                for step in work:
                    step(u)

    def finish(self):
        for copy in self.started:
            copy.wait_send()


def gather_kernel(
    units, z_count, sq_ref, in_ref, out_ref, gain_ref, x_ref,
    sq_o, in_o, out_o, gain_o, x_o,
    sq_w, in_w, out_w, gain_w, sq_r, in_r, out_r, gain_r,
    send, recv, first_send, first_recv, x_send, x_recv, local,
):
    z, s, c = place()[:3]
    sibling = (z, s, 1 - c)
    n_sq, n_ff = sq_ref.shape[0], in_ref.shape[0]
    greet(z, s, c, z_count)

    first = []

    def to_sibling(src, dst):
        copy = remote(src, dst, first_send.at[len(first)], first_recv.at[len(first)], sibling)
        copy.start()
        first.append(copy)

    to_sibling(gain_ref, gain_r)
    to_sibling(sq_ref.at[:, :, cols(1 - c)], sq_r)
    for n in range(n_ff):
        for j in range(4):
            to_sibling(in_ref.at[n, :, cols(1 - c, 2 * HALF * j)], in_r.at[n, j])
        to_sibling(out_ref.at[n, :, cols(1 - c)], out_r.at[n])
    x_copies = []
    for d in range(1, 4):
        peer = (s + d) % 4
        copy = remote(
            x_ref.at[peer], x_o.at[s], x_send.at[d - 1], x_recv.at[d - 1], (z, peer, c)
        )
        copy.start()
        x_copies.append(copy)
    mine = pltpu.make_async_copy(x_ref.at[s], x_o.at[s], local.at[0])
    mine.start()

    def joined(own, other):
        top = jnp.where(c == 0, own, other)
        bottom = jnp.where(c == 0, other, own)
        return jnp.concatenate([top, bottom], axis=0).astype(bf16)

    first[0].wait_recv()
    gain_w[z, s] = joined(gain_ref[...], gain_r[...])
    first[1].wait_recv()
    for n in range(n_sq):
        sq_w[n, z, s, :, cols(c)] = joined(sq_ref[n, :, cols(c)], sq_r[n])
    k = 2
    for n in range(n_ff):
        for j in range(4):
            first[k].wait_recv()
            k += 1
            at = cols(c, 2 * HALF * j)
            in_w[n, z, s, :, at] = joined(in_ref[n, :, at], in_r[n, j])
        first[k].wait_recv()
        k += 1
        out_w[n, z, s, :, cols(c)] = joined(out_ref[n, :, cols(c)], out_r[n])

    gather = Gather(
        units,
        {"square": sq_w, "cols": in_w, "rows": out_w, "gain": gain_w},
        send,
        recv,
        z_count,
    )
    outs = {"square": sq_o, "cols": in_o, "rows": out_o, "gain": gain_o}
    drains = []

    def done(u):
        kind, n = units[u]
        if kind == "square":
            src, dst = sq_w.at[n], sq_o.at[n]
        elif kind == "gain":
            src, dst = gain_w, gain_o
        elif n % 4 != 3:
            return
        elif kind == "cols":
            src, dst = in_w.at[n // 4], in_o.at[n // 4]
        else:
            src, dst = out_w.at[n // 4], out_o.at[n // 4]
        copy = pltpu.make_async_copy(src, dst, local.at[1 + len(drains)])
        copy.start()
        drains.append(copy)

    del outs
    skew = 2
    for t in range(len(units) + 4 * skew):
        gather.tick(t, skew, done)
    gather.finish()
    for copy in first:
        copy.wait_send()
    for copy in x_copies:
        copy.wait()
    mine.wait()
    for copy in drains:
        copy.wait()


def gather_weights(square, ffn_in, ffn_out, gains_t, x, z_count):
    n_sq, n_ff = square.shape[0], ffn_in.shape[0]
    order = [("gain", 0)]
    order += [("square", n) for n in (0, 1, 2, 3)]
    order += [("cols", n) for n in range(4)] + [("rows", n) for n in range(4)]
    order += [("square", n) for n in (7, 8, 4, 5, 6, 9)]
    order += [("cols", n) for n in range(4, 8)] + [("rows", n) for n in range(4, 8)]
    sq_s = (n_sq, z_count, 4, ROWS, 2 * HALF)
    in_s = (n_ff, z_count, 4, ROWS, 8 * HALF)
    out_s = (n_ff, z_count, 4, 4 * ROWS, 2 * HALF)
    gain_s = (z_count, 4, ROWS, 128)
    firsts = 2 + 5 * n_ff
    vmem = pl.BlockSpec(memory_space=pltpu.VMEM)
    hbm = pl.BlockSpec(memory_space=pltpu.HBM)
    return pl.pallas_call(
        functools.partial(gather_kernel, order, z_count),
        out_shape=[jax.ShapeDtypeStruct(shape, bf16) for shape in (sq_s, in_s, out_s, gain_s)]
        + [jax.ShapeDtypeStruct(x.shape, bf16)],
        in_specs=[vmem] * 4 + [hbm],
        out_specs=[hbm] * 5,
        scratch_shapes=[
            pltpu.VMEM(sq_s, bf16),
            pltpu.VMEM(in_s, bf16),
            pltpu.VMEM(out_s, bf16),
            pltpu.VMEM(gain_s, bf16),
            pltpu.VMEM((n_sq, ROWS // 2, HALF), f32),
            pltpu.VMEM((n_ff, 4, ROWS // 2, HALF), f32),
            pltpu.VMEM((n_ff, 2 * ROWS, HALF), f32),
            pltpu.VMEM((ROWS // 2, 128), f32),
            pltpu.SemaphoreType.DMA((len(order), 7)),
            pltpu.SemaphoreType.DMA((len(order), 7)),
            pltpu.SemaphoreType.DMA((firsts,)),
            pltpu.SemaphoreType.DMA((firsts,)),
            pltpu.SemaphoreType.DMA((3,)),
            pltpu.SemaphoreType.DMA((3,)),
            pltpu.SemaphoreType.DMA((20,)),
        ],
        compiler_params=pltpu.CompilerParams(
            collective_id=0, has_side_effects=True, vmem_limit_bytes=60 * MIB
        ),
        name="gather_weights",
    )(square, ffn_in, ffn_out, gains_t, x)


class Scatter:
    def __init__(self, units, refs, bufs, sems, z_count):
        self.units, self.refs, self.z_count = units, refs, z_count
        self.r0, self.own, self.r1, self.r2, self.r3, self.fin, self.sib = bufs
        self.send, self.recv, self.local = sems
        self.where = place()
        self.started = []
        self.loads = {}

    def go(self, u, slot, src, dst, peer):
        copy = remote(src, dst, self.send.at[u, slot], self.recv.at[u, slot], peer)
        copy.start()
        self.started.append(copy)

    def got(self, u, slot, ref):
        z, s, c = self.where[:3]
        remote(ref, ref, self.send.at[u, slot], self.recv.at[u, slot], (z, s, 1 - c)).wait_recv()

    def view(self, u, c):
        kind, n = self.units[u]
        return unit_view(kind, n, self.refs[kind], slice(None), slice(None), c)

    def c_start(self, u):
        z, s, c = self.where[:3]
        self.go(u, 0, self.view(u, 1 - c), self.r0.at[u], (z, s, 1 - c))
        copy = pltpu.make_async_copy(self.view(u, c), self.own.at[u % 4], self.local.at[u])
        copy.start()
        self.loads[u] = copy

    def b_start(self, u):
        z, s, c, first, second, both = self.where
        self.loads[u].wait()
        self.got(u, 0, self.r0.at[u])
        for n in range(self.z_count):
            for m in range(4):
                total = self.own[u % 4, n, m].astype(f32) + self.r0[u, n, m].astype(f32)
                self.r0[u, n, m] = total.astype(bf16)
        self.go(u, 1, self.r0.at[u, :, second], self.r1.at[u, 0], (z, second, c))
        self.go(u, 2, self.r0.at[u, :, both], self.r1.at[u, 1], (z, second, c))

    def a_start(self, u):
        z, s, c, first, second, both = self.where
        self.got(u, 2, self.r1.at[u, 1])
        for n in range(self.z_count):
            total = self.r0[u, n, first].astype(f32) + self.r1[u, 1, n].astype(f32)
            self.r1[u, 1, n] = total.astype(bf16)
        self.go(u, 3, self.r1.at[u, 1], self.r2.at[u], (z, first, c))
        self.got(u, 1, self.r1.at[u, 0])
        for n in range(self.z_count):
            total = self.r0[u, n, s].astype(f32) + self.r1[u, 0, n].astype(f32)
            self.r1[u, 0, n] = total.astype(bf16)

    def z_start(self, u):
        z, s, c = self.where[:3]
        self.got(u, 3, self.r2.at[u])
        for n in range(self.z_count):
            total = self.r1[u, 0, n].astype(f32) + self.r2[u, n].astype(f32)
            self.r2[u, n] = total.astype(bf16)
        for d in range(1, self.z_count):
            to = (z + d) % self.z_count
            self.go(u, 3 + d, self.r2.at[u, to], self.r3.at[u, d - 1], (to, s, c))

    def f_start(self, u):
        z, s, c = self.where[:3]
        total = self.r2[u, z].astype(f32)
        for d in range(1, self.z_count):
            self.got(u, 3 + d, self.r3.at[u, d - 1])
            total = total + self.r3[u, d - 1].astype(f32)
        self.fin[u] = total
        kind, n = self.units[u]
        if kind == "rows":
            if n % 2 == 1:
                @pl.when(c != n // 2)
                def _():
                    remote(
                        self.fin.at[pl.ds(u - 1, 2)],
                        self.sib.at[pl.ds(u - 1, 2)],
                        self.send.at[u, 7],
                        self.recv.at[u, 7],
                        (z, s, 1 - c),
                    ).start()
        else:
            rows = pl.ds(pl.multiple_of((1 - c) * (ROWS // 2), 8), ROWS // 2)
            self.go(
                u, 7, self.fin.at[u, rows], self.sib.at[u, pl.ds(0, ROWS // 2)], (z, s, 1 - c)
            )

    def finish_unit(self, u, put):
        z, s, c = self.where[:3]
        kind, n = self.units[u]
        if kind == "rows":
            if n % 2 == 1:

                @pl.when(c == n // 2)
                def _():
                    pair = self.sib.at[pl.ds(u - 1, 2)]
                    self.got(u, 7, pair)
                    for k in range(2):
                        put(kind, (n % 2 - 1 + k) * ROWS, c, self.fin[u - 1 + k])
                        put(kind, (n % 2 - 1 + k) * ROWS, 1 - c, self.sib[u - 1 + k])

                @pl.when(c != n // 2)
                def _():
                    pair = self.fin.at[pl.ds(u - 1, 2)]
                    remote(
                        pair, pair, self.send.at[u, 7], self.recv.at[u, 7], (z, s, 1 - c)
                    ).wait_send()
        else:
            self.got(u, 7, self.sib.at[u, pl.ds(0, ROWS // 2)])
            rows = pl.ds(pl.multiple_of(c * (ROWS // 2), 8), ROWS // 2)
            put(kind, n, c, self.fin[u, rows])
            put(kind, n, 1 - c, self.sib[u, : ROWS // 2])

    def tick(self, t, put, skew=1):
        steps = (self.c_start, self.b_start, self.a_start, self.z_start, self.f_start)
        last = t - 5 * skew
        if 0 <= last < len(self.units):
            self.finish_unit(last, put)
        for n in reversed(range(5)):
            u = t - n * skew
            if 0 <= u < len(self.units):
                steps[n](u)

    def finish(self):
        for copy in self.started:
            copy.wait_send()


def scatter_kernel(
    units, z_count, sq_ref, in_ref, out_ref, x_ref, sq_o, in_o, out_o, x_o,
    r0, own, r1, r2, r3, fin, sib, send, recv, local, x_send, x_recv, x_local,
):
    z, s, c = place()[:3]
    greet(z, s, c, z_count)
    scatter = Scatter(
        units,
        {"square": sq_ref, "cols": in_ref, "rows": out_ref},
        (r0, own, r1, r2, r3, fin, sib),
        (send, recv, local),
        z_count,
    )

    def put(kind, n, side, value):
        if kind == "square":
            sq_o[n, :, cols(side)] = value
        elif kind == "cols":
            in_o[:, cols(side, n * 2 * HALF)] = value
        else:
            out_o[n : n + ROWS, cols(side)] = value

    x_copies = []
    for d in range(1, 4):
        peer = (s + d) % 4
        copy = remote(
            x_ref.at[peer], x_o.at[s], x_send.at[d - 1], x_recv.at[d - 1], (z, peer, c)
        )
        copy.start()
        x_copies.append(copy)
    mine = pltpu.make_async_copy(x_ref.at[s], x_o.at[s], x_local.at[0])
    mine.start()
    skew = 1
    for t in range(len(units) + 5 * skew):
        scatter.tick(t, put, skew)
    scatter.finish()
    for copy in x_copies:
        copy.wait()
    mine.wait()


def scatter_grads(g_sq, g_in, g_out, g_x, z_count):
    n_sq = g_sq.shape[0]
    order = [("square", n) for n in range(4, n_sq)]
    order += [("rows", n) for n in range(4)] + [("cols", n) for n in range(4)]
    order += [("square", n) for n in (3, 0, 1, 2)]
    n = len(order)
    vmem = pl.BlockSpec(memory_space=pltpu.VMEM)
    hbm = pl.BlockSpec(memory_space=pltpu.HBM)
    out_shape = [
        jax.ShapeDtypeStruct((n_sq, ROWS // 2, 2 * HALF), f32),
        jax.ShapeDtypeStruct((ROWS // 2, 8 * HALF), f32),
        jax.ShapeDtypeStruct((2 * ROWS, 2 * HALF), f32),
        jax.ShapeDtypeStruct(g_x.shape, bf16),
    ]
    return pl.pallas_call(
        functools.partial(scatter_kernel, order, z_count),
        out_shape=out_shape,
        in_specs=[hbm] * 4,
        out_specs=[vmem] * 3 + [hbm],
        scratch_shapes=[
            pltpu.VMEM((n, z_count, 4, ROWS, HALF), bf16),
            pltpu.VMEM((4, z_count, 4, ROWS, HALF), bf16),
            pltpu.VMEM((n, 2, z_count, ROWS, HALF), bf16),
            pltpu.VMEM((n, z_count, ROWS, HALF), bf16),
            pltpu.VMEM((n, z_count - 1, ROWS, HALF), bf16),
            pltpu.VMEM((n, ROWS, HALF), f32),
            pltpu.VMEM((n, ROWS, HALF), f32),
            pltpu.SemaphoreType.DMA((n, 8)),
            pltpu.SemaphoreType.DMA((n, 8)),
            pltpu.SemaphoreType.DMA((n,)),
            pltpu.SemaphoreType.DMA((3,)),
            pltpu.SemaphoreType.DMA((3,)),
            pltpu.SemaphoreType.DMA((1,)),
        ],
        compiler_params=pltpu.CompilerParams(
            collective_id=1, has_side_effects=True, vmem_limit_bytes=60 * MIB
        ),
        name="scatter_grads",
    )(g_sq, g_in, g_out, g_x)


def total_kernel(z_count, in_ref, out_ref, acc, got, send, recv):
    z, s, c = place()[:3]
    greet(z, s, c, z_count)
    started = []
    slot = 0

    def exchange(peers):
        nonlocal slot
        base = slot
        for peer in peers:
            copy = remote(acc, got.at[slot], send.at[slot], recv.at[slot], peer)
            copy.start()
            started.append(copy)
            slot += 1
        for copy in started[base:]:
            copy.wait()
        total = acc[...]
        for k in range(base, slot):
            total = total + got[k]
        acc[...] = total

    acc[...] = in_ref[...]
    exchange([(z, s, 1 - c)])
    exchange([(z, (s + d) % 4, c) for d in range(1, 4)])
    exchange([((z + d) % z_count, s, c) for d in range(1, z_count)])
    out_ref[...] = acc[...]


def total_all(x, z_count):
    vmem = pl.BlockSpec(memory_space=pltpu.VMEM)
    slots = z_count + 3
    return pl.pallas_call(
        functools.partial(total_kernel, z_count),
        out_shape=jax.ShapeDtypeStruct(x.shape, f32),
        in_specs=[vmem],
        out_specs=vmem,
        scratch_shapes=[
            pltpu.VMEM(x.shape, f32),
            pltpu.VMEM((slots,) + x.shape, f32),
            pltpu.SemaphoreType.DMA((slots,)),
            pltpu.SemaphoreType.DMA((slots,)),
        ],
        compiler_params=pltpu.CompilerParams(collective_id=2, has_side_effects=True),
        name="total_all",
    )(x)


def on_device(
    inputs,
    dec_in,
    cotangent,
    lengths,
    bucket_table,
    square,
    square_m,
    square_v,
    ffn_in,
    ffn_in_m,
    ffn_in_v,
    ffn_out,
    ffn_out_m,
    ffn_out_v,
    gains,
    gains_m,
    gains_v,
    rel_bias,
    rel_bias_m,
    rel_bias_v,
):
    z_count = lax.axis_size("dp")
    width = inputs.shape[2]
    direct = lax.axis_size("seq") == 4 and width == 2 * HALF and width == 4 * z_count * ROWS
    w = {}
    if direct:
        gains_t = jnp.pad(gains.T, ((0, 0), (0, 128 - gains.shape[0])))
        sq_g, in_g, out_g, gain_g, x_b = gather_weights(
            square, ffn_in, ffn_out, gains_t, inputs, z_count
        )
        sq_g = sq_g.reshape(-1, width, width)
        in_g = in_g.reshape(2, width, -1)
        out_g = out_g.reshape(2, -1, width)
        w_in_e, w_in_d = in_g[0], in_g[1]
        w_out_e, w_out_d = out_g[0], out_g[1]
        gain_f = gain_g.reshape(width, 128)[:, : gains.shape[0]].T.astype(f32)
        x_b = x_b.reshape(-1, width)
        for i in range(square.shape[0]):
            w[i] = sq_g[i]
    else:

        def gather_rows(x):
            return lax.all_gather(x.astype(bf16), AXES, axis=x.ndim - 2, tiled=True)

        sq_a = gather_rows(square[:4])
        w_in_e = gather_rows(ffn_in[0])
        w_out_e = gather_rows(ffn_out[0])
        sq_b = gather_rows(square[4:])
        w_in_d = gather_rows(ffn_in[1])
        w_out_d = gather_rows(ffn_out[1])
        gain_f = lax.all_gather(gains.astype(bf16), AXES, axis=1, tiled=True).astype(f32)
        for i in range(square.shape[0]):
            w[i] = sq_a[i] if i < 4 else sq_b[i - 4]
        x_b = lax.all_to_all(inputs, "seq", split_axis=0, concat_axis=1, tiled=True)[0]

    seq_pos = lax.axis_index("seq")
    local_len = inputs.shape[1]
    span = local_len * lax.axis_size("seq")
    bucket_count = rel_bias.shape[0]
    scale = 1.0 / math.sqrt(HD)
    x_f = x_b.astype(f32)
    length = lax.dynamic_slice_in_dim(lengths, seq_pos, 1, 0)
    key_valid = jnp.arange(span)[None, :] < length[:, None]
    one_hot = (
        jnp.pad(bucket_table, (0, 1), constant_values=-1)[:, None]
        == jnp.arange(bucket_count)[None, :]
    ).astype(f32)
    table = jnp.einsum("ob,bh->ho", one_hot, rel_bias, precision=highest_precision)[:, None, :]

    normed = rms_gain(x_f, gain_f[0]).astype(bf16)
    q = matmul(normed, w[0]).astype(bf16)
    k = matmul(normed, w[1]).astype(bf16)
    v = matmul(normed, w[2]).astype(bf16)
    attended = attend_fwd(length, table, q, k, v)
    hidden = x_f + matmul(attended, w[3])
    normed_two = rms_gain(hidden, gain_f[1]).astype(bf16)
    pre_act = matmul(normed_two, w_in_e)
    inner_act = gelu_tanh(pre_act).astype(bf16)
    hidden_two = hidden + matmul(inner_act, w_out_e)
    encoded = rms_gain(hidden_two, gain_f[2]).astype(bf16)
    cross_k = matmul(encoded, w[7]).astype(bf16)
    cross_v = matmul(encoded, w[8]).astype(bf16)

    dec_row = dec_in.reshape(1, width).astype(f32)
    self_norm = rms_gain(dec_row, gain_f[3]).astype(bf16)
    self_values = matmul(self_norm, w[4]).astype(bf16)
    dec_one = dec_row + matmul(self_values, w[5])
    cross_norm = rms_gain(dec_one, gain_f[4]).astype(bf16)
    cross_q = matmul(cross_norm, w[6]).astype(bf16)
    head_of = (jnp.arange(width)[None, :] // HD == jnp.arange(H)[:, None]).astype(bf16)
    q_heads = head_of * cross_q
    cross_scores = jnp.where(key_valid, mm_t(q_heads, cross_k) * scale, neg_fill)
    cross_probs = jax.nn.softmax(cross_scores, axis=-1)
    cross_probs_b = cross_probs.astype(bf16)
    cross_att = jnp.sum(
        matmul(cross_probs_b, cross_v) * head_of.astype(f32), axis=0, keepdims=True
    ).astype(bf16)
    dec_two = dec_one + matmul(cross_att, w[9])
    ffn_norm = rms_gain(dec_two, gain_f[5]).astype(bf16)
    pre_dec = matmul(ffn_norm, w_in_d)
    inner_dec = gelu_tanh(pre_dec).astype(bf16)
    dec_out = dec_two + matmul(inner_dec, w_out_d)

    g_top_b = cotangent.reshape(1, width)
    g_top = g_top_b.astype(f32)
    g_pre_dec = gelu_pull(pre_dec, mm_t(g_top_b, w_out_d)).astype(bf16)
    g_two_norm, g_gain_five = rms_pull(dec_two, gain_f[5], mm_t(g_pre_dec, w_in_d))
    g_two = g_top + g_two_norm
    g_two_b = g_two.astype(bf16)
    g_att = mm_t(g_two_b, w[9]).astype(bf16)
    g_att_heads = head_of * g_att
    g_probs = mm_t(g_att_heads, cross_v)
    g_cross_v = mm_outer(cross_probs_b, g_att_heads).astype(bf16)
    g_scores = cross_probs * (g_probs - jnp.sum(g_probs * cross_probs, axis=-1, keepdims=True))
    g_scores_b = g_scores.astype(bf16)
    g_cross_q = (
        jnp.sum(matmul(g_scores_b, cross_k) * head_of.astype(f32), axis=0, keepdims=True) * scale
    ).astype(bf16)
    g_cross_k = (mm_outer(g_scores_b, q_heads) * scale).astype(bf16)
    g_one_norm, g_gain_four = rms_pull(dec_one, gain_f[4], mm_t(g_cross_q, w[6]))
    g_one_b = (g_two + g_one_norm).astype(bf16)
    g_self_values = mm_t(g_one_b, w[5]).astype(bf16)
    g_gain_three = rms_pull(dec_row, gain_f[3], mm_t(g_self_values, w[4]))[1]

    lefts = (self_norm, self_values, cross_norm, cross_att, ffn_norm, inner_dec)
    rights = (g_self_values, g_one_b, g_cross_q, g_two_b, g_pre_dec, g_top_b)
    own_row = jnp.concatenate(lefts + rights, axis=1)
    own_row = jnp.pad(own_row, ((0, 0), (0, 20 * 1024 - own_row.shape[1])))
    packed = lax.all_gather(own_row, AXES, axis=0, tiled=True)
    me = (
        lax.axis_index("dp") * lax.axis_size("seq") + seq_pos
    ) * lax.axis_size("head") + lax.axis_index("head")
    devices = packed.shape[0]
    cuts = [0]
    for piece in lefts + rights:
        cuts.append(cuts[-1] + piece.shape[1])
    dec_grads = []
    for n in range(6):
        share = lefts[n].shape[1] // devices
        left = lax.dynamic_slice_in_dim(packed, cuts[n] + me * share, share, 1)
        right = packed[:, cuts[6 + n] : cuts[7 + n]]
        dec_grads.append(mm_outer(left, right))

    g_w7 = mm_outer(encoded, g_cross_k)
    g_w8 = mm_outer(encoded, g_cross_v)
    g_encoded = mm_t(g_cross_k, w[7]) + mm_t(g_cross_v, w[8])
    g_hidden_two, g_gain_two = rms_pull(hidden_two, gain_f[2], g_encoded)
    g_hidden_two_b = g_hidden_two.astype(bf16)
    g_out_e = mm_outer(inner_act, g_hidden_two_b)
    g_pre = gelu_pull(pre_act, mm_t(g_hidden_two_b, w_out_e)).astype(bf16)
    g_in_e = mm_outer(normed_two, g_pre)
    g_hidden_norm, g_gain_one = rms_pull(hidden, gain_f[1], mm_t(g_pre, w_in_e))
    g_hidden = g_hidden_two + g_hidden_norm
    g_hidden_b = g_hidden.astype(bf16)
    g_w3 = mm_outer(attended, g_hidden_b)
    g_attended = mm_t(g_hidden_b, w[3]).astype(bf16)
    gq, gk, gv, g_table = attend_bwd(length, table, q, k, v, g_attended)
    g_bias_here = jnp.einsum("ob,ho->bh", one_hot, g_table[:, 0, :], precision=highest_precision)
    g_w0 = mm_outer(normed, gq)
    g_w1 = mm_outer(normed, gk)
    g_w2 = mm_outer(normed, gv)
    g_normed = mm_t(gq, w[0]) + mm_t(gk, w[1]) + mm_t(gv, w[2])
    g_input_norm, g_gain_zero = rms_pull(x_f, gain_f[0], g_normed)
    g_x = (g_hidden + g_input_norm).astype(bf16)
    if direct:
        g_sq = jnp.stack([g.astype(bf16) for g in (g_w0, g_w1, g_w2, g_w3, g_w7, g_w8)])
        s_sq, s_in, s_out, input_grad = scatter_grads(
            g_sq.reshape(6, z_count, 4, ROWS, width),
            g_in_e.astype(bf16).reshape(1, z_count, 4, ROWS, -1),
            g_out_e.astype(bf16).reshape(1, z_count, 4, -1, width),
            g_x.reshape(inputs.shape),
            z_count,
        )
        s_0123, s_78 = s_sq[:4], s_sq[4:]
        input_grad = input_grad.astype(f32)
    else:
        input_grad = lax.all_to_all(
            g_x[None], "seq", split_axis=1, concat_axis=0, tiled=True
        ).astype(f32)

        def scatter_rows(x):
            return lax.psum_scatter(
                x.astype(bf16), AXES, scatter_dimension=x.ndim - 2, tiled=True
            ).astype(f32)

        s_78 = scatter_rows(jnp.stack((g_w7, g_w8)))
        s_out = scatter_rows(g_out_e)
        s_in = scatter_rows(g_in_e)
        s_0123 = scatter_rows(jnp.stack((g_w0, g_w1, g_w2, g_w3)))
    summed_sq = jnp.stack(
        (
            s_0123[0],
            s_0123[1],
            s_0123[2],
            s_0123[3],
            dec_grads[0],
            dec_grads[1],
            dec_grads[2],
            s_78[0],
            s_78[1],
            dec_grads[3],
        )
    )
    summed_in = jnp.stack((s_in, dec_grads[4]))
    summed_out = jnp.stack((s_out, dec_grads[5]))
    g_gains = jnp.stack(
        (g_gain_zero, g_gain_one, g_gain_two, g_gain_three, g_gain_four, g_gain_five)
    )
    gain_share = gains.shape[1]
    local_squares = (
        jnp.sum(summed_sq * summed_sq)
        + jnp.sum(summed_in * summed_in)
        + jnp.sum(summed_out * summed_out)
    )
    if direct:
        rest = jnp.concatenate((g_bias_here.reshape(-1), local_squares[None]))
        rest = jnp.pad(rest, (0, 1024 - rest.shape[0])).reshape(8, 128)
        wide = jnp.concatenate((jnp.pad(g_gains, ((0, 2), (0, 0))), rest), axis=1)
        wide = total_all(wide, z_count)
        g_gains = wide[:6, :width]
        rest = wide[:, width:].reshape(-1)
        g_bias = rest[: g_bias_here.size].reshape(g_bias_here.shape)
        shard_squares = rest[g_bias_here.size]
    else:
        g_gains, g_bias, shard_squares = lax.psum((g_gains, g_bias_here, local_squares), AXES)
    summed_gain = lax.dynamic_slice_in_dim(g_gains, me * gain_share, gain_share, 1)
    grad_norm = jnp.sqrt(shard_squares + jnp.sum(g_gains * g_gains) + jnp.sum(g_bias * g_bias))
    factor = clip_bound / jnp.maximum(grad_norm, clip_bound)
    return (
        dec_out.astype(bf16).reshape(dec_in.shape),
        input_grad,
        grad_norm,
        *adam_step(square, square_m, square_v, summed_sq, factor, rate_matrix, decay_rate),
        *adam_step(ffn_in, ffn_in_m, ffn_in_v, summed_in, factor, rate_matrix, decay_rate),
        *adam_step(ffn_out, ffn_out_m, ffn_out_v, summed_out, factor, rate_matrix, decay_rate),
        *adam_step(gains, gains_m, gains_v, summed_gain, factor, rate_small, 0.0),
        *adam_step(rel_bias, rel_bias_m, rel_bias_v, g_bias, factor, rate_small, 0.0),
    )


def solution(mesh):
    rows = P(("dp", "head"), "seq", None)
    shard = P(None, AXES, None)
    small = P(None, AXES)
    return jax.shard_map(
        on_device,
        mesh=mesh,
        in_specs=(rows, rows, rows, P(("dp", "head")), P())
        + (shard,) * 9
        + (small,) * 3
        + (P(),) * 3,
        out_specs=(rows, rows, P()) + (shard,) * 9 + (small,) * 3 + (P(),) * 3,
        check_vma=False,
    )
```

```python
import functools
import math

import jax
import jax.numpy as jnp
from jax import lax
from jax.experimental import pallas as pl
from jax.experimental.pallas import tpu as pltpu
from jax.sharding import PartitionSpec as P

H = 12
HD = 64
STEP = 5
AXES = ("dp", "seq", "head")

norm_eps = 1e-06
neg_fill = -1e30
beta_one = 0.9
beta_two = 0.999
adam_eps = 1e-08
decay_rate = 0.01
rate_matrix = 0.05
rate_small = 0.5
clip_bound = 1.0
highest_precision = lax.Precision.HIGHEST
bf16 = jnp.bfloat16
f32 = jnp.float32
BAND = 128


def rms_gain(values_in, gain_row):
    return (
        values_in
        * lax.rsqrt(jnp.mean(values_in * values_in, axis=-1, keepdims=True) + norm_eps)
        * gain_row
    )


def gelu_tanh(values_in):
    return jax.nn.gelu(values_in, approximate=True)


def matmul(left, right):
    return jnp.dot(left, right, preferred_element_type=f32)


def mm_t(left, right):
    return lax.dot_general(left, right, (((1,), (1,)), ((), ())), preferred_element_type=f32)


def mm_outer(left, right):
    return lax.dot_general(left, right, (((0,), (0,)), ((), ())), preferred_element_type=f32)


def rms_pull(values_in, gain_row, incoming):
    _, pull = jax.vjp(rms_gain, values_in, gain_row)
    return pull(incoming)


def gelu_pull(values_in, incoming):
    _, pull = jax.vjp(gelu_tanh, values_in)
    return pull(incoming)[0]


def adam_step(weight, first, second, grad, factor, rate, decay):
    grad = grad * factor
    first = beta_one * first + (1.0 - beta_one) * grad
    second = beta_two * second + (1.0 - beta_two) * grad * grad
    first_hat = first / (1.0 - beta_one**STEP)
    second_hat = second / (1.0 - beta_two**STEP)
    weight = weight - rate * (first_hat / (jnp.sqrt(second_hat) + adam_eps) + decay * weight)
    return (weight, first, second)


def bias_band(table_row, span):
    wide = jnp.broadcast_to(table_row, (BAND, 2 * span))
    shift = (2 * span - (BAND - 1)) % (2 * span)
    return pltpu.roll(wide, shift, 1, stride=1, stride_axis=0)


def band_sums(band, span):
    wide = 2 * span
    rows = BAND
    while rows > 8:
        rows //= 2
        band = band[:rows] + pltpu.roll(band[rows:], wide - rows, 1)
    row = lax.broadcasted_iota(jnp.int32, band.shape, 0)
    for step in (4, 2, 1):
        band = jnp.where((row // step) % 2 == 1, pltpu.roll(band, wide - step, 1), band)
    return pltpu.roll(jnp.sum(band, axis=0, keepdims=True), BAND - 1, 1)


def softmax_rows(q_rows, k_all, band, block, span, valid):
    start = span - BAND * (block + 1)
    scores = mm_t(q_rows, k_all) * (1.0 / math.sqrt(HD)) + band[:, start : start + span]
    scores = jnp.where(valid, scores, neg_fill)
    peak = jnp.max(scores, axis=-1, keepdims=True)
    raised = jnp.exp(scores - peak)
    return raised / jnp.sum(raised, axis=-1, keepdims=True)


def attend_fwd_kernel(len_ref, table_ref, q_ref, k_ref, v_ref, o_ref):
    span = k_ref.shape[0]
    valid = lax.broadcasted_iota(jnp.int32, (1, span), 1) < len_ref[0]
    lane = lax.broadcasted_iota(jnp.int32, (1, 2 * HD), 1)
    k_all = k_ref[...]
    v_all = v_ref[...]
    bands = [bias_band(table_ref[t], span) for t in range(2)]
    for block in range(span // BAND):
        rows = slice(block * BAND, (block + 1) * BAND)
        q_rows = q_ref[rows, :]
        parts = []
        for t in range(2):
            own = (lane // HD) == t
            probs = softmax_rows(
                jnp.where(own, q_rows, jnp.zeros_like(q_rows)), k_all, bands[t], block, span, valid
            )
            parts.append(matmul(probs.astype(bf16), v_all))
        o_ref[rows, :] = jnp.where(lane < HD, parts[0], parts[1]).astype(bf16)


def attend_bwd_kernel(
    len_ref, table_ref, q_ref, k_ref, v_ref, do_ref, dq_ref, dk_ref, dv_ref, dt_ref
):
    span = k_ref.shape[0]
    scale = 1.0 / math.sqrt(HD)
    valid = lax.broadcasted_iota(jnp.int32, (1, span), 1) < len_ref[0]
    lane = lax.broadcasted_iota(jnp.int32, (1, 2 * HD), 1)
    k_all = k_ref[...]
    v_all = v_ref[...]
    count = span // BAND
    dks, dvs = [], []
    dqs = [[None, None] for _ in range(count)]
    for t in range(2):
        own = (lane // HD) == t
        band = bias_band(table_ref[t], span)
        dk = jnp.zeros((span, 2 * HD), f32)
        dv = jnp.zeros((span, 2 * HD), f32)
        dband = jnp.zeros((BAND, 2 * span), f32)
        for block in range(count):
            rows = slice(block * BAND, (block + 1) * BAND)
            q_rows = q_ref[rows, :]
            do_rows = do_ref[rows, :]
            zero = jnp.zeros_like(q_rows)
            probs = softmax_rows(
                jnp.where(own, q_rows, zero), k_all, band, block, span, valid
            )
            dprobs = mm_t(jnp.where(own, do_rows, zero), v_all)
            dscore = probs * (dprobs - jnp.sum(dprobs * probs, axis=-1, keepdims=True))
            start = span - BAND * (block + 1)
            pieces = []
            if start:
                pieces.append(jnp.zeros((BAND, start), f32))
            pieces.append(dscore)
            if span - start:
                pieces.append(jnp.zeros((BAND, span - start), f32))
            dband = dband + jnp.concatenate(pieces, axis=1)
            dscore_b = dscore.astype(bf16)
            dv = dv + mm_outer(probs.astype(bf16), do_rows)
            dk = dk + mm_outer(dscore_b, q_rows)
            dqs[block][t] = matmul(dscore_b, k_all)
        dks.append(dk)
        dvs.append(dv)
        dt_ref[t] = band_sums(dband, span)
    dk_ref[...] = (jnp.where(lane < HD, dks[0], dks[1]) * scale).astype(bf16)
    dv_ref[...] = jnp.where(lane < HD, dvs[0], dvs[1]).astype(bf16)
    for block in range(count):
        rows = slice(block * BAND, (block + 1) * BAND)
        dq_ref[rows, :] = (jnp.where(lane < HD, dqs[block][0], dqs[block][1]) * scale).astype(bf16)


def head_specs(span, width, n):
    return [pl.BlockSpec((span, 2 * HD), lambda i: (0, i)) for _ in range(n)]


def attend_fwd(length, table, q, k, v):
    span, width = q.shape
    return pl.pallas_call(
        attend_fwd_kernel,
        grid=(width // (2 * HD),),
        out_shape=jax.ShapeDtypeStruct((span, width), bf16),
        in_specs=[
            pl.BlockSpec(memory_space=pltpu.SMEM),
            pl.BlockSpec((2, 1, 2 * span), lambda i: (i, 0, 0)),
            *head_specs(span, width, 3),
        ],
        out_specs=head_specs(span, width, 1)[0],
        compiler_params=pltpu.CompilerParams(vmem_limit_bytes=48 * 1024 * 1024),
        name="attend_fwd",
    )(length, table, q, k, v)


def attend_bwd(length, table, q, k, v, do):
    span, width = q.shape
    like = jax.ShapeDtypeStruct((span, width), bf16)
    return pl.pallas_call(
        attend_bwd_kernel,
        grid=(width // (2 * HD),),
        out_shape=(like, like, like, jax.ShapeDtypeStruct(table.shape, f32)),
        in_specs=[
            pl.BlockSpec(memory_space=pltpu.SMEM),
            pl.BlockSpec((2, 1, 2 * span), lambda i: (i, 0, 0)),
            *head_specs(span, width, 4),
        ],
        out_specs=(
            *head_specs(span, width, 3),
            pl.BlockSpec((2, 1, 2 * span), lambda i: (i, 0, 0)),
        ),
        compiler_params=pltpu.CompilerParams(vmem_limit_bytes=48 * 1024 * 1024),
        name="attend_bwd",
    )(length, table, q, k, v, do)


MESH_ID = pl.DeviceIdType.MESH
HALF = 384
ROWS = 48
MIB = 1024 * 1024


def place():
    z, s, c = lax.axis_index("dp"), lax.axis_index("seq"), lax.axis_index("head")
    near = s + 1 - 2 * (s % 2)
    far = (s + 2) % 4
    first = near + c * (far - near)
    second = far + c * (near - far)
    return z, s, c, first, second, 3 - s


def greet(z, s, c, z_count):
    barrier = pltpu.get_barrier_semaphore()
    for d in range(1, z_count):
        peer = ((z + d) % z_count, s, c)
        pl.semaphore_signal(barrier, 1, device_id=peer, device_id_type=MESH_ID)
    for d in range(1, 4):
        peer = (z, (s + d) % 4, c)
        pl.semaphore_signal(barrier, 1, device_id=peer, device_id_type=MESH_ID)
    pl.semaphore_signal(barrier, 1, device_id=(z, s, 1 - c), device_id_type=MESH_ID)
    pl.semaphore_wait(barrier, z_count + 3)


def remote(src, dst, send, recv, peer):
    return pltpu.make_async_remote_copy(
        src, dst, send, recv, device_id=peer, device_id_type=MESH_ID
    )


def cols(c, base=0):
    return pl.ds(pl.multiple_of(base + c * HALF, 128), HALF)


def unit_view(kind, n, ref, z, s, c):
    if kind == "square":
        return ref.at[n, z, s, :, cols(c)]
    if kind == "cols":
        return ref.at[n // 4, z, s, :, cols(c, (n % 4) * 2 * HALF)]
    if kind == "rows":
        return ref.at[n // 4, z, s, pl.ds((n % 4) * ROWS, ROWS), cols(c)]
    return ref.at[z, s]


class Gather:
    def __init__(self, units, refs, send, recv, z_count):
        self.units, self.refs, self.send, self.recv = units, refs, send, recv
        self.z_count = z_count
        self.where = place()
        self.started = []

    def view(self, u, z, s, c):
        kind, n = self.units[u]
        return unit_view(kind, n, self.refs[kind], z, s, c)

    def go(self, u, slot, ref, peer):
        copy = remote(ref, ref, self.send.at[u, slot], self.recv.at[u, slot], peer)
        copy.start()
        self.started.append(copy)

    def got(self, u, slot, ref):
        z, s, c = self.where[:3]
        remote(ref, ref, self.send.at[u, slot], self.recv.at[u, slot], (z, s, 1 - c)).wait_recv()

    def z_start(self, u):
        z, s, c = self.where[:3]
        for d in range(1, self.z_count):
            self.go(u, d - 1, self.view(u, z, s, c), ((z + d) % self.z_count, s, c))

    def z_wait(self, u):
        z, s, c = self.where[:3]
        for d in range(1, self.z_count):
            self.got(u, d - 1, self.view(u, (z + self.z_count - d) % self.z_count, s, c))

    def a_start(self, u):
        z, s, c, first, second, both = self.where
        self.go(u, 3, self.view(u, slice(None), s, c), (z, first, c))

    def a_wait(self, u):
        z, s, c, first, second, both = self.where
        self.got(u, 3, self.view(u, slice(None), first, c))

    def b_start(self, u):
        z, s, c, first, second, both = self.where
        self.go(u, 4, self.view(u, slice(None), s, c), (z, second, c))
        self.go(u, 5, self.view(u, slice(None), first, c), (z, second, c))

    def b_wait(self, u):
        z, s, c, first, second, both = self.where
        self.got(u, 4, self.view(u, slice(None), second, c))
        self.got(u, 5, self.view(u, slice(None), both, c))

    def s_start(self, u):
        z, s, c = self.where[:3]
        if self.units[u][0] != "gain":
            self.go(u, 6, self.view(u, slice(None), slice(None), c), (z, s, 1 - c))

    def s_wait(self, u):
        z, s, c = self.where[:3]
        if self.units[u][0] != "gain":
            self.got(u, 6, self.view(u, slice(None), slice(None), 1 - c))

    def tick(self, t, skew=2, done=None):
        steps = (
            (self.z_start,),
            (self.z_wait, self.a_start),
            (self.a_wait, self.b_start),
            (self.b_wait, self.s_start),
            (self.s_wait,) + ((done,) if done else ()),
        )
        for n, work in enumerate(steps):
            u = t - n * skew
            if 0 <= u < len(self.units):
                for step in work:
                    step(u)

    def finish(self):
        for copy in self.started:
            copy.wait_send()


def row_blocks(count, work):
    def body(i, carry):
        work(i, pl.ds(pl.multiple_of(i * BAND, BAND), BAND))
        return carry

    lax.fori_loop(0, count, body, 0)


def col_tiles(width, tile, work):
    def body(i, carry):
        work(pl.ds(pl.multiple_of(i * tile, tile), tile))
        return carry

    lax.fori_loop(0, width // tile, body, 0)


def wide(value):
    return value.reshape(value.shape[0] * value.shape[1] * value.shape[2], value.shape[3])


def attend_pair_fwd(pair, length, table_ref, q_ref, k_ref, v_ref, o_ref):
    span = k_ref.shape[0]
    at = pl.ds(pl.multiple_of(pair * 2 * HD, 2 * HD), 2 * HD)
    valid = lax.broadcasted_iota(jnp.int32, (1, span), 1) < length
    lane = lax.broadcasted_iota(jnp.int32, (1, 2 * HD), 1)
    k_all = k_ref[:, at]
    v_all = v_ref[:, at]
    bands = [bias_band(table_ref[2 * pair + t], span) for t in range(2)]
    for block in range(span // BAND):
        rows = slice(block * BAND, (block + 1) * BAND)
        q_rows = q_ref[rows, at]
        parts = []
        for t in range(2):
            own = (lane // HD) == t
            probs = softmax_rows(
                jnp.where(own, q_rows, jnp.zeros_like(q_rows)), k_all, bands[t], block, span, valid
            )
            parts.append(matmul(probs.astype(bf16), v_all))
        o_ref[rows, at] = jnp.where(lane < HD, parts[0], parts[1]).astype(bf16)


def forward_kernel(units, z_count, *refs):
    (
        len_ref, table_ref, sq_ref, in_ref, out_ref, gain_ref, x_ref,
        in_o, out_o, in_d, out_d, gain_o, x_o, q_o, k_o, v_o, att_o, hid_o, pre_o,
        hid2_o, enc_o, ck_o, cv_o,
        sq_o0, sq_o1, sq_o2, sq_o3, sq_o4, sq_o5, sq_o6, sq_o7, sq_o8, sq_o9,
        sq_w, in_w, out_w, gain_w, sq_r, in_r, out_r, gain_r,
        x_s, n_s, q_s, k_s, v_s, att_s, hid_s, pre_s, inner_s, hid2_s, enc_s, ck_s, cv_s, gains,
        send, recv, first_send, first_recv, x_send, x_recv, local,
    ) = refs
    z, s, c = place()[:3]
    sibling = (z, s, 1 - c)
    sq_o = (sq_o0, sq_o1, sq_o2, sq_o3, sq_o4, sq_o5, sq_o6, sq_o7, sq_o8, sq_o9)
    n_sq, n_ff = sq_ref.shape[0], in_ref.shape[0]
    blocks = x_s.shape[0] * x_s.shape[1] // BAND
    greet(z, s, c, z_count)

    first = []

    def to_sibling(src, dst):
        copy = remote(src, dst, first_send.at[len(first)], first_recv.at[len(first)], sibling)
        copy.start()
        first.append(copy)

    to_sibling(gain_ref, gain_r)
    to_sibling(sq_ref.at[:, :, cols(1 - c)], sq_r)
    x_copies = []
    for d in range(1, 4):
        peer = (s + d) % 4
        copy = remote(
            x_ref.at[peer], x_s.at[s], x_send.at[d - 1], x_recv.at[d - 1], (z, peer, c)
        )
        copy.start()
        x_copies.append(copy)
    mine = pltpu.make_async_copy(x_ref.at[s], x_s.at[s], local.at[0])
    mine.start()
    for n in range(n_ff):
        for j in range(4):
            to_sibling(in_ref.at[n, :, cols(1 - c, 2 * HALF * j)], in_r.at[n, j])
        to_sibling(out_ref.at[n, :, cols(1 - c)], out_r.at[n])

    def joined(own, other):
        top = jnp.where(c == 0, own, other)
        bottom = jnp.where(c == 0, other, own)
        return jnp.concatenate([top, bottom], axis=0).astype(bf16)

    gather = Gather(
        units,
        {"square": sq_w, "cols": in_w, "rows": out_w, "gain": gain_w},
        send,
        recv,
        z_count,
    )
    first[0].wait_recv()
    gain_w[z, s] = joined(gain_ref[...], gain_r[...])
    first[1].wait_recv()
    for n in range(n_sq):
        sq_w[n, z, s, :, cols(c)] = joined(sq_ref[n, :, cols(c)], sq_r[n])
    drains = []

    def drain(src, dst):
        copy = pltpu.make_async_copy(src, dst, local.at[1 + len(drains)])
        copy.start()
        drains.append(copy)

    def done(u):
        kind, n = units[u]
        if kind == "square":
            drain(sq_w.at[n], sq_o[n])
        elif kind == "cols" and n % 4 == 3:
            drain(in_w.at[n // 4], (in_o, in_d)[n // 4])
        elif kind == "rows" and n % 4 == 3:
            drain(out_w.at[n // 4], (out_o, out_d)[n // 4])

    def normed(src, gain_row, dst):
        def work(i, at):
            dst[at, :] = rms_gain(src(i, at), gains[gain_row : gain_row + 1, :]).astype(bf16)

        row_blocks(blocks, work)

    def x_rows(i, at):
        return x_s[i].astype(f32)

    def start_piece():
        for copy in x_copies:
            copy.wait_recv()
        mine.wait()
        drain(x_s, x_o)
        gains[...] = wide(gain_w[...]).astype(f32).T[:8]
        drain(gains, gain_o)
        normed(x_rows, 0, n_s)

    def square_dot(left, n, tile=256):
        def weight(at):
            return wide(sq_w[n, :, :, :, at])

        return lambda at: matmul(left[...], weight(at))

    def project(n, left, dst, out):
        dot = square_dot(left, n)

        def work(at):
            dst[:, at] = dot(at).astype(bf16)

        col_tiles(2 * HALF, 256, work)
        drain(dst, out)

    def attention(pairs):
        def body(pair, carry):
            attend_pair_fwd(pair, len_ref[0], table_ref, q_s, k_s, v_s, att_s)
            return carry

        lax.fori_loop(pairs[0], pairs[1], body, 0)

    def hidden_piece():
        drain(att_s, att_o)
        dot = square_dot(att_s, 3)

        def work(at):
            hid_s[:, at] = dot(at)

        col_tiles(2 * HALF, 256, work)

        def add(i, at):
            total = hid_s[at, :] + x_rows(i, at)
            hid_s[at, :] = total
            n_s[at, :] = rms_gain(total, gains[1:2, :]).astype(bf16)

        row_blocks(blocks, add)
        drain(hid_s, hid_o)

    def ffn_piece(j):
        def work(i, carry):
            at = pl.ds(pl.multiple_of(j * 2 * HALF + i * 256, 256), 256)
            pre = matmul(n_s[...], wide(in_w[0, :, :, :, at]))
            pre_s[:, at] = pre
            inner_s[:, at] = gelu_tanh(pre).astype(bf16)
            return carry

        lax.fori_loop(0, 3, work, 0)

    def hidden_two_piece():
        drain(pre_s, pre_o)

        def work(at):
            hid2_s[:, at] = hid_s[:, at] + matmul(inner_s[...], wide(out_w[0, :, :, :, at]))

        col_tiles(2 * HALF, 256, work)
        normed(lambda i, at: hid2_s[at, :], 2, enc_s)
        drain(hid2_s, hid2_o)
        drain(enc_s, enc_o)

    skew = 2
    pieces = {
        6: [start_piece],
        9: [lambda: project(0, n_s, q_s, q_o)],
        10: [lambda: project(1, n_s, k_s, k_o)],
        11: [lambda: project(2, n_s, v_s, v_o), lambda: attention((0, 2))],
        12: [lambda: attention((2, 4))],
        13: [lambda: attention((4, 6))],
        14: [hidden_piece, lambda: ffn_piece(0)],
        15: [lambda: ffn_piece(1), lambda: ffn_piece(2)],
        16: [lambda: ffn_piece(3)],
        20: [hidden_two_piece],
        21: [lambda: project(7, enc_s, ck_s, ck_o)],
        22: [lambda: project(8, enc_s, cv_s, cv_o)],
    }
    k = 2
    for t in range(len(units) + 4 * skew):
        gather.tick(t, skew, done)
        if t == 1:
            for n in range(n_ff):
                for j in range(4):
                    first[k].wait_recv()
                    k += 1
                    at = cols(c, 2 * HALF * j)
                    in_w[n, z, s, :, at] = joined(in_ref[n, :, at], in_r[n, j])
                first[k].wait_recv()
                k += 1
                out_w[n, z, s, :, cols(c)] = joined(out_ref[n, :, cols(c)], out_r[n])
        for piece in pieces.get(t, ()):
            piece()
    gather.finish()
    for copy in first:
        copy.wait_send()
    for copy in x_copies:
        copy.wait_send()
    for copy in drains:
        copy.wait()


def forward(length, table, square, ffn_in, ffn_out, gains_t, x, z_count):
    n_sq, n_ff = square.shape[0], ffn_in.shape[0]
    order = [("gain", 0)]
    order += [("square", n) for n in (0, 1, 2, 3)]
    order += [("cols", n) for n in range(4)] + [("rows", n) for n in range(4)]
    order += [("square", n) for n in (7, 8, 4, 5, 6, 9)]
    order += [("cols", n) for n in range(4, 8)] + [("rows", n) for n in range(4, 8)]
    blocks, band, width = x.shape
    span = blocks * band
    hidden_units = 8 * HALF
    sq_s = (n_sq, z_count, 4, ROWS, width)
    in_s = (n_ff, z_count, 4, ROWS, hidden_units)
    out_s = (n_ff, z_count, 4, 4 * ROWS, width)
    gain_s = (z_count, 4, ROWS, 128)
    firsts = 2 + 5 * n_ff
    vmem = pl.BlockSpec(memory_space=pltpu.VMEM)
    hbm = pl.BlockSpec(memory_space=pltpu.HBM)
    token = ((span, width), bf16)
    token_f = ((span, width), f32)
    outs = [(in_s[1:], bf16), (out_s[1:], bf16), (in_s[1:], bf16), (out_s[1:], bf16)]
    outs += [((8, width), f32), (x.shape, bf16), token, token, token, token, token_f]
    outs += [((span, hidden_units), f32), token_f, token, token, token]
    outs += [(sq_s[1:], bf16)] * n_sq
    scratch = [(sq_s, bf16), (in_s, bf16), (out_s, bf16), (gain_s, bf16)]
    scratch += [((n_sq, ROWS // 2, HALF), f32), ((n_ff, 4, ROWS // 2, HALF), f32)]
    scratch += [((n_ff, 2 * ROWS, HALF), f32), ((ROWS // 2, 128), f32)]
    scratch += [(x.shape, bf16), token, token, token, token, token, token_f]
    scratch += [((span, hidden_units), f32), ((span, hidden_units), bf16), token_f]
    scratch += [token, token, token, ((8, width), f32)]
    dma = pltpu.SemaphoreType.DMA
    return pl.pallas_call(
        functools.partial(forward_kernel, order, z_count),
        out_shape=[jax.ShapeDtypeStruct(*o) for o in outs],
        in_specs=[pl.BlockSpec(memory_space=pltpu.SMEM)] + [vmem] * 5 + [hbm],
        out_specs=[hbm] * len(outs),
        scratch_shapes=[pltpu.VMEM(*o) for o in scratch]
        + [dma((len(order), 7)), dma((len(order), 7)), dma((firsts,)), dma((firsts,))]
        + [dma((3,)), dma((3,)), dma((40,))],
        compiler_params=pltpu.CompilerParams(
            collective_id=0, has_side_effects=True, vmem_limit_bytes=62 * MIB
        ),
        name="forward",
    )(length, table, square, ffn_in, ffn_out, gains_t, x)


class Scatter:
    def __init__(self, units, refs, bufs, sems, z_count):
        self.units, self.refs, self.z_count = units, refs, z_count
        self.r0, self.own, self.r1, self.r2, self.r3, self.fin, self.sib = bufs
        self.send, self.recv, self.local = sems
        self.where = place()
        self.started = []
        self.loads = {}

    def go(self, u, slot, src, dst, peer):
        copy = remote(src, dst, self.send.at[u, slot], self.recv.at[u, slot], peer)
        copy.start()
        self.started.append(copy)

    def got(self, u, slot, ref):
        z, s, c = self.where[:3]
        remote(ref, ref, self.send.at[u, slot], self.recv.at[u, slot], (z, s, 1 - c)).wait_recv()

    def view(self, u, c):
        kind, n = self.units[u]
        return unit_view(kind, n, self.refs[kind], slice(None), slice(None), c)

    def c_start(self, u):
        z, s, c = self.where[:3]
        self.go(u, 0, self.view(u, 1 - c), self.r0.at[u], (z, s, 1 - c))
        copy = pltpu.make_async_copy(self.view(u, c), self.own.at[u % 4], self.local.at[u])
        copy.start()
        self.loads[u] = copy

    def b_start(self, u):
        z, s, c, first, second, both = self.where
        self.loads[u].wait()
        self.got(u, 0, self.r0.at[u])
        for n in range(self.z_count):
            for m in range(4):
                total = self.own[u % 4, n, m].astype(f32) + self.r0[u, n, m].astype(f32)
                self.r0[u, n, m] = total.astype(bf16)
        self.go(u, 1, self.r0.at[u, :, second], self.r1.at[u, 0], (z, second, c))
        self.go(u, 2, self.r0.at[u, :, both], self.r1.at[u, 1], (z, second, c))

    def a_start(self, u):
        z, s, c, first, second, both = self.where
        self.got(u, 2, self.r1.at[u, 1])
        for n in range(self.z_count):
            total = self.r0[u, n, first].astype(f32) + self.r1[u, 1, n].astype(f32)
            self.r1[u, 1, n] = total.astype(bf16)
        self.go(u, 3, self.r1.at[u, 1], self.r2.at[u], (z, first, c))
        self.got(u, 1, self.r1.at[u, 0])
        for n in range(self.z_count):
            total = self.r0[u, n, s].astype(f32) + self.r1[u, 0, n].astype(f32)
            self.r1[u, 0, n] = total.astype(bf16)

    def z_start(self, u):
        z, s, c = self.where[:3]
        self.got(u, 3, self.r2.at[u])
        for n in range(self.z_count):
            total = self.r1[u, 0, n].astype(f32) + self.r2[u, n].astype(f32)
            self.r2[u, n] = total.astype(bf16)
        for d in range(1, self.z_count):
            to = (z + d) % self.z_count
            self.go(u, 3 + d, self.r2.at[u, to], self.r3.at[u, d - 1], (to, s, c))

    def f_start(self, u):
        z, s, c = self.where[:3]
        total = self.r2[u, z].astype(f32)
        for d in range(1, self.z_count):
            self.got(u, 3 + d, self.r3.at[u, d - 1])
            total = total + self.r3[u, d - 1].astype(f32)
        self.fin[u] = total
        kind, n = self.units[u]
        if kind == "rows":
            if n % 2 == 1:
                @pl.when(c != n // 2)
                def _():
                    remote(
                        self.fin.at[pl.ds(u - 1, 2)],
                        self.sib.at[pl.ds(u - 1, 2)],
                        self.send.at[u, 7],
                        self.recv.at[u, 7],
                        (z, s, 1 - c),
                    ).start()
        else:
            rows = pl.ds(pl.multiple_of((1 - c) * (ROWS // 2), 8), ROWS // 2)
            self.go(
                u, 7, self.fin.at[u, rows], self.sib.at[u, pl.ds(0, ROWS // 2)], (z, s, 1 - c)
            )

    def finish_unit(self, u, put):
        z, s, c = self.where[:3]
        kind, n = self.units[u]
        if kind == "rows":
            if n % 2 == 1:

                @pl.when(c == n // 2)
                def _():
                    pair = self.sib.at[pl.ds(u - 1, 2)]
                    self.got(u, 7, pair)
                    for k in range(2):
                        put(kind, (n % 2 - 1 + k) * ROWS, c, self.fin[u - 1 + k])
                        put(kind, (n % 2 - 1 + k) * ROWS, 1 - c, self.sib[u - 1 + k])

                @pl.when(c != n // 2)
                def _():
                    pair = self.fin.at[pl.ds(u - 1, 2)]
                    remote(
                        pair, pair, self.send.at[u, 7], self.recv.at[u, 7], (z, s, 1 - c)
                    ).wait_send()
        else:
            self.got(u, 7, self.sib.at[u, pl.ds(0, ROWS // 2)])
            rows = pl.ds(pl.multiple_of(c * (ROWS // 2), 8), ROWS // 2)
            put(kind, n, c, self.fin[u, rows])
            put(kind, n, 1 - c, self.sib[u, : ROWS // 2])

    def tick(self, t, put, skew=1):
        steps = (self.c_start, self.b_start, self.a_start, self.z_start, self.f_start)
        last = t - 5 * skew
        if 0 <= last < len(self.units):
            self.finish_unit(last, put)
        for n in reversed(range(5)):
            u = t - n * skew
            if 0 <= u < len(self.units):
                steps[n](u)

    def finish(self):
        for copy in self.started:
            copy.wait_send()


def scatter_kernel(
    units, z_count, sq_ref, in_ref, out_ref, x_ref, sq_o, in_o, out_o, x_o,
    r0, own, r1, r2, r3, fin, sib, send, recv, local, x_send, x_recv, x_local,
):
    z, s, c = place()[:3]
    greet(z, s, c, z_count)
    scatter = Scatter(
        units,
        {"square": sq_ref, "cols": in_ref, "rows": out_ref},
        (r0, own, r1, r2, r3, fin, sib),
        (send, recv, local),
        z_count,
    )

    def put(kind, n, side, value):
        if kind == "square":
            sq_o[n, :, cols(side)] = value
        elif kind == "cols":
            in_o[:, cols(side, n * 2 * HALF)] = value
        else:
            out_o[n : n + ROWS, cols(side)] = value

    x_copies = []
    for d in range(1, 4):
        peer = (s + d) % 4
        copy = remote(
            x_ref.at[peer], x_o.at[s], x_send.at[d - 1], x_recv.at[d - 1], (z, peer, c)
        )
        copy.start()
        x_copies.append(copy)
    mine = pltpu.make_async_copy(x_ref.at[s], x_o.at[s], x_local.at[0])
    mine.start()
    skew = 1
    for t in range(len(units) + 5 * skew):
        scatter.tick(t, put, skew)
    scatter.finish()
    for copy in x_copies:
        copy.wait()
    mine.wait()


def scatter_grads(g_sq, g_in, g_out, g_x, z_count):
    n_sq = g_sq.shape[0]
    order = [("square", n) for n in range(4, n_sq)]
    order += [("rows", n) for n in range(4)] + [("cols", n) for n in range(4)]
    order += [("square", n) for n in (3, 0, 1, 2)]
    n = len(order)
    vmem = pl.BlockSpec(memory_space=pltpu.VMEM)
    hbm = pl.BlockSpec(memory_space=pltpu.HBM)
    out_shape = [
        jax.ShapeDtypeStruct((n_sq, ROWS // 2, 2 * HALF), f32),
        jax.ShapeDtypeStruct((ROWS // 2, 8 * HALF), f32),
        jax.ShapeDtypeStruct((2 * ROWS, 2 * HALF), f32),
        jax.ShapeDtypeStruct(g_x.shape, bf16),
    ]
    return pl.pallas_call(
        functools.partial(scatter_kernel, order, z_count),
        out_shape=out_shape,
        in_specs=[hbm] * 4,
        out_specs=[vmem] * 3 + [hbm],
        scratch_shapes=[
            pltpu.VMEM((n, z_count, 4, ROWS, HALF), bf16),
            pltpu.VMEM((4, z_count, 4, ROWS, HALF), bf16),
            pltpu.VMEM((n, 2, z_count, ROWS, HALF), bf16),
            pltpu.VMEM((n, z_count, ROWS, HALF), bf16),
            pltpu.VMEM((n, z_count - 1, ROWS, HALF), bf16),
            pltpu.VMEM((n, ROWS, HALF), f32),
            pltpu.VMEM((n, ROWS, HALF), f32),
            pltpu.SemaphoreType.DMA((n, 8)),
            pltpu.SemaphoreType.DMA((n, 8)),
            pltpu.SemaphoreType.DMA((n,)),
            pltpu.SemaphoreType.DMA((3,)),
            pltpu.SemaphoreType.DMA((3,)),
            pltpu.SemaphoreType.DMA((1,)),
        ],
        compiler_params=pltpu.CompilerParams(
            collective_id=1, has_side_effects=True, vmem_limit_bytes=60 * MIB
        ),
        name="scatter_grads",
    )(g_sq, g_in, g_out, g_x)


def total_kernel(z_count, in_ref, out_ref, acc, got, send, recv):
    z, s, c = place()[:3]
    greet(z, s, c, z_count)
    started = []
    slot = 0

    def exchange(peers):
        nonlocal slot
        base = slot
        for peer in peers:
            copy = remote(acc, got.at[slot], send.at[slot], recv.at[slot], peer)
            copy.start()
            started.append(copy)
            slot += 1
        for copy in started[base:]:
            copy.wait()
        total = acc[...]
        for k in range(base, slot):
            total = total + got[k]
        acc[...] = total

    acc[...] = in_ref[...]
    exchange([(z, s, 1 - c)])
    exchange([(z, (s + d) % 4, c) for d in range(1, 4)])
    exchange([((z + d) % z_count, s, c) for d in range(1, z_count)])
    out_ref[...] = acc[...]


def total_all(x, z_count):
    vmem = pl.BlockSpec(memory_space=pltpu.VMEM)
    slots = z_count + 3
    return pl.pallas_call(
        functools.partial(total_kernel, z_count),
        out_shape=jax.ShapeDtypeStruct(x.shape, f32),
        in_specs=[vmem],
        out_specs=vmem,
        scratch_shapes=[
            pltpu.VMEM(x.shape, f32),
            pltpu.VMEM((slots,) + x.shape, f32),
            pltpu.SemaphoreType.DMA((slots,)),
            pltpu.SemaphoreType.DMA((slots,)),
        ],
        compiler_params=pltpu.CompilerParams(collective_id=2, has_side_effects=True),
        name="total_all",
    )(x)


def on_device(
    inputs,
    dec_in,
    cotangent,
    lengths,
    bucket_table,
    square,
    square_m,
    square_v,
    ffn_in,
    ffn_in_m,
    ffn_in_v,
    ffn_out,
    ffn_out_m,
    ffn_out_v,
    gains,
    gains_m,
    gains_v,
    rel_bias,
    rel_bias_m,
    rel_bias_v,
):
    z_count = lax.axis_size("dp")
    width = inputs.shape[2]
    direct = lax.axis_size("seq") == 4 and width == 2 * HALF and width == 4 * z_count * ROWS
    direct = direct and inputs.shape[:2] == (4, BAND)
    w = {}
    seq_pos = lax.axis_index("seq")
    local_len = inputs.shape[1]
    span = local_len * lax.axis_size("seq")
    bucket_count = rel_bias.shape[0]
    scale = 1.0 / math.sqrt(HD)
    length = lax.dynamic_slice_in_dim(lengths, seq_pos, 1, 0)
    key_valid = jnp.arange(span)[None, :] < length[:, None]
    one_hot = (
        jnp.pad(bucket_table, (0, 1), constant_values=-1)[:, None]
        == jnp.arange(bucket_count)[None, :]
    ).astype(f32)
    table = jnp.einsum("ob,bh->ho", one_hot, rel_bias, precision=highest_precision)[:, None, :]

    if direct:
        gains_t = jnp.pad(gains.T, ((0, 0), (0, 128 - gains.shape[0])))
        outs = forward(length, table, square, ffn_in, ffn_out, gains_t, inputs, z_count)
        w_in_e, w_out_e, w_in_d, w_out_d = (
            outs[0].reshape(width, -1),
            outs[1].reshape(-1, width),
            outs[2].reshape(width, -1),
            outs[3].reshape(-1, width),
        )
        gain_f = outs[4][: gains.shape[0]]
        x_b = outs[5].reshape(-1, width)
        q, k, v, attended, hidden, pre_act, hidden_two, encoded, cross_k, cross_v = outs[6:16]
        for i in range(square.shape[0]):
            w[i] = outs[16 + i].reshape(width, width)
        x_f = x_b.astype(f32)
        normed = rms_gain(x_f, gain_f[0]).astype(bf16)
        normed_two = rms_gain(hidden, gain_f[1]).astype(bf16)
        inner_act = gelu_tanh(pre_act).astype(bf16)
    else:

        def gather_rows(x):
            return lax.all_gather(x.astype(bf16), AXES, axis=x.ndim - 2, tiled=True)

        sq_a = gather_rows(square[:4])
        w_in_e = gather_rows(ffn_in[0])
        w_out_e = gather_rows(ffn_out[0])
        sq_b = gather_rows(square[4:])
        w_in_d = gather_rows(ffn_in[1])
        w_out_d = gather_rows(ffn_out[1])
        gain_f = lax.all_gather(gains.astype(bf16), AXES, axis=1, tiled=True).astype(f32)
        for i in range(square.shape[0]):
            w[i] = sq_a[i] if i < 4 else sq_b[i - 4]
        x_b = lax.all_to_all(inputs, "seq", split_axis=0, concat_axis=1, tiled=True)[0]
        x_f = x_b.astype(f32)
        normed = rms_gain(x_f, gain_f[0]).astype(bf16)
        q = matmul(normed, w[0]).astype(bf16)
        k = matmul(normed, w[1]).astype(bf16)
        v = matmul(normed, w[2]).astype(bf16)
        attended = attend_fwd(length, table, q, k, v)
        hidden = x_f + matmul(attended, w[3])
        normed_two = rms_gain(hidden, gain_f[1]).astype(bf16)
        pre_act = matmul(normed_two, w_in_e)
        inner_act = gelu_tanh(pre_act).astype(bf16)
        hidden_two = hidden + matmul(inner_act, w_out_e)
        encoded = rms_gain(hidden_two, gain_f[2]).astype(bf16)
        cross_k = matmul(encoded, w[7]).astype(bf16)
        cross_v = matmul(encoded, w[8]).astype(bf16)

    dec_row = dec_in.reshape(1, width).astype(f32)
    self_norm = rms_gain(dec_row, gain_f[3]).astype(bf16)
    self_values = matmul(self_norm, w[4]).astype(bf16)
    dec_one = dec_row + matmul(self_values, w[5])
    cross_norm = rms_gain(dec_one, gain_f[4]).astype(bf16)
    cross_q = matmul(cross_norm, w[6]).astype(bf16)
    head_of = (jnp.arange(width)[None, :] // HD == jnp.arange(H)[:, None]).astype(bf16)
    q_heads = head_of * cross_q
    cross_scores = jnp.where(key_valid, mm_t(q_heads, cross_k) * scale, neg_fill)
    cross_probs = jax.nn.softmax(cross_scores, axis=-1)
    cross_probs_b = cross_probs.astype(bf16)
    cross_att = jnp.sum(
        matmul(cross_probs_b, cross_v) * head_of.astype(f32), axis=0, keepdims=True
    ).astype(bf16)
    dec_two = dec_one + matmul(cross_att, w[9])
    ffn_norm = rms_gain(dec_two, gain_f[5]).astype(bf16)
    pre_dec = matmul(ffn_norm, w_in_d)
    inner_dec = gelu_tanh(pre_dec).astype(bf16)
    dec_out = dec_two + matmul(inner_dec, w_out_d)

    g_top_b = cotangent.reshape(1, width)
    g_top = g_top_b.astype(f32)
    g_pre_dec = gelu_pull(pre_dec, mm_t(g_top_b, w_out_d)).astype(bf16)
    g_two_norm, g_gain_five = rms_pull(dec_two, gain_f[5], mm_t(g_pre_dec, w_in_d))
    g_two = g_top + g_two_norm
    g_two_b = g_two.astype(bf16)
    g_att = mm_t(g_two_b, w[9]).astype(bf16)
    g_att_heads = head_of * g_att
    g_probs = mm_t(g_att_heads, cross_v)
    g_cross_v = mm_outer(cross_probs_b, g_att_heads).astype(bf16)
    g_scores = cross_probs * (g_probs - jnp.sum(g_probs * cross_probs, axis=-1, keepdims=True))
    g_scores_b = g_scores.astype(bf16)
    g_cross_q = (
        jnp.sum(matmul(g_scores_b, cross_k) * head_of.astype(f32), axis=0, keepdims=True) * scale
    ).astype(bf16)
    g_cross_k = (mm_outer(g_scores_b, q_heads) * scale).astype(bf16)
    g_one_norm, g_gain_four = rms_pull(dec_one, gain_f[4], mm_t(g_cross_q, w[6]))
    g_one_b = (g_two + g_one_norm).astype(bf16)
    g_self_values = mm_t(g_one_b, w[5]).astype(bf16)
    g_gain_three = rms_pull(dec_row, gain_f[3], mm_t(g_self_values, w[4]))[1]

    lefts = (self_norm, self_values, cross_norm, cross_att, ffn_norm, inner_dec)
    rights = (g_self_values, g_one_b, g_cross_q, g_two_b, g_pre_dec, g_top_b)
    own_row = jnp.concatenate(lefts + rights, axis=1)
    own_row = jnp.pad(own_row, ((0, 0), (0, 20 * 1024 - own_row.shape[1])))
    packed = lax.all_gather(own_row, AXES, axis=0, tiled=True)
    me = (
        lax.axis_index("dp") * lax.axis_size("seq") + seq_pos
    ) * lax.axis_size("head") + lax.axis_index("head")
    devices = packed.shape[0]
    cuts = [0]
    for piece in lefts + rights:
        cuts.append(cuts[-1] + piece.shape[1])
    dec_grads = []
    for n in range(6):
        share = lefts[n].shape[1] // devices
        left = lax.dynamic_slice_in_dim(packed, cuts[n] + me * share, share, 1)
        right = packed[:, cuts[6 + n] : cuts[7 + n]]
        dec_grads.append(mm_outer(left, right))

    g_w7 = mm_outer(encoded, g_cross_k)
    g_w8 = mm_outer(encoded, g_cross_v)
    g_encoded = mm_t(g_cross_k, w[7]) + mm_t(g_cross_v, w[8])
    g_hidden_two, g_gain_two = rms_pull(hidden_two, gain_f[2], g_encoded)
    g_hidden_two_b = g_hidden_two.astype(bf16)
    g_out_e = mm_outer(inner_act, g_hidden_two_b)
    g_pre = gelu_pull(pre_act, mm_t(g_hidden_two_b, w_out_e)).astype(bf16)
    g_in_e = mm_outer(normed_two, g_pre)
    g_hidden_norm, g_gain_one = rms_pull(hidden, gain_f[1], mm_t(g_pre, w_in_e))
    g_hidden = g_hidden_two + g_hidden_norm
    g_hidden_b = g_hidden.astype(bf16)
    g_w3 = mm_outer(attended, g_hidden_b)
    g_attended = mm_t(g_hidden_b, w[3]).astype(bf16)
    gq, gk, gv, g_table = attend_bwd(length, table, q, k, v, g_attended)
    g_bias_here = jnp.einsum("ob,ho->bh", one_hot, g_table[:, 0, :], precision=highest_precision)
    g_w0 = mm_outer(normed, gq)
    g_w1 = mm_outer(normed, gk)
    g_w2 = mm_outer(normed, gv)
    g_normed = mm_t(gq, w[0]) + mm_t(gk, w[1]) + mm_t(gv, w[2])
    g_input_norm, g_gain_zero = rms_pull(x_f, gain_f[0], g_normed)
    g_x = (g_hidden + g_input_norm).astype(bf16)
    if direct:
        g_sq = jnp.stack([g.astype(bf16) for g in (g_w0, g_w1, g_w2, g_w3, g_w7, g_w8)])
        s_sq, s_in, s_out, input_grad = scatter_grads(
            g_sq.reshape(6, z_count, 4, ROWS, width),
            g_in_e.astype(bf16).reshape(1, z_count, 4, ROWS, -1),
            g_out_e.astype(bf16).reshape(1, z_count, 4, -1, width),
            g_x.reshape(inputs.shape),
            z_count,
        )
        s_0123, s_78 = s_sq[:4], s_sq[4:]
        input_grad = input_grad.astype(f32)
    else:
        input_grad = lax.all_to_all(
            g_x[None], "seq", split_axis=1, concat_axis=0, tiled=True
        ).astype(f32)

        def scatter_rows(x):
            return lax.psum_scatter(
                x.astype(bf16), AXES, scatter_dimension=x.ndim - 2, tiled=True
            ).astype(f32)

        s_78 = scatter_rows(jnp.stack((g_w7, g_w8)))
        s_out = scatter_rows(g_out_e)
        s_in = scatter_rows(g_in_e)
        s_0123 = scatter_rows(jnp.stack((g_w0, g_w1, g_w2, g_w3)))
    summed_sq = jnp.stack(
        (
            s_0123[0],
            s_0123[1],
            s_0123[2],
            s_0123[3],
            dec_grads[0],
            dec_grads[1],
            dec_grads[2],
            s_78[0],
            s_78[1],
            dec_grads[3],
        )
    )
    summed_in = jnp.stack((s_in, dec_grads[4]))
    summed_out = jnp.stack((s_out, dec_grads[5]))
    g_gains = jnp.stack(
        (g_gain_zero, g_gain_one, g_gain_two, g_gain_three, g_gain_four, g_gain_five)
    )
    gain_share = gains.shape[1]
    local_squares = (
        jnp.sum(summed_sq * summed_sq)
        + jnp.sum(summed_in * summed_in)
        + jnp.sum(summed_out * summed_out)
    )
    if direct:
        rest = jnp.concatenate((g_bias_here.reshape(-1), local_squares[None]))
        rest = jnp.pad(rest, (0, 1024 - rest.shape[0])).reshape(8, 128)
        wide = jnp.concatenate((jnp.pad(g_gains, ((0, 2), (0, 0))), rest), axis=1)
        wide = total_all(wide, z_count)
        g_gains = wide[:6, :width]
        rest = wide[:, width:].reshape(-1)
        g_bias = rest[: g_bias_here.size].reshape(g_bias_here.shape)
        shard_squares = rest[g_bias_here.size]
    else:
        g_gains, g_bias, shard_squares = lax.psum((g_gains, g_bias_here, local_squares), AXES)
    summed_gain = lax.dynamic_slice_in_dim(g_gains, me * gain_share, gain_share, 1)
    grad_norm = jnp.sqrt(shard_squares + jnp.sum(g_gains * g_gains) + jnp.sum(g_bias * g_bias))
    factor = clip_bound / jnp.maximum(grad_norm, clip_bound)
    return (
        dec_out.astype(bf16).reshape(dec_in.shape),
        input_grad,
        grad_norm,
        *adam_step(square, square_m, square_v, summed_sq, factor, rate_matrix, decay_rate),
        *adam_step(ffn_in, ffn_in_m, ffn_in_v, summed_in, factor, rate_matrix, decay_rate),
        *adam_step(ffn_out, ffn_out_m, ffn_out_v, summed_out, factor, rate_matrix, decay_rate),
        *adam_step(gains, gains_m, gains_v, summed_gain, factor, rate_small, 0.0),
        *adam_step(rel_bias, rel_bias_m, rel_bias_v, g_bias, factor, rate_small, 0.0),
    )


def solution(mesh):
    rows = P(("dp", "head"), "seq", None)
    shard = P(None, AXES, None)
    small = P(None, AXES)
    return jax.shard_map(
        on_device,
        mesh=mesh,
        in_specs=(rows, rows, rows, P(("dp", "head")), P())
        + (shard,) * 9
        + (small,) * 3
        + (P(),) * 3,
        out_specs=(rows, rows, P()) + (shard,) * 9 + (small,) * 3 + (P(),) * 3,
        check_vma=False,
    )
```

```python
import functools
import math

import jax
import jax.numpy as jnp
from jax import lax
from jax.experimental import pallas as pl
from jax.experimental.pallas import tpu as pltpu
from jax.sharding import PartitionSpec as P

H = 12
HD = 64
STEP = 5
AXES = ("dp", "seq", "head")

norm_eps = 1e-06
neg_fill = -1e30
beta_one = 0.9
beta_two = 0.999
adam_eps = 1e-08
decay_rate = 0.01
rate_matrix = 0.05
rate_small = 0.5
clip_bound = 1.0
highest_precision = lax.Precision.HIGHEST
bf16 = jnp.bfloat16
f32 = jnp.float32
BAND = 128


def rms_gain(values_in, gain_row):
    return (
        values_in
        * lax.rsqrt(jnp.mean(values_in * values_in, axis=-1, keepdims=True) + norm_eps)
        * gain_row
    )


def gelu_tanh(values_in):
    return jax.nn.gelu(values_in, approximate=True)


def matmul(left, right):
    return jnp.dot(left, right, preferred_element_type=f32)


def mm_t(left, right):
    return lax.dot_general(left, right, (((1,), (1,)), ((), ())), preferred_element_type=f32)


def mm_outer(left, right):
    return lax.dot_general(left, right, (((0,), (0,)), ((), ())), preferred_element_type=f32)


def rms_pull(values_in, gain_row, incoming):
    _, pull = jax.vjp(rms_gain, values_in, gain_row)
    return pull(incoming)


def gelu_pull(values_in, incoming):
    _, pull = jax.vjp(gelu_tanh, values_in)
    return pull(incoming)[0]


def adam_step(weight, first, second, grad, factor, rate, decay):
    grad = grad * factor
    first = beta_one * first + (1.0 - beta_one) * grad
    second = beta_two * second + (1.0 - beta_two) * grad * grad
    first_hat = first / (1.0 - beta_one**STEP)
    second_hat = second / (1.0 - beta_two**STEP)
    weight = weight - rate * (first_hat / (jnp.sqrt(second_hat) + adam_eps) + decay * weight)
    return (weight, first, second)


def bias_band(table_row, span):
    wide = jnp.broadcast_to(table_row, (BAND, 2 * span))
    shift = (2 * span - (BAND - 1)) % (2 * span)
    return pltpu.roll(wide, shift, 1, stride=1, stride_axis=0)


def band_sums(band, span):
    wide = 2 * span
    rows = BAND
    while rows > 8:
        rows //= 2
        band = band[:rows] + pltpu.roll(band[rows:], wide - rows, 1)
    row = lax.broadcasted_iota(jnp.int32, band.shape, 0)
    for step in (4, 2, 1):
        band = jnp.where((row // step) % 2 == 1, pltpu.roll(band, wide - step, 1), band)
    return pltpu.roll(jnp.sum(band, axis=0, keepdims=True), BAND - 1, 1)


def softmax_rows(q_rows, k_all, band, block, span, valid):
    start = span - BAND * (block + 1)
    scores = mm_t(q_rows, k_all) * (1.0 / math.sqrt(HD)) + band[:, start : start + span]
    scores = jnp.where(valid, scores, neg_fill)
    peak = jnp.max(scores, axis=-1, keepdims=True)
    raised = jnp.exp(scores - peak)
    return raised / jnp.sum(raised, axis=-1, keepdims=True)


def attend_fwd_kernel(len_ref, table_ref, q_ref, k_ref, v_ref, o_ref):
    span = k_ref.shape[0]
    valid = lax.broadcasted_iota(jnp.int32, (1, span), 1) < len_ref[0]
    lane = lax.broadcasted_iota(jnp.int32, (1, 2 * HD), 1)
    k_all = k_ref[...]
    v_all = v_ref[...]
    bands = [bias_band(table_ref[t], span) for t in range(2)]
    for block in range(span // BAND):
        rows = slice(block * BAND, (block + 1) * BAND)
        q_rows = q_ref[rows, :]
        parts = []
        for t in range(2):
            own = (lane // HD) == t
            probs = softmax_rows(
                jnp.where(own, q_rows, jnp.zeros_like(q_rows)), k_all, bands[t], block, span, valid
            )
            parts.append(matmul(probs.astype(bf16), v_all))
        o_ref[rows, :] = jnp.where(lane < HD, parts[0], parts[1]).astype(bf16)


def attend_bwd_kernel(
    len_ref, table_ref, q_ref, k_ref, v_ref, do_ref, dq_ref, dk_ref, dv_ref, dt_ref
):
    span = k_ref.shape[0]
    scale = 1.0 / math.sqrt(HD)
    valid = lax.broadcasted_iota(jnp.int32, (1, span), 1) < len_ref[0]
    lane = lax.broadcasted_iota(jnp.int32, (1, 2 * HD), 1)
    k_all = k_ref[...]
    v_all = v_ref[...]
    count = span // BAND
    dks, dvs = [], []
    dqs = [[None, None] for _ in range(count)]
    for t in range(2):
        own = (lane // HD) == t
        band = bias_band(table_ref[t], span)
        dk = jnp.zeros((span, 2 * HD), f32)
        dv = jnp.zeros((span, 2 * HD), f32)
        dband = jnp.zeros((BAND, 2 * span), f32)
        for block in range(count):
            rows = slice(block * BAND, (block + 1) * BAND)
            q_rows = q_ref[rows, :]
            do_rows = do_ref[rows, :]
            zero = jnp.zeros_like(q_rows)
            probs = softmax_rows(
                jnp.where(own, q_rows, zero), k_all, band, block, span, valid
            )
            dprobs = mm_t(jnp.where(own, do_rows, zero), v_all)
            dscore = probs * (dprobs - jnp.sum(dprobs * probs, axis=-1, keepdims=True))
            start = span - BAND * (block + 1)
            pieces = []
            if start:
                pieces.append(jnp.zeros((BAND, start), f32))
            pieces.append(dscore)
            if span - start:
                pieces.append(jnp.zeros((BAND, span - start), f32))
            dband = dband + jnp.concatenate(pieces, axis=1)
            dscore_b = dscore.astype(bf16)
            dv = dv + mm_outer(probs.astype(bf16), do_rows)
            dk = dk + mm_outer(dscore_b, q_rows)
            dqs[block][t] = matmul(dscore_b, k_all)
        dks.append(dk)
        dvs.append(dv)
        dt_ref[t] = band_sums(dband, span)
    dk_ref[...] = (jnp.where(lane < HD, dks[0], dks[1]) * scale).astype(bf16)
    dv_ref[...] = jnp.where(lane < HD, dvs[0], dvs[1]).astype(bf16)
    for block in range(count):
        rows = slice(block * BAND, (block + 1) * BAND)
        dq_ref[rows, :] = (jnp.where(lane < HD, dqs[block][0], dqs[block][1]) * scale).astype(bf16)


def head_specs(span, width, n):
    return [pl.BlockSpec((span, 2 * HD), lambda i: (0, i)) for _ in range(n)]


def attend_fwd(length, table, q, k, v):
    span, width = q.shape
    return pl.pallas_call(
        attend_fwd_kernel,
        grid=(width // (2 * HD),),
        out_shape=jax.ShapeDtypeStruct((span, width), bf16),
        in_specs=[
            pl.BlockSpec(memory_space=pltpu.SMEM),
            pl.BlockSpec((2, 1, 2 * span), lambda i: (i, 0, 0)),
            *head_specs(span, width, 3),
        ],
        out_specs=head_specs(span, width, 1)[0],
        compiler_params=pltpu.CompilerParams(vmem_limit_bytes=48 * 1024 * 1024),
        name="attend_fwd",
    )(length, table, q, k, v)


def attend_bwd(length, table, q, k, v, do):
    span, width = q.shape
    like = jax.ShapeDtypeStruct((span, width), bf16)
    return pl.pallas_call(
        attend_bwd_kernel,
        grid=(width // (2 * HD),),
        out_shape=(like, like, like, jax.ShapeDtypeStruct(table.shape, f32)),
        in_specs=[
            pl.BlockSpec(memory_space=pltpu.SMEM),
            pl.BlockSpec((2, 1, 2 * span), lambda i: (i, 0, 0)),
            *head_specs(span, width, 4),
        ],
        out_specs=(
            *head_specs(span, width, 3),
            pl.BlockSpec((2, 1, 2 * span), lambda i: (i, 0, 0)),
        ),
        compiler_params=pltpu.CompilerParams(vmem_limit_bytes=48 * 1024 * 1024),
        name="attend_bwd",
    )(length, table, q, k, v, do)


MESH_ID = pl.DeviceIdType.MESH
HALF = 384
ROWS = 48
MIB = 1024 * 1024


def place():
    z, s, c = lax.axis_index("dp"), lax.axis_index("seq"), lax.axis_index("head")
    near = s + 1 - 2 * (s % 2)
    far = (s + 2) % 4
    first = near + c * (far - near)
    second = far + c * (near - far)
    return z, s, c, first, second, 3 - s


def greet(z, s, c, z_count):
    barrier = pltpu.get_barrier_semaphore()
    for d in range(1, z_count):
        peer = ((z + d) % z_count, s, c)
        pl.semaphore_signal(barrier, 1, device_id=peer, device_id_type=MESH_ID)
    for d in range(1, 4):
        peer = (z, (s + d) % 4, c)
        pl.semaphore_signal(barrier, 1, device_id=peer, device_id_type=MESH_ID)
    pl.semaphore_signal(barrier, 1, device_id=(z, s, 1 - c), device_id_type=MESH_ID)
    pl.semaphore_wait(barrier, z_count + 3)


def remote(src, dst, send, recv, peer):
    return pltpu.make_async_remote_copy(
        src, dst, send, recv, device_id=peer, device_id_type=MESH_ID
    )


def cols(c, base=0):
    return pl.ds(pl.multiple_of(base + c * HALF, 128), HALF)


def unit_view(kind, n, ref, z, s, c):
    if kind == "square":
        return ref.at[n, z, s, :, cols(c)]
    if kind == "cols":
        return ref.at[n // 4, z, s, :, cols(c, (n % 4) * 2 * HALF)]
    if kind == "rows":
        return ref.at[n // 4, z, s, pl.ds((n % 4) * ROWS, ROWS), cols(c)]
    return ref.at[z, s]


class Gather:
    def __init__(self, units, refs, send, recv, z_count):
        self.units, self.refs, self.send, self.recv = units, refs, send, recv
        self.z_count = z_count
        self.where = place()
        self.started = []

    def view(self, u, z, s, c):
        kind, n = self.units[u]
        return unit_view(kind, n, self.refs[kind], z, s, c)

    def go(self, u, slot, ref, peer):
        copy = remote(ref, ref, self.send.at[u, slot], self.recv.at[u, slot], peer)
        copy.start()
        self.started.append(copy)

    def got(self, u, slot, ref):
        z, s, c = self.where[:3]
        remote(ref, ref, self.send.at[u, slot], self.recv.at[u, slot], (z, s, 1 - c)).wait_recv()

    def z_start(self, u):
        z, s, c = self.where[:3]
        for d in range(1, self.z_count):
            self.go(u, d - 1, self.view(u, z, s, c), ((z + d) % self.z_count, s, c))

    def z_wait(self, u):
        z, s, c = self.where[:3]
        for d in range(1, self.z_count):
            self.got(u, d - 1, self.view(u, (z + self.z_count - d) % self.z_count, s, c))

    def a_start(self, u):
        z, s, c, first, second, both = self.where
        self.go(u, 3, self.view(u, slice(None), s, c), (z, first, c))

    def a_wait(self, u):
        z, s, c, first, second, both = self.where
        self.got(u, 3, self.view(u, slice(None), first, c))

    def b_start(self, u):
        z, s, c, first, second, both = self.where
        self.go(u, 4, self.view(u, slice(None), s, c), (z, second, c))
        self.go(u, 5, self.view(u, slice(None), first, c), (z, second, c))

    def b_wait(self, u):
        z, s, c, first, second, both = self.where
        self.got(u, 4, self.view(u, slice(None), second, c))
        self.got(u, 5, self.view(u, slice(None), both, c))

    def s_start(self, u):
        z, s, c = self.where[:3]
        if self.units[u][0] != "gain":
            self.go(u, 6, self.view(u, slice(None), slice(None), c), (z, s, 1 - c))

    def s_wait(self, u):
        z, s, c = self.where[:3]
        if self.units[u][0] != "gain":
            self.got(u, 6, self.view(u, slice(None), slice(None), 1 - c))

    def tick(self, t, skew=2, done=None):
        steps = (
            (self.z_start,),
            (self.z_wait, self.a_start),
            (self.a_wait, self.b_start),
            (self.b_wait, self.s_start),
            (self.s_wait,) + ((done,) if done else ()),
        )
        for n, work in enumerate(steps):
            u = t - n * skew
            if 0 <= u < len(self.units):
                for step in work:
                    step(u)

    def finish(self):
        for copy in self.started:
            copy.wait_send()


def row_blocks(count, work):
    def body(i, carry):
        work(i, pl.ds(pl.multiple_of(i * BAND, BAND), BAND))
        return carry

    lax.fori_loop(0, count, body, 0)


def col_tiles(width, tile, work):
    def body(i, carry):
        work(pl.ds(pl.multiple_of(i * tile, tile), tile))
        return carry

    lax.fori_loop(0, width // tile, body, 0)


def wide(value):
    return value.reshape(value.shape[0] * value.shape[1] * value.shape[2], value.shape[3])


def attend_pair_fwd(pair, length, table_ref, q_ref, k_ref, v_ref, o_ref):
    span = k_ref.shape[0]
    at = pl.ds(pl.multiple_of(pair * 2 * HD, 2 * HD), 2 * HD)
    valid = lax.broadcasted_iota(jnp.int32, (1, span), 1) < length
    lane = lax.broadcasted_iota(jnp.int32, (1, 2 * HD), 1)
    k_all = k_ref[:, at]
    v_all = v_ref[:, at]
    bands = [bias_band(table_ref[2 * pair + t], span) for t in range(2)]
    for block in range(span // BAND):
        rows = slice(block * BAND, (block + 1) * BAND)
        q_rows = q_ref[rows, at]
        parts = []
        for t in range(2):
            own = (lane // HD) == t
            probs = softmax_rows(
                jnp.where(own, q_rows, jnp.zeros_like(q_rows)), k_all, bands[t], block, span, valid
            )
            parts.append(matmul(probs.astype(bf16), v_all))
        o_ref[rows, at] = jnp.where(lane < HD, parts[0], parts[1]).astype(bf16)


def forward_kernel(units, z_count, *refs):
    (
        len_ref, table_ref, sq_ref, in_ref, out_ref, gain_ref, x_ref,
        in_o, out_o, in_d, out_d, gain_o, x_o, q_o, k_o, v_o, att_o, hid_o, pre_o,
        hid2_o, enc_o, ck_o, cv_o,
        sq_o0, sq_o1, sq_o2, sq_o3, sq_o4, sq_o5, sq_o6, sq_o7, sq_o8, sq_o9,
        sq_w, in_w, out_w, gain_w, sq_r, in_r, out_r, gain_r,
        x_s, n_s, q_s, k_s, v_s, att_s, hid_s, pre_s, inner_s, hid2_s, enc_s, ck_s, cv_s, gains,
        send, recv, first_send, first_recv, x_send, x_recv, local,
    ) = refs
    z, s, c = place()[:3]
    sibling = (z, s, 1 - c)
    sq_o = (sq_o0, sq_o1, sq_o2, sq_o3, sq_o4, sq_o5, sq_o6, sq_o7, sq_o8, sq_o9)
    n_sq, n_ff = sq_ref.shape[0], in_ref.shape[0]
    blocks = x_s.shape[0] * x_s.shape[1] // BAND
    greet(z, s, c, z_count)

    first = []

    def to_sibling(src, dst):
        copy = remote(src, dst, first_send.at[len(first)], first_recv.at[len(first)], sibling)
        copy.start()
        first.append(copy)

    to_sibling(gain_ref, gain_r)
    to_sibling(sq_ref.at[:, :, cols(1 - c)], sq_r)
    x_copies = []
    for d in range(1, 4):
        peer = (s + d) % 4
        copy = remote(
            x_ref.at[peer], x_s.at[s], x_send.at[d - 1], x_recv.at[d - 1], (z, peer, c)
        )
        copy.start()
        x_copies.append(copy)
    mine = pltpu.make_async_copy(x_ref.at[s], x_s.at[s], local.at[0])
    mine.start()
    for n in range(n_ff):
        for j in range(4):
            to_sibling(in_ref.at[n, :, cols(1 - c, 2 * HALF * j)], in_r.at[n, j])
        to_sibling(out_ref.at[n, :, cols(1 - c)], out_r.at[n])

    def joined(own, other):
        top = jnp.where(c == 0, own, other)
        bottom = jnp.where(c == 0, other, own)
        return jnp.concatenate([top, bottom], axis=0).astype(bf16)

    gather = Gather(
        units,
        {"square": sq_w, "cols": in_w, "rows": out_w, "gain": gain_w},
        send,
        recv,
        z_count,
    )
    first[0].wait_recv()
    gain_w[z, s] = joined(gain_ref[...], gain_r[...])
    first[1].wait_recv()
    for n in range(n_sq):
        sq_w[n, z, s, :, cols(c)] = joined(sq_ref[n, :, cols(c)], sq_r[n])
    drains = []

    def drain(src, dst):
        copy = pltpu.make_async_copy(src, dst, local.at[1 + len(drains)])
        copy.start()
        drains.append(copy)

    def done(u):
        kind, n = units[u]
        if kind == "square":
            drain(sq_w.at[n], sq_o[n])
        elif kind == "cols" and n % 4 == 3:
            drain(in_w.at[n // 4], (in_o, in_d)[n // 4])
        elif kind == "rows" and n % 4 == 3:
            drain(out_w.at[n // 4], (out_o, out_d)[n // 4])

    def normed(src, gain_row, dst):
        def work(i, at):
            dst[at, :] = rms_gain(src(i, at), gains[gain_row : gain_row + 1, :]).astype(bf16)

        row_blocks(blocks, work)

    def x_rows(i, at):
        return x_s[i].astype(f32)

    def start_piece():
        for copy in x_copies:
            copy.wait_recv()
        mine.wait()
        drain(x_s, x_o)
        gains[...] = wide(gain_w[...]).astype(f32).T[:8]
        drain(gains, gain_o)
        normed(x_rows, 0, n_s)

    def square_dot(left, n, tile=256):
        def weight(at):
            return wide(sq_w[n, :, :, :, at])

        return lambda at: matmul(left[...], weight(at))

    def project(n, left, dst, out):
        dot = square_dot(left, n)

        def work(at):
            dst[:, at] = dot(at).astype(bf16)

        col_tiles(2 * HALF, 256, work)
        drain(dst, out)

    def attention(pairs):
        def body(pair, carry):
            attend_pair_fwd(pair, len_ref[0], table_ref, q_s, k_s, v_s, att_s)
            return carry

        lax.fori_loop(pairs[0], pairs[1], body, 0)

    def hidden_piece():
        drain(att_s, att_o)
        dot = square_dot(att_s, 3)

        def work(at):
            hid_s[:, at] = dot(at)

        col_tiles(2 * HALF, 256, work)

        def add(i, at):
            total = hid_s[at, :] + x_rows(i, at)
            hid_s[at, :] = total
            n_s[at, :] = rms_gain(total, gains[1:2, :]).astype(bf16)

        row_blocks(blocks, add)
        drain(hid_s, hid_o)

    def ffn_piece(j):
        def work(i, carry):
            at = pl.ds(pl.multiple_of(j * 2 * HALF + i * 256, 256), 256)
            pre = matmul(n_s[...], wide(in_w[0, :, :, :, at]))
            pre_s[:, at] = pre
            inner_s[:, at] = gelu_tanh(pre).astype(bf16)
            return carry

        lax.fori_loop(0, 3, work, 0)

    def hidden_two_piece():
        drain(pre_s, pre_o)

        def work(at):
            hid2_s[:, at] = hid_s[:, at] + matmul(inner_s[...], wide(out_w[0, :, :, :, at]))

        col_tiles(2 * HALF, 256, work)
        normed(lambda i, at: hid2_s[at, :], 2, enc_s)
        drain(hid2_s, hid2_o)
        drain(enc_s, enc_o)

    skew = 2
    pieces = {
        6: [start_piece],
        9: [lambda: project(0, n_s, q_s, q_o)],
        10: [lambda: project(1, n_s, k_s, k_o)],
        11: [lambda: project(2, n_s, v_s, v_o), lambda: attention((0, 2))],
        12: [lambda: attention((2, 4))],
        13: [lambda: attention((4, 6))],
        14: [hidden_piece, lambda: ffn_piece(0)],
        15: [lambda: ffn_piece(1), lambda: ffn_piece(2)],
        16: [lambda: ffn_piece(3)],
        20: [hidden_two_piece],
        21: [lambda: project(7, enc_s, ck_s, ck_o)],
        22: [lambda: project(8, enc_s, cv_s, cv_o)],
    }
    k = 2
    for t in range(len(units) + 4 * skew):
        gather.tick(t, skew, done)
        if t == 1:
            for n in range(n_ff):
                for j in range(4):
                    first[k].wait_recv()
                    k += 1
                    at = cols(c, 2 * HALF * j)
                    in_w[n, z, s, :, at] = joined(in_ref[n, :, at], in_r[n, j])
                first[k].wait_recv()
                k += 1
                out_w[n, z, s, :, cols(c)] = joined(out_ref[n, :, cols(c)], out_r[n])
        for piece in pieces.get(t, ()):
            piece()
    gather.finish()
    for copy in first:
        copy.wait_send()
    for copy in x_copies:
        copy.wait_send()
    for copy in drains:
        copy.wait()


def forward(length, table, square, ffn_in, ffn_out, gains_t, x, z_count):
    n_sq, n_ff = square.shape[0], ffn_in.shape[0]
    order = [("gain", 0)]
    order += [("square", n) for n in (0, 1, 2, 3)]
    order += [("cols", n) for n in range(4)] + [("rows", n) for n in range(4)]
    order += [("square", n) for n in (7, 8, 4, 5, 6, 9)]
    order += [("cols", n) for n in range(4, 8)] + [("rows", n) for n in range(4, 8)]
    blocks, band, width = x.shape
    span = blocks * band
    hidden_units = 8 * HALF
    sq_s = (n_sq, z_count, 4, ROWS, width)
    in_s = (n_ff, z_count, 4, ROWS, hidden_units)
    out_s = (n_ff, z_count, 4, 4 * ROWS, width)
    gain_s = (z_count, 4, ROWS, 128)
    firsts = 2 + 5 * n_ff
    vmem = pl.BlockSpec(memory_space=pltpu.VMEM)
    hbm = pl.BlockSpec(memory_space=pltpu.HBM)
    token = ((span, width), bf16)
    token_f = ((span, width), f32)
    outs = [(in_s[1:], bf16), (out_s[1:], bf16), (in_s[1:], bf16), (out_s[1:], bf16)]
    outs += [((8, width), f32), (x.shape, bf16), token, token, token, token, token_f]
    outs += [((span, hidden_units), f32), token_f, token, token, token]
    outs += [(sq_s[1:], bf16)] * n_sq
    scratch = [(sq_s, bf16), (in_s, bf16), (out_s, bf16), (gain_s, bf16)]
    scratch += [((n_sq, ROWS // 2, HALF), f32), ((n_ff, 4, ROWS // 2, HALF), f32)]
    scratch += [((n_ff, 2 * ROWS, HALF), f32), ((ROWS // 2, 128), f32)]
    scratch += [(x.shape, bf16), token, token, token, token, token, token_f]
    scratch += [((span, hidden_units), f32), ((span, hidden_units), bf16), token_f]
    scratch += [token, token, token, ((8, width), f32)]
    dma = pltpu.SemaphoreType.DMA
    return pl.pallas_call(
        functools.partial(forward_kernel, order, z_count),
        out_shape=[jax.ShapeDtypeStruct(*o) for o in outs],
        in_specs=[pl.BlockSpec(memory_space=pltpu.SMEM)] + [vmem] * 5 + [hbm],
        out_specs=[hbm] * len(outs),
        scratch_shapes=[pltpu.VMEM(*o) for o in scratch]
        + [dma((len(order), 7)), dma((len(order), 7)), dma((firsts,)), dma((firsts,))]
        + [dma((3,)), dma((3,)), dma((40,))],
        compiler_params=pltpu.CompilerParams(
            collective_id=0, has_side_effects=True, vmem_limit_bytes=62 * MIB
        ),
        name="forward",
    )(length, table, square, ffn_in, ffn_out, gains_t, x)


class Scatter:
    def __init__(self, units, sources, bufs, sems, z_count, put):
        self.units, self.sources, self.z_count, self.put = units, sources, z_count, put
        self.r0, self.r1, self.r2, self.r3, self.fin, self.sib = bufs
        self.send, self.recv = sems
        self.where = place()
        self.started = []
        self.lent = {}

    def go(self, u, slot, src, dst, peer):
        copy = remote(src, dst, self.send.at[u, slot], self.recv.at[u, slot], peer)
        copy.start()
        return copy

    def got(self, u, slot, ref):
        z, s, c = self.where[:3]
        remote(ref, ref, self.send.at[u, slot], self.recv.at[u, slot], (z, s, 1 - c)).wait_recv()

    def view(self, u, c, z=slice(None), s=slice(None)):
        kind, n = self.sources[u]
        if kind == "rows":
            return unit_view(kind, n, self.refs[kind], z, s, c)
        return self.refs["slots"].at[n, z, s, :, cols(c)]

    def c_start(self, u):
        z, s, c = self.where[:3]
        self.lent[u] = self.go(u, 0, self.view(u, 1 - c), self.r0.at[u], (z, s, 1 - c))

    def b_start(self, u):
        z, s, c, first, second, both = self.where
        self.got(u, 0, self.r0.at[u])

        def body(i, carry):
            n, m = i // 4, i % 4
            own = self.view(u, c, n, m)[...]
            total = own.astype(f32) + self.r0[u, n, m].astype(f32)
            self.r0[u, n, m] = total.astype(bf16)
            return carry

        lax.fori_loop(0, 4 * self.z_count, body, 0, unroll=4)
        self.started.append(self.go(u, 1, self.r0.at[u, :, second], self.r1.at[u, 0], (z, second, c)))
        self.started.append(self.go(u, 2, self.r0.at[u, :, both], self.r1.at[u, 1], (z, second, c)))
        self.lent.pop(u).wait_send()

    def a_start(self, u):
        z, s, c, first, second, both = self.where
        self.got(u, 2, self.r1.at[u, 1])
        for n in range(self.z_count):
            total = self.r0[u, n, first].astype(f32) + self.r1[u, 1, n].astype(f32)
            self.r1[u, 1, n] = total.astype(bf16)
        self.started.append(self.go(u, 3, self.r1.at[u, 1], self.r2.at[u], (z, first, c)))
        self.got(u, 1, self.r1.at[u, 0])
        for n in range(self.z_count):
            total = self.r0[u, n, s].astype(f32) + self.r1[u, 0, n].astype(f32)
            self.r1[u, 0, n] = total.astype(bf16)

    def z_start(self, u):
        z, s, c = self.where[:3]
        self.got(u, 3, self.r2.at[u])
        for n in range(self.z_count):
            total = self.r1[u, 0, n].astype(f32) + self.r2[u, n].astype(f32)
            self.r2[u, n] = total.astype(bf16)
        for d in range(1, self.z_count):
            to = (z + d) % self.z_count
            self.started.append(
                self.go(u, 3 + d, self.r2.at[u, to], self.r3.at[u, d - 1], (to, s, c))
            )

    def f_start(self, u):
        z, s, c = self.where[:3]
        total = self.r2[u, z].astype(f32)
        for d in range(1, self.z_count):
            self.got(u, 3 + d, self.r3.at[u, d - 1])
            total = total + self.r3[u, d - 1].astype(f32)
        self.fin[u] = total
        kind, n = self.units[u]
        if kind == "rows":
            if n % 2 == 1:
                @pl.when(c != n // 2)
                def _():
                    pair = pl.ds(u - 1, 2)
                    self.go(u, 7, self.fin.at[pair], self.sib.at[pair], (z, s, 1 - c))
        else:
            rows = pl.ds(pl.multiple_of((1 - c) * (ROWS // 2), 8), ROWS // 2)
            self.started.append(
                self.go(
                    u, 7, self.fin.at[u, rows], self.sib.at[u, pl.ds(0, ROWS // 2)], (z, s, 1 - c)
                )
            )

    def finish_unit(self, u):
        z, s, c = self.where[:3]
        kind, n = self.units[u]
        if kind == "rows":
            if n % 2 == 1:

                @pl.when(c == n // 2)
                def _():
                    self.got(u, 7, self.sib.at[pl.ds(u - 1, 2)])
                    for k in range(2):
                        self.put(kind, k, c, self.fin[u - 1 + k])
                        self.put(kind, k, 1 - c, self.sib[u - 1 + k])

                @pl.when(c != n // 2)
                def _():
                    pair = self.fin.at[pl.ds(u - 1, 2)]
                    remote(
                        pair, pair, self.send.at[u, 7], self.recv.at[u, 7], (z, s, 1 - c)
                    ).wait_send()
        else:
            self.got(u, 7, self.sib.at[u, pl.ds(0, ROWS // 2)])
            rows = pl.ds(pl.multiple_of(c * (ROWS // 2), 8), ROWS // 2)
            self.put(kind, n, c, self.fin[u, rows])
            self.put(kind, n, 1 - c, self.sib[u, : ROWS // 2])

    def tick(self, t):
        steps = (self.c_start, self.b_start, self.a_start, self.z_start, self.f_start)
        if 0 <= t - 5 < len(self.units):
            self.finish_unit(t - 5)
        for n in reversed(range(5)):
            if 0 <= t - n < len(self.units):
                steps[n](t - n)

    def finish(self):
        for copy in self.started:
            copy.wait_send()


def pull_rows(values_in, gain_row, incoming):
    inverse = lax.rsqrt(jnp.mean(values_in * values_in, axis=-1, keepdims=True) + norm_eps)
    scaled = incoming * gain_row
    inner = jnp.mean(scaled * values_in, axis=-1, keepdims=True)
    grad = inverse * scaled - values_in * (inverse * inverse * inverse * inner)
    return grad, jnp.sum(incoming * values_in * inverse, axis=0, keepdims=True)


def gelu_both(values_in):
    square = values_in * values_in
    slope = 0.7978845608028654
    bend = jnp.tanh(slope * values_in * (1.0 + 0.044715 * square))
    value = 0.5 * values_in * (1.0 + bend)
    grad = 0.5 * (1.0 + bend) + 0.5 * values_in * (1.0 - bend * bend) * slope * (
        1.0 + 3.0 * 0.044715 * square
    )
    return value, grad


def attend_pair_bwd(
    pair, length, table_ref, q_ref, k_ref, v_ref, do_ref, dq_ref, dk_ref, dv_ref, dt_ref
):
    span = k_ref.shape[0]
    scale = 1.0 / math.sqrt(HD)
    at = pl.ds(pl.multiple_of(pair * 2 * HD, 2 * HD), 2 * HD)
    valid = lax.broadcasted_iota(jnp.int32, (1, span), 1) < length
    lane = lax.broadcasted_iota(jnp.int32, (1, 2 * HD), 1)
    k_all = k_ref[:, at]
    v_all = v_ref[:, at]
    count = span // BAND
    dks, dvs = [], []
    dqs = [[None, None] for _ in range(count)]
    for t in range(2):
        own = (lane // HD) == t
        band = bias_band(table_ref[2 * pair + t], span)
        dk = jnp.zeros((span, 2 * HD), f32)
        dv = jnp.zeros((span, 2 * HD), f32)
        dband = jnp.zeros((BAND, 2 * span), f32)
        for block in range(count):
            rows = slice(block * BAND, (block + 1) * BAND)
            q_rows = q_ref[rows, at]
            do_rows = do_ref[rows, at]
            zero = jnp.zeros_like(q_rows)
            probs = softmax_rows(jnp.where(own, q_rows, zero), k_all, band, block, span, valid)
            dprobs = mm_t(jnp.where(own, do_rows, zero), v_all)
            dscore = probs * (dprobs - jnp.sum(dprobs * probs, axis=-1, keepdims=True))
            start = span - BAND * (block + 1)
            pieces = []
            if start:
                pieces.append(jnp.zeros((BAND, start), f32))
            pieces.append(dscore)
            if span - start:
                pieces.append(jnp.zeros((BAND, span - start), f32))
            dband = dband + jnp.concatenate(pieces, axis=1)
            dscore_b = dscore.astype(bf16)
            dv = dv + mm_outer(probs.astype(bf16), do_rows)
            dk = dk + mm_outer(dscore_b, q_rows)
            dqs[block][t] = matmul(dscore_b, k_all)
        dks.append(dk)
        dvs.append(dv)
        dt_ref[2 * pair + t] = band_sums(dband, span)
    dk_ref[:, at] = (jnp.where(lane < HD, dks[0], dks[1]) * scale).astype(bf16)
    dv_ref[:, at] = jnp.where(lane < HD, dvs[0], dvs[1]).astype(bf16)
    for block in range(count):
        rows = slice(block * BAND, (block + 1) * BAND)
        dq_ref[rows, at] = (jnp.where(lane < HD, dqs[block][0], dqs[block][1]) * scale).astype(bf16)


def backward_kernel(z_count, *refs):
    (
        len_ref, table_ref, gain_ref, w0, w1, w2, w3, w7, w8, win, wout,
        x_i, q_i, k_i, v_i, att_i, hid_i, pre_i, hid2_i, enc_i, gck_i, gcv_i,
        sq_o, in_o, out_o, x_o, dt_o, gg_o,
        slots, d_out, r0, r1, r2, r3, fin, sib,
        wbuf, x_s, q_s, k_s, v_s, att_s, enc_s, gck_s, gcv_s, hid_s, hid2_s, pre_s,
        gh, gh_b, acc, inner_s, gpre_s, turned, gatt, gq, gk, gv, gx, gx_r,
        send, recv, w_sem, p_sem, a_sem, x_send, x_recv, o_sem,
    ) = refs
    z, s, c = place()[:3]
    blocks = x_s.shape[0]
    width = 2 * HALF

    loads = {}
    for n, (src, dst) in enumerate(
        (
            (enc_i, enc_s), (gck_i, gck_s), (gcv_i, gcv_s), (hid2_i, hid2_s), (hid_i, hid_s),
            (att_i, att_s), (q_i, q_s), (k_i, k_s), (v_i, v_s), (x_i, x_s),
        )
    ):
        copy = pltpu.make_async_copy(src, dst, a_sem.at[n])
        copy.start()
        loads[n] = copy
    tiles = [w7, w8]
    for j in range(4):
        tiles.append(wout.at[pl.ds(j * width, width)])
        tiles.append(win.at[:, pl.ds(j * width, width)])
    tiles += [w3, w0, w1, w2]
    w_loads = {}

    def fetch(n):
        if n < len(tiles):
            copy = pltpu.make_async_copy(tiles[n], wbuf.at[n % 4], w_sem.at[n])
            copy.start()
            w_loads[n] = copy

    p_loads = {}

    def fetch_pre(j):
        if j < 4:
            copy = pltpu.make_async_copy(
                pre_i.at[:, pl.ds(j * width, width)], pre_s.at[j % 2], p_sem.at[j]
            )
            copy.start()
            p_loads[j] = copy

    for n in range(4):
        fetch(n)
    fetch_pre(0)
    fetch_pre(1)
    greet(z, s, c, z_count)

    units = [("square", 4), ("square", 5)] + [("cols", j) for j in range(4)] + [("square", 3)]
    units += [("rows", n) for n in range(4)] + [("heads", m) for m in range(3)]
    sources, held = [], 0
    for kind, n in units:
        if kind == "rows":
            sources.append((kind, n))
        else:
            sources.append(("slot", held % 3))
            held += 1

    def put(kind, n, side, value):
        if kind == "square":
            sq_o[n, :, cols(side)] = value
        elif kind == "cols":
            in_o[:, cols(side, n * width)] = value
        elif kind == "rows":
            out_o[n * ROWS : (n + 1) * ROWS, cols(side)] = value
        else:
            at = pl.ds(pl.multiple_of((2 * n + side) * 128, 128), 128)
            for t in range(3):
                sq_o[t, :, at] = value[:, t * 128 : (t + 1) * 128]

    scatter = Scatter(units, sources, (r0, r1, r2, r3, fin, sib), (send, recv), z_count, put)
    scatter.refs = {"slots": slots, "rows": d_out}

    def turn(src):
        def body(i, carry):
            at = pl.ds(pl.multiple_of(i * 256, 256), 256)
            turned[at, :] = src[:, at].T
            return carry

        lax.fori_loop(0, 3, body, 0)

    def grad_to_slot(n, right):
        def work(at):
            value = matmul(turned[...], right[:, at]).astype(bf16)
            slots[n, :, :, :, at] = value.reshape(z_count, 4, ROWS, 256)

        col_tiles(width, 256, work)

    def back(left, n, dst, add):
        w_loads[n].wait()

        def work(at):
            value = mm_t(left[...], wbuf[n % 4, at, :])
            if add:
                value = value + dst[:, at]
            dst[:, at] = value

        col_tiles(width, 256, work)
        fetch(n + 4)

    gg_o[...] = jnp.zeros_like(gg_o)
    loads[0].wait()
    loads[1].wait()
    turn(enc_s)
    grad_to_slot(0, gck_s)
    scatter.tick(0)
    loads[2].wait()
    grad_to_slot(1, gcv_s)
    scatter.tick(1)
    back(gck_s, 0, acc, False)
    back(gcv_s, 1, acc, True)
    loads[3].wait()
    loads[4].wait()

    def pull_hid2(i, at):
        grad, gain = pull_rows(hid2_s[at, :], gain_ref[2:3, :], acc[at, :])
        gh[at, :] = grad
        gh_b[at, :] = grad.astype(bf16)
        gg_o[2:3, :] += gain
        enc_s[at, :] = rms_gain(hid_s[at, :], gain_ref[1:2, :]).astype(bf16)

    row_blocks(blocks, pull_hid2)
    turn(enc_s)

    for j in range(4):
        p_loads[j].wait()
        w_loads[2 + 2 * j].wait()

        def hidden_tile(at):
            value, slope = gelu_both(pre_s[j % 2, :, at])
            inner_s[:, at] = value.astype(bf16)
            grad = mm_t(gh_b[...], wbuf[(2 + 2 * j) % 4, at, :])
            gpre_s[:, at] = (grad * slope).astype(bf16)

        col_tiles(width, 256, hidden_tile)
        fetch(6 + 2 * j)
        fetch_pre(j + 2)
        grad_to_slot((2 + j) % 3, gpre_s)
        scatter.tick(2 + j)

        def out_rows(i, carry):
            at = pl.ds(pl.multiple_of(i * HALF, HALF), HALF)
            value = mm_outer(inner_s[:, at], gh_b[...]).astype(bf16)
            d_out[0, j, pl.ds(2 * i, 2)] = value.reshape(2, 4 * ROWS, width)
            return carry

        lax.fori_loop(0, 2, out_rows, 0)
        back(gpre_s, 3 + 2 * j, acc, j > 0)

    loads[5].wait()

    def pull_hid(i, at):
        grad, gain = pull_rows(hid_s[at, :], gain_ref[1:2, :], acc[at, :])
        total = gh[at, :] + grad
        gh[at, :] = total
        gh_b[at, :] = total.astype(bf16)
        gg_o[1:2, :] += gain

    row_blocks(blocks, pull_hid)
    turn(att_s)
    grad_to_slot(0, gh_b)
    scatter.tick(6)
    w_loads[10].wait()

    def attended_grad(at):
        gatt[:, at] = mm_t(gh_b[...], wbuf[10 % 4, at, :]).astype(bf16)

    col_tiles(width, 256, attended_grad)
    for n in (6, 7, 8, 9):
        loads[n].wait()

    def x_norm(i, at):
        enc_s[at, :] = rms_gain(x_s[i].astype(f32), gain_ref[0:1, :]).astype(bf16)

    row_blocks(blocks, x_norm)
    turn(enc_s)
    scatter.tick(7)

    def pair_grads(pairs):
        def body(pair, carry):
            attend_pair_bwd(
                pair, len_ref[0], table_ref, q_s, k_s, v_s, gatt, gq, gk, gv, dt_o
            )
            return carry

        lax.fori_loop(pairs[0], pairs[1], body, 0)

    def heads_to_slot(m, n):
        for t, right in enumerate((gq, gk, gv)):
            value = matmul(turned[...], right[:, m * 256 : (m + 1) * 256]).astype(bf16)
            value = value.reshape(z_count, 4, ROWS, 256)
            slots[n, :, :, :, t * 128 : (t + 1) * 128] = value[..., :128]
            slots[n, :, :, :, HALF + t * 128 : HALF + (t + 1) * 128] = value[..., 128:]

    pair_grads((0, 1))
    scatter.tick(8)
    pair_grads((1, 2))
    heads_to_slot(0, 1)
    scatter.tick(9)
    pair_grads((2, 3))
    scatter.tick(10)
    pair_grads((3, 4))
    heads_to_slot(1, 2)
    scatter.tick(11)
    pair_grads((4, 5))
    scatter.tick(12)
    pair_grads((5, 6))
    heads_to_slot(2, 0)
    scatter.tick(13)
    back(gq, 11, acc, False)
    back(gk, 12, acc, True)
    scatter.tick(14)
    back(gv, 13, acc, True)

    def pull_x(i, at):
        grad, gain = pull_rows(x_s[i].astype(f32), gain_ref[0:1, :], acc[at, :])
        gx[i] = (gh[at, :] + grad).astype(bf16)
        gg_o[0:1, :] += gain

    row_blocks(blocks, pull_x)
    x_copies = []
    for d in range(1, 4):
        peer = (s + d) % 4
        copy = remote(
            gx.at[peer], gx_r.at[s], x_send.at[d - 1], x_recv.at[d - 1], (z, peer, c)
        )
        copy.start()
        x_copies.append(copy)
    scatter.tick(15)
    scatter.tick(16)
    gx_r[s] = gx[s]
    scatter.tick(17)
    scatter.tick(18)
    for copy in x_copies:
        copy.wait()

    def widen(i, at):
        gh[at, :] = gx_r[i].astype(f32)

    row_blocks(blocks, widen)
    copy = pltpu.make_async_copy(gh, x_o, o_sem.at[0])
    copy.start()
    scatter.finish()
    copy.wait()


def backward(length, table, gain, weights, win, wout, acts, z_count):
    x = acts[0]
    blocks, band, width = x.shape
    span = blocks * band
    heads = table.shape[0]
    vmem = pl.BlockSpec(memory_space=pltpu.VMEM)
    hbm = pl.BlockSpec(memory_space=pltpu.HBM)
    n = 14
    token = ((span, width), bf16)
    token_f = ((span, width), f32)
    scratch = [((3, z_count, 4, ROWS, width), bf16), ((1, z_count, 4, 4 * ROWS, width), bf16)]
    scratch += [((n, z_count, 4, ROWS, HALF), bf16), ((n, 2, z_count, ROWS, HALF), bf16)]
    scratch += [((n, z_count, ROWS, HALF), bf16), ((n, z_count - 1, ROWS, HALF), bf16)]
    scratch += [((n, ROWS, HALF), f32), ((n, ROWS, HALF), f32)]
    scratch += [((4, width, width), bf16), (x.shape, bf16)] + [token] * 7 + [token_f] * 2
    scratch += [((2, span, width), f32), token_f, token, token_f, token, token]
    scratch += [((width, span), bf16)] + [token] * 4 + [(x.shape, bf16)] * 2
    dma = pltpu.SemaphoreType.DMA
    return pl.pallas_call(
        functools.partial(backward_kernel, z_count),
        out_shape=[
            jax.ShapeDtypeStruct((6, ROWS // 2, width), f32),
            jax.ShapeDtypeStruct((ROWS // 2, 4 * width), f32),
            jax.ShapeDtypeStruct((2 * ROWS, width), f32),
            jax.ShapeDtypeStruct((span, width), f32),
            jax.ShapeDtypeStruct(table.shape, f32),
            jax.ShapeDtypeStruct((8, width), f32),
        ],
        in_specs=[pl.BlockSpec(memory_space=pltpu.SMEM), vmem, vmem] + [hbm] * 19,
        out_specs=[vmem] * 3 + [hbm] + [vmem] * 2,
        scratch_shapes=[pltpu.VMEM(*o) for o in scratch]
        + [dma((n, 8)), dma((n, 8)), dma((n,)), dma((4,)), dma((10,)), dma((3,)), dma((3,))]
        + [dma((1,))],
        compiler_params=pltpu.CompilerParams(
            collective_id=1, has_side_effects=True, vmem_limit_bytes=62 * MIB
        ),
        name="backward",
    )(length, table, gain, *weights, win, wout, *acts)


def total_kernel(z_count, in_ref, out_ref, acc, got, send, recv):
    z, s, c = place()[:3]
    greet(z, s, c, z_count)
    started = []
    slot = 0

    def exchange(peers):
        nonlocal slot
        base = slot
        for peer in peers:
            copy = remote(acc, got.at[slot], send.at[slot], recv.at[slot], peer)
            copy.start()
            started.append(copy)
            slot += 1
        for copy in started[base:]:
            copy.wait()
        total = acc[...]
        for k in range(base, slot):
            total = total + got[k]
        acc[...] = total

    acc[...] = in_ref[...]
    exchange([(z, s, 1 - c)])
    exchange([(z, (s + d) % 4, c) for d in range(1, 4)])
    exchange([((z + d) % z_count, s, c) for d in range(1, z_count)])
    out_ref[...] = acc[...]


def total_all(x, z_count):
    vmem = pl.BlockSpec(memory_space=pltpu.VMEM)
    slots = z_count + 3
    return pl.pallas_call(
        functools.partial(total_kernel, z_count),
        out_shape=jax.ShapeDtypeStruct(x.shape, f32),
        in_specs=[vmem],
        out_specs=vmem,
        scratch_shapes=[
            pltpu.VMEM(x.shape, f32),
            pltpu.VMEM((slots,) + x.shape, f32),
            pltpu.SemaphoreType.DMA((slots,)),
            pltpu.SemaphoreType.DMA((slots,)),
        ],
        compiler_params=pltpu.CompilerParams(collective_id=2, has_side_effects=True),
        name="total_all",
    )(x)


def on_device(
    inputs,
    dec_in,
    cotangent,
    lengths,
    bucket_table,
    square,
    square_m,
    square_v,
    ffn_in,
    ffn_in_m,
    ffn_in_v,
    ffn_out,
    ffn_out_m,
    ffn_out_v,
    gains,
    gains_m,
    gains_v,
    rel_bias,
    rel_bias_m,
    rel_bias_v,
):
    z_count = lax.axis_size("dp")
    width = inputs.shape[2]
    direct = lax.axis_size("seq") == 4 and width == 2 * HALF and width == 4 * z_count * ROWS
    direct = direct and inputs.shape[:2] == (4, BAND)
    w = {}
    seq_pos = lax.axis_index("seq")
    local_len = inputs.shape[1]
    span = local_len * lax.axis_size("seq")
    bucket_count = rel_bias.shape[0]
    scale = 1.0 / math.sqrt(HD)
    length = lax.dynamic_slice_in_dim(lengths, seq_pos, 1, 0)
    key_valid = jnp.arange(span)[None, :] < length[:, None]
    one_hot = (
        jnp.pad(bucket_table, (0, 1), constant_values=-1)[:, None]
        == jnp.arange(bucket_count)[None, :]
    ).astype(f32)
    table = jnp.einsum("ob,bh->ho", one_hot, rel_bias, precision=highest_precision)[:, None, :]

    if direct:
        gains_t = jnp.pad(gains.T, ((0, 0), (0, 128 - gains.shape[0])))
        outs = forward(length, table, square, ffn_in, ffn_out, gains_t, inputs, z_count)
        w_in_e, w_out_e, w_in_d, w_out_d = (
            outs[0].reshape(width, -1),
            outs[1].reshape(-1, width),
            outs[2].reshape(width, -1),
            outs[3].reshape(-1, width),
        )
        gain_f = outs[4][: gains.shape[0]]
        q, k, v, attended, hidden, pre_act, hidden_two, encoded, cross_k, cross_v = outs[6:16]
        for i in range(square.shape[0]):
            w[i] = outs[16 + i].reshape(width, width)
    else:

        def gather_rows(x):
            return lax.all_gather(x.astype(bf16), AXES, axis=x.ndim - 2, tiled=True)

        sq_a = gather_rows(square[:4])
        w_in_e = gather_rows(ffn_in[0])
        w_out_e = gather_rows(ffn_out[0])
        sq_b = gather_rows(square[4:])
        w_in_d = gather_rows(ffn_in[1])
        w_out_d = gather_rows(ffn_out[1])
        gain_f = lax.all_gather(gains.astype(bf16), AXES, axis=1, tiled=True).astype(f32)
        for i in range(square.shape[0]):
            w[i] = sq_a[i] if i < 4 else sq_b[i - 4]
        x_b = lax.all_to_all(inputs, "seq", split_axis=0, concat_axis=1, tiled=True)[0]
        x_f = x_b.astype(f32)
        normed = rms_gain(x_f, gain_f[0]).astype(bf16)
        q = matmul(normed, w[0]).astype(bf16)
        k = matmul(normed, w[1]).astype(bf16)
        v = matmul(normed, w[2]).astype(bf16)
        attended = attend_fwd(length, table, q, k, v)
        hidden = x_f + matmul(attended, w[3])
        normed_two = rms_gain(hidden, gain_f[1]).astype(bf16)
        pre_act = matmul(normed_two, w_in_e)
        inner_act = gelu_tanh(pre_act).astype(bf16)
        hidden_two = hidden + matmul(inner_act, w_out_e)
        encoded = rms_gain(hidden_two, gain_f[2]).astype(bf16)
        cross_k = matmul(encoded, w[7]).astype(bf16)
        cross_v = matmul(encoded, w[8]).astype(bf16)

    dec_row = dec_in.reshape(1, width).astype(f32)
    self_norm = rms_gain(dec_row, gain_f[3]).astype(bf16)
    self_values = matmul(self_norm, w[4]).astype(bf16)
    dec_one = dec_row + matmul(self_values, w[5])
    cross_norm = rms_gain(dec_one, gain_f[4]).astype(bf16)
    cross_q = matmul(cross_norm, w[6]).astype(bf16)
    head_of = (jnp.arange(width)[None, :] // HD == jnp.arange(H)[:, None]).astype(bf16)
    q_heads = head_of * cross_q
    cross_scores = jnp.where(key_valid, mm_t(q_heads, cross_k) * scale, neg_fill)
    cross_probs = jax.nn.softmax(cross_scores, axis=-1)
    cross_probs_b = cross_probs.astype(bf16)
    cross_att = jnp.sum(
        matmul(cross_probs_b, cross_v) * head_of.astype(f32), axis=0, keepdims=True
    ).astype(bf16)
    dec_two = dec_one + matmul(cross_att, w[9])
    ffn_norm = rms_gain(dec_two, gain_f[5]).astype(bf16)
    pre_dec = matmul(ffn_norm, w_in_d)
    inner_dec = gelu_tanh(pre_dec).astype(bf16)
    dec_out = dec_two + matmul(inner_dec, w_out_d)

    g_top_b = cotangent.reshape(1, width)
    g_top = g_top_b.astype(f32)
    g_pre_dec = gelu_pull(pre_dec, mm_t(g_top_b, w_out_d)).astype(bf16)
    g_two_norm, g_gain_five = rms_pull(dec_two, gain_f[5], mm_t(g_pre_dec, w_in_d))
    g_two = g_top + g_two_norm
    g_two_b = g_two.astype(bf16)
    g_att = mm_t(g_two_b, w[9]).astype(bf16)
    g_att_heads = head_of * g_att
    g_probs = mm_t(g_att_heads, cross_v)
    g_cross_v = mm_outer(cross_probs_b, g_att_heads).astype(bf16)
    g_scores = cross_probs * (g_probs - jnp.sum(g_probs * cross_probs, axis=-1, keepdims=True))
    g_scores_b = g_scores.astype(bf16)
    g_cross_q = (
        jnp.sum(matmul(g_scores_b, cross_k) * head_of.astype(f32), axis=0, keepdims=True) * scale
    ).astype(bf16)
    g_cross_k = (mm_outer(g_scores_b, q_heads) * scale).astype(bf16)
    g_one_norm, g_gain_four = rms_pull(dec_one, gain_f[4], mm_t(g_cross_q, w[6]))
    g_one_b = (g_two + g_one_norm).astype(bf16)
    g_self_values = mm_t(g_one_b, w[5]).astype(bf16)
    g_gain_three = rms_pull(dec_row, gain_f[3], mm_t(g_self_values, w[4]))[1]

    lefts = (self_norm, self_values, cross_norm, cross_att, ffn_norm, inner_dec)
    rights = (g_self_values, g_one_b, g_cross_q, g_two_b, g_pre_dec, g_top_b)
    own_row = jnp.concatenate(lefts + rights, axis=1)
    own_row = jnp.pad(own_row, ((0, 0), (0, 20 * 1024 - own_row.shape[1])))
    packed = lax.all_gather(own_row, AXES, axis=0, tiled=True)
    me = (
        lax.axis_index("dp") * lax.axis_size("seq") + seq_pos
    ) * lax.axis_size("head") + lax.axis_index("head")
    devices = packed.shape[0]
    cuts = [0]
    for piece in lefts + rights:
        cuts.append(cuts[-1] + piece.shape[1])
    dec_grads = []
    for n in range(6):
        share = lefts[n].shape[1] // devices
        left = lax.dynamic_slice_in_dim(packed, cuts[n] + me * share, share, 1)
        right = packed[:, cuts[6 + n] : cuts[7 + n]]
        dec_grads.append(mm_outer(left, right))

    if direct:
        s_sq, s_in, s_out, input_grad, g_table, g_low = backward(
            length,
            table,
            outs[4],
            [w[i] for i in (0, 1, 2, 3, 7, 8)],
            w_in_e,
            w_out_e,
            (outs[5], q, k, v, attended, hidden, pre_act, hidden_two, encoded)
            + (g_cross_k, g_cross_v),
            z_count,
        )
        s_0123, s_78 = s_sq[:4], s_sq[4:]
        input_grad = input_grad.reshape(inputs.shape)
        g_gain_zero, g_gain_one, g_gain_two = g_low[0], g_low[1], g_low[2]
        g_bias_here = jnp.einsum(
            "ob,ho->bh", one_hot, g_table[:, 0, :], precision=highest_precision
        )
    else:
        g_w7 = mm_outer(encoded, g_cross_k)
        g_w8 = mm_outer(encoded, g_cross_v)
        g_encoded = mm_t(g_cross_k, w[7]) + mm_t(g_cross_v, w[8])
        g_hidden_two, g_gain_two = rms_pull(hidden_two, gain_f[2], g_encoded)
        g_hidden_two_b = g_hidden_two.astype(bf16)
        g_out_e = mm_outer(inner_act, g_hidden_two_b)
        g_pre = gelu_pull(pre_act, mm_t(g_hidden_two_b, w_out_e)).astype(bf16)
        g_in_e = mm_outer(normed_two, g_pre)
        g_hidden_norm, g_gain_one = rms_pull(hidden, gain_f[1], mm_t(g_pre, w_in_e))
        g_hidden = g_hidden_two + g_hidden_norm
        g_hidden_b = g_hidden.astype(bf16)
        g_w3 = mm_outer(attended, g_hidden_b)
        g_attended = mm_t(g_hidden_b, w[3]).astype(bf16)
        gq, gk, gv, g_table = attend_bwd(length, table, q, k, v, g_attended)
        g_bias_here = jnp.einsum("ob,ho->bh", one_hot, g_table[:, 0, :], precision=highest_precision)
        g_w0 = mm_outer(normed, gq)
        g_w1 = mm_outer(normed, gk)
        g_w2 = mm_outer(normed, gv)
        g_normed = mm_t(gq, w[0]) + mm_t(gk, w[1]) + mm_t(gv, w[2])
        g_input_norm, g_gain_zero = rms_pull(x_f, gain_f[0], g_normed)
        g_x = (g_hidden + g_input_norm).astype(bf16)
        input_grad = lax.all_to_all(
            g_x[None], "seq", split_axis=1, concat_axis=0, tiled=True
        ).astype(f32)

        def scatter_rows(x):
            return lax.psum_scatter(
                x.astype(bf16), AXES, scatter_dimension=x.ndim - 2, tiled=True
            ).astype(f32)

        s_78 = scatter_rows(jnp.stack((g_w7, g_w8)))
        s_out = scatter_rows(g_out_e)
        s_in = scatter_rows(g_in_e)
        s_0123 = scatter_rows(jnp.stack((g_w0, g_w1, g_w2, g_w3)))
    summed_sq = jnp.stack(
        (
            s_0123[0],
            s_0123[1],
            s_0123[2],
            s_0123[3],
            dec_grads[0],
            dec_grads[1],
            dec_grads[2],
            s_78[0],
            s_78[1],
            dec_grads[3],
        )
    )
    summed_in = jnp.stack((s_in, dec_grads[4]))
    summed_out = jnp.stack((s_out, dec_grads[5]))
    g_gains = jnp.stack(
        (g_gain_zero, g_gain_one, g_gain_two, g_gain_three, g_gain_four, g_gain_five)
    )
    gain_share = gains.shape[1]
    local_squares = (
        jnp.sum(summed_sq * summed_sq)
        + jnp.sum(summed_in * summed_in)
        + jnp.sum(summed_out * summed_out)
    )
    if direct:
        rest = jnp.concatenate((g_bias_here.reshape(-1), local_squares[None]))
        rest = jnp.pad(rest, (0, 1024 - rest.shape[0])).reshape(8, 128)
        wide = jnp.concatenate((jnp.pad(g_gains, ((0, 2), (0, 0))), rest), axis=1)
        wide = total_all(wide, z_count)
        g_gains = wide[:6, :width]
        rest = wide[:, width:].reshape(-1)
        g_bias = rest[: g_bias_here.size].reshape(g_bias_here.shape)
        shard_squares = rest[g_bias_here.size]
    else:
        g_gains, g_bias, shard_squares = lax.psum((g_gains, g_bias_here, local_squares), AXES)
    summed_gain = lax.dynamic_slice_in_dim(g_gains, me * gain_share, gain_share, 1)
    grad_norm = jnp.sqrt(shard_squares + jnp.sum(g_gains * g_gains) + jnp.sum(g_bias * g_bias))
    factor = clip_bound / jnp.maximum(grad_norm, clip_bound)
    return (
        dec_out.astype(bf16).reshape(dec_in.shape),
        input_grad,
        grad_norm,
        *adam_step(square, square_m, square_v, summed_sq, factor, rate_matrix, decay_rate),
        *adam_step(ffn_in, ffn_in_m, ffn_in_v, summed_in, factor, rate_matrix, decay_rate),
        *adam_step(ffn_out, ffn_out_m, ffn_out_v, summed_out, factor, rate_matrix, decay_rate),
        *adam_step(gains, gains_m, gains_v, summed_gain, factor, rate_small, 0.0),
        *adam_step(rel_bias, rel_bias_m, rel_bias_v, g_bias, factor, rate_small, 0.0),
    )


def solution(mesh):
    rows = P(("dp", "head"), "seq", None)
    shard = P(None, AXES, None)
    small = P(None, AXES)
    return jax.shard_map(
        on_device,
        mesh=mesh,
        in_specs=(rows, rows, rows, P(("dp", "head")), P())
        + (shard,) * 9
        + (small,) * 3
        + (P(),) * 3,
        out_specs=(rows, rows, P()) + (shard,) * 9 + (small,) * 3 + (P(),) * 3,
        check_vma=False,
    )
```

```python
import functools
import math

import jax
import jax.numpy as jnp
from jax import lax
from jax.experimental import pallas as pl
from jax.experimental.pallas import tpu as pltpu
from jax.sharding import PartitionSpec as P

H = 12
HD = 64
STEP = 5
AXES = ("dp", "seq", "head")

norm_eps = 1e-06
neg_fill = -1e30
beta_one = 0.9
beta_two = 0.999
adam_eps = 1e-08
decay_rate = 0.01
rate_matrix = 0.05
rate_small = 0.5
clip_bound = 1.0
highest_precision = lax.Precision.HIGHEST
bf16 = jnp.bfloat16
f32 = jnp.float32
BAND = 128


def rms_gain(values_in, gain_row):
    return (
        values_in
        * lax.rsqrt(jnp.mean(values_in * values_in, axis=-1, keepdims=True) + norm_eps)
        * gain_row
    )


def gelu_tanh(values_in):
    return jax.nn.gelu(values_in, approximate=True)


def matmul(left, right):
    return jnp.dot(left, right, preferred_element_type=f32)


def mm_t(left, right):
    return lax.dot_general(left, right, (((1,), (1,)), ((), ())), preferred_element_type=f32)


def mm_outer(left, right):
    return lax.dot_general(left, right, (((0,), (0,)), ((), ())), preferred_element_type=f32)


def rms_pull(values_in, gain_row, incoming):
    _, pull = jax.vjp(rms_gain, values_in, gain_row)
    return pull(incoming)


def gelu_pull(values_in, incoming):
    _, pull = jax.vjp(gelu_tanh, values_in)
    return pull(incoming)[0]


def adam_step(weight, first, second, grad, factor, rate, decay):
    grad = grad * factor
    first = beta_one * first + (1.0 - beta_one) * grad
    second = beta_two * second + (1.0 - beta_two) * grad * grad
    first_hat = first / (1.0 - beta_one**STEP)
    second_hat = second / (1.0 - beta_two**STEP)
    weight = weight - rate * (first_hat / (jnp.sqrt(second_hat) + adam_eps) + decay * weight)
    return (weight, first, second)


def bias_band(table_row, span):
    wide = jnp.broadcast_to(table_row, (BAND, 2 * span))
    shift = (2 * span - (BAND - 1)) % (2 * span)
    return pltpu.roll(wide, shift, 1, stride=1, stride_axis=0)


def band_sums(band, span):
    wide = 2 * span
    rows = BAND
    while rows > 8:
        rows //= 2
        band = band[:rows] + pltpu.roll(band[rows:], wide - rows, 1)
    row = lax.broadcasted_iota(jnp.int32, band.shape, 0)
    for step in (4, 2, 1):
        band = jnp.where((row // step) % 2 == 1, pltpu.roll(band, wide - step, 1), band)
    return pltpu.roll(jnp.sum(band, axis=0, keepdims=True), BAND - 1, 1)


def softmax_rows(q_rows, k_all, band, block, span, valid):
    start = span - BAND * (block + 1)
    scores = mm_t(q_rows, k_all) * (1.0 / math.sqrt(HD)) + band[:, start : start + span]
    scores = jnp.where(valid, scores, neg_fill)
    peak = jnp.max(scores, axis=-1, keepdims=True)
    raised = jnp.exp(scores - peak)
    return raised / jnp.sum(raised, axis=-1, keepdims=True)


def attend_fwd_kernel(len_ref, table_ref, q_ref, k_ref, v_ref, o_ref):
    span = k_ref.shape[0]
    valid = lax.broadcasted_iota(jnp.int32, (1, span), 1) < len_ref[0]
    lane = lax.broadcasted_iota(jnp.int32, (1, 2 * HD), 1)
    k_all = k_ref[...]
    v_all = v_ref[...]
    bands = [bias_band(table_ref[t], span) for t in range(2)]
    for block in range(span // BAND):
        rows = slice(block * BAND, (block + 1) * BAND)
        q_rows = q_ref[rows, :]
        parts = []
        for t in range(2):
            own = (lane // HD) == t
            probs = softmax_rows(
                jnp.where(own, q_rows, jnp.zeros_like(q_rows)), k_all, bands[t], block, span, valid
            )
            parts.append(matmul(probs.astype(bf16), v_all))
        o_ref[rows, :] = jnp.where(lane < HD, parts[0], parts[1]).astype(bf16)


def attend_bwd_kernel(
    len_ref, table_ref, q_ref, k_ref, v_ref, do_ref, dq_ref, dk_ref, dv_ref, dt_ref
):
    span = k_ref.shape[0]
    scale = 1.0 / math.sqrt(HD)
    valid = lax.broadcasted_iota(jnp.int32, (1, span), 1) < len_ref[0]
    lane = lax.broadcasted_iota(jnp.int32, (1, 2 * HD), 1)
    k_all = k_ref[...]
    v_all = v_ref[...]
    count = span // BAND
    dks, dvs = [], []
    dqs = [[None, None] for _ in range(count)]
    for t in range(2):
        own = (lane // HD) == t
        band = bias_band(table_ref[t], span)
        dk = jnp.zeros((span, 2 * HD), f32)
        dv = jnp.zeros((span, 2 * HD), f32)
        dband = jnp.zeros((BAND, 2 * span), f32)
        for block in range(count):
            rows = slice(block * BAND, (block + 1) * BAND)
            q_rows = q_ref[rows, :]
            do_rows = do_ref[rows, :]
            zero = jnp.zeros_like(q_rows)
            probs = softmax_rows(
                jnp.where(own, q_rows, zero), k_all, band, block, span, valid
            )
            dprobs = mm_t(jnp.where(own, do_rows, zero), v_all)
            dscore = probs * (dprobs - jnp.sum(dprobs * probs, axis=-1, keepdims=True))
            start = span - BAND * (block + 1)
            pieces = []
            if start:
                pieces.append(jnp.zeros((BAND, start), f32))
            pieces.append(dscore)
            if span - start:
                pieces.append(jnp.zeros((BAND, span - start), f32))
            dband = dband + jnp.concatenate(pieces, axis=1)
            dscore_b = dscore.astype(bf16)
            dv = dv + mm_outer(probs.astype(bf16), do_rows)
            dk = dk + mm_outer(dscore_b, q_rows)
            dqs[block][t] = matmul(dscore_b, k_all)
        dks.append(dk)
        dvs.append(dv)
        dt_ref[t] = band_sums(dband, span)
    dk_ref[...] = (jnp.where(lane < HD, dks[0], dks[1]) * scale).astype(bf16)
    dv_ref[...] = jnp.where(lane < HD, dvs[0], dvs[1]).astype(bf16)
    for block in range(count):
        rows = slice(block * BAND, (block + 1) * BAND)
        dq_ref[rows, :] = (jnp.where(lane < HD, dqs[block][0], dqs[block][1]) * scale).astype(bf16)


def head_specs(span, width, n):
    return [pl.BlockSpec((span, 2 * HD), lambda i: (0, i)) for _ in range(n)]


def attend_fwd(length, table, q, k, v):
    span, width = q.shape
    return pl.pallas_call(
        attend_fwd_kernel,
        grid=(width // (2 * HD),),
        out_shape=jax.ShapeDtypeStruct((span, width), bf16),
        in_specs=[
            pl.BlockSpec(memory_space=pltpu.SMEM),
            pl.BlockSpec((2, 1, 2 * span), lambda i: (i, 0, 0)),
            *head_specs(span, width, 3),
        ],
        out_specs=head_specs(span, width, 1)[0],
        compiler_params=pltpu.CompilerParams(vmem_limit_bytes=48 * 1024 * 1024),
        name="attend_fwd",
    )(length, table, q, k, v)


def attend_bwd(length, table, q, k, v, do):
    span, width = q.shape
    like = jax.ShapeDtypeStruct((span, width), bf16)
    return pl.pallas_call(
        attend_bwd_kernel,
        grid=(width // (2 * HD),),
        out_shape=(like, like, like, jax.ShapeDtypeStruct(table.shape, f32)),
        in_specs=[
            pl.BlockSpec(memory_space=pltpu.SMEM),
            pl.BlockSpec((2, 1, 2 * span), lambda i: (i, 0, 0)),
            *head_specs(span, width, 4),
        ],
        out_specs=(
            *head_specs(span, width, 3),
            pl.BlockSpec((2, 1, 2 * span), lambda i: (i, 0, 0)),
        ),
        compiler_params=pltpu.CompilerParams(vmem_limit_bytes=48 * 1024 * 1024),
        name="attend_bwd",
    )(length, table, q, k, v, do)


MESH_ID = pl.DeviceIdType.MESH
HALF = 384
ROWS = 48
MIB = 1024 * 1024


def place():
    z, s, c = lax.axis_index("dp"), lax.axis_index("seq"), lax.axis_index("head")
    near = s + 1 - 2 * (s % 2)
    far = (s + 2) % 4
    first = near + c * (far - near)
    second = far + c * (near - far)
    return z, s, c, first, second, 3 - s


def greet(z, s, c, z_count):
    barrier = pltpu.get_barrier_semaphore()
    for d in range(1, z_count):
        peer = ((z + d) % z_count, s, c)
        pl.semaphore_signal(barrier, 1, device_id=peer, device_id_type=MESH_ID)
    for d in range(1, 4):
        peer = (z, (s + d) % 4, c)
        pl.semaphore_signal(barrier, 1, device_id=peer, device_id_type=MESH_ID)
    pl.semaphore_signal(barrier, 1, device_id=(z, s, 1 - c), device_id_type=MESH_ID)
    pl.semaphore_wait(barrier, z_count + 3)


def remote(src, dst, send, recv, peer):
    return pltpu.make_async_remote_copy(
        src, dst, send, recv, device_id=peer, device_id_type=MESH_ID
    )


def cols(c, base=0):
    return pl.ds(pl.multiple_of(base + c * HALF, 128), HALF)


def unit_view(kind, n, ref, z, s, c):
    if kind == "square":
        return ref.at[n, z, s, :, cols(c)]
    if kind == "cols":
        return ref.at[n // 4, z, s, :, cols(c, (n % 4) * 2 * HALF)]
    if kind == "rows":
        return ref.at[n // 4, z, s, pl.ds((n % 4) * ROWS, ROWS), cols(c)]
    if kind == "line square":
        return ref.at[n, z]
    if kind == "line cols":
        return ref.at[z, :, pl.ds(n * HALF, HALF)]
    if kind == "line rows":
        return ref.at[z, pl.ds(n * ROWS, ROWS)]
    return ref.at[z, s]


class Gather:
    def __init__(self, units, refs, send, recv, z_count):
        self.units, self.refs, self.send, self.recv = units, refs, send, recv
        self.z_count = z_count
        self.where = place()
        self.started = []
        self.base = 2 * (z_count - 1)

    def view(self, u, z, s, c):
        kind, n = self.units[u]
        return unit_view(kind, n, self.refs[kind], z, s, c)

    def go(self, u, slot, ref, peer):
        copy = remote(ref, ref, self.send.at[u, slot], self.recv.at[u, slot], peer)
        copy.start()
        self.started.append(copy)

    def got(self, u, slot, ref):
        z, s, c = self.where[:3]
        remote(ref, ref, self.send.at[u, slot], self.recv.at[u, slot], (z, s, 1 - c)).wait_recv()

    def z_sends(self, u, i):
        z, s, c = self.where[:3]
        top = self.z_count - 1
        for slot, near, block, live in (
            (i, z + 1, z - i, (z >= i) & (z < top)),
            (top + i, z - 1, z + i, (z + i <= top) & (z > 0)),
        ):
            ref = self.view(u, block, s, c)
            copy = remote(
                ref, ref, self.send.at[u, slot], self.recv.at[u, slot], (near, s, c)
            )
            yield copy, live

    def z_send(self, u, i):
        for copy, live in self.z_sends(u, i):

            @pl.when(live)
            def _():
                copy.start()

    def z_got(self, u, i):
        z, s, c = self.where[:3]
        top = self.z_count - 1
        for slot, block, live in (
            (i, z - 1 - i, z - 1 - i >= 0),
            (top + i, z + 1 + i, z + 1 + i <= top),
        ):

            @pl.when(live)
            def _():
                self.got(u, slot, self.view(u, block, s, c))

    def a_start(self, u):
        z, s, c, first, second, both = self.where
        self.go(u, self.base, self.view(u, slice(None), s, c), (z, first, c))

    def a_wait(self, u):
        z, s, c, first, second, both = self.where
        self.got(u, self.base, self.view(u, slice(None), first, c))

    def b_start(self, u):
        z, s, c, first, second, both = self.where
        self.go(u, self.base + 1, self.view(u, slice(None), s, c), (z, second, c))
        self.go(u, self.base + 2, self.view(u, slice(None), first, c), (z, second, c))

    def b_wait(self, u):
        z, s, c, first, second, both = self.where
        self.got(u, self.base + 1, self.view(u, slice(None), second, c))
        self.got(u, self.base + 2, self.view(u, slice(None), both, c))

    def s_start(self, u):
        z, s, c = self.where[:3]
        if self.units[u][0] != "gain":
            self.go(u, self.base + 3, self.view(u, slice(None), slice(None), c), (z, s, 1 - c))

    def s_wait(self, u):
        z, s, c = self.where[:3]
        if self.units[u][0] != "gain":
            self.got(u, self.base + 3, self.view(u, slice(None), slice(None), 1 - c))

    def line(self, u, i):
        if i:
            self.z_got(u, i - 1)
        if i < self.z_count - 1:
            self.z_send(u, i)

    def tick(self, t, done):
        lines = self.z_count
        for n in range(lines + 4):
            u = t - n
            if not 0 <= u < len(self.units):
                continue
            if n < lines:
                self.line(u, n)
            plain = not self.units[u][0].startswith("line")
            if plain and n == lines - 1:
                self.a_start(u)
            if plain and n == lines:
                self.a_wait(u)
                self.b_start(u)
            if plain and n == lines + 1:
                self.b_wait(u)
                self.s_start(u)
            if plain and n == lines + 2:
                self.s_wait(u)
                done(u)

    def finish(self):
        for copy in self.started:
            copy.wait_send()
        for u in range(len(self.units)):
            for i in range(self.z_count - 1):
                for copy, live in self.z_sends(u, i):

                    @pl.when(live)
                    def _():
                        copy.wait_send()


ENC = (0, 1, 2, 3, 7, 8)
DEC = (4, 5, 6, 9)


def plane_peers(z, s, c):
    peers = []
    for ds in range(4):
        for dc in range(2):
            if ds or dc:
                peers.append(((z, (s + ds) % 4, (c + dc) % 2), ((s + 4 - ds) % 4, (c + dc) % 2)))
    return peers


class Plane:
    def __init__(self, send, recv):
        self.send, self.recv = send, recv
        self.z, self.s, self.c = place()[:3]
        self.peers = plane_peers(self.z, self.s, self.c)
        self.started = []

    def start(self, k, ref):
        for i, (peer, _) in enumerate(self.peers):
            mine = ref.at[self.s, self.c]
            copy = remote(mine, mine, self.send.at[k, i], self.recv.at[k, i], peer)
            copy.start()
            self.started.append(copy)

    def wait(self, k, ref):
        for i, (_, (s, c)) in enumerate(self.peers):
            slot = ref.at[s, c]
            remote(
                slot, slot, self.send.at[k, i], self.recv.at[k, i], (self.z, self.s, 1 - self.c)
            ).wait_recv()

    def finish(self):
        for copy in self.started:
            copy.wait_send()


def rounded(value):
    return value.astype(bf16).astype(f32)


def pick(value, start, size):
    full = value.shape[1]
    return pltpu.roll(value, full - start, 1)[:, :size].astype(bf16)


def halves(ref):
    parts = []
    for c in range(2):
        parts.append(ref[0, c] + ref[1, c] + ref[2, c] + ref[3, c])
    return parts


def blocks_of(ref, size, z_count):
    group = HALF // size
    lanes = ref.shape[-1]
    pieces = []
    for n in range(4 * z_count // group):
        total = None
        for m in range(group):
            z, s = (n * group + m) // 4, (n * group + m) % 4
            piece = ref[s, 0, z] + ref[s, 1, z]
            piece = jnp.concatenate([piece, jnp.zeros((8, HALF - lanes), f32)], axis=1)
            if m:
                piece = pltpu.roll(piece, m * size, 1)
            total = piece if total is None else total + piece
        pieces.append(total)
    return jnp.concatenate(pieces, axis=1)


def half_of(value, c):
    return jnp.where(c == 0, value[:, :HALF], value[:, HALF : 2 * HALF])


def mm_down(value, weight, s, z_count, size):
    total = None
    for z in range(z_count):
        term = matmul(pick(value, (4 * z + s) * size, size), weight(z))
        total = term if total is None else total + term
    return total


def own_row(value, s, c):
    row = lax.broadcasted_iota(jnp.int32, value.shape, 0)
    return jnp.sum(jnp.where(row == 2 * s + c, value, 0.0), axis=0, keepdims=True)


def as_own_row(value, s, c):
    wide = jnp.broadcast_to(value, (8, value.shape[1]))
    row = lax.broadcasted_iota(jnp.int32, wide.shape, 0)
    return jnp.where(row == 2 * s + c, wide, 0.0)


def pull_own(values_in, gain_row, incoming, s, c):
    inverse = lax.rsqrt(jnp.mean(values_in * values_in, axis=-1, keepdims=True) + norm_eps)
    scaled = incoming * gain_row
    inner = jnp.mean(scaled * values_in, axis=-1, keepdims=True)
    grad = inverse * scaled - values_in * (inverse * inverse * inverse * inner)
    return grad, own_row(incoming * values_in * inverse, s, c)


def put_blocks(ref, s, c, terms, size):
    for z, term in enumerate(terms):
        ref[s, c, z] = jnp.zeros(ref.shape[3:], f32)
        ref[s, c, z, :, :size] = term


def head_rows(width):
    lane = lax.broadcasted_iota(jnp.int32, (16, width), 1)
    row = lax.broadcasted_iota(jnp.int32, (16, width), 0)
    return (lane // HD) == row


def ffn_halves(parts):
    pieces = []
    for j in range(4):
        for c in range(2):
            pieces.append(parts[c][:, j * HALF : (j + 1) * HALF])
    return jnp.concatenate(pieces, axis=1)


class Decoder:
    (ROWS_IN, SELF_NORM, SELF_VALUES, ONE, CROSS_NORM, CROSS_ATT, FFN_NORM, TWO, TOP, QUERY) = range(10)
    INNER, PRE = 10, 14
    COUNT = 18

    def __init__(self, plane, st, gains, z_count):
        self.plane, self.st, self.gains, self.z_count = plane, st, gains, z_count
        self.s, self.c = plane.s, plane.c

    def gain(self, n):
        return self.gains[n : n + 1, :]

    def square_down(self, k, ref, value, wd, n):
        ref[self.s, self.c] = mm_down(value, lambda z: wd[n, z], self.s, self.z_count, ROWS)
        self.plane.start(k, ref)

    def square_sum(self, k, ref):
        self.plane.wait(k, ref)
        return jnp.concatenate(halves(ref), axis=1)

    def square_up(self, k, ref, value, wd, n):
        own = half_of(value, self.c).astype(bf16)
        put_blocks(
            ref, self.s, self.c, [mm_t(own, wd[n, z]) for z in range(self.z_count)], ROWS
        )
        self.plane.start(k, ref)

    def square_up_sum(self, k, ref):
        self.plane.wait(k, ref)
        return blocks_of(ref, ROWS, self.z_count)


def row_blocks(count, work):
    def body(i, carry):
        work(i, pl.ds(pl.multiple_of(i * BAND, BAND), BAND))
        return carry

    lax.fori_loop(0, count, body, 0)


def col_tiles(width, tile, work):
    def body(i, carry):
        work(pl.ds(pl.multiple_of(i * tile, tile), tile))
        return carry

    lax.fori_loop(0, width // tile, body, 0)


def wide(value):
    return value.reshape(value.shape[0] * value.shape[1] * value.shape[2], value.shape[3])


def attend_pair_fwd(pair, length, table_ref, q_ref, k_ref, v_ref, o_ref):
    span = k_ref.shape[0]
    at = pl.ds(pl.multiple_of(pair * 2 * HD, 2 * HD), 2 * HD)
    valid = lax.broadcasted_iota(jnp.int32, (1, span), 1) < length
    lane = lax.broadcasted_iota(jnp.int32, (1, 2 * HD), 1)
    k_all = k_ref[:, at]
    v_all = v_ref[:, at]
    bands = [bias_band(table_ref[2 * pair + t], span) for t in range(2)]
    for block in range(span // BAND):
        rows = slice(block * BAND, (block + 1) * BAND)
        q_rows = q_ref[rows, at]
        parts = []
        for t in range(2):
            own = (lane // HD) == t
            probs = softmax_rows(
                jnp.where(own, q_rows, jnp.zeros_like(q_rows)), k_all, bands[t], block, span, valid
            )
            parts.append(matmul(probs.astype(bf16), v_all))
        o_ref[rows, at] = jnp.where(lane < HD, parts[0], parts[1]).astype(bf16)


def forward_kernel(units, lines, z_count, *refs):
    (
        len_ref, table_ref, sq_ref, in_ref, out_ref, gain_ref, dec_ref, x_ref,
        in_o, out_o, x_o, q_o, k_o, v_o, att_o, hid_o, pre_o, hid2_o, enc_o, gck_o, gcv_o, wd_o,
        sq_o0, sq_o1, sq_o2, sq_o3, sq_o4, sq_o5, gain_o, st_o, gg_o, dec_o,
        sq_w, in_w, out_w, gain_w, sq_r, in_r, out_r, gain_r,
        x_s, n_s, q_s, k_s, v_s, att_s, hid_s, pre_s, inner_s, hid2_s, enc_s, ck_s, cv_s, gains,
        wd, wdi, wdo, st, e_rows, e_sq, e_att, e_pre, e_out, e_inner, e_up,
        send, recv, first_send, first_recv, x_send, x_recv, d_send, d_recv, p_send, p_recv, local,
    ) = refs
    z, s, c = place()[:3]
    sibling = (z, s, 1 - c)
    sq_o = (sq_o0, sq_o1, sq_o2, sq_o3, sq_o4, sq_o5)
    n_sq, n_ff = sq_ref.shape[0], in_ref.shape[0]
    blocks = x_s.shape[0] * x_s.shape[1] // BAND
    greet_plane(z, s, c, z_count)
    plane = Plane(p_send, p_recv)
    dec = Decoder(plane, st, gains, z_count)
    for n in range(2):
        e_rows[s, c, n] = as_own_row(dec_ref[n : n + 1, :].astype(f32), s, c)
    plane.start(0, e_rows)

    first = []

    def to_sibling(src, dst):
        copy = remote(src, dst, first_send.at[len(first)], first_recv.at[len(first)], sibling)
        copy.start()
        first.append(copy)

    to_sibling(gain_ref, gain_r)
    to_sibling(sq_ref.at[:, :, cols(1 - c)], sq_r)
    x_copies = []
    for d in range(1, 4):
        peer = (s + d) % 4
        copy = remote(
            x_ref.at[peer], x_s.at[s], x_send.at[d - 1], x_recv.at[d - 1], (z, peer, c)
        )
        copy.start()
        x_copies.append(copy)
    mine = pltpu.make_async_copy(x_ref.at[s], x_s.at[s], local.at[0])
    mine.start()
    for n in range(n_ff):
        for j in range(4):
            to_sibling(in_ref.at[n, :, cols(1 - c, 2 * HALF * j)], in_r.at[n, j])
        to_sibling(out_ref.at[n, :, cols(1 - c)], out_r.at[n])

    def joined(own, other):
        top = jnp.where(c == 0, own, other)
        bottom = jnp.where(c == 0, other, own)
        return jnp.concatenate([top, bottom], axis=0).astype(bf16)

    gather = Gather(
        units,
        {
            "square": sq_w,
            "cols": in_w,
            "rows": out_w,
            "gain": gain_w,
            "line square": wd,
            "line cols": wdi,
            "line rows": wdo,
        },
        send,
        recv,
        z_count,
    )
    lined = Gather(lines, gather.refs, d_send, d_recv, z_count)
    first[0].wait_recv()
    gain_w[z, s] = joined(gain_ref[...], gain_r[...])
    first[1].wait_recv()
    for i, n in enumerate(ENC):
        sq_w[i, z, s, :, cols(c)] = joined(sq_ref[n, :, cols(c)], sq_r[n])
    drains = []

    def drain(src, dst):
        copy = pltpu.make_async_copy(src, dst, local.at[1 + len(drains)])
        copy.start()
        drains.append(copy)

    def done(u):
        kind, n = units[u]
        if kind == "square":
            drain(sq_w.at[n], sq_o[n])
        elif kind == "cols" and n % 4 == 3:
            drain(in_w.at[n // 4], in_o)
        elif kind == "rows" and n % 4 == 3:
            drain(out_w.at[n // 4], out_o)

    def normed(src, gain_row, dst):
        def work(i, at):
            dst[at, :] = rms_gain(src(i, at), gains[gain_row : gain_row + 1, :]).astype(bf16)

        row_blocks(blocks, work)

    def x_rows(i, at):
        return x_s[i].astype(f32)

    def start_piece():
        for copy in x_copies:
            copy.wait_recv()
        mine.wait()
        drain(x_s, x_o)
        gains[...] = wide(gain_w[...]).astype(f32).T[:8]
        gain_o[...] = gains[...]
        normed(x_rows, 0, n_s)

    def square_dot(left, n, tile=256):
        def weight(at):
            return wide(sq_w[n, :, :, :, at])

        return lambda at: matmul(left[...], weight(at))

    def project(n, left, dst, out):
        dot = square_dot(left, n)

        def work(at):
            dst[:, at] = dot(at).astype(bf16)

        col_tiles(2 * HALF, 256, work)
        if out is not None:
            drain(dst, out)

    def attention(pairs):
        def body(pair, carry):
            attend_pair_fwd(pair, len_ref[0], table_ref, q_s, k_s, v_s, att_s)
            return carry

        lax.fori_loop(pairs[0], pairs[1], body, 0)

    def hidden_piece():
        drain(att_s, att_o)
        dot = square_dot(att_s, 3)

        def work(at):
            hid_s[:, at] = dot(at)

        col_tiles(2 * HALF, 256, work)

        def add(i, at):
            total = hid_s[at, :] + x_rows(i, at)
            hid_s[at, :] = total
            n_s[at, :] = rms_gain(total, gains[1:2, :]).astype(bf16)

        row_blocks(blocks, add)
        drain(hid_s, hid_o)

    def ffn_piece(j):
        def work(i, carry):
            at = pl.ds(pl.multiple_of(j * 2 * HALF + i * 256, 256), 256)
            pre = matmul(n_s[...], wide(in_w[0, :, :, :, at]))
            pre_s[:, at] = pre
            inner_s[:, at] = gelu_tanh(pre).astype(bf16)
            return carry

        lax.fori_loop(0, 3, work, 0)

    def hidden_two_piece():
        drain(pre_s, pre_o)

        def work(at):
            hid2_s[:, at] = hid_s[:, at] + matmul(inner_s[...], wide(out_w[0, :, :, :, at]))

        col_tiles(2 * HALF, 256, work)
        normed(lambda i, at: hid2_s[at, :], 2, enc_s)
        drain(hid2_s, hid2_o)
        drain(enc_s, enc_o)

    def dec_start():
        plane.wait(0, e_rows)
        for n, to in ((0, Decoder.ROWS_IN), (1, Decoder.TOP)):
            total = e_rows[0, 0, n]
            for p in range(1, 8):
                total = total + e_rows[p // 2, p % 2, n]
            st[to] = total
        value = rounded(rms_gain(st[Decoder.ROWS_IN], dec.gain(3)))
        st[Decoder.SELF_NORM] = value
        drain(wd, wd_o)
        dec.square_down(1, e_sq.at[0], value, wd, 0)

    def dec_self_values():
        value = rounded(dec.square_sum(1, e_sq.at[0]))
        st[Decoder.SELF_VALUES] = value
        dec.square_down(2, e_sq.at[1], value, wd, 1)

    def dec_self_out():
        value = st[Decoder.ROWS_IN] + dec.square_sum(2, e_sq.at[1])
        st[Decoder.ONE] = value
        value = rounded(rms_gain(value, dec.gain(4)))
        st[Decoder.CROSS_NORM] = value
        dec.square_down(3, e_sq.at[2], value, wd, 2)

    def dec_query():
        st[Decoder.QUERY] = rounded(dec.square_sum(3, e_sq.at[2]))

    def dec_main():
        width = 2 * HALF
        scale = 1.0 / math.sqrt(HD)
        mask = head_rows(width)
        valid = lax.broadcasted_iota(jnp.int32, (1, x_s.shape[0] * BAND), 1) < len_ref[0]
        query = own_row(st[Decoder.QUERY], s, c)
        q_heads = jnp.where(mask, query, 0.0).astype(bf16)
        scores = jnp.where(valid, mm_t(q_heads, ck_s[...]) * scale, neg_fill)
        raised = jnp.exp(scores - jnp.max(scores, axis=-1, keepdims=True))
        probs = raised / jnp.sum(raised, axis=-1, keepdims=True)
        probs_b = probs.astype(bf16)
        att = jnp.where(mask, matmul(probs_b, cv_s[...]), 0.0)
        e_att[s, c] = as_own_row(rounded(jnp.sum(att, axis=0, keepdims=True)), s, c)
        plane.start(4, e_att)
        plane.wait(4, e_att)
        value = e_att[0, 0]
        for p in range(1, 8):
            value = value + e_att[p // 2, p % 2]
        st[Decoder.CROSS_ATT] = value
        dec.square_down(5, e_sq.at[3], value, wd, 3)
        two = st[Decoder.ONE] + dec.square_sum(5, e_sq.at[3])
        value = rounded(rms_gain(two, dec.gain(5)))
        st[Decoder.FFN_NORM] = value
        e_pre[s, c] = mm_down(value, lambda n: wdi[n], s, z_count, ROWS)
        plane.start(6, e_pre)
        own = half_of(st[Decoder.TOP], c).astype(bf16)
        put_blocks(e_inner, s, c, [mm_t(own, wdo[n]) for n in range(z_count)], 4 * ROWS)
        plane.start(7, e_inner)
        plane.wait(6, e_pre)
        inner, slope = gelu_both(ffn_halves(halves(e_pre)))
        inner = rounded(inner)
        e_out[s, c] = mm_down(inner, lambda n: wdo[n], s, z_count, 4 * ROWS)
        plane.start(8, e_out)
        plane.wait(7, e_inner)
        g_pre = rounded(blocks_of(e_inner, 4 * ROWS, z_count) * slope)
        own = jnp.concatenate(
            [
                half_of(g_pre[:, j * width : (j + 1) * width], c) for j in range(4)
            ],
            axis=1,
        ).astype(bf16)
        put_blocks(e_up.at[0], s, c, [mm_t(own, wdi[n]) for n in range(z_count)], ROWS)
        plane.start(9, e_up.at[0])
        for j in range(4):
            st[Decoder.INNER + j] = inner[:, j * width : (j + 1) * width]
            st[Decoder.PRE + j] = g_pre[:, j * width : (j + 1) * width]
        g_norm = dec.square_up_sum(9, e_up.at[0])
        grad, gain = pull_own(two, dec.gain(5), g_norm, s, c)
        gg_o[...] = jnp.zeros_like(gg_o)
        gg_o[5:6, :] = gain
        g_two = st[Decoder.TOP] + grad
        st[Decoder.TWO] = g_two
        dec.square_up(10, e_up.at[1], g_two, wd, 3)
        plane.wait(8, e_out)
        out = two + jnp.concatenate(halves(e_out), axis=1)
        dec_o[...] = jnp.broadcast_to(own_row(out, s, c), dec_o.shape)
        g_att = own_row(rounded(dec.square_up_sum(10, e_up.at[1])), s, c)
        g_heads = jnp.where(mask, g_att, 0.0).astype(bf16)
        g_probs = mm_t(g_heads, cv_s[...])
        g_scores = probs * (g_probs - jnp.sum(g_probs * probs, axis=-1, keepdims=True))
        row = lax.broadcasted_iota(jnp.int32, g_scores.shape, 0)
        g_scores_b = jnp.where(row < H, g_scores, 0.0).astype(bf16)
        g_query = jnp.where(mask, matmul(g_scores_b, ck_s[...]), 0.0)
        g_query = jnp.sum(g_query, axis=0, keepdims=True) * scale
        st[Decoder.QUERY] = as_own_row(rounded(g_query), s, c)
        live_b = jnp.where(row < H, probs_b.astype(f32), 0.0).astype(bf16)
        n_s[...] = (mm_outer(g_scores_b, q_heads) * scale).astype(bf16)
        drain(n_s, gck_o)
        cv_s[...] = mm_outer(live_b, g_heads).astype(bf16)
        drain(cv_s, gcv_o)
        st_o[...] = st[...]

    pieces = {
        ("gain", 0): [start_piece],
        ("square", 0): [lambda: project(0, n_s, q_s, q_o)],
        ("square", 1): [lambda: project(1, n_s, k_s, k_o)],
        ("square", 2): [lambda: project(2, n_s, v_s, v_o), dec_start, lambda: attention((0, 2))],
        ("square", 3): [lambda: attention((2, 4)), dec_self_values],
        ("cols", 0): [lambda: attention((4, 6)), dec_self_out],
        ("cols", 1): [hidden_piece, lambda: ffn_piece(0), dec_query],
        ("cols", 2): [lambda: ffn_piece(1), lambda: ffn_piece(2)],
        ("cols", 3): [lambda: ffn_piece(3)],
        ("rows", 3): [hidden_two_piece],
        ("square", 4): [lambda: project(4, enc_s, ck_s, None)],
        ("square", 5): [lambda: project(5, enc_s, cv_s, None), dec_main],
    }
    k = 2
    for t in range(len(units) + z_count + 2):
        gather.tick(t, done)
        if t >= 2:
            lined.tick(t - 2, done)
        if t == 1:
            for i, n in enumerate(DEC):
                wd[i, z] = joined(sq_ref[n, :, cols(c)], sq_r[n])
            for n in range(n_ff):
                for j in range(4):
                    first[k].wait_recv()
                    k += 1
                    at = cols(c, 2 * HALF * j)
                    value = joined(in_ref[n, :, at], in_r[n, j])
                    if n == 0:
                        in_w[n, z, s, :, at] = value
                    else:
                        wdi[z, :, j * HALF : (j + 1) * HALF] = value
                first[k].wait_recv()
                k += 1
                value = joined(out_ref[n, :, cols(c)], out_r[n])
                if n == 0:
                    out_w[n, z, s, :, cols(c)] = value
                else:
                    wdo[z] = value
        ready = 0 if t == z_count + 1 else t - z_count - 2
        if ready > 0 or t == z_count + 1:
            for piece in pieces.get(units[ready], ()):
                piece()
    gather.finish()
    lined.finish()
    plane.finish()
    for copy in first:
        copy.wait_send()
    for copy in x_copies:
        copy.wait_send()
    for copy in drains:
        copy.wait()


def greet_plane(z, s, c, z_count):
    barrier = pltpu.get_barrier_semaphore()
    for d in range(1, z_count):
        peer = ((z + d) % z_count, s, c)
        pl.semaphore_signal(barrier, 1, device_id=peer, device_id_type=MESH_ID)
    for peer, _ in plane_peers(z, s, c):
        pl.semaphore_signal(barrier, 1, device_id=peer, device_id_type=MESH_ID)
    pl.semaphore_wait(barrier, z_count - 1 + 7)


def forward(length, table, square, ffn_in, ffn_out, gains_t, dec_rows, x, z_count):
    n_sq, n_ff = square.shape[0], ffn_in.shape[0]
    order = [("gain", 0)]
    order += [("square", n) for n in (0, 1, 2)]
    lines = [("line square", n) for n in range(4)]
    lines += [("line cols", n) for n in range(4)] + [("line rows", n) for n in range(4)]
    plain = [("square", 3)] + [("cols", n) for n in range(4)] + [("rows", n) for n in range(4)]
    plain += [("square", n) for n in (4, 5)]
    order = order + plain
    blocks, band, width = x.shape
    span = blocks * band
    hidden_units = 8 * HALF
    sq_s = (len(ENC), z_count, 4, ROWS, width)
    in_s = (1, z_count, 4, ROWS, hidden_units)
    out_s = (1, z_count, 4, 4 * ROWS, width)
    gain_s = (z_count, 4, ROWS, 128)
    wd_s = (len(DEC), z_count, ROWS, HALF)
    firsts = 2 + 5 * n_ff
    slots = 2 * (z_count - 1) + 4
    vmem = pl.BlockSpec(memory_space=pltpu.VMEM)
    hbm = pl.BlockSpec(memory_space=pltpu.HBM)
    token = ((span, width), bf16)
    token_f = ((span, width), f32)
    st_s = ((Decoder.COUNT, 8, width), f32)
    outs = [(in_s[1:], bf16), (out_s[1:], bf16)]
    outs += [(x.shape, bf16), token, token, token, token, token_f]
    outs += [((span, hidden_units), f32), token_f, token, token, token, (wd_s, bf16)]
    outs += [(sq_s[1:], bf16)] * len(ENC)
    small = [((8, width), f32), st_s, ((8, width), f32), ((8, width), f32)]
    scratch = [(sq_s, bf16), (in_s, bf16), (out_s, bf16), (gain_s, bf16)]
    scratch += [((n_sq, ROWS // 2, HALF), f32), ((n_ff, 4, ROWS // 2, HALF), f32)]
    scratch += [((n_ff, 2 * ROWS, HALF), f32), ((ROWS // 2, 128), f32)]
    scratch += [(x.shape, bf16), token, token, token, token, token, token_f]
    scratch += [((span, hidden_units), f32), ((span, hidden_units), bf16), token_f]
    scratch += [token, token, token, ((8, width), f32)]
    scratch += [(wd_s, bf16), ((z_count, ROWS, 4 * HALF), bf16), ((z_count, 4 * ROWS, HALF), bf16)]
    scratch += [st_s, ((4, 2, 2, 8, width), f32), ((4, 4, 2, 8, HALF), f32)]
    scratch += [((4, 2, 8, width), f32), ((4, 2, 8, 4 * HALF), f32), ((4, 2, 8, HALF), f32)]
    scratch += [((4, 2, z_count, 8, 256), f32), ((2, 4, 2, z_count, 8, 128), f32)]
    dma = pltpu.SemaphoreType.DMA
    return pl.pallas_call(
        functools.partial(forward_kernel, order, lines, z_count),
        out_shape=[jax.ShapeDtypeStruct(*o) for o in outs + small],
        in_specs=[pl.BlockSpec(memory_space=pltpu.SMEM)] + [vmem] * 6 + [hbm],
        out_specs=[hbm] * len(outs) + [vmem] * len(small),
        scratch_shapes=[pltpu.VMEM(*o) for o in scratch]
        + [dma((len(order), slots)), dma((len(order), slots)), dma((firsts,)), dma((firsts,))]
        + [dma((3,)), dma((3,)), dma((len(lines), slots)), dma((len(lines), slots))]
        + [dma((11, 7)), dma((11, 7)), dma((40,))],
        compiler_params=pltpu.CompilerParams(
            collective_id=0, has_side_effects=True, vmem_limit_bytes=62 * MIB
        ),
        name="forward",
    )(length, table, square, ffn_in, ffn_out, gains_t, dec_rows, x)


class Scatter:
    def __init__(self, units, sources, bufs, sems, z_count, put):
        self.units, self.sources, self.z_count, self.put = units, sources, z_count, put
        self.r0, self.r1, self.r2, self.r3, self.fin, self.sib = bufs
        self.send, self.recv = sems
        self.where = place()
        self.started = []
        self.lent = {}

    def go(self, u, slot, src, dst, peer):
        copy = remote(src, dst, self.send.at[u, slot], self.recv.at[u, slot], peer)
        copy.start()
        return copy

    def got(self, u, slot, ref):
        z, s, c = self.where[:3]
        remote(ref, ref, self.send.at[u, slot], self.recv.at[u, slot], (z, s, 1 - c)).wait_recv()

    def view(self, u, c, z=slice(None), s=slice(None)):
        kind, n = self.sources[u]
        if kind == "rows":
            return unit_view(kind, n, self.refs[kind], z, s, c)
        return self.refs["slots"].at[n, z, s, :, cols(c)]

    def c_start(self, u):
        z, s, c = self.where[:3]
        self.lent[u] = self.go(u, 0, self.view(u, 1 - c), self.r0.at[u], (z, s, 1 - c))

    def b_start(self, u):
        z, s, c, first, second, both = self.where
        self.got(u, 0, self.r0.at[u])

        def body(i, carry):
            n, m = i // 4, i % 4
            own = self.view(u, c, n, m)[...]
            total = own.astype(f32) + self.r0[u, n, m].astype(f32)
            self.r0[u, n, m] = total.astype(bf16)
            return carry

        lax.fori_loop(0, 4 * self.z_count, body, 0, unroll=4)
        self.started.append(self.go(u, 1, self.r0.at[u, :, second], self.r1.at[u, 0], (z, second, c)))
        self.started.append(self.go(u, 2, self.r0.at[u, :, both], self.r1.at[u, 1], (z, second, c)))
        self.lent.pop(u).wait_send()

    def a_start(self, u):
        z, s, c, first, second, both = self.where
        self.got(u, 2, self.r1.at[u, 1])
        for n in range(self.z_count):
            total = self.r0[u, n, first].astype(f32) + self.r1[u, 1, n].astype(f32)
            self.r1[u, 1, n] = total.astype(bf16)
        self.started.append(self.go(u, 3, self.r1.at[u, 1], self.r2.at[u], (z, first, c)))
        self.got(u, 1, self.r1.at[u, 0])
        for n in range(self.z_count):
            total = self.r0[u, n, s].astype(f32) + self.r1[u, 0, n].astype(f32)
            self.r1[u, 0, n] = total.astype(bf16)

    def z_start(self, u):
        z, s, c = self.where[:3]
        self.got(u, 3, self.r2.at[u])
        for n in range(self.z_count):
            total = self.r1[u, 0, n].astype(f32) + self.r2[u, n].astype(f32)
            self.r2[u, n] = total.astype(bf16)
        for d in range(1, self.z_count):
            to = (z + d) % self.z_count
            self.started.append(
                self.go(u, 3 + d, self.r2.at[u, to], self.r3.at[u, d - 1], (to, s, c))
            )

    def f_start(self, u):
        z, s, c = self.where[:3]
        total = self.r2[u, z].astype(f32)
        for d in range(1, self.z_count):
            self.got(u, 3 + d, self.r3.at[u, d - 1])
            total = total + self.r3[u, d - 1].astype(f32)
        self.fin[u] = total
        kind, n = self.units[u]
        if kind == "rows":
            if n % 2 == 1:
                @pl.when(c != n // 2)
                def _():
                    pair = pl.ds(u - 1, 2)
                    self.go(u, 7, self.fin.at[pair], self.sib.at[pair], (z, s, 1 - c))
        else:
            rows = pl.ds(pl.multiple_of((1 - c) * (ROWS // 2), 8), ROWS // 2)
            self.started.append(
                self.go(
                    u, 7, self.fin.at[u, rows], self.sib.at[u, pl.ds(0, ROWS // 2)], (z, s, 1 - c)
                )
            )

    def finish_unit(self, u):
        z, s, c = self.where[:3]
        kind, n = self.units[u]
        if kind == "rows":
            if n % 2 == 1:

                @pl.when(c == n // 2)
                def _():
                    self.got(u, 7, self.sib.at[pl.ds(u - 1, 2)])
                    for k in range(2):
                        self.put(kind, k, c, self.fin[u - 1 + k])
                        self.put(kind, k, 1 - c, self.sib[u - 1 + k])

                @pl.when(c != n // 2)
                def _():
                    pair = self.fin.at[pl.ds(u - 1, 2)]
                    remote(
                        pair, pair, self.send.at[u, 7], self.recv.at[u, 7], (z, s, 1 - c)
                    ).wait_send()
        else:
            self.got(u, 7, self.sib.at[u, pl.ds(0, ROWS // 2)])
            rows = pl.ds(pl.multiple_of(c * (ROWS // 2), 8), ROWS // 2)
            self.put(kind, n, c, self.fin[u, rows])
            self.put(kind, n, 1 - c, self.sib[u, : ROWS // 2])

    def tick(self, t):
        steps = (self.c_start, self.b_start, self.a_start, self.z_start, self.f_start)
        for n in range(5):
            if 0 <= t - n < len(self.units):
                steps[n](t - n)
        if 0 <= t - 5 < len(self.units):
            self.finish_unit(t - 5)

    def finish(self):
        for copy in self.started:
            copy.wait_send()


def pull_rows(values_in, gain_row, incoming):
    inverse = lax.rsqrt(jnp.mean(values_in * values_in, axis=-1, keepdims=True) + norm_eps)
    scaled = incoming * gain_row
    inner = jnp.mean(scaled * values_in, axis=-1, keepdims=True)
    grad = inverse * scaled - values_in * (inverse * inverse * inverse * inner)
    return grad, jnp.sum(incoming * values_in * inverse, axis=0, keepdims=True)


def gelu_both(values_in):
    square = values_in * values_in
    slope = 0.7978845608028654
    bend = jnp.tanh(slope * values_in * (1.0 + 0.044715 * square))
    value = 0.5 * values_in * (1.0 + bend)
    grad = 0.5 * (1.0 + bend) + 0.5 * values_in * (1.0 - bend * bend) * slope * (
        1.0 + 3.0 * 0.044715 * square
    )
    return value, grad


def attend_pair_bwd(
    pair, length, table_ref, q_ref, k_ref, v_ref, do_ref, dq_ref, dk_ref, dv_ref, dt_ref
):
    span = k_ref.shape[0]
    scale = 1.0 / math.sqrt(HD)
    at = pl.ds(pl.multiple_of(pair * 2 * HD, 2 * HD), 2 * HD)
    valid = lax.broadcasted_iota(jnp.int32, (1, span), 1) < length
    lane = lax.broadcasted_iota(jnp.int32, (1, 2 * HD), 1)
    k_all = k_ref[:, at]
    v_all = v_ref[:, at]
    count = span // BAND
    dks, dvs = [], []
    dqs = [[None, None] for _ in range(count)]
    for t in range(2):
        own = (lane // HD) == t
        band = bias_band(table_ref[2 * pair + t], span)
        dk = jnp.zeros((span, 2 * HD), f32)
        dv = jnp.zeros((span, 2 * HD), f32)
        dband = jnp.zeros((BAND, 2 * span), f32)
        for block in range(count):
            rows = slice(block * BAND, (block + 1) * BAND)
            q_rows = q_ref[rows, at]
            do_rows = do_ref[rows, at]
            zero = jnp.zeros_like(q_rows)
            probs = softmax_rows(jnp.where(own, q_rows, zero), k_all, band, block, span, valid)
            dprobs = mm_t(jnp.where(own, do_rows, zero), v_all)
            dscore = probs * (dprobs - jnp.sum(dprobs * probs, axis=-1, keepdims=True))
            start = span - BAND * (block + 1)
            pieces = []
            if start:
                pieces.append(jnp.zeros((BAND, start), f32))
            pieces.append(dscore)
            if span - start:
                pieces.append(jnp.zeros((BAND, span - start), f32))
            dband = dband + jnp.concatenate(pieces, axis=1)
            dscore_b = dscore.astype(bf16)
            dv = dv + mm_outer(probs.astype(bf16), do_rows)
            dk = dk + mm_outer(dscore_b, q_rows)
            dqs[block][t] = matmul(dscore_b, k_all)
        dks.append(dk)
        dvs.append(dv)
        dt_ref[2 * pair + t] = band_sums(dband, span)
    dk_ref[:, at] = (jnp.where(lane < HD, dks[0], dks[1]) * scale).astype(bf16)
    dv_ref[:, at] = jnp.where(lane < HD, dvs[0], dvs[1]).astype(bf16)
    for block in range(count):
        rows = slice(block * BAND, (block + 1) * BAND)
        dq_ref[rows, at] = (jnp.where(lane < HD, dqs[block][0], dqs[block][1]) * scale).astype(bf16)


def backward_kernel(z_count, *refs):
    (
        len_ref, table_ref, gain_ref, w0, w1, w2, w3, w7, w8, win, wout,
        x_i, q_i, k_i, v_i, att_i, hid_i, pre_i, hid2_i, enc_i, gck_i, gcv_i, wd_i, st, gg_i,
        sq_o, in_o, out_o, x_o, dt_o, gg_o, dsq_o, din_o, dout_o,
        slots, d_out, r0, r1, r2, r3, fin, sib,
        wbuf, x_s, q_s, k_s, v_s, att_s, enc_s, gck_s, gcv_s, hid_s, hid2_s, pre_s,
        gh, gh_b, acc, inner_s, gpre_s, turned, gatt, gq, gk, gv, gx, gx_r,
        wd, e_q, e_up, left_w, left_r, right_r, acc_one,
        send, recv, w_sem, p_sem, a_sem, x_send, x_recv, o_sem, p_send, p_recv, z_send, z_recv,
    ) = refs
    z, s, c = place()[:3]
    blocks = x_s.shape[0]
    width = 2 * HALF

    loads = {}
    for n, (src, dst) in enumerate(
        (
            (enc_i, enc_s), (gck_i, gck_s), (gcv_i, gcv_s), (hid2_i, hid2_s), (hid_i, hid_s),
            (att_i, att_s), (q_i, q_s), (k_i, k_s), (v_i, v_s), (x_i, x_s), (wd_i, wd),
        )
    ):
        copy = pltpu.make_async_copy(src, dst, a_sem.at[n])
        copy.start()
        loads[n] = copy
    tiles = [w7, w8]
    for j in range(4):
        tiles.append(wout.at[pl.ds(j * width, width)])
        tiles.append(win.at[:, pl.ds(j * width, width)])
    tiles += [w3, w0, w1, w2]
    w_loads = {}

    def fetch(n):
        if n < len(tiles):
            copy = pltpu.make_async_copy(tiles[n], wbuf.at[n % 4], w_sem.at[n])
            copy.start()
            w_loads[n] = copy

    p_loads = {}

    def fetch_pre(j):
        if j < 4:
            copy = pltpu.make_async_copy(
                pre_i.at[:, pl.ds(j * width, width)], pre_s.at[j % 2], p_sem.at[j]
            )
            copy.start()
            p_loads[j] = copy

    for n in range(4):
        fetch(n)
    fetch_pre(0)
    fetch_pre(1)
    greet_plane(z, s, c, z_count)
    plane = Plane(p_send, p_recv)
    dec = Decoder(plane, st, gain_ref, z_count)
    e_q[s, c] = st[Decoder.QUERY]
    plane.start(0, e_q)
    z_copies = []

    def dec_query():
        plane.wait(0, e_q)
        value = e_q[0, 0]
        for p in range(1, 8):
            value = value + e_q[p // 2, p % 2]
        acc_one[1] = value
        loads[10].wait()
        dec.square_up(1, e_up.at[0], value, wd, 2)

    def dec_one():
        grad, gain = pull_own(st[Decoder.ONE], dec.gain(4), dec.square_up_sum(1, e_up.at[0]), s, c)
        gg_o[4:5, :] += gain
        value = rounded(st[Decoder.TWO] + grad)
        acc_one[0] = value
        dec.square_up(2, e_up.at[1], value, wd, 1)

    def dec_self():
        value = rounded(dec.square_up_sum(2, e_up.at[1]))
        dec.square_up(3, e_up.at[2], value, wd, 0)
        rights = [value, acc_one[0], acc_one[1], rounded(st[Decoder.TWO])]
        rights += [st[Decoder.PRE + j] for j in range(4)] + [st[Decoder.TOP], jnp.zeros_like(value)]
        right_r[z] = jnp.concatenate(rights, axis=0).astype(bf16)
        lefts = [st[n] for n in range(Decoder.SELF_NORM, Decoder.SELF_VALUES + 1)]
        lefts += [st[n] for n in range(Decoder.CROSS_NORM, Decoder.FFN_NORM + 1)]
        lefts = jnp.concatenate(lefts + [jnp.zeros_like(value)], axis=0).astype(bf16)
        row = lax.broadcasted_iota(jnp.int32, (width, 128), 0)
        lane = lax.broadcasted_iota(jnp.int32, (width, 128), 1)
        share = ROWS // 2
        hidden_at = (2 * s + c) * 4 * share
        hidden_pick = jnp.where((row == hidden_at + lane) & (lane < 4 * share), 1.0, 0.0)
        for to in range(z_count):
            at = (to * 8 + 2 * s + c) * share
            chosen = jnp.where((row == at + lane) & (lane < share), 1.0, 0.0).astype(bf16)
            inner = jnp.concatenate([st[Decoder.INNER + to], jnp.zeros_like(value)], axis=0)
            left_w[to] = jnp.concatenate(
                [
                    matmul(lefts, chosen).astype(bf16),
                    matmul(inner.astype(bf16), hidden_pick.astype(bf16)).astype(bf16),
                ],
                axis=0,
            )
        k = 0
        for d in range(1, z_count):
            to = (z + d) % z_count
            for src, dst in ((right_r.at[z], right_r.at[z]), (left_w.at[to], left_r.at[z])):
                copy = remote(src, dst, z_send.at[k], z_recv.at[k], (to, s, c))
                copy.start()
                z_copies.append(copy)
                k += 1
        left_r[z] = left_w[z]

    def dec_last():
        _, gain = pull_own(
            st[Decoder.ROWS_IN], dec.gain(3), dec.square_up_sum(3, e_up.at[2]), s, c
        )
        gg_o[3:4, :] += gain

    def dec_grads():
        for copy in z_copies:
            copy.wait()
        lefts = [left_r[n].astype(f32) for n in range(z_count)]
        rights = [right_r[n].astype(f32) for n in range(z_count)]

        def gathered(parts, n):
            return jnp.concatenate([p[8 * n : 8 * n + 8] for p in parts], axis=0).astype(bf16)

        share = ROWS // 2
        for n in range(4):
            dsq_o[n] = mm_outer(gathered(lefts, n), gathered(rights, n))[:share]
        for j in range(4):
            din_o[:, j * width : (j + 1) * width] = mm_outer(
                gathered(lefts, 4), gathered(rights, 4 + j)
            )[:share]
        dout_o[...] = mm_outer(gathered(lefts, 6), gathered(rights, 8))[: 4 * share]

    units = [("square", 4), ("square", 5)] + [("cols", j) for j in range(4)] + [("square", 3)]
    units += [("rows", n) for n in range(4)] + [("heads", m) for m in range(3)]
    sources, held = [], 0
    for kind, n in units:
        if kind == "rows":
            sources.append((kind, n))
        else:
            sources.append(("slot", held % 3))
            held += 1

    def put(kind, n, side, value):
        if kind == "square":
            sq_o[n, :, cols(side)] = value
        elif kind == "cols":
            in_o[:, cols(side, n * width)] = value
        elif kind == "rows":
            out_o[n * ROWS : (n + 1) * ROWS, cols(side)] = value
        else:
            at = pl.ds(pl.multiple_of((2 * n + side) * 128, 128), 128)
            for t in range(3):
                sq_o[t, :, at] = value[:, t * 128 : (t + 1) * 128]

    scatter = Scatter(units, sources, (r0, r1, r2, r3, fin, sib), (send, recv), z_count, put)
    scatter.refs = {"slots": slots, "rows": d_out}

    def turn(src):
        def body(i, carry):
            at = pl.ds(pl.multiple_of(i * 256, 256), 256)
            turned[at, :] = src[:, at].T
            return carry

        lax.fori_loop(0, 3, body, 0)

    def grad_to_slot(n, right):
        def work(at):
            value = matmul(turned[...], right[:, at]).astype(bf16)
            slots[n, :, :, :, at] = value.reshape(z_count, 4, ROWS, 256)

        col_tiles(width, 256, work)

    def back(left, n, dst, add):
        w_loads[n].wait()

        def work(at):
            value = mm_t(left[...], wbuf[n % 4, at, :])
            if add:
                value = value + dst[:, at]
            dst[:, at] = value

        col_tiles(width, 256, work)
        fetch(n + 4)

    gg_o[...] = gg_i[...]
    loads[0].wait()
    loads[1].wait()
    turn(enc_s)
    grad_to_slot(0, gck_s)
    scatter.tick(0)
    dec_query()
    loads[2].wait()
    grad_to_slot(1, gcv_s)
    scatter.tick(1)
    back(gck_s, 0, acc, False)
    back(gcv_s, 1, acc, True)
    loads[3].wait()
    loads[4].wait()

    def pull_hid2(i, at):
        grad, gain = pull_rows(hid2_s[at, :], gain_ref[2:3, :], acc[at, :])
        gh[at, :] = grad
        gh_b[at, :] = grad.astype(bf16)
        gg_o[2:3, :] += gain
        enc_s[at, :] = rms_gain(hid_s[at, :], gain_ref[1:2, :]).astype(bf16)

    dec_one()
    row_blocks(blocks, pull_hid2)
    turn(enc_s)

    for j in range(4):
        p_loads[j].wait()
        w_loads[2 + 2 * j].wait()

        def hidden_tile(at):
            value, slope = gelu_both(pre_s[j % 2, :, at])
            inner_s[:, at] = value.astype(bf16)
            grad = mm_t(gh_b[...], wbuf[(2 + 2 * j) % 4, at, :])
            gpre_s[:, at] = (grad * slope).astype(bf16)

        col_tiles(width, 256, hidden_tile)
        fetch(6 + 2 * j)
        fetch_pre(j + 2)
        grad_to_slot((2 + j) % 3, gpre_s)
        scatter.tick(2 + j)

        def out_rows(i, carry):
            at = pl.ds(pl.multiple_of(i * HALF, HALF), HALF)
            value = mm_outer(inner_s[:, at], gh_b[...]).astype(bf16)
            d_out[0, j, pl.ds(2 * i, 2)] = value.reshape(2, 4 * ROWS, width)
            return carry

        lax.fori_loop(0, 2, out_rows, 0)
        back(gpre_s, 3 + 2 * j, acc, j > 0)
        if j < 2:
            (dec_self, dec_last)[j]()

    loads[5].wait()

    def pull_hid(i, at):
        grad, gain = pull_rows(hid_s[at, :], gain_ref[1:2, :], acc[at, :])
        total = gh[at, :] + grad
        gh[at, :] = total
        gh_b[at, :] = total.astype(bf16)
        gg_o[1:2, :] += gain

    row_blocks(blocks, pull_hid)
    turn(att_s)
    grad_to_slot(0, gh_b)
    scatter.tick(6)
    w_loads[10].wait()

    def attended_grad(at):
        gatt[:, at] = mm_t(gh_b[...], wbuf[10 % 4, at, :]).astype(bf16)

    col_tiles(width, 256, attended_grad)
    for n in (6, 7, 8, 9):
        loads[n].wait()

    def x_norm(i, at):
        enc_s[at, :] = rms_gain(x_s[i].astype(f32), gain_ref[0:1, :]).astype(bf16)

    row_blocks(blocks, x_norm)
    turn(enc_s)
    scatter.tick(7)

    def pair_grads(pairs):
        def body(pair, carry):
            attend_pair_bwd(
                pair, len_ref[0], table_ref, q_s, k_s, v_s, gatt, gq, gk, gv, dt_o
            )
            return carry

        lax.fori_loop(pairs[0], pairs[1], body, 0)

    def heads_to_slot(m, n):
        for t, right in enumerate((gq, gk, gv)):
            value = matmul(turned[...], right[:, m * 256 : (m + 1) * 256]).astype(bf16)
            value = value.reshape(z_count, 4, ROWS, 256)
            slots[n, :, :, :, t * 128 : (t + 1) * 128] = value[..., :128]
            slots[n, :, :, :, HALF + t * 128 : HALF + (t + 1) * 128] = value[..., 128:]

    pair_grads((0, 1))
    scatter.tick(8)
    pair_grads((1, 2))
    heads_to_slot(0, 1)
    scatter.tick(9)
    pair_grads((2, 3))
    scatter.tick(10)
    pair_grads((3, 4))
    heads_to_slot(1, 2)
    scatter.tick(11)
    pair_grads((4, 5))
    scatter.tick(12)
    pair_grads((5, 6))
    heads_to_slot(2, 0)
    scatter.tick(13)
    back(gq, 11, acc, False)
    back(gk, 12, acc, True)
    scatter.tick(14)
    back(gv, 13, acc, True)

    def pull_x(i, at):
        grad, gain = pull_rows(x_s[i].astype(f32), gain_ref[0:1, :], acc[at, :])
        gx[i] = (gh[at, :] + grad).astype(bf16)
        gg_o[0:1, :] += gain

    row_blocks(blocks, pull_x)
    x_copies = []
    for d in range(1, 4):
        peer = (s + d) % 4
        copy = remote(
            gx.at[peer], gx_r.at[s], x_send.at[d - 1], x_recv.at[d - 1], (z, peer, c)
        )
        copy.start()
        x_copies.append(copy)
    scatter.tick(15)
    dec_grads()
    scatter.tick(16)
    gx_r[s] = gx[s]
    scatter.tick(17)
    scatter.tick(18)
    for copy in x_copies:
        copy.wait()

    def widen(i, at):
        gh[at, :] = gx_r[i].astype(f32)

    row_blocks(blocks, widen)
    copy = pltpu.make_async_copy(gh, x_o, o_sem.at[0])
    copy.start()
    scatter.finish()
    plane.finish()
    copy.wait()


def backward(length, table, gain, weights, win, wout, acts, small, z_count):
    x = acts[0]
    blocks, band, width = x.shape
    span = blocks * band
    heads = table.shape[0]
    vmem = pl.BlockSpec(memory_space=pltpu.VMEM)
    hbm = pl.BlockSpec(memory_space=pltpu.HBM)
    n = 14
    token = ((span, width), bf16)
    token_f = ((span, width), f32)
    scratch = [((3, z_count, 4, ROWS, width), bf16), ((1, z_count, 4, 4 * ROWS, width), bf16)]
    scratch += [((n, z_count, 4, ROWS, HALF), bf16), ((n, 2, z_count, ROWS, HALF), bf16)]
    scratch += [((n, z_count, ROWS, HALF), bf16), ((n, z_count - 1, ROWS, HALF), bf16)]
    scratch += [((n, ROWS, HALF), f32), ((n, ROWS, HALF), f32)]
    scratch += [((4, width, width), bf16), (x.shape, bf16)] + [token] * 7 + [token_f] * 2
    scratch += [((2, span, width), f32), token_f, token, token_f, token, token]
    scratch += [((width, span), bf16)] + [token] * 4 + [(x.shape, bf16)] * 2
    scratch += [((len(DEC), z_count, ROWS, HALF), bf16), ((4, 2, 8, width), f32)]
    scratch += [((3, 4, 2, z_count, 8, 128), f32), ((z_count, 64, 128), bf16)]
    scratch += [((z_count, 64, 128), bf16), ((z_count, 80, width), bf16), ((2, 8, width), f32)]
    dma = pltpu.SemaphoreType.DMA
    return pl.pallas_call(
        functools.partial(backward_kernel, z_count),
        out_shape=[
            jax.ShapeDtypeStruct((6, ROWS // 2, width), f32),
            jax.ShapeDtypeStruct((ROWS // 2, 4 * width), f32),
            jax.ShapeDtypeStruct((2 * ROWS, width), f32),
            jax.ShapeDtypeStruct((span, width), f32),
            jax.ShapeDtypeStruct(table.shape, f32),
            jax.ShapeDtypeStruct((8, width), f32),
            jax.ShapeDtypeStruct((4, ROWS // 2, width), f32),
            jax.ShapeDtypeStruct((ROWS // 2, 4 * width), f32),
            jax.ShapeDtypeStruct((2 * ROWS, width), f32),
        ],
        in_specs=[pl.BlockSpec(memory_space=pltpu.SMEM), vmem, vmem] + [hbm] * 20 + [vmem] * 2,
        out_specs=[vmem] * 3 + [hbm] + [vmem] * 5,
        scratch_shapes=[pltpu.VMEM(*o) for o in scratch]
        + [dma((n, 8)), dma((n, 8)), dma((n,)), dma((4,)), dma((11,)), dma((3,)), dma((3,))]
        + [dma((1,)), dma((4, 7)), dma((4, 7)), dma((6,)), dma((6,))],
        compiler_params=pltpu.CompilerParams(
            collective_id=1, has_side_effects=True, vmem_limit_bytes=62 * MIB
        ),
        name="backward",
    )(length, table, gain, *weights, win, wout, *acts, *small)


def total_kernel(z_count, in_ref, out_ref, acc, got, send, recv):
    z, s, c = place()[:3]
    greet(z, s, c, z_count)
    started = []
    slot = 0

    def exchange(peers):
        nonlocal slot
        base = slot
        for peer in peers:
            copy = remote(acc, got.at[slot], send.at[slot], recv.at[slot], peer)
            copy.start()
            started.append(copy)
            slot += 1
        for copy in started[base:]:
            copy.wait()
        total = acc[...]
        for k in range(base, slot):
            total = total + got[k]
        acc[...] = total

    acc[...] = in_ref[...]
    exchange([(z, s, 1 - c)])
    exchange([(z, (s + d) % 4, c) for d in range(1, 4)])
    exchange([((z + d) % z_count, s, c) for d in range(1, z_count)])
    out_ref[...] = acc[...]


def total_all(x, z_count):
    vmem = pl.BlockSpec(memory_space=pltpu.VMEM)
    slots = z_count + 3
    return pl.pallas_call(
        functools.partial(total_kernel, z_count),
        out_shape=jax.ShapeDtypeStruct(x.shape, f32),
        in_specs=[vmem],
        out_specs=vmem,
        scratch_shapes=[
            pltpu.VMEM(x.shape, f32),
            pltpu.VMEM((slots,) + x.shape, f32),
            pltpu.SemaphoreType.DMA((slots,)),
            pltpu.SemaphoreType.DMA((slots,)),
        ],
        compiler_params=pltpu.CompilerParams(collective_id=2, has_side_effects=True),
        name="total_all",
    )(x)


def on_device(
    inputs,
    dec_in,
    cotangent,
    lengths,
    bucket_table,
    square,
    square_m,
    square_v,
    ffn_in,
    ffn_in_m,
    ffn_in_v,
    ffn_out,
    ffn_out_m,
    ffn_out_v,
    gains,
    gains_m,
    gains_v,
    rel_bias,
    rel_bias_m,
    rel_bias_v,
):
    z_count = lax.axis_size("dp")
    width = inputs.shape[2]
    direct = lax.axis_size("seq") == 4 and width == 2 * HALF and width == 4 * z_count * ROWS
    direct = direct and inputs.shape[:2] == (4, BAND)
    w = {}
    seq_pos = lax.axis_index("seq")
    local_len = inputs.shape[1]
    span = local_len * lax.axis_size("seq")
    bucket_count = rel_bias.shape[0]
    scale = 1.0 / math.sqrt(HD)
    length = lax.dynamic_slice_in_dim(lengths, seq_pos, 1, 0)
    key_valid = jnp.arange(span)[None, :] < length[:, None]
    one_hot = (
        jnp.pad(bucket_table, (0, 1), constant_values=-1)[:, None]
        == jnp.arange(bucket_count)[None, :]
    ).astype(f32)
    table = jnp.einsum("ob,bh->ho", one_hot, rel_bias, precision=highest_precision)[:, None, :]

    me = (
        lax.axis_index("dp") * lax.axis_size("seq") + seq_pos
    ) * lax.axis_size("head") + lax.axis_index("head")
    if direct:
        gains_t = jnp.pad(gains.T, ((0, 0), (0, 128 - gains.shape[0])))
        rows = jnp.concatenate((dec_in.reshape(1, width), cotangent.reshape(1, width)))
        rows = jnp.pad(rows.astype(f32), ((0, 6), (0, 0)))
        outs = forward(
            length, table, square, ffn_in, ffn_out, gains_t, rows, inputs, z_count
        )
        weights = [o.reshape(width, width) for o in outs[14:20]]
        gain_f, state, g_high, dec_out = outs[20:]
        dec_out = dec_out[:1]
        s_sq, s_in, s_out, input_grad, g_table, g_gains, d_sq, d_in, d_out = backward(
            length,
            table,
            gain_f,
            weights,
            outs[0].reshape(width, -1),
            outs[1].reshape(-1, width),
            outs[2:14],
            (state, g_high),
            z_count,
        )
        input_grad = input_grad.reshape(inputs.shape)
        g_bias_here = jnp.einsum(
            "ob,ho->bh", one_hot, g_table[:, 0, :], precision=highest_precision
        )
        g_gains = g_gains[: gains.shape[0]]
        s_0123, s_78 = s_sq[:4], s_sq[4:]
        dec_grads = [d_sq[0], d_sq[1], d_sq[2], d_sq[3], d_in, d_out]
    else:

        def gather_rows(x):
            return lax.all_gather(x.astype(bf16), AXES, axis=x.ndim - 2, tiled=True)

        sq_a = gather_rows(square[:4])
        w_in_e = gather_rows(ffn_in[0])
        w_out_e = gather_rows(ffn_out[0])
        sq_b = gather_rows(square[4:])
        w_in_d = gather_rows(ffn_in[1])
        w_out_d = gather_rows(ffn_out[1])
        gain_f = lax.all_gather(gains.astype(bf16), AXES, axis=1, tiled=True).astype(f32)
        for i in range(square.shape[0]):
            w[i] = sq_a[i] if i < 4 else sq_b[i - 4]
        x_b = lax.all_to_all(inputs, "seq", split_axis=0, concat_axis=1, tiled=True)[0]
        x_f = x_b.astype(f32)
        normed = rms_gain(x_f, gain_f[0]).astype(bf16)
        q = matmul(normed, w[0]).astype(bf16)
        k = matmul(normed, w[1]).astype(bf16)
        v = matmul(normed, w[2]).astype(bf16)
        attended = attend_fwd(length, table, q, k, v)
        hidden = x_f + matmul(attended, w[3])
        normed_two = rms_gain(hidden, gain_f[1]).astype(bf16)
        pre_act = matmul(normed_two, w_in_e)
        inner_act = gelu_tanh(pre_act).astype(bf16)
        hidden_two = hidden + matmul(inner_act, w_out_e)
        encoded = rms_gain(hidden_two, gain_f[2]).astype(bf16)
        cross_k = matmul(encoded, w[7]).astype(bf16)
        cross_v = matmul(encoded, w[8]).astype(bf16)

        dec_row = dec_in.reshape(1, width).astype(f32)
        self_norm = rms_gain(dec_row, gain_f[3]).astype(bf16)
        self_values = matmul(self_norm, w[4]).astype(bf16)
        dec_one = dec_row + matmul(self_values, w[5])
        cross_norm = rms_gain(dec_one, gain_f[4]).astype(bf16)
        cross_q = matmul(cross_norm, w[6]).astype(bf16)
        head_of = (jnp.arange(width)[None, :] // HD == jnp.arange(H)[:, None]).astype(bf16)
        q_heads = head_of * cross_q
        cross_scores = jnp.where(key_valid, mm_t(q_heads, cross_k) * scale, neg_fill)
        cross_probs = jax.nn.softmax(cross_scores, axis=-1)
        cross_probs_b = cross_probs.astype(bf16)
        cross_att = jnp.sum(
            matmul(cross_probs_b, cross_v) * head_of.astype(f32), axis=0, keepdims=True
        ).astype(bf16)
        dec_two = dec_one + matmul(cross_att, w[9])
        ffn_norm = rms_gain(dec_two, gain_f[5]).astype(bf16)
        pre_dec = matmul(ffn_norm, w_in_d)
        inner_dec = gelu_tanh(pre_dec).astype(bf16)
        dec_out = dec_two + matmul(inner_dec, w_out_d)

        g_top_b = cotangent.reshape(1, width)
        g_top = g_top_b.astype(f32)
        g_pre_dec = gelu_pull(pre_dec, mm_t(g_top_b, w_out_d)).astype(bf16)
        g_two_norm, g_gain_five = rms_pull(dec_two, gain_f[5], mm_t(g_pre_dec, w_in_d))
        g_two = g_top + g_two_norm
        g_two_b = g_two.astype(bf16)
        g_att = mm_t(g_two_b, w[9]).astype(bf16)
        g_att_heads = head_of * g_att
        g_probs = mm_t(g_att_heads, cross_v)
        g_cross_v = mm_outer(cross_probs_b, g_att_heads).astype(bf16)
        g_scores = cross_probs * (g_probs - jnp.sum(g_probs * cross_probs, axis=-1, keepdims=True))
        g_scores_b = g_scores.astype(bf16)
        g_cross_q = (
            jnp.sum(matmul(g_scores_b, cross_k) * head_of.astype(f32), axis=0, keepdims=True) * scale
        ).astype(bf16)
        g_cross_k = (mm_outer(g_scores_b, q_heads) * scale).astype(bf16)
        g_one_norm, g_gain_four = rms_pull(dec_one, gain_f[4], mm_t(g_cross_q, w[6]))
        g_one_b = (g_two + g_one_norm).astype(bf16)
        g_self_values = mm_t(g_one_b, w[5]).astype(bf16)
        g_gain_three = rms_pull(dec_row, gain_f[3], mm_t(g_self_values, w[4]))[1]

        lefts = (self_norm, self_values, cross_norm, cross_att, ffn_norm, inner_dec)
        rights = (g_self_values, g_one_b, g_cross_q, g_two_b, g_pre_dec, g_top_b)
        packed = lax.all_gather(jnp.concatenate(lefts + rights, axis=1), AXES, axis=0, tiled=True)
        devices = packed.shape[0]
        cuts = [0]
        for piece in lefts + rights:
            cuts.append(cuts[-1] + piece.shape[1])
        dec_grads = []
        for n in range(6):
            share = lefts[n].shape[1] // devices
            left = lax.dynamic_slice_in_dim(packed, cuts[n] + me * share, share, 1)
            right = packed[:, cuts[6 + n] : cuts[7 + n]]
            dec_grads.append(mm_outer(left, right))
        g_w7 = mm_outer(encoded, g_cross_k)
        g_w8 = mm_outer(encoded, g_cross_v)
        g_encoded = mm_t(g_cross_k, w[7]) + mm_t(g_cross_v, w[8])
        g_hidden_two, g_gain_two = rms_pull(hidden_two, gain_f[2], g_encoded)
        g_hidden_two_b = g_hidden_two.astype(bf16)
        g_out_e = mm_outer(inner_act, g_hidden_two_b)
        g_pre = gelu_pull(pre_act, mm_t(g_hidden_two_b, w_out_e)).astype(bf16)
        g_in_e = mm_outer(normed_two, g_pre)
        g_hidden_norm, g_gain_one = rms_pull(hidden, gain_f[1], mm_t(g_pre, w_in_e))
        g_hidden = g_hidden_two + g_hidden_norm
        g_hidden_b = g_hidden.astype(bf16)
        g_w3 = mm_outer(attended, g_hidden_b)
        g_attended = mm_t(g_hidden_b, w[3]).astype(bf16)
        gq, gk, gv, g_table = attend_bwd(length, table, q, k, v, g_attended)
        g_bias_here = jnp.einsum("ob,ho->bh", one_hot, g_table[:, 0, :], precision=highest_precision)
        g_w0 = mm_outer(normed, gq)
        g_w1 = mm_outer(normed, gk)
        g_w2 = mm_outer(normed, gv)
        g_normed = mm_t(gq, w[0]) + mm_t(gk, w[1]) + mm_t(gv, w[2])
        g_input_norm, g_gain_zero = rms_pull(x_f, gain_f[0], g_normed)
        g_x = (g_hidden + g_input_norm).astype(bf16)
        input_grad = lax.all_to_all(
            g_x[None], "seq", split_axis=1, concat_axis=0, tiled=True
        ).astype(f32)

        def scatter_rows(x):
            return lax.psum_scatter(
                x.astype(bf16), AXES, scatter_dimension=x.ndim - 2, tiled=True
            ).astype(f32)

        s_78 = scatter_rows(jnp.stack((g_w7, g_w8)))
        s_out = scatter_rows(g_out_e)
        s_in = scatter_rows(g_in_e)
        s_0123 = scatter_rows(jnp.stack((g_w0, g_w1, g_w2, g_w3)))
        g_gains = jnp.stack(
            (g_gain_zero, g_gain_one, g_gain_two, g_gain_three, g_gain_four, g_gain_five)
        )
    summed_sq = jnp.stack(
        (
            s_0123[0],
            s_0123[1],
            s_0123[2],
            s_0123[3],
            dec_grads[0],
            dec_grads[1],
            dec_grads[2],
            s_78[0],
            s_78[1],
            dec_grads[3],
        )
    )
    summed_in = jnp.stack((s_in, dec_grads[4]))
    summed_out = jnp.stack((s_out, dec_grads[5]))
    gain_share = gains.shape[1]
    local_squares = (
        jnp.sum(summed_sq * summed_sq)
        + jnp.sum(summed_in * summed_in)
        + jnp.sum(summed_out * summed_out)
    )
    if direct:
        rest = jnp.concatenate((g_bias_here.reshape(-1), local_squares[None]))
        rest = jnp.pad(rest, (0, 1024 - rest.shape[0])).reshape(8, 128)
        wide = jnp.concatenate((jnp.pad(g_gains, ((0, 2), (0, 0))), rest), axis=1)
        wide = total_all(wide, z_count)
        g_gains = wide[:6, :width]
        rest = wide[:, width:].reshape(-1)
        g_bias = rest[: g_bias_here.size].reshape(g_bias_here.shape)
        shard_squares = rest[g_bias_here.size]
    else:
        g_gains, g_bias, shard_squares = lax.psum((g_gains, g_bias_here, local_squares), AXES)
    summed_gain = lax.dynamic_slice_in_dim(g_gains, me * gain_share, gain_share, 1)
    grad_norm = jnp.sqrt(shard_squares + jnp.sum(g_gains * g_gains) + jnp.sum(g_bias * g_bias))
    factor = clip_bound / jnp.maximum(grad_norm, clip_bound)
    return (
        dec_out.astype(bf16).reshape(dec_in.shape),
        input_grad,
        grad_norm,
        *adam_step(square, square_m, square_v, summed_sq, factor, rate_matrix, decay_rate),
        *adam_step(ffn_in, ffn_in_m, ffn_in_v, summed_in, factor, rate_matrix, decay_rate),
        *adam_step(ffn_out, ffn_out_m, ffn_out_v, summed_out, factor, rate_matrix, decay_rate),
        *adam_step(gains, gains_m, gains_v, summed_gain, factor, rate_small, 0.0),
        *adam_step(rel_bias, rel_bias_m, rel_bias_v, g_bias, factor, rate_small, 0.0),
    )


def solution(mesh):
    rows = P(("dp", "head"), "seq", None)
    shard = P(None, AXES, None)
    small = P(None, AXES)
    return jax.shard_map(
        on_device,
        mesh=mesh,
        in_specs=(rows, rows, rows, P(("dp", "head")), P())
        + (shard,) * 9
        + (small,) * 3
        + (P(),) * 3,
        out_specs=(rows, rows, P()) + (shard,) * 9 + (small,) * 3 + (P(),) * 3,
        check_vma=False,
    )
```

```python
import functools
import math

import jax
import jax.numpy as jnp
from jax import lax
from jax.experimental import pallas as pl
from jax.experimental.pallas import tpu as pltpu
from jax.sharding import PartitionSpec as P

H = 12
HD = 64
STEP = 5
AXES = ("dp", "seq", "head")

norm_eps = 1e-06
neg_fill = -1e30
beta_one = 0.9
beta_two = 0.999
adam_eps = 1e-08
decay_rate = 0.01
rate_matrix = 0.05
rate_small = 0.5
clip_bound = 1.0
highest_precision = lax.Precision.HIGHEST
bf16 = jnp.bfloat16
f32 = jnp.float32
BAND = 128


def rms_gain(values_in, gain_row):
    return (
        values_in
        * lax.rsqrt(jnp.mean(values_in * values_in, axis=-1, keepdims=True) + norm_eps)
        * gain_row
    )


def gelu_tanh(values_in):
    return jax.nn.gelu(values_in, approximate=True)


def matmul(left, right):
    return jnp.dot(left, right, preferred_element_type=f32)


def mm_t(left, right):
    return lax.dot_general(left, right, (((1,), (1,)), ((), ())), preferred_element_type=f32)


def mm_outer(left, right):
    return lax.dot_general(left, right, (((0,), (0,)), ((), ())), preferred_element_type=f32)


def rms_pull(values_in, gain_row, incoming):
    _, pull = jax.vjp(rms_gain, values_in, gain_row)
    return pull(incoming)


def gelu_pull(values_in, incoming):
    _, pull = jax.vjp(gelu_tanh, values_in)
    return pull(incoming)[0]


def adam_step(weight, first, second, grad, factor, rate, decay):
    grad = grad * factor
    first = beta_one * first + (1.0 - beta_one) * grad
    second = beta_two * second + (1.0 - beta_two) * grad * grad
    first_hat = first / (1.0 - beta_one**STEP)
    second_hat = second / (1.0 - beta_two**STEP)
    weight = weight - rate * (first_hat / (jnp.sqrt(second_hat) + adam_eps) + decay * weight)
    return (weight, first, second)


def bias_band(table_row, span):
    wide = jnp.broadcast_to(table_row, (BAND, 2 * span))
    shift = (2 * span - (BAND - 1)) % (2 * span)
    return pltpu.roll(wide, shift, 1, stride=1, stride_axis=0)


def band_sums(band, span):
    wide = 2 * span
    rows = BAND
    while rows > 8:
        rows //= 2
        band = band[:rows] + pltpu.roll(band[rows:], wide - rows, 1)
    row = lax.broadcasted_iota(jnp.int32, band.shape, 0)
    for step in (4, 2, 1):
        band = jnp.where((row // step) % 2 == 1, pltpu.roll(band, wide - step, 1), band)
    return pltpu.roll(jnp.sum(band, axis=0, keepdims=True), BAND - 1, 1)


def softmax_rows(q_rows, k_all, band, block, span, valid):
    start = span - BAND * (block + 1)
    scores = mm_t(q_rows, k_all) * (1.0 / math.sqrt(HD)) + band[:, start : start + span]
    scores = jnp.where(valid, scores, neg_fill)
    peak = jnp.max(scores, axis=-1, keepdims=True)
    raised = jnp.exp(scores - peak)
    return raised / jnp.sum(raised, axis=-1, keepdims=True)


def attend_fwd_kernel(len_ref, table_ref, q_ref, k_ref, v_ref, o_ref):
    span = k_ref.shape[0]
    valid = lax.broadcasted_iota(jnp.int32, (1, span), 1) < len_ref[0]
    lane = lax.broadcasted_iota(jnp.int32, (1, 2 * HD), 1)
    k_all = k_ref[...]
    v_all = v_ref[...]
    bands = [bias_band(table_ref[t], span) for t in range(2)]
    for block in range(span // BAND):
        rows = slice(block * BAND, (block + 1) * BAND)
        q_rows = q_ref[rows, :]
        parts = []
        for t in range(2):
            own = (lane // HD) == t
            probs = softmax_rows(
                jnp.where(own, q_rows, jnp.zeros_like(q_rows)), k_all, bands[t], block, span, valid
            )
            parts.append(matmul(probs.astype(bf16), v_all))
        o_ref[rows, :] = jnp.where(lane < HD, parts[0], parts[1]).astype(bf16)


def attend_bwd_kernel(
    len_ref, table_ref, q_ref, k_ref, v_ref, do_ref, dq_ref, dk_ref, dv_ref, dt_ref
):
    span = k_ref.shape[0]
    scale = 1.0 / math.sqrt(HD)
    valid = lax.broadcasted_iota(jnp.int32, (1, span), 1) < len_ref[0]
    lane = lax.broadcasted_iota(jnp.int32, (1, 2 * HD), 1)
    k_all = k_ref[...]
    v_all = v_ref[...]
    count = span // BAND
    dks, dvs = [], []
    dqs = [[None, None] for _ in range(count)]
    for t in range(2):
        own = (lane // HD) == t
        band = bias_band(table_ref[t], span)
        dk = jnp.zeros((span, 2 * HD), f32)
        dv = jnp.zeros((span, 2 * HD), f32)
        dband = jnp.zeros((BAND, 2 * span), f32)
        for block in range(count):
            rows = slice(block * BAND, (block + 1) * BAND)
            q_rows = q_ref[rows, :]
            do_rows = do_ref[rows, :]
            zero = jnp.zeros_like(q_rows)
            probs = softmax_rows(
                jnp.where(own, q_rows, zero), k_all, band, block, span, valid
            )
            dprobs = mm_t(jnp.where(own, do_rows, zero), v_all)
            dscore = probs * (dprobs - jnp.sum(dprobs * probs, axis=-1, keepdims=True))
            start = span - BAND * (block + 1)
            pieces = []
            if start:
                pieces.append(jnp.zeros((BAND, start), f32))
            pieces.append(dscore)
            if span - start:
                pieces.append(jnp.zeros((BAND, span - start), f32))
            dband = dband + jnp.concatenate(pieces, axis=1)
            dscore_b = dscore.astype(bf16)
            dv = dv + mm_outer(probs.astype(bf16), do_rows)
            dk = dk + mm_outer(dscore_b, q_rows)
            dqs[block][t] = matmul(dscore_b, k_all)
        dks.append(dk)
        dvs.append(dv)
        dt_ref[t] = band_sums(dband, span)
    dk_ref[...] = (jnp.where(lane < HD, dks[0], dks[1]) * scale).astype(bf16)
    dv_ref[...] = jnp.where(lane < HD, dvs[0], dvs[1]).astype(bf16)
    for block in range(count):
        rows = slice(block * BAND, (block + 1) * BAND)
        dq_ref[rows, :] = (jnp.where(lane < HD, dqs[block][0], dqs[block][1]) * scale).astype(bf16)


def head_specs(span, width, n):
    return [pl.BlockSpec((span, 2 * HD), lambda i: (0, i)) for _ in range(n)]


def attend_fwd(length, table, q, k, v):
    span, width = q.shape
    return pl.pallas_call(
        attend_fwd_kernel,
        grid=(width // (2 * HD),),
        out_shape=jax.ShapeDtypeStruct((span, width), bf16),
        in_specs=[
            pl.BlockSpec(memory_space=pltpu.SMEM),
            pl.BlockSpec((2, 1, 2 * span), lambda i: (i, 0, 0)),
            *head_specs(span, width, 3),
        ],
        out_specs=head_specs(span, width, 1)[0],
        compiler_params=pltpu.CompilerParams(vmem_limit_bytes=48 * 1024 * 1024),
        name="attend_fwd",
    )(length, table, q, k, v)


def attend_bwd(length, table, q, k, v, do):
    span, width = q.shape
    like = jax.ShapeDtypeStruct((span, width), bf16)
    return pl.pallas_call(
        attend_bwd_kernel,
        grid=(width // (2 * HD),),
        out_shape=(like, like, like, jax.ShapeDtypeStruct(table.shape, f32)),
        in_specs=[
            pl.BlockSpec(memory_space=pltpu.SMEM),
            pl.BlockSpec((2, 1, 2 * span), lambda i: (i, 0, 0)),
            *head_specs(span, width, 4),
        ],
        out_specs=(
            *head_specs(span, width, 3),
            pl.BlockSpec((2, 1, 2 * span), lambda i: (i, 0, 0)),
        ),
        compiler_params=pltpu.CompilerParams(vmem_limit_bytes=48 * 1024 * 1024),
        name="attend_bwd",
    )(length, table, q, k, v, do)


MESH_ID = pl.DeviceIdType.MESH
HALF = 384
ROWS = 48
MIB = 1024 * 1024


def place():
    z, s, c = lax.axis_index("dp"), lax.axis_index("seq"), lax.axis_index("head")
    near = s + 1 - 2 * (s % 2)
    far = (s + 2) % 4
    first = near + c * (far - near)
    second = far + c * (near - far)
    return z, s, c, first, second, 3 - s


def greet(z, s, c, z_count):
    barrier = pltpu.get_barrier_semaphore()
    for d in range(1, z_count):
        peer = ((z + d) % z_count, s, c)
        pl.semaphore_signal(barrier, 1, device_id=peer, device_id_type=MESH_ID)
    for d in range(1, 4):
        peer = (z, (s + d) % 4, c)
        pl.semaphore_signal(barrier, 1, device_id=peer, device_id_type=MESH_ID)
    pl.semaphore_signal(barrier, 1, device_id=(z, s, 1 - c), device_id_type=MESH_ID)
    pl.semaphore_wait(barrier, z_count + 3)


def remote(src, dst, send, recv, peer):
    return pltpu.make_async_remote_copy(
        src, dst, send, recv, device_id=peer, device_id_type=MESH_ID
    )


def cols(c, base=0):
    return pl.ds(pl.multiple_of(base + c * HALF, 128), HALF)


def unit_view(kind, n, ref, z, s, c):
    if kind == "square":
        return ref.at[n, z, s, :, cols(c)]
    if kind == "cols":
        return ref.at[n // 4, z, s, :, cols(c, (n % 4) * 2 * HALF)]
    if kind == "rows":
        return ref.at[n // 4, z, s, pl.ds((n % 4) * ROWS, ROWS), cols(c)]
    if kind == "line square":
        return ref.at[n, z]
    if kind == "line cols":
        return ref.at[z, :, pl.ds(n * HALF, HALF)]
    if kind == "line rows":
        return ref.at[z, pl.ds(n * ROWS, ROWS)]
    return ref.at[z, s]


class Gather:
    def __init__(self, units, refs, send, recv, z_count):
        self.units, self.refs, self.send, self.recv = units, refs, send, recv
        self.z_count = z_count
        self.where = place()
        self.started = []
        self.base = 2 * (z_count - 1)

    def view(self, u, z, s, c):
        kind, n = self.units[u]
        return unit_view(kind, n, self.refs[kind], z, s, c)

    def go(self, u, slot, ref, peer):
        copy = remote(ref, ref, self.send.at[u, slot], self.recv.at[u, slot], peer)
        copy.start()
        self.started.append(copy)

    def got(self, u, slot, ref):
        z, s, c = self.where[:3]
        remote(ref, ref, self.send.at[u, slot], self.recv.at[u, slot], (z, s, 1 - c)).wait_recv()

    def z_sends(self, u, i):
        z, s, c = self.where[:3]
        top = self.z_count - 1
        for slot, near, block, live in (
            (i, z + 1, z - i, (z >= i) & (z < top)),
            (top + i, z - 1, z + i, (z + i <= top) & (z > 0)),
        ):
            ref = self.view(u, block, s, c)
            copy = remote(
                ref, ref, self.send.at[u, slot], self.recv.at[u, slot], (near, s, c)
            )
            yield copy, live

    def z_send(self, u, i):
        for copy, live in self.z_sends(u, i):

            @pl.when(live)
            def _():
                copy.start()

    def z_got(self, u, i):
        z, s, c = self.where[:3]
        top = self.z_count - 1
        for slot, block, live in (
            (i, z - 1 - i, z - 1 - i >= 0),
            (top + i, z + 1 + i, z + 1 + i <= top),
        ):

            @pl.when(live)
            def _():
                self.got(u, slot, self.view(u, block, s, c))

    def a_start(self, u):
        z, s, c, first, second, both = self.where
        self.go(u, self.base, self.view(u, slice(None), s, c), (z, first, c))

    def a_wait(self, u):
        z, s, c, first, second, both = self.where
        self.got(u, self.base, self.view(u, slice(None), first, c))

    def b_start(self, u):
        z, s, c, first, second, both = self.where
        self.go(u, self.base + 1, self.view(u, slice(None), s, c), (z, second, c))
        self.go(u, self.base + 2, self.view(u, slice(None), first, c), (z, second, c))

    def b_wait(self, u):
        z, s, c, first, second, both = self.where
        self.got(u, self.base + 1, self.view(u, slice(None), second, c))
        self.got(u, self.base + 2, self.view(u, slice(None), both, c))

    def s_start(self, u):
        z, s, c = self.where[:3]
        if self.units[u][0] != "gain":
            self.go(u, self.base + 3, self.view(u, slice(None), slice(None), c), (z, s, 1 - c))

    def s_wait(self, u):
        z, s, c = self.where[:3]
        if self.units[u][0] != "gain":
            self.got(u, self.base + 3, self.view(u, slice(None), slice(None), 1 - c))

    def line(self, u, i):
        if i:
            self.z_got(u, i - 1)
        if i < self.z_count - 1:
            self.z_send(u, i)

    def lag(self, stage):
        return stage if stage < self.z_count else self.z_count - 1 + (0, 2, 4, 5)[stage - self.z_count + 1]

    def tick(self, t, done):
        lines = self.z_count
        for n in range(lines + 3):
            u = t - self.lag(n)
            if not 0 <= u < len(self.units):
                continue
            if n < lines:
                self.line(u, n)
            plain = not self.units[u][0].startswith("line")
            if plain and n == lines - 1:
                self.a_start(u)
            if plain and n == lines:
                self.a_wait(u)
                self.b_start(u)
            if plain and n == lines + 1:
                self.b_wait(u)
                self.s_start(u)
            if plain and n == lines + 2:
                self.s_wait(u)
                done(u)

    def finish(self):
        for copy in self.started:
            copy.wait_send()
        for u in range(len(self.units)):
            for i in range(self.z_count - 1):
                for copy, live in self.z_sends(u, i):

                    @pl.when(live)
                    def _():
                        copy.wait_send()


ENC = (0, 1, 2, 3, 7, 8)
DEC = (4, 5, 6, 9)


def plane_peers(z, s, c):
    peers = []
    for ds in range(4):
        for dc in range(2):
            if ds or dc:
                peers.append(((z, (s + ds) % 4, (c + dc) % 2), ((s + 4 - ds) % 4, (c + dc) % 2)))
    return peers


class Plane:
    def __init__(self, send, recv):
        self.send, self.recv = send, recv
        self.z, self.s, self.c = place()[:3]
        self.peers = plane_peers(self.z, self.s, self.c)
        self.started = []

    def start(self, k, ref):
        for i, (peer, _) in enumerate(self.peers):
            mine = ref.at[self.s, self.c]
            copy = remote(mine, mine, self.send.at[k, i], self.recv.at[k, i], peer)
            copy.start()
            self.started.append(copy)

    def wait(self, k, ref):
        for i, (_, (s, c)) in enumerate(self.peers):
            slot = ref.at[s, c]
            remote(
                slot, slot, self.send.at[k, i], self.recv.at[k, i], (self.z, self.s, 1 - self.c)
            ).wait_recv()

    def finish(self):
        for copy in self.started:
            copy.wait_send()


def rounded(value):
    return value.astype(bf16).astype(f32)


def pick(value, start, size):
    full = value.shape[1]
    return pltpu.roll(value, full - start, 1)[:, :size].astype(bf16)


def halves(ref):
    parts = []
    for c in range(2):
        parts.append(ref[0, c] + ref[1, c] + ref[2, c] + ref[3, c])
    return parts


def blocks_of(ref, size, z_count):
    group = HALF // size
    lanes = ref.shape[-1]
    pieces = []
    for n in range(4 * z_count // group):
        total = None
        for m in range(group):
            z, s = (n * group + m) // 4, (n * group + m) % 4
            piece = ref[s, 0, z] + ref[s, 1, z]
            piece = jnp.concatenate([piece, jnp.zeros((8, HALF - lanes), f32)], axis=1)
            if m:
                piece = pltpu.roll(piece, m * size, 1)
            total = piece if total is None else total + piece
        pieces.append(total)
    return jnp.concatenate(pieces, axis=1)


def half_of(value, c):
    return jnp.where(c == 0, value[:, :HALF], value[:, HALF : 2 * HALF])


def mm_down(value, weight, s, z_count, size):
    total = None
    for z in range(z_count):
        term = matmul(pick(value, (4 * z + s) * size, size), weight(z))
        total = term if total is None else total + term
    return total


def own_row(value, s, c):
    row = lax.broadcasted_iota(jnp.int32, value.shape, 0)
    return jnp.sum(jnp.where(row == 2 * s + c, value, 0.0), axis=0, keepdims=True)


def as_own_row(value, s, c):
    wide = jnp.broadcast_to(value, (8, value.shape[1]))
    row = lax.broadcasted_iota(jnp.int32, wide.shape, 0)
    return jnp.where(row == 2 * s + c, wide, 0.0)


def pull_own(values_in, gain_row, incoming, s, c):
    inverse = lax.rsqrt(jnp.mean(values_in * values_in, axis=-1, keepdims=True) + norm_eps)
    scaled = incoming * gain_row
    inner = jnp.mean(scaled * values_in, axis=-1, keepdims=True)
    grad = inverse * scaled - values_in * (inverse * inverse * inverse * inner)
    return grad, own_row(incoming * values_in * inverse, s, c)


def put_blocks(ref, s, c, terms, size):
    for z, term in enumerate(terms):
        ref[s, c, z] = jnp.zeros(ref.shape[3:], f32)
        ref[s, c, z, :, :size] = term


def head_rows(width):
    lane = lax.broadcasted_iota(jnp.int32, (16, width), 1)
    row = lax.broadcasted_iota(jnp.int32, (16, width), 0)
    return (lane // HD) == row


def ffn_halves(parts):
    pieces = []
    for j in range(4):
        for c in range(2):
            pieces.append(parts[c][:, j * HALF : (j + 1) * HALF])
    return jnp.concatenate(pieces, axis=1)


class Decoder:
    (ROWS_IN, SELF_NORM, SELF_VALUES, ONE, CROSS_NORM, CROSS_ATT, FFN_NORM, TWO, TOP, QUERY) = range(10)
    INNER, PRE = 10, 14
    COUNT = 18

    def __init__(self, plane, st, gains, z_count):
        self.plane, self.st, self.gains, self.z_count = plane, st, gains, z_count
        self.s, self.c = plane.s, plane.c

    def gain(self, n):
        return self.gains[n : n + 1, :]

    def square_down(self, k, ref, value, wd, n):
        ref[self.s, self.c] = mm_down(value, lambda z: wd[n, z], self.s, self.z_count, ROWS)
        self.plane.start(k, ref)

    def square_sum(self, k, ref):
        self.plane.wait(k, ref)
        return jnp.concatenate(halves(ref), axis=1)

    def square_up(self, k, ref, value, wd, n):
        own = half_of(value, self.c).astype(bf16)
        put_blocks(
            ref, self.s, self.c, [mm_t(own, wd[n, z]) for z in range(self.z_count)], ROWS
        )
        self.plane.start(k, ref)

    def square_up_sum(self, k, ref):
        self.plane.wait(k, ref)
        return blocks_of(ref, ROWS, self.z_count)


def row_blocks(count, work):
    def body(i, carry):
        work(i, pl.ds(pl.multiple_of(i * BAND, BAND), BAND))
        return carry

    lax.fori_loop(0, count, body, 0)


def col_tiles(width, tile, work):
    def body(i, carry):
        work(pl.ds(pl.multiple_of(i * tile, tile), tile))
        return carry

    lax.fori_loop(0, width // tile, body, 0)


def wide(value):
    return value.reshape(value.shape[0] * value.shape[1] * value.shape[2], value.shape[3])


def softmax_keys(k_own, q_rows, band, block, span, live):
    scores = mm_t(k_own, q_rows) * (1.0 / math.sqrt(HD))
    count = span // BAND
    bias = [
        band[:, (block - n + count - 1) * BAND : (block - n + count) * BAND] for n in range(count)
    ]
    scores = jnp.where(live, scores + jnp.concatenate(bias, axis=0), neg_fill)
    raised = jnp.exp(scores - jnp.max(scores, axis=0, keepdims=True))
    return raised * (1.0 / jnp.sum(raised, axis=0, keepdims=True))


def own_lanes(value, t):
    lane = lax.broadcasted_iota(jnp.int32, value.shape, 1)
    return jnp.where((lane // HD) == t, value, jnp.zeros_like(value))


def attend_pair_fwd(pair, length, table_ref, q_ref, k_ref, v_ref, o_ref):
    span = k_ref.shape[0]
    at = pl.ds(pl.multiple_of(pair * 2 * HD, 2 * HD), 2 * HD)
    live = lax.broadcasted_iota(jnp.int32, (span, BAND), 0) < length
    k_all = k_ref[:, at]
    v_turned = v_ref[:, at].T
    keys = [own_lanes(k_all, t) for t in range(2)]
    bands = [bias_band(table_ref[2 * pair + t], span) for t in range(2)]
    row = lax.broadcasted_iota(jnp.int32, (2 * HD, BAND), 0)
    for block in range(span // BAND):
        rows = slice(block * BAND, (block + 1) * BAND)
        q_rows = q_ref[rows, at]
        parts = []
        for t in range(2):
            probs = softmax_keys(keys[t], q_rows, bands[t], block, span, live)
            parts.append(matmul(v_turned, probs.astype(bf16)))
        o_ref[rows, at] = jnp.where(row < HD, parts[0], parts[1]).T.astype(bf16)


def attend_pair_bwd(
    pair, length, table_ref, q_ref, k_ref, v_ref, do_ref, dq_ref, dk_ref, dv_ref, dt_ref, sums
):
    span = k_ref.shape[0]
    count = span // BAND
    scale = 1.0 / math.sqrt(HD)
    at = pl.ds(pl.multiple_of(pair * 2 * HD, 2 * HD), 2 * HD)
    live = lax.broadcasted_iota(jnp.int32, (span, BAND), 0) < length
    lane = lax.broadcasted_iota(jnp.int32, (1, 2 * HD), 1)
    row = lax.broadcasted_iota(jnp.int32, (2 * HD, BAND), 0)
    k_all = k_ref[:, at]
    k_turned = k_all.T
    v_all = v_ref[:, at]
    dks, dvs = [], []
    dqs = [[None, None] for _ in range(count)]
    for t in range(2):
        k_own = own_lanes(k_all, t)
        v_own = own_lanes(v_all, t)
        band = bias_band(table_ref[2 * pair + t], span)
        dk = jnp.zeros((span, 2 * HD), f32)
        dv = jnp.zeros((span, 2 * HD), f32)
        sums[...] = jnp.zeros_like(sums)
        for block in range(count):
            rows = slice(block * BAND, (block + 1) * BAND)
            q_rows = q_ref[rows, at]
            do_rows = do_ref[rows, at]
            probs = softmax_keys(k_own, q_rows, band, block, span, live)
            dprobs = mm_t(v_own, do_rows)
            dscore = probs * (dprobs - jnp.sum(dprobs * probs, axis=0, keepdims=True))
            for n in range(count):
                start = (block - n + count - 1) * BAND
                sums[:, start : start + BAND] += dscore[n * BAND : (n + 1) * BAND]
            dscore_b = dscore.astype(bf16)
            dv = dv + matmul(probs.astype(bf16), do_rows)
            dk = dk + matmul(dscore_b, q_rows)
            dqs[block][t] = matmul(k_turned, dscore_b)
        dks.append(dk)
        dvs.append(dv)
        dt_ref[2 * pair + t] = band_sums(sums[...], span)
    dk_ref[:, at] = (jnp.where(lane < HD, dks[0], dks[1]) * scale).astype(bf16)
    dv_ref[:, at] = jnp.where(lane < HD, dvs[0], dvs[1]).astype(bf16)
    for block in range(count):
        rows = slice(block * BAND, (block + 1) * BAND)
        value = jnp.where(row < HD, dqs[block][0], dqs[block][1]).T
        dq_ref[rows, at] = (value * scale).astype(bf16)


def forward_kernel(units, lines, z_count, *refs):
    (
        len_ref, bias_ref, bucket_ref, sq_ref, in_ref, out_ref, gains_ref, dec_ref, cot_ref, x_ref,
        in_o, out_o, x_o, q_o, k_o, v_o, att_o, hid_o, pre_o, hid2_o, enc_o, gck_o, gcv_o, wd_o,
        sq_o0, sq_o1, sq_o2, sq_o3, sq_o4, sq_o5, gain_o, st_o, gg_o, dec_o, table_ref,
        sq_w, in_w, out_w, gain_w, sq_r, in_r, out_r, gain_r,
        x_s, n_s, q_s, k_s, v_s, att_s, hid_s, pre_s, inner_s, hid2_s, enc_s, ck_s, cv_s, gains,
        gain_ref, wd, wdi, wdo, st, e_rows, e_sq, e_att, e_pre, e_out, e_inner, e_up,
        send, recv, first_send, first_recv, x_send, x_recv, d_send, d_recv, p_send, p_recv, local,
    ) = refs
    z, s, c = place()[:3]
    sibling = (z, s, 1 - c)
    sq_o = (sq_o0, sq_o1, sq_o2, sq_o3, sq_o4, sq_o5)
    n_sq, n_ff = sq_ref.shape[0], in_ref.shape[0]
    blocks = x_s.shape[0] * x_s.shape[1] // BAND
    greet_plane(z, s, c, z_count)
    plane = Plane(p_send, p_recv)
    dec = Decoder(plane, st, gains, z_count)
    length = len_ref[s]
    for n, ref in enumerate((dec_ref, cot_ref)):
        e_rows[s, c, n] = as_own_row(ref[0].astype(f32), s, c)
    row = lax.broadcasted_iota(jnp.int32, (gains_ref.shape[0], 128), 0)
    lane = lax.broadcasted_iota(jnp.int32, (gains_ref.shape[0], 128), 1)
    gain_ref[...] = lax.dot_general(
        gains_ref[...],
        jnp.where(row == lane, 1.0, 0.0),
        (((0,), (0,)), ((), ())),
        precision=highest_precision,
        preferred_element_type=f32,
    )
    plane.start(0, e_rows)

    first = []

    def to_sibling(src, dst):
        copy = remote(src, dst, first_send.at[len(first)], first_recv.at[len(first)], sibling)
        copy.start()
        first.append(copy)

    to_sibling(gain_ref, gain_r)
    to_sibling(sq_ref.at[:, :, cols(1 - c)], sq_r)
    x_copies = []
    for d in range(1, 4):
        peer = (s + d) % 4
        copy = remote(
            x_ref.at[peer], x_s.at[s], x_send.at[d - 1], x_recv.at[d - 1], (z, peer, c)
        )
        copy.start()
        x_copies.append(copy)
    mine = pltpu.make_async_copy(x_ref.at[s], x_s.at[s], local.at[0])
    mine.start()
    for n in range(n_ff):
        for j in range(4):
            to_sibling(in_ref.at[n, :, cols(1 - c, 2 * HALF * j)], in_r.at[n, j])
        to_sibling(out_ref.at[n, :, cols(1 - c)], out_r.at[n])

    def joined(own, other):
        top = jnp.where(c == 0, own, other)
        bottom = jnp.where(c == 0, other, own)
        return jnp.concatenate([top, bottom], axis=0).astype(bf16)

    gather = Gather(
        units,
        {
            "square": sq_w,
            "cols": in_w,
            "rows": out_w,
            "gain": gain_w,
            "line square": wd,
            "line cols": wdi,
            "line rows": wdo,
        },
        send,
        recv,
        z_count,
    )
    lined = Gather(lines, gather.refs, d_send, d_recv, z_count)
    first[0].wait_recv()
    gain_w[z, s] = joined(gain_ref[...], gain_r[...])
    first[1].wait_recv()
    for i, n in enumerate(ENC):
        sq_w[i, z, s, :, cols(c)] = joined(sq_ref[n, :, cols(c)], sq_r[n])
    drains = []

    def drain(src, dst):
        copy = pltpu.make_async_copy(src, dst, local.at[1 + len(drains)])
        copy.start()
        drains.append(copy)

    def done(u):
        kind, n = units[u]
        if kind == "square":
            drain(sq_w.at[n], sq_o[n])
        elif kind == "cols" and n % 4 == 3:
            drain(in_w.at[n // 4], in_o)
        elif kind == "rows" and n % 4 == 3:
            drain(out_w.at[n // 4], out_o)

    def normed(src, gain_row, dst):
        def work(i, at):
            dst[at, :] = rms_gain(src(i, at), gains[gain_row : gain_row + 1, :]).astype(bf16)

        row_blocks(blocks, work)

    def x_rows(i, at):
        return x_s[i].astype(f32)

    def start_piece():
        hot = bucket_hot(bucket_ref, bias_ref.shape[0])
        table = lax.dot_general(
            bias_ref[...],
            hot,
            (((0,), (0,)), ((), ())),
            precision=highest_precision,
            preferred_element_type=f32,
        )
        for h in range(table_ref.shape[0]):
            table_ref[h] = table[h : h + 1]
        for copy in x_copies:
            copy.wait_recv()
        mine.wait()
        drain(x_s, x_o)
        gains[...] = wide(gain_w[...]).astype(f32).T[:8]
        gain_o[...] = gains[...]
        normed(x_rows, 0, n_s)

    def square_dot(left, n, tile=256):
        def weight(at):
            return wide(sq_w[n, :, :, :, at])

        return lambda at: matmul(left[...], weight(at))

    def project(n, left, dst, out):
        dot = square_dot(left, n)

        def work(at):
            dst[:, at] = dot(at).astype(bf16)

        col_tiles(2 * HALF, 256, work)
        if out is not None:
            drain(dst, out)

    def attention(pairs):
        def body(pair, carry):
            attend_pair_fwd(pair, length, table_ref, q_s, k_s, v_s, att_s)
            return carry

        lax.fori_loop(pairs[0], pairs[1], body, 0)

    def hidden_piece():
        drain(att_s, att_o)
        dot = square_dot(att_s, 3)

        def work(at):
            hid_s[:, at] = dot(at)

        col_tiles(2 * HALF, 256, work)

        def add(i, at):
            total = hid_s[at, :] + x_rows(i, at)
            hid_s[at, :] = total
            n_s[at, :] = rms_gain(total, gains[1:2, :]).astype(bf16)

        row_blocks(blocks, add)
        drain(hid_s, hid_o)

    def ffn_piece(j):
        def work(i, carry):
            at = pl.ds(pl.multiple_of(j * 2 * HALF + i * 256, 256), 256)
            pre = matmul(n_s[...], wide(in_w[0, :, :, :, at]))
            pre_s[:, at] = pre
            inner_s[:, at] = gelu_tanh(pre).astype(bf16)
            return carry

        lax.fori_loop(0, 3, work, 0)

    def hidden_two_piece():
        drain(pre_s, pre_o)

        def work(at):
            hid2_s[:, at] = hid_s[:, at] + matmul(inner_s[...], wide(out_w[0, :, :, :, at]))

        col_tiles(2 * HALF, 256, work)
        normed(lambda i, at: hid2_s[at, :], 2, enc_s)
        drain(hid2_s, hid2_o)
        drain(enc_s, enc_o)

    def dec_start():
        plane.wait(0, e_rows)
        for n, to in ((0, Decoder.ROWS_IN), (1, Decoder.TOP)):
            total = e_rows[0, 0, n]
            for p in range(1, 8):
                total = total + e_rows[p // 2, p % 2, n]
            st[to] = total
        value = rounded(rms_gain(st[Decoder.ROWS_IN], dec.gain(3)))
        st[Decoder.SELF_NORM] = value
        drain(wd, wd_o)
        dec.square_down(1, e_sq.at[0], value, wd, 0)

    def dec_self_values():
        value = rounded(dec.square_sum(1, e_sq.at[0]))
        st[Decoder.SELF_VALUES] = value
        dec.square_down(2, e_sq.at[1], value, wd, 1)

    def dec_self_out():
        value = st[Decoder.ROWS_IN] + dec.square_sum(2, e_sq.at[1])
        st[Decoder.ONE] = value
        value = rounded(rms_gain(value, dec.gain(4)))
        st[Decoder.CROSS_NORM] = value
        dec.square_down(3, e_sq.at[2], value, wd, 2)

    def dec_query():
        st[Decoder.QUERY] = rounded(dec.square_sum(3, e_sq.at[2]))

    def dec_main():
        width = 2 * HALF
        scale = 1.0 / math.sqrt(HD)
        mask = head_rows(width)
        valid = lax.broadcasted_iota(jnp.int32, (1, x_s.shape[0] * BAND), 1) < length
        query = own_row(st[Decoder.QUERY], s, c)
        q_heads = jnp.where(mask, query, 0.0).astype(bf16)
        scores = jnp.where(valid, mm_t(q_heads, ck_s[...]) * scale, neg_fill)
        raised = jnp.exp(scores - jnp.max(scores, axis=-1, keepdims=True))
        probs = raised / jnp.sum(raised, axis=-1, keepdims=True)
        probs_b = probs.astype(bf16)
        att = jnp.where(mask, matmul(probs_b, cv_s[...]), 0.0)
        e_att[s, c] = as_own_row(rounded(jnp.sum(att, axis=0, keepdims=True)), s, c)
        plane.start(4, e_att)
        plane.wait(4, e_att)
        value = e_att[0, 0]
        for p in range(1, 8):
            value = value + e_att[p // 2, p % 2]
        st[Decoder.CROSS_ATT] = value
        dec.square_down(5, e_sq.at[3], value, wd, 3)
        two = st[Decoder.ONE] + dec.square_sum(5, e_sq.at[3])
        value = rounded(rms_gain(two, dec.gain(5)))
        st[Decoder.FFN_NORM] = value
        e_pre[s, c] = mm_down(value, lambda n: wdi[n], s, z_count, ROWS)
        plane.start(6, e_pre)
        own = half_of(st[Decoder.TOP], c).astype(bf16)
        put_blocks(e_inner, s, c, [mm_t(own, wdo[n]) for n in range(z_count)], 4 * ROWS)
        plane.start(7, e_inner)
        plane.wait(6, e_pre)
        inner, slope = gelu_both(ffn_halves(halves(e_pre)))
        inner = rounded(inner)
        e_out[s, c] = mm_down(inner, lambda n: wdo[n], s, z_count, 4 * ROWS)
        plane.start(8, e_out)
        plane.wait(7, e_inner)
        g_pre = rounded(blocks_of(e_inner, 4 * ROWS, z_count) * slope)
        own = jnp.concatenate(
            [
                half_of(g_pre[:, j * width : (j + 1) * width], c) for j in range(4)
            ],
            axis=1,
        ).astype(bf16)
        put_blocks(e_up.at[0], s, c, [mm_t(own, wdi[n]) for n in range(z_count)], ROWS)
        plane.start(9, e_up.at[0])
        for j in range(4):
            st[Decoder.INNER + j] = inner[:, j * width : (j + 1) * width]
            st[Decoder.PRE + j] = g_pre[:, j * width : (j + 1) * width]
        g_norm = dec.square_up_sum(9, e_up.at[0])
        grad, gain = pull_own(two, dec.gain(5), g_norm, s, c)
        gg_o[...] = jnp.zeros_like(gg_o)
        gg_o[5:6, :] = gain
        g_two = st[Decoder.TOP] + grad
        st[Decoder.TWO] = g_two
        dec.square_up(10, e_up.at[1], g_two, wd, 3)
        plane.wait(8, e_out)
        out = two + jnp.concatenate(halves(e_out), axis=1)
        dec_o[...] = jnp.broadcast_to(own_row(out, s, c), dec_o.shape)
        g_att = own_row(rounded(dec.square_up_sum(10, e_up.at[1])), s, c)
        g_heads = jnp.where(mask, g_att, 0.0).astype(bf16)
        g_probs = mm_t(g_heads, cv_s[...])
        g_scores = probs * (g_probs - jnp.sum(g_probs * probs, axis=-1, keepdims=True))
        row = lax.broadcasted_iota(jnp.int32, g_scores.shape, 0)
        g_scores_b = jnp.where(row < H, g_scores, 0.0).astype(bf16)
        g_query = jnp.where(mask, matmul(g_scores_b, ck_s[...]), 0.0)
        g_query = jnp.sum(g_query, axis=0, keepdims=True) * scale
        st[Decoder.QUERY] = as_own_row(rounded(g_query), s, c)
        live_b = jnp.where(row < H, probs_b.astype(f32), 0.0).astype(bf16)
        n_s[...] = (mm_outer(g_scores_b, q_heads) * scale).astype(bf16)
        drain(n_s, gck_o)
        cv_s[...] = mm_outer(live_b, g_heads).astype(bf16)
        drain(cv_s, gcv_o)
        st_o[...] = st[...]

    pieces = {
        ("gain", 0): [start_piece],
        ("square", 0): [lambda: project(0, n_s, q_s, q_o)],
        ("square", 1): [lambda: project(1, n_s, k_s, k_o)],
        ("square", 2): [lambda: project(2, n_s, v_s, v_o), dec_start, lambda: attention((0, 2))],
        ("square", 3): [lambda: attention((2, 4)), dec_self_values],
        ("cols", 0): [lambda: attention((4, 6)), dec_self_out],
        ("cols", 1): [hidden_piece, lambda: ffn_piece(0), dec_query],
        ("cols", 2): [lambda: ffn_piece(1), lambda: ffn_piece(2)],
        ("cols", 3): [lambda: ffn_piece(3)],
        ("rows", 3): [hidden_two_piece],
        ("square", 4): [lambda: project(4, enc_s, ck_s, None)],
        ("square", 5): [lambda: project(5, enc_s, cv_s, None), dec_main],
    }
    k = 2
    there, early = gather.lag(z_count + 2), gather.lag(z_count + 1)
    for t in range(len(units) + there):
        gather.tick(t, done)
        if t >= 2:
            lined.tick(t - 2, done)
        if t == 1:
            for i, n in enumerate(DEC):
                wd[i, z] = joined(sq_ref[n, :, cols(c)], sq_r[n])
            for n in range(n_ff):
                for j in range(4):
                    first[k].wait_recv()
                    k += 1
                    at = cols(c, 2 * HALF * j)
                    value = joined(in_ref[n, :, at], in_r[n, j])
                    if n == 0:
                        in_w[n, z, s, :, at] = value
                    else:
                        wdi[z, :, j * HALF : (j + 1) * HALF] = value
                first[k].wait_recv()
                k += 1
                value = joined(out_ref[n, :, cols(c)], out_r[n])
                if n == 0:
                    out_w[n, z, s, :, cols(c)] = value
                else:
                    wdo[z] = value
        ready = 0 if t == early else t - there
        if ready > 0 or t == early:
            for piece in pieces.get(units[ready], ()):
                piece()
    gather.finish()
    lined.finish()
    plane.finish()
    for copy in first:
        copy.wait_send()
    for copy in x_copies:
        copy.wait_send()
    for copy in drains:
        copy.wait()


def bucket_hot(bucket_ref, count):
    row = lax.broadcasted_iota(jnp.int32, (count, bucket_ref.shape[1]), 0)
    return jnp.where(bucket_ref[...] == row, 1.0, 0.0)


def greet_plane(z, s, c, z_count):
    barrier = pltpu.get_barrier_semaphore()
    for d in range(1, z_count):
        peer = ((z + d) % z_count, s, c)
        pl.semaphore_signal(barrier, 1, device_id=peer, device_id_type=MESH_ID)
    for peer, _ in plane_peers(z, s, c):
        pl.semaphore_signal(barrier, 1, device_id=peer, device_id_type=MESH_ID)
    pl.semaphore_wait(barrier, z_count - 1 + 7)


def forward(
    lengths, rel_bias, buckets, square, ffn_in, ffn_out, gains, dec_in, cotangent, x, z_count
):
    n_sq, n_ff = square.shape[0], ffn_in.shape[0]
    order = [("gain", 0)]
    order += [("square", n) for n in (0, 1, 2)]
    lines = [("line square", n) for n in range(4)]
    lines += [("line cols", n) for n in range(4)] + [("line rows", n) for n in range(4)]
    plain = [("square", 3)] + [("cols", n) for n in range(4)] + [("rows", n) for n in range(4)]
    plain += [("square", n) for n in (4, 5)]
    order = order + plain
    blocks, band, width = x.shape
    span = blocks * band
    hidden_units = 8 * HALF
    sq_s = (len(ENC), z_count, 4, ROWS, width)
    in_s = (1, z_count, 4, ROWS, hidden_units)
    out_s = (1, z_count, 4, 4 * ROWS, width)
    gain_s = (z_count, 4, ROWS, 128)
    wd_s = (len(DEC), z_count, ROWS, HALF)
    firsts = 2 + 5 * n_ff
    slots = 2 * (z_count - 1) + 4
    vmem = pl.BlockSpec(memory_space=pltpu.VMEM)
    hbm = pl.BlockSpec(memory_space=pltpu.HBM)
    token = ((span, width), bf16)
    token_f = ((span, width), f32)
    st_s = ((Decoder.COUNT, 8, width), f32)
    outs = [(in_s[1:], bf16), (out_s[1:], bf16)]
    outs += [(x.shape, bf16), token, token, token, token, token_f]
    outs += [((span, hidden_units), f32), token_f, token, token, token, (wd_s, bf16)]
    outs += [(sq_s[1:], bf16)] * len(ENC)
    small = [((8, width), f32), st_s, ((8, width), f32), ((8, width), f32)]
    small += [((rel_bias.shape[1], 1, 2 * span), f32)]
    scratch = [(sq_s, bf16), (in_s, bf16), (out_s, bf16), (gain_s, bf16)]
    scratch += [((n_sq, ROWS // 2, HALF), f32), ((n_ff, 4, ROWS // 2, HALF), f32)]
    scratch += [((n_ff, 2 * ROWS, HALF), f32), ((ROWS // 2, 128), f32)]
    scratch += [(x.shape, bf16), token, token, token, token, token, token_f]
    scratch += [((span, hidden_units), f32), ((span, hidden_units), bf16), token_f]
    scratch += [token, token, token, ((8, width), f32)]
    scratch += [((gains.shape[1], 128), f32)]
    scratch += [(wd_s, bf16), ((z_count, ROWS, 4 * HALF), bf16), ((z_count, 4 * ROWS, HALF), bf16)]
    scratch += [st_s, ((4, 2, 2, 8, width), f32), ((4, 4, 2, 8, HALF), f32)]
    scratch += [((4, 2, 8, width), f32), ((4, 2, 8, 4 * HALF), f32), ((4, 2, 8, HALF), f32)]
    scratch += [((4, 2, z_count, 8, 256), f32), ((2, 4, 2, z_count, 8, 128), f32)]
    dma = pltpu.SemaphoreType.DMA
    return pl.pallas_call(
        functools.partial(forward_kernel, order, lines, z_count),
        out_shape=[jax.ShapeDtypeStruct(*o) for o in outs + small],
        in_specs=[pl.BlockSpec(memory_space=pltpu.SMEM)] + [vmem] * 8 + [hbm],
        out_specs=[hbm] * len(outs) + [vmem] * len(small),
        scratch_shapes=[pltpu.VMEM(*o) for o in scratch]
        + [dma((len(order), slots)), dma((len(order), slots)), dma((firsts,)), dma((firsts,))]
        + [dma((3,)), dma((3,)), dma((len(lines), slots)), dma((len(lines), slots))]
        + [dma((11, 7)), dma((11, 7)), dma((40,))],
        compiler_params=pltpu.CompilerParams(
            collective_id=0, has_side_effects=True, vmem_limit_bytes=62 * MIB
        ),
        name="forward",
    )(lengths, rel_bias, buckets, square, ffn_in, ffn_out, gains, dec_in, cotangent, x)


class Scatter:
    def __init__(self, units, sources, bufs, sems, z_count, put):
        self.units, self.sources, self.z_count, self.put = units, sources, z_count, put
        self.r0, self.r1, self.r2, self.r3, self.fin, self.sib = bufs
        self.send, self.recv = sems
        self.where = place()
        self.started = []
        self.lent = {}
        self.at = [0] * 6

    def go(self, u, slot, src, dst, peer):
        copy = remote(src, dst, self.send.at[u, slot], self.recv.at[u, slot], peer)
        copy.start()
        return copy

    def got(self, u, slot, ref):
        z, s, c = self.where[:3]
        remote(ref, ref, self.send.at[u, slot], self.recv.at[u, slot], (z, s, 1 - c)).wait_recv()

    def view(self, u, c, z=slice(None), s=slice(None)):
        kind, n = self.sources[u]
        if kind == "rows":
            return unit_view(kind, n, self.refs[kind], z, s, c)
        return self.refs["slots"].at[n, z, s, :, cols(c)]

    def c_start(self, u):
        z, s, c = self.where[:3]
        self.lent[u] = self.go(u, 0, self.view(u, 1 - c), self.r0.at[u], (z, s, 1 - c))

    def b_start(self, u):
        z, s, c, first, second, both = self.where
        self.got(u, 0, self.r0.at[u])

        def body(i, carry):
            n, m = i // 4, i % 4
            own = self.view(u, c, n, m)[...]
            total = own.astype(f32) + self.r0[u, n, m].astype(f32)
            self.r0[u, n, m] = total.astype(bf16)
            return carry

        lax.fori_loop(0, 4 * self.z_count, body, 0, unroll=4)
        self.started.append(self.go(u, 1, self.r0.at[u, :, second], self.r1.at[u, 0], (z, second, c)))
        self.started.append(self.go(u, 2, self.r0.at[u, :, both], self.r1.at[u, 1], (z, second, c)))
        self.lent.pop(u).wait_send()

    def a_start(self, u):
        z, s, c, first, second, both = self.where
        self.got(u, 2, self.r1.at[u, 1])
        for n in range(self.z_count):
            total = self.r0[u, n, first].astype(f32) + self.r1[u, 1, n].astype(f32)
            self.r1[u, 1, n] = total.astype(bf16)
        self.started.append(self.go(u, 3, self.r1.at[u, 1], self.r2.at[u], (z, first, c)))
        self.got(u, 1, self.r1.at[u, 0])
        for n in range(self.z_count):
            total = self.r0[u, n, s].astype(f32) + self.r1[u, 0, n].astype(f32)
            self.r1[u, 0, n] = total.astype(bf16)

    def z_start(self, u):
        z, s, c = self.where[:3]
        self.got(u, 3, self.r2.at[u])
        for n in range(self.z_count):
            total = self.r1[u, 0, n].astype(f32) + self.r2[u, n].astype(f32)
            self.r2[u, n] = total.astype(bf16)
        for d in range(1, self.z_count):
            to = (z + d) % self.z_count
            self.started.append(
                self.go(u, 3 + d, self.r2.at[u, to], self.r3.at[u, d - 1], (to, s, c))
            )

    def f_start(self, u):
        z, s, c = self.where[:3]
        total = self.r2[u, z].astype(f32)
        for d in range(1, self.z_count):
            self.got(u, 3 + d, self.r3.at[u, d - 1])
            total = total + self.r3[u, d - 1].astype(f32)
        self.fin[u] = total
        kind, n = self.units[u]
        if kind == "rows":
            if n % 2 == 1:
                @pl.when(c != n // 2)
                def _():
                    pair = pl.ds(u - 1, 2)
                    self.go(u, 7, self.fin.at[pair], self.sib.at[pair], (z, s, 1 - c))
        else:
            rows = pl.ds(pl.multiple_of((1 - c) * (ROWS // 2), 8), ROWS // 2)
            self.started.append(
                self.go(
                    u, 7, self.fin.at[u, rows], self.sib.at[u, pl.ds(0, ROWS // 2)], (z, s, 1 - c)
                )
            )

    def finish_unit(self, u):
        z, s, c = self.where[:3]
        kind, n = self.units[u]
        if kind == "rows":
            if n % 2 == 1:

                @pl.when(c == n // 2)
                def _():
                    self.got(u, 7, self.sib.at[pl.ds(u - 1, 2)])
                    for k in range(2):
                        self.put(kind, k, c, self.fin[u - 1 + k])
                        self.put(kind, k, 1 - c, self.sib[u - 1 + k])

                @pl.when(c != n // 2)
                def _():
                    pair = self.fin.at[pl.ds(u - 1, 2)]
                    remote(
                        pair, pair, self.send.at[u, 7], self.recv.at[u, 7], (z, s, 1 - c)
                    ).wait_send()
        else:
            self.got(u, 7, self.sib.at[u, pl.ds(0, ROWS // 2)])
            rows = pl.ds(pl.multiple_of(c * (ROWS // 2), 8), ROWS // 2)
            self.put(kind, n, c, self.fin[u, rows])
            self.put(kind, n, 1 - c, self.sib[u, : ROWS // 2])

    def reach(self, limits):
        steps = (self.c_start, self.b_start, self.a_start, self.z_start, self.f_start)
        for n, step in enumerate(steps + (self.finish_unit,)):
            while self.at[n] <= min(limits[n], len(self.units) - 1):
                step(self.at[n])
                self.at[n] += 1

    def tick(self, t):
        self.reach([t - lag for lag in (0, 1, 3, 5, 6, 7)])

    def flush(self):
        self.reach([len(self.units) - 1] + [n - 1 for n in self.at[:-1]])

    def finish(self):
        for copy in self.started:
            copy.wait_send()


def pull_rows(values_in, gain_row, incoming):
    inverse = lax.rsqrt(jnp.mean(values_in * values_in, axis=-1, keepdims=True) + norm_eps)
    scaled = incoming * gain_row
    inner = jnp.mean(scaled * values_in, axis=-1, keepdims=True)
    grad = inverse * scaled - values_in * (inverse * inverse * inverse * inner)
    return grad, jnp.sum(incoming * values_in * inverse, axis=0, keepdims=True)


def gelu_both(values_in):
    square = values_in * values_in
    slope = 0.7978845608028654
    bend = jnp.tanh(slope * values_in * (1.0 + 0.044715 * square))
    value = 0.5 * values_in * (1.0 + bend)
    grad = 0.5 * (1.0 + bend) + 0.5 * values_in * (1.0 - bend * bend) * slope * (
        1.0 + 3.0 * 0.044715 * square
    )
    return value, grad


def backward_kernel(z_count, *refs):
    (
        len_ref, table_ref, gain_ref, bucket_ref, w0, w1, w2, w3, w7, w8, win, wout,
        x_i, q_i, k_i, v_i, att_i, hid_i, pre_i, hid2_i, enc_i, gck_i, gcv_i, wd_i, st, gg_i,
        sq_o, in_o, out_o, x_o, own_o, bias_o, norm_o,
        slots, d_out, r0, r1, r2, r3, fin, sib,
        wbuf, x_s, q_s, k_s, v_s, att_s, enc_s, gck_s, gcv_s, hid_s, hid2_s, pre_s,
        gh, gh_b, acc, inner_s, gpre_s, turned, gatt, gq, gk, gv, gx, gx_r,
        wd, e_q, e_up, left_w, left_r, right_r, acc_one,
        sums, dt_o, gg_o, ss, e_small, z_small, e_sq, z_sq,
        send, recv, w_sem, p_sem, a_sem, x_send, x_recv, o_sem, p_send, p_recv, z_send, z_recv, t_send, t_recv,
    ) = refs
    z, s, c = place()[:3]
    blocks = x_s.shape[0]
    width = 2 * HALF

    loads = {}
    for n, (src, dst) in enumerate(
        (
            (enc_i, enc_s), (gck_i, gck_s), (gcv_i, gcv_s), (hid2_i, hid2_s), (hid_i, hid_s),
            (att_i, att_s), (q_i, q_s), (k_i, k_s), (v_i, v_s), (x_i, x_s), (wd_i, wd),
        )
    ):
        copy = pltpu.make_async_copy(src, dst, a_sem.at[n])
        copy.start()
        loads[n] = copy
    tiles = [w7, w8]
    for j in range(4):
        tiles.append(wout.at[pl.ds(j * width, width)])
        tiles.append(win.at[:, pl.ds(j * width, width)])
    tiles += [w3, w0, w1, w2]
    w_loads = {}

    def fetch(n):
        if n < len(tiles):
            copy = pltpu.make_async_copy(tiles[n], wbuf.at[n % 4], w_sem.at[n])
            copy.start()
            w_loads[n] = copy

    p_loads = {}

    def fetch_pre(j):
        if j < 4:
            copy = pltpu.make_async_copy(
                pre_i.at[:, pl.ds(j * width, width)], pre_s.at[j % 2], p_sem.at[j]
            )
            copy.start()
            p_loads[j] = copy

    for n in range(4):
        fetch(n)
    fetch_pre(0)
    fetch_pre(1)
    greet_plane(z, s, c, z_count)
    plane = Plane(p_send, p_recv)
    dec = Decoder(plane, st, gain_ref, z_count)
    e_q[s, c] = st[Decoder.QUERY]
    plane.start(0, e_q)
    z_copies = []

    def dec_query():
        plane.wait(0, e_q)
        value = e_q[0, 0]
        for p in range(1, 8):
            value = value + e_q[p // 2, p % 2]
        acc_one[1] = value
        loads[10].wait()
        dec.square_up(1, e_up.at[0], value, wd, 2)

    def dec_one():
        grad, gain = pull_own(st[Decoder.ONE], dec.gain(4), dec.square_up_sum(1, e_up.at[0]), s, c)
        gg_o[4:5, :] += gain
        value = rounded(st[Decoder.TWO] + grad)
        acc_one[0] = value
        dec.square_up(2, e_up.at[1], value, wd, 1)

    def dec_self():
        value = rounded(dec.square_up_sum(2, e_up.at[1]))
        dec.square_up(3, e_up.at[2], value, wd, 0)
        rights = [value, acc_one[0], acc_one[1], rounded(st[Decoder.TWO])]
        rights += [st[Decoder.PRE + j] for j in range(4)] + [st[Decoder.TOP], jnp.zeros_like(value)]
        right_r[z] = jnp.concatenate(rights, axis=0).astype(bf16)
        lefts = [st[n] for n in range(Decoder.SELF_NORM, Decoder.SELF_VALUES + 1)]
        lefts += [st[n] for n in range(Decoder.CROSS_NORM, Decoder.FFN_NORM + 1)]
        lefts = jnp.concatenate(lefts + [jnp.zeros_like(value)], axis=0).astype(bf16)
        row = lax.broadcasted_iota(jnp.int32, (width, 128), 0)
        lane = lax.broadcasted_iota(jnp.int32, (width, 128), 1)
        share = ROWS // 2
        hidden_at = (2 * s + c) * 4 * share
        hidden_pick = jnp.where((row == hidden_at + lane) & (lane < 4 * share), 1.0, 0.0)
        for to in range(z_count):
            at = (to * 8 + 2 * s + c) * share
            chosen = jnp.where((row == at + lane) & (lane < share), 1.0, 0.0).astype(bf16)
            inner = jnp.concatenate([st[Decoder.INNER + to], jnp.zeros_like(value)], axis=0)
            left_w[to] = jnp.concatenate(
                [
                    matmul(lefts, chosen).astype(bf16),
                    matmul(inner.astype(bf16), hidden_pick.astype(bf16)).astype(bf16),
                ],
                axis=0,
            )
        k = 0
        for d in range(1, z_count):
            to = (z + d) % z_count
            for src, dst in ((right_r.at[z], right_r.at[z]), (left_w.at[to], left_r.at[z])):
                copy = remote(src, dst, z_send.at[k], z_recv.at[k], (to, s, c))
                copy.start()
                z_copies.append(copy)
                k += 1
        left_r[z] = left_w[z]

    def dec_last():
        _, gain = pull_own(
            st[Decoder.ROWS_IN], dec.gain(3), dec.square_up_sum(3, e_up.at[2]), s, c
        )
        gg_o[3:4, :] += gain

    def dec_grads():
        for copy in z_copies:
            copy.wait()
        lefts = [left_r[n].astype(f32) for n in range(z_count)]
        rights = [right_r[n].astype(f32) for n in range(z_count)]

        def gathered(parts, n):
            return jnp.concatenate([p[8 * n : 8 * n + 8] for p in parts], axis=0).astype(bf16)

        share = ROWS // 2
        for n in range(4):
            value = mm_outer(gathered(lefts, n), gathered(rights, n))[:share]
            count(value)
            sq_o[DEC[n]] = value
        for j in range(4):
            value = mm_outer(gathered(lefts, 4), gathered(rights, 4 + j))[:share]
            count(value)
            in_o[1, :, j * width : (j + 1) * width] = value
        value = mm_outer(gathered(lefts, 6), gathered(rights, 8))[: 4 * share]
        count(value)
        out_o[1] = value

    z_started = []

    def line_start(k, ref):
        for d in range(1, z_count):
            mine = ref.at[z]
            copy = remote(
                mine, mine, t_send.at[k, d - 1], t_recv.at[k, d - 1], ((z + d) % z_count, s, c)
            )
            copy.start()
            z_started.append(copy)

    def line_sum(k, ref):
        for d in range(1, z_count):
            slot = ref.at[(z + z_count - d) % z_count]
            remote(slot, slot, t_send.at[k, d - 1], t_recv.at[k, d - 1], (z, s, 1 - c)).wait_recv()
        total = ref[0]
        for n in range(1, z_count):
            total = total + ref[n]
        return total

    def plane_sum(k, ref):
        plane.wait(k, ref)
        total = ref[0, 0]
        for p in range(1, 8):
            total = total + ref[p // 2, p % 2]
        return total

    def small_start():
        offsets = dt_o[...].reshape(dt_o.shape[0], dt_o.shape[2])
        hot = bucket_hot(bucket_ref, bias_o.shape[0])
        heads = lax.broadcasted_iota(jnp.int32, (128, dt_o.shape[0]), 0)
        lane = lax.broadcasted_iota(jnp.int32, (128, dt_o.shape[0]), 1)
        spread = jnp.where(heads == lane, 1.0, 0.0)
        padded = lax.dot_general(
            spread,
            offsets,
            (((1,), (0,)), ((), ())),
            precision=highest_precision,
            preferred_element_type=f32,
        )
        sums = lax.dot_general(
            hot,
            padded,
            (((1,), (1,)), ((), ())),
            precision=highest_precision,
            preferred_element_type=f32,
        )
        pieces = [gg_o[...]] + [sums[8 * n : 8 * n + 8] for n in range(4)]
        e_small[s, c] = jnp.concatenate(pieces, axis=1)
        plane.start(4, e_small)

    def small_line():
        z_small[z] = plane_sum(4, e_small)
        line_start(0, z_small)

    def small_end():
        total = line_sum(0, z_small)
        gg_o[...] = total[:, :width]
        own_o[...] = pltpu.roll(total[:, :width], width - (z * 8 + 2 * s + c) * (ROWS // 2), 1)[
            :, :128
        ]
        sums = [total[:, width + 128 * n : width + 128 * (n + 1)] for n in range(4)]
        bias_o[...] = jnp.concatenate(sums, axis=0)

    def norm_end():
        e_sq[s, c] = ss[:, :128] + ss[:, 128:256] + ss[:, 256:]
        plane.start(5, e_sq)
        z_sq[z] = plane_sum(5, e_sq)
        line_start(1, z_sq)
        rest = jnp.sum(gg_o[...] * gg_o[...]) + jnp.sum(bias_o[...] * bias_o[...])
        total = jnp.sum(line_sum(1, z_sq)) + rest
        norm_o[...] = jnp.sqrt(jnp.full(norm_o.shape, total, f32))

    units = [("square", 7), ("square", 8)] + [("cols", j) for j in range(4)] + [("square", 3)]
    units += [("rows", n) for n in range(4)] + [("heads", m) for m in range(3)]
    sources, held = [], 0
    for kind, n in units:
        if kind == "rows":
            sources.append((kind, n))
        else:
            sources.append(("slot", held % 3))
            held += 1

    def count(value):
        squares = value * value
        total = squares[:8]
        for n in range(8, value.shape[0], 8):
            total = total + squares[n : n + 8]
        for n in range(0, value.shape[1], HALF):
            ss[...] += total[:, n : n + HALF]

    def put(kind, n, side, value):
        count(value)
        if kind == "square":
            sq_o[n, :, cols(side)] = value
        elif kind == "cols":
            in_o[0, :, cols(side, n * width)] = value
        elif kind == "rows":
            out_o[0, n * ROWS : (n + 1) * ROWS, cols(side)] = value
        else:
            at = pl.ds(pl.multiple_of((2 * n + side) * 128, 128), 128)
            for t in range(3):
                sq_o[t, :, at] = value[:, t * 128 : (t + 1) * 128]

    scatter = Scatter(units, sources, (r0, r1, r2, r3, fin, sib), (send, recv), z_count, put)
    scatter.refs = {"slots": slots, "rows": d_out}

    def turn(src):
        def body(i, carry):
            at = pl.ds(pl.multiple_of(i * 256, 256), 256)
            turned[at, :] = src[:, at].T
            return carry

        lax.fori_loop(0, 3, body, 0)

    def grad_to_slot(n, right):
        def work(at):
            value = matmul(turned[...], right[:, at]).astype(bf16)
            slots[n, :, :, :, at] = value.reshape(z_count, 4, ROWS, 256)

        col_tiles(width, 256, work)

    def back(left, n, dst, add):
        w_loads[n].wait()

        def work(at):
            value = mm_t(left[...], wbuf[n % 4, at, :])
            if add:
                value = value + dst[:, at]
            dst[:, at] = value

        col_tiles(width, 256, work)
        fetch(n + 4)

    gg_o[...] = gg_i[...]
    ss[...] = jnp.zeros_like(ss)
    loads[0].wait()
    loads[1].wait()
    turn(enc_s)
    grad_to_slot(0, gck_s)
    scatter.tick(0)
    dec_query()
    loads[2].wait()
    grad_to_slot(1, gcv_s)
    scatter.tick(1)
    back(gck_s, 0, acc, False)
    back(gcv_s, 1, acc, True)
    loads[3].wait()
    loads[4].wait()

    def pull_hid2(i, at):
        grad, gain = pull_rows(hid2_s[at, :], gain_ref[2:3, :], acc[at, :])
        gh[at, :] = grad
        gh_b[at, :] = grad.astype(bf16)
        gg_o[2:3, :] += gain
        enc_s[at, :] = rms_gain(hid_s[at, :], gain_ref[1:2, :]).astype(bf16)

    dec_one()
    row_blocks(blocks, pull_hid2)
    turn(enc_s)

    for j in range(4):
        p_loads[j].wait()
        w_loads[2 + 2 * j].wait()

        def hidden_tile(at):
            value, slope = gelu_both(pre_s[j % 2, :, at])
            inner_s[:, at] = value.astype(bf16)
            grad = mm_t(gh_b[...], wbuf[(2 + 2 * j) % 4, at, :])
            gpre_s[:, at] = (grad * slope).astype(bf16)

        col_tiles(width, 256, hidden_tile)
        fetch(6 + 2 * j)
        fetch_pre(j + 2)
        grad_to_slot((2 + j) % 3, gpre_s)
        scatter.tick(2 + j)

        def out_rows(i, carry):
            at = pl.ds(pl.multiple_of(i * HALF, HALF), HALF)
            value = mm_outer(inner_s[:, at], gh_b[...]).astype(bf16)
            d_out[0, j, pl.ds(2 * i, 2)] = value.reshape(2, 4 * ROWS, width)
            return carry

        lax.fori_loop(0, 2, out_rows, 0)
        back(gpre_s, 3 + 2 * j, acc, j > 0)
        if j < 2:
            (dec_self, dec_last)[j]()

    loads[5].wait()

    def pull_hid(i, at):
        grad, gain = pull_rows(hid_s[at, :], gain_ref[1:2, :], acc[at, :])
        total = gh[at, :] + grad
        gh[at, :] = total
        gh_b[at, :] = total.astype(bf16)
        gg_o[1:2, :] += gain

    row_blocks(blocks, pull_hid)
    turn(att_s)
    grad_to_slot(0, gh_b)
    scatter.tick(6)
    w_loads[10].wait()

    def attended_grad(at):
        gatt[:, at] = mm_t(gh_b[...], wbuf[10 % 4, at, :]).astype(bf16)

    col_tiles(width, 256, attended_grad)
    for n in (6, 7, 8, 9):
        loads[n].wait()

    def x_norm(i, at):
        enc_s[at, :] = rms_gain(x_s[i].astype(f32), gain_ref[0:1, :]).astype(bf16)

    row_blocks(blocks, x_norm)
    turn(enc_s)
    scatter.tick(7)

    def pair_grads(pairs):
        def body(pair, carry):
            attend_pair_bwd(
                pair, len_ref[s], table_ref, q_s, k_s, v_s, gatt, gq, gk, gv, dt_o, sums
            )
            return carry

        lax.fori_loop(pairs[0], pairs[1], body, 0)

    def heads_to_slot(m, n):
        for t, right in enumerate((gq, gk, gv)):
            value = matmul(turned[...], right[:, m * 256 : (m + 1) * 256]).astype(bf16)
            value = value.reshape(z_count, 4, ROWS, 256)
            slots[n, :, :, :, t * 128 : (t + 1) * 128] = value[..., :128]
            slots[n, :, :, :, HALF + t * 128 : HALF + (t + 1) * 128] = value[..., 128:]

    pair_grads((0, 1))
    scatter.tick(8)
    pair_grads((1, 2))
    heads_to_slot(0, 1)
    scatter.tick(9)
    pair_grads((2, 3))
    scatter.tick(10)
    pair_grads((3, 4))
    heads_to_slot(1, 2)
    scatter.tick(11)
    pair_grads((4, 5))
    scatter.tick(12)
    pair_grads((5, 6))
    heads_to_slot(2, 0)
    scatter.tick(13)
    back(gq, 11, acc, False)
    scatter.flush()
    back(gk, 12, acc, True)
    back(gv, 13, acc, True)

    def pull_x(i, at):
        grad, gain = pull_rows(x_s[i].astype(f32), gain_ref[0:1, :], acc[at, :])
        gx[i] = (gh[at, :] + grad).astype(bf16)
        gg_o[0:1, :] += gain

    row_blocks(blocks, pull_x)
    small_start()
    scatter.flush()
    x_copies = []
    for d in range(1, 4):
        peer = (s + d) % 4
        copy = remote(
            gx.at[peer], gx_r.at[s], x_send.at[d - 1], x_recv.at[d - 1], (z, peer, c)
        )
        copy.start()
        x_copies.append(copy)
    dec_grads()
    small_line()
    scatter.flush()
    gx_r[s] = gx[s]
    scatter.flush()
    small_end()
    scatter.flush()
    norm_end()
    for copy in x_copies:
        copy.wait()

    def widen(i, at):
        gh[at, :] = gx_r[i].astype(f32)

    row_blocks(blocks, widen)
    copy = pltpu.make_async_copy(gh, x_o, o_sem.at[0])
    copy.start()
    scatter.finish()
    plane.finish()
    for sent in z_started:
        sent.wait_send()
    copy.wait()


def backward(lengths, table, gain, buckets, weights, win, wout, acts, small, z_count):
    x = acts[0]
    blocks, band, width = x.shape
    span = blocks * band
    vmem = pl.BlockSpec(memory_space=pltpu.VMEM)
    hbm = pl.BlockSpec(memory_space=pltpu.HBM)
    n = 14
    token = ((span, width), bf16)
    token_f = ((span, width), f32)
    scratch = [((3, z_count, 4, ROWS, width), bf16), ((1, z_count, 4, 4 * ROWS, width), bf16)]
    scratch += [((n, z_count, 4, ROWS, HALF), bf16), ((n, 2, z_count, ROWS, HALF), bf16)]
    scratch += [((n, z_count, ROWS, HALF), bf16), ((n, z_count - 1, ROWS, HALF), bf16)]
    scratch += [((n, ROWS, HALF), f32), ((n, ROWS, HALF), f32)]
    scratch += [((4, width, width), bf16), (x.shape, bf16)] + [token] * 7 + [token_f] * 2
    scratch += [((2, span, width), f32), token_f, token, token_f, token, token]
    scratch += [((width, span), bf16)] + [token] * 4 + [(x.shape, bf16)] * 2
    scratch += [((len(DEC), z_count, ROWS, HALF), bf16), ((4, 2, 8, width), f32)]
    scratch += [((3, 4, 2, z_count, 8, 128), f32), ((z_count, 64, 128), bf16)]
    scratch += [((z_count, 64, 128), bf16), ((z_count, 80, width), bf16), ((2, 8, width), f32)]
    scratch += [((BAND, 2 * span), f32), (table.shape, f32), ((8, width), f32), ((8, HALF), f32)]
    scratch += [((4, 2, 8, width + 512), f32), ((z_count, 8, width + 512), f32)]
    scratch += [((4, 2, 8, 128), f32), ((z_count, 8, 128), f32)]
    dma = pltpu.SemaphoreType.DMA
    return pl.pallas_call(
        functools.partial(backward_kernel, z_count),
        out_shape=[
            jax.ShapeDtypeStruct((10, ROWS // 2, width), f32),
            jax.ShapeDtypeStruct((2, ROWS // 2, 4 * width), f32),
            jax.ShapeDtypeStruct((2, 2 * ROWS, width), f32),
            jax.ShapeDtypeStruct((span, width), f32),
            jax.ShapeDtypeStruct((8, 128), f32),
            jax.ShapeDtypeStruct((32, 128), f32),
            jax.ShapeDtypeStruct((8, 128), f32),
        ],
        in_specs=[pl.BlockSpec(memory_space=pltpu.SMEM)] + [vmem] * 3 + [hbm] * 20 + [vmem] * 2,
        out_specs=[vmem] * 3 + [hbm] + [vmem] * 3,
        scratch_shapes=[pltpu.VMEM(*o) for o in scratch]
        + [dma((n, 8)), dma((n, 8)), dma((n,)), dma((4,)), dma((11,)), dma((3,)), dma((3,))]
        + [dma((1,)), dma((6, 7)), dma((6, 7)), dma((6,)), dma((6,)), dma((2, 3)), dma((2, 3))],
        compiler_params=pltpu.CompilerParams(
            collective_id=1, has_side_effects=True, vmem_limit_bytes=62 * MIB
        ),
        name="backward",
    )(lengths, table, gain, buckets, *weights, win, wout, *acts, *small)


def on_device(
    inputs,
    dec_in,
    cotangent,
    lengths,
    bucket_table,
    square,
    square_m,
    square_v,
    ffn_in,
    ffn_in_m,
    ffn_in_v,
    ffn_out,
    ffn_out_m,
    ffn_out_v,
    gains,
    gains_m,
    gains_v,
    rel_bias,
    rel_bias_m,
    rel_bias_v,
):
    z_count = lax.axis_size("dp")
    width = inputs.shape[2]
    direct = lax.axis_size("seq") == 4 and width == 2 * HALF and width == 4 * z_count * ROWS
    direct = direct and inputs.shape[:2] == (4, BAND)
    w = {}
    seq_pos = lax.axis_index("seq")
    local_len = inputs.shape[1]
    span = local_len * lax.axis_size("seq")
    bucket_count = rel_bias.shape[0]
    scale = 1.0 / math.sqrt(HD)
    length = lax.dynamic_slice_in_dim(lengths, seq_pos, 1, 0)
    key_valid = jnp.arange(span)[None, :] < length[:, None]
    one_hot = (
        jnp.pad(bucket_table, (0, 1), constant_values=-1)[:, None]
        == jnp.arange(bucket_count)[None, :]
    ).astype(f32)
    table = jnp.einsum("ob,bh->ho", one_hot, rel_bias, precision=highest_precision)[:, None, :]

    me = (
        lax.axis_index("dp") * lax.axis_size("seq") + seq_pos
    ) * lax.axis_size("head") + lax.axis_index("head")
    if direct:
        buckets = jnp.pad(bucket_table[::-1], (0, 1), constant_values=-1)[None]
        outs = forward(
            lengths,
            rel_bias,
            buckets,
            square,
            ffn_in,
            ffn_out,
            gains,
            dec_in,
            cotangent,
            inputs,
            z_count,
        )
        weights = [o.reshape(width, width) for o in outs[14:20]]
        gain_f, state, g_high, dec_out, table = outs[20:]
        dec_out = dec_out[:1]
        summed_sq, summed_in, summed_out, input_grad, summed_gain, g_bias, norm = backward(
            lengths,
            table,
            gain_f,
            buckets,
            weights,
            outs[0].reshape(width, -1),
            outs[1].reshape(-1, width),
            outs[2:14],
            (state, g_high),
            z_count,
        )
        input_grad = input_grad.reshape(inputs.shape)
        summed_gain = summed_gain[: gains.shape[0], : gains.shape[1]]
        g_bias = g_bias[:, : rel_bias.shape[1]]
        grad_norm = norm[0, 0]
    else:

        def gather_rows(x):
            return lax.all_gather(x.astype(bf16), AXES, axis=x.ndim - 2, tiled=True)

        sq_a = gather_rows(square[:4])
        w_in_e = gather_rows(ffn_in[0])
        w_out_e = gather_rows(ffn_out[0])
        sq_b = gather_rows(square[4:])
        w_in_d = gather_rows(ffn_in[1])
        w_out_d = gather_rows(ffn_out[1])
        gain_f = lax.all_gather(gains.astype(bf16), AXES, axis=1, tiled=True).astype(f32)
        for i in range(square.shape[0]):
            w[i] = sq_a[i] if i < 4 else sq_b[i - 4]
        x_b = lax.all_to_all(inputs, "seq", split_axis=0, concat_axis=1, tiled=True)[0]
        x_f = x_b.astype(f32)
        normed = rms_gain(x_f, gain_f[0]).astype(bf16)
        q = matmul(normed, w[0]).astype(bf16)
        k = matmul(normed, w[1]).astype(bf16)
        v = matmul(normed, w[2]).astype(bf16)
        attended = attend_fwd(length, table, q, k, v)
        hidden = x_f + matmul(attended, w[3])
        normed_two = rms_gain(hidden, gain_f[1]).astype(bf16)
        pre_act = matmul(normed_two, w_in_e)
        inner_act = gelu_tanh(pre_act).astype(bf16)
        hidden_two = hidden + matmul(inner_act, w_out_e)
        encoded = rms_gain(hidden_two, gain_f[2]).astype(bf16)
        cross_k = matmul(encoded, w[7]).astype(bf16)
        cross_v = matmul(encoded, w[8]).astype(bf16)

        dec_row = dec_in.reshape(1, width).astype(f32)
        self_norm = rms_gain(dec_row, gain_f[3]).astype(bf16)
        self_values = matmul(self_norm, w[4]).astype(bf16)
        dec_one = dec_row + matmul(self_values, w[5])
        cross_norm = rms_gain(dec_one, gain_f[4]).astype(bf16)
        cross_q = matmul(cross_norm, w[6]).astype(bf16)
        head_of = (jnp.arange(width)[None, :] // HD == jnp.arange(H)[:, None]).astype(bf16)
        q_heads = head_of * cross_q
        cross_scores = jnp.where(key_valid, mm_t(q_heads, cross_k) * scale, neg_fill)
        cross_probs = jax.nn.softmax(cross_scores, axis=-1)
        cross_probs_b = cross_probs.astype(bf16)
        cross_att = jnp.sum(
            matmul(cross_probs_b, cross_v) * head_of.astype(f32), axis=0, keepdims=True
        ).astype(bf16)
        dec_two = dec_one + matmul(cross_att, w[9])
        ffn_norm = rms_gain(dec_two, gain_f[5]).astype(bf16)
        pre_dec = matmul(ffn_norm, w_in_d)
        inner_dec = gelu_tanh(pre_dec).astype(bf16)
        dec_out = dec_two + matmul(inner_dec, w_out_d)

        g_top_b = cotangent.reshape(1, width)
        g_top = g_top_b.astype(f32)
        g_pre_dec = gelu_pull(pre_dec, mm_t(g_top_b, w_out_d)).astype(bf16)
        g_two_norm, g_gain_five = rms_pull(dec_two, gain_f[5], mm_t(g_pre_dec, w_in_d))
        g_two = g_top + g_two_norm
        g_two_b = g_two.astype(bf16)
        g_att = mm_t(g_two_b, w[9]).astype(bf16)
        g_att_heads = head_of * g_att
        g_probs = mm_t(g_att_heads, cross_v)
        g_cross_v = mm_outer(cross_probs_b, g_att_heads).astype(bf16)
        g_scores = cross_probs * (g_probs - jnp.sum(g_probs * cross_probs, axis=-1, keepdims=True))
        g_scores_b = g_scores.astype(bf16)
        g_cross_q = (
            jnp.sum(matmul(g_scores_b, cross_k) * head_of.astype(f32), axis=0, keepdims=True) * scale
        ).astype(bf16)
        g_cross_k = (mm_outer(g_scores_b, q_heads) * scale).astype(bf16)
        g_one_norm, g_gain_four = rms_pull(dec_one, gain_f[4], mm_t(g_cross_q, w[6]))
        g_one_b = (g_two + g_one_norm).astype(bf16)
        g_self_values = mm_t(g_one_b, w[5]).astype(bf16)
        g_gain_three = rms_pull(dec_row, gain_f[3], mm_t(g_self_values, w[4]))[1]

        lefts = (self_norm, self_values, cross_norm, cross_att, ffn_norm, inner_dec)
        rights = (g_self_values, g_one_b, g_cross_q, g_two_b, g_pre_dec, g_top_b)
        packed = lax.all_gather(jnp.concatenate(lefts + rights, axis=1), AXES, axis=0, tiled=True)
        devices = packed.shape[0]
        cuts = [0]
        for piece in lefts + rights:
            cuts.append(cuts[-1] + piece.shape[1])
        dec_grads = []
        for n in range(6):
            share = lefts[n].shape[1] // devices
            left = lax.dynamic_slice_in_dim(packed, cuts[n] + me * share, share, 1)
            right = packed[:, cuts[6 + n] : cuts[7 + n]]
            dec_grads.append(mm_outer(left, right))
        g_w7 = mm_outer(encoded, g_cross_k)
        g_w8 = mm_outer(encoded, g_cross_v)
        g_encoded = mm_t(g_cross_k, w[7]) + mm_t(g_cross_v, w[8])
        g_hidden_two, g_gain_two = rms_pull(hidden_two, gain_f[2], g_encoded)
        g_hidden_two_b = g_hidden_two.astype(bf16)
        g_out_e = mm_outer(inner_act, g_hidden_two_b)
        g_pre = gelu_pull(pre_act, mm_t(g_hidden_two_b, w_out_e)).astype(bf16)
        g_in_e = mm_outer(normed_two, g_pre)
        g_hidden_norm, g_gain_one = rms_pull(hidden, gain_f[1], mm_t(g_pre, w_in_e))
        g_hidden = g_hidden_two + g_hidden_norm
        g_hidden_b = g_hidden.astype(bf16)
        g_w3 = mm_outer(attended, g_hidden_b)
        g_attended = mm_t(g_hidden_b, w[3]).astype(bf16)
        gq, gk, gv, g_table = attend_bwd(length, table, q, k, v, g_attended)
        g_bias_here = jnp.einsum("ob,ho->bh", one_hot, g_table[:, 0, :], precision=highest_precision)
        g_w0 = mm_outer(normed, gq)
        g_w1 = mm_outer(normed, gk)
        g_w2 = mm_outer(normed, gv)
        g_normed = mm_t(gq, w[0]) + mm_t(gk, w[1]) + mm_t(gv, w[2])
        g_input_norm, g_gain_zero = rms_pull(x_f, gain_f[0], g_normed)
        g_x = (g_hidden + g_input_norm).astype(bf16)
        input_grad = lax.all_to_all(
            g_x[None], "seq", split_axis=1, concat_axis=0, tiled=True
        ).astype(f32)

        def scatter_rows(x):
            return lax.psum_scatter(
                x.astype(bf16), AXES, scatter_dimension=x.ndim - 2, tiled=True
            ).astype(f32)

        s_78 = scatter_rows(jnp.stack((g_w7, g_w8)))
        s_out = scatter_rows(g_out_e)
        s_in = scatter_rows(g_in_e)
        s_0123 = scatter_rows(jnp.stack((g_w0, g_w1, g_w2, g_w3)))
        g_gains = jnp.stack(
            (g_gain_zero, g_gain_one, g_gain_two, g_gain_three, g_gain_four, g_gain_five)
        )
        summed_sq = jnp.stack(
            (
                s_0123[0],
                s_0123[1],
                s_0123[2],
                s_0123[3],
                dec_grads[0],
                dec_grads[1],
                dec_grads[2],
                s_78[0],
                s_78[1],
                dec_grads[3],
            )
        )
        summed_in = jnp.stack((s_in, dec_grads[4]))
        summed_out = jnp.stack((s_out, dec_grads[5]))
        gain_share = gains.shape[1]
        local_squares = (
            jnp.sum(summed_sq * summed_sq)
            + jnp.sum(summed_in * summed_in)
            + jnp.sum(summed_out * summed_out)
        )
        g_gains, g_bias, shard_squares = lax.psum((g_gains, g_bias_here, local_squares), AXES)
        summed_gain = lax.dynamic_slice_in_dim(g_gains, me * gain_share, gain_share, 1)
        grad_norm = jnp.sqrt(shard_squares + jnp.sum(g_gains * g_gains) + jnp.sum(g_bias * g_bias))
    factor = clip_bound / jnp.maximum(grad_norm, clip_bound)
    return (
        dec_out.astype(bf16).reshape(dec_in.shape),
        input_grad,
        grad_norm,
        *adam_step(square, square_m, square_v, summed_sq, factor, rate_matrix, decay_rate),
        *adam_step(ffn_in, ffn_in_m, ffn_in_v, summed_in, factor, rate_matrix, decay_rate),
        *adam_step(ffn_out, ffn_out_m, ffn_out_v, summed_out, factor, rate_matrix, decay_rate),
        *adam_step(gains, gains_m, gains_v, summed_gain, factor, rate_small, 0.0),
        *adam_step(rel_bias, rel_bias_m, rel_bias_v, g_bias, factor, rate_small, 0.0),
    )


def solution(mesh):
    rows = P(("dp", "head"), "seq", None)
    shard = P(None, AXES, None)
    small = P(None, AXES)
    return jax.shard_map(
        on_device,
        mesh=mesh,
        in_specs=(rows, rows, rows, P(("dp", "head")), P())
        + (shard,) * 9
        + (small,) * 3
        + (P(),) * 3,
        out_specs=(rows, rows, P()) + (shard,) * 9 + (small,) * 3 + (P(),) * 3,
        check_vma=False,
    )
```

```python
import functools
import math

import jax
import jax.numpy as jnp
from jax import lax
from jax.experimental import pallas as pl
from jax.experimental.pallas import tpu as pltpu
from jax.sharding import PartitionSpec as P

H = 12
HD = 64
STEP = 5
AXES = ("dp", "seq", "head")

norm_eps = 1e-06
neg_fill = -1e30
beta_one = 0.9
beta_two = 0.999
adam_eps = 1e-08
decay_rate = 0.01
rate_matrix = 0.05
rate_small = 0.5
clip_bound = 1.0
highest_precision = lax.Precision.HIGHEST
bf16 = jnp.bfloat16
f32 = jnp.float32
BAND = 128


def rms_gain(values_in, gain_row):
    return (
        values_in
        * lax.rsqrt(jnp.mean(values_in * values_in, axis=-1, keepdims=True) + norm_eps)
        * gain_row
    )


def gelu_tanh(values_in):
    return jax.nn.gelu(values_in, approximate=True)


def matmul(left, right):
    return jnp.dot(left, right, preferred_element_type=f32)


def mm_t(left, right):
    return lax.dot_general(left, right, (((1,), (1,)), ((), ())), preferred_element_type=f32)


def mm_outer(left, right):
    return lax.dot_general(left, right, (((0,), (0,)), ((), ())), preferred_element_type=f32)


def rms_pull(values_in, gain_row, incoming):
    _, pull = jax.vjp(rms_gain, values_in, gain_row)
    return pull(incoming)


def gelu_pull(values_in, incoming):
    _, pull = jax.vjp(gelu_tanh, values_in)
    return pull(incoming)[0]


def adam_step(weight, first, second, grad, factor, rate, decay):
    grad = grad * factor
    first = beta_one * first + (1.0 - beta_one) * grad
    second = beta_two * second + (1.0 - beta_two) * grad * grad
    first_hat = first / (1.0 - beta_one**STEP)
    second_hat = second / (1.0 - beta_two**STEP)
    weight = weight - rate * (first_hat / (jnp.sqrt(second_hat) + adam_eps) + decay * weight)
    return (weight, first, second)


def bias_band(table_row, span):
    wide = jnp.broadcast_to(table_row, (BAND, 2 * span))
    shift = (2 * span - (BAND - 1)) % (2 * span)
    return pltpu.roll(wide, shift, 1, stride=1, stride_axis=0)


def band_sums(band, span):
    wide = 2 * span
    rows = BAND
    while rows > 8:
        rows //= 2
        band = band[:rows] + pltpu.roll(band[rows:], wide - rows, 1)
    row = lax.broadcasted_iota(jnp.int32, band.shape, 0)
    for step in (4, 2, 1):
        band = jnp.where((row // step) % 2 == 1, pltpu.roll(band, wide - step, 1), band)
    return pltpu.roll(jnp.sum(band, axis=0, keepdims=True), BAND - 1, 1)


def softmax_rows(q_rows, k_all, band, block, span, valid):
    start = span - BAND * (block + 1)
    scores = mm_t(q_rows, k_all) * (1.0 / math.sqrt(HD)) + band[:, start : start + span]
    scores = jnp.where(valid, scores, neg_fill)
    peak = jnp.max(scores, axis=-1, keepdims=True)
    raised = jnp.exp(scores - peak)
    return raised / jnp.sum(raised, axis=-1, keepdims=True)


def attend_fwd_kernel(len_ref, table_ref, q_ref, k_ref, v_ref, o_ref):
    span = k_ref.shape[0]
    valid = lax.broadcasted_iota(jnp.int32, (1, span), 1) < len_ref[0]
    lane = lax.broadcasted_iota(jnp.int32, (1, 2 * HD), 1)
    k_all = k_ref[...]
    v_all = v_ref[...]
    bands = [bias_band(table_ref[t], span) for t in range(2)]
    for block in range(span // BAND):
        rows = slice(block * BAND, (block + 1) * BAND)
        q_rows = q_ref[rows, :]
        parts = []
        for t in range(2):
            own = (lane // HD) == t
            probs = softmax_rows(
                jnp.where(own, q_rows, jnp.zeros_like(q_rows)), k_all, bands[t], block, span, valid
            )
            parts.append(matmul(probs.astype(bf16), v_all))
        o_ref[rows, :] = jnp.where(lane < HD, parts[0], parts[1]).astype(bf16)


def attend_bwd_kernel(
    len_ref, table_ref, q_ref, k_ref, v_ref, do_ref, dq_ref, dk_ref, dv_ref, dt_ref
):
    span = k_ref.shape[0]
    scale = 1.0 / math.sqrt(HD)
    valid = lax.broadcasted_iota(jnp.int32, (1, span), 1) < len_ref[0]
    lane = lax.broadcasted_iota(jnp.int32, (1, 2 * HD), 1)
    k_all = k_ref[...]
    v_all = v_ref[...]
    count = span // BAND
    dks, dvs = [], []
    dqs = [[None, None] for _ in range(count)]
    for t in range(2):
        own = (lane // HD) == t
        band = bias_band(table_ref[t], span)
        dk = jnp.zeros((span, 2 * HD), f32)
        dv = jnp.zeros((span, 2 * HD), f32)
        dband = jnp.zeros((BAND, 2 * span), f32)
        for block in range(count):
            rows = slice(block * BAND, (block + 1) * BAND)
            q_rows = q_ref[rows, :]
            do_rows = do_ref[rows, :]
            zero = jnp.zeros_like(q_rows)
            probs = softmax_rows(
                jnp.where(own, q_rows, zero), k_all, band, block, span, valid
            )
            dprobs = mm_t(jnp.where(own, do_rows, zero), v_all)
            dscore = probs * (dprobs - jnp.sum(dprobs * probs, axis=-1, keepdims=True))
            start = span - BAND * (block + 1)
            pieces = []
            if start:
                pieces.append(jnp.zeros((BAND, start), f32))
            pieces.append(dscore)
            if span - start:
                pieces.append(jnp.zeros((BAND, span - start), f32))
            dband = dband + jnp.concatenate(pieces, axis=1)
            dscore_b = dscore.astype(bf16)
            dv = dv + mm_outer(probs.astype(bf16), do_rows)
            dk = dk + mm_outer(dscore_b, q_rows)
            dqs[block][t] = matmul(dscore_b, k_all)
        dks.append(dk)
        dvs.append(dv)
        dt_ref[t] = band_sums(dband, span)
    dk_ref[...] = (jnp.where(lane < HD, dks[0], dks[1]) * scale).astype(bf16)
    dv_ref[...] = jnp.where(lane < HD, dvs[0], dvs[1]).astype(bf16)
    for block in range(count):
        rows = slice(block * BAND, (block + 1) * BAND)
        dq_ref[rows, :] = (jnp.where(lane < HD, dqs[block][0], dqs[block][1]) * scale).astype(bf16)


def head_specs(span, width, n):
    return [pl.BlockSpec((span, 2 * HD), lambda i: (0, i)) for _ in range(n)]


def attend_fwd(length, table, q, k, v):
    span, width = q.shape
    return pl.pallas_call(
        attend_fwd_kernel,
        grid=(width // (2 * HD),),
        out_shape=jax.ShapeDtypeStruct((span, width), bf16),
        in_specs=[
            pl.BlockSpec(memory_space=pltpu.SMEM),
            pl.BlockSpec((2, 1, 2 * span), lambda i: (i, 0, 0)),
            *head_specs(span, width, 3),
        ],
        out_specs=head_specs(span, width, 1)[0],
        compiler_params=pltpu.CompilerParams(vmem_limit_bytes=48 * 1024 * 1024),
        name="attend_fwd",
    )(length, table, q, k, v)


def attend_bwd(length, table, q, k, v, do):
    span, width = q.shape
    like = jax.ShapeDtypeStruct((span, width), bf16)
    return pl.pallas_call(
        attend_bwd_kernel,
        grid=(width // (2 * HD),),
        out_shape=(like, like, like, jax.ShapeDtypeStruct(table.shape, f32)),
        in_specs=[
            pl.BlockSpec(memory_space=pltpu.SMEM),
            pl.BlockSpec((2, 1, 2 * span), lambda i: (i, 0, 0)),
            *head_specs(span, width, 4),
        ],
        out_specs=(
            *head_specs(span, width, 3),
            pl.BlockSpec((2, 1, 2 * span), lambda i: (i, 0, 0)),
        ),
        compiler_params=pltpu.CompilerParams(vmem_limit_bytes=48 * 1024 * 1024),
        name="attend_bwd",
    )(length, table, q, k, v, do)


MESH_ID = pl.DeviceIdType.MESH
HALF = 384
ROWS = 48
MIB = 1024 * 1024


def place():
    z, s, c = lax.axis_index("dp"), lax.axis_index("seq"), lax.axis_index("head")
    near = s + 1 - 2 * (s % 2)
    far = (s + 2) % 4
    first = near + c * (far - near)
    second = far + c * (near - far)
    return z, s, c, first, second, 3 - s


def greet(z, s, c, z_count):
    barrier = pltpu.get_barrier_semaphore()
    for d in range(1, z_count):
        peer = ((z + d) % z_count, s, c)
        pl.semaphore_signal(barrier, 1, device_id=peer, device_id_type=MESH_ID)
    for d in range(1, 4):
        peer = (z, (s + d) % 4, c)
        pl.semaphore_signal(barrier, 1, device_id=peer, device_id_type=MESH_ID)
    pl.semaphore_signal(barrier, 1, device_id=(z, s, 1 - c), device_id_type=MESH_ID)
    pl.semaphore_wait(barrier, z_count + 3)


def remote(src, dst, send, recv, peer):
    return pltpu.make_async_remote_copy(
        src, dst, send, recv, device_id=peer, device_id_type=MESH_ID
    )


def cols(c, base=0):
    return pl.ds(pl.multiple_of(base + c * HALF, 128), HALF)


def unit_view(kind, n, ref, z, s, c):
    if kind == "square":
        return ref.at[n, z, s, :, cols(c)]
    if kind == "cols":
        return ref.at[n // 4, z, s, :, cols(c, (n % 4) * 2 * HALF)]
    if kind == "rows":
        return ref.at[n // 4, z, s, pl.ds((n % 4) * ROWS, ROWS), cols(c)]
    if kind == "line square":
        return ref.at[n, z]
    if kind == "line cols":
        return ref.at[z, :, pl.ds(n * HALF, HALF)]
    if kind == "line rows":
        return ref.at[z, pl.ds(n * ROWS, ROWS)]
    return ref.at[z, s]


class Gather:
    def __init__(self, units, refs, send, recv, z_count):
        self.units, self.refs, self.send, self.recv = units, refs, send, recv
        self.z_count = z_count
        self.where = place()
        self.started = []
        self.base = 2 * (z_count - 1)

    def view(self, u, z, s, c):
        kind, n = self.units[u]
        return unit_view(kind, n, self.refs[kind], z, s, c)

    def go(self, u, slot, ref, peer):
        copy = remote(ref, ref, self.send.at[u, slot], self.recv.at[u, slot], peer)
        copy.start()
        self.started.append(copy)

    def got(self, u, slot, ref):
        z, s, c = self.where[:3]
        remote(ref, ref, self.send.at[u, slot], self.recv.at[u, slot], (z, s, 1 - c)).wait_recv()

    def z_sends(self, u, i):
        z, s, c = self.where[:3]
        top = self.z_count - 1
        for slot, near, block, live in (
            (i, z + 1, z - i, (z >= i) & (z < top)),
            (top + i, z - 1, z + i, (z + i <= top) & (z > 0)),
        ):
            ref = self.view(u, block, s, c)
            copy = remote(
                ref, ref, self.send.at[u, slot], self.recv.at[u, slot], (near, s, c)
            )
            yield copy, live

    def z_send(self, u, i):
        for copy, live in self.z_sends(u, i):

            @pl.when(live)
            def _():
                copy.start()

    def z_got(self, u, i):
        z, s, c = self.where[:3]
        top = self.z_count - 1
        for slot, block, live in (
            (i, z - 1 - i, z - 1 - i >= 0),
            (top + i, z + 1 + i, z + 1 + i <= top),
        ):

            @pl.when(live)
            def _():
                self.got(u, slot, self.view(u, block, s, c))

    def a_start(self, u):
        z, s, c, first, second, both = self.where
        self.go(u, self.base, self.view(u, slice(None), s, c), (z, first, c))

    def a_wait(self, u):
        z, s, c, first, second, both = self.where
        self.got(u, self.base, self.view(u, slice(None), first, c))

    def b_start(self, u):
        z, s, c, first, second, both = self.where
        self.go(u, self.base + 1, self.view(u, slice(None), s, c), (z, second, c))
        self.go(u, self.base + 2, self.view(u, slice(None), first, c), (z, second, c))

    def b_wait(self, u):
        z, s, c, first, second, both = self.where
        self.got(u, self.base + 1, self.view(u, slice(None), second, c))
        self.got(u, self.base + 2, self.view(u, slice(None), both, c))

    def s_start(self, u):
        z, s, c = self.where[:3]
        if self.units[u][0] != "gain":
            self.go(u, self.base + 3, self.view(u, slice(None), slice(None), c), (z, s, 1 - c))

    def s_wait(self, u):
        z, s, c = self.where[:3]
        if self.units[u][0] != "gain":
            self.got(u, self.base + 3, self.view(u, slice(None), slice(None), 1 - c))

    def line(self, u, i):
        if i:
            self.z_got(u, i - 1)
        if i < self.z_count - 1:
            self.z_send(u, i)

    def lag(self, stage):
        return stage if stage < self.z_count else self.z_count - 1 + (0, 2, 4, 5)[stage - self.z_count + 1]

    def tick(self, t, done):
        lines = self.z_count
        for n in range(lines + 3):
            u = t - self.lag(n)
            if not 0 <= u < len(self.units):
                continue
            if n < lines:
                self.line(u, n)
            plain = not self.units[u][0].startswith("line")
            if plain and n == lines - 1:
                self.a_start(u)
            if plain and n == lines:
                self.a_wait(u)
                self.b_start(u)
            if plain and n == lines + 1:
                self.b_wait(u)
                self.s_start(u)
            if plain and n == lines + 2:
                self.s_wait(u)
                done(u)

    def finish(self):
        for copy in self.started:
            copy.wait_send()
        for u in range(len(self.units)):
            for i in range(self.z_count - 1):
                for copy, live in self.z_sends(u, i):

                    @pl.when(live)
                    def _():
                        copy.wait_send()


ENC = (0, 1, 2, 3, 7, 8)
DEC = (4, 5, 6, 9)
SAME_CORE = (1, 3, 5)


def plane_peers(z, s, c):
    peers = []
    for ds in range(4):
        for dc in range(2):
            if ds or dc:
                peers.append(((z, (s + ds) % 4, (c + dc) % 2), ((s + 4 - ds) % 4, (c + dc) % 2)))
    return peers


class Plane:
    def __init__(self, send, recv):
        self.send, self.recv = send, recv
        self.z, self.s, self.c = place()[:3]
        self.peers = plane_peers(self.z, self.s, self.c)
        self.started = []

    def start(self, k, ref, only=range(7)):
        for i in only:
            peer = self.peers[i][0]
            mine = ref.at[self.s, self.c]
            copy = remote(mine, mine, self.send.at[k, i], self.recv.at[k, i], peer)
            copy.start()
            self.started.append(copy)

    def wait(self, k, ref, only=range(7)):
        for i in only:
            s, c = self.peers[i][1]
            slot = ref.at[s, c]
            remote(
                slot, slot, self.send.at[k, i], self.recv.at[k, i], (self.z, self.s, 1 - self.c)
            ).wait_recv()

    def finish(self):
        for copy in self.started:
            copy.wait_send()


def rounded(value):
    return value.astype(bf16).astype(f32)


def pick(value, start, size):
    full = value.shape[1]
    return pltpu.roll(value, full - start, 1)[:, :size].astype(bf16)


def halves(ref):
    parts = []
    for c in range(2):
        parts.append(ref[0, c] + ref[1, c] + ref[2, c] + ref[3, c])
    return parts


def blocks_of(ref, size, z_count):
    group = HALF // size
    lanes = ref.shape[-1]
    pieces = []
    for n in range(4 * z_count // group):
        total = None
        for m in range(group):
            z, s = (n * group + m) // 4, (n * group + m) % 4
            piece = ref[s, 0, z] + ref[s, 1, z]
            piece = jnp.concatenate([piece, jnp.zeros((8, HALF - lanes), f32)], axis=1)
            if m:
                piece = pltpu.roll(piece, m * size, 1)
            total = piece if total is None else total + piece
        pieces.append(total)
    return jnp.concatenate(pieces, axis=1)


def half_of(value, c):
    return jnp.where(c == 0, value[:, :HALF], value[:, HALF : 2 * HALF])


def mm_down(value, weight, s, z_count, size):
    total = None
    for z in range(z_count):
        term = matmul(pick(value, (4 * z + s) * size, size), weight(z))
        total = term if total is None else total + term
    return total


def own_row(value, s, c):
    row = lax.broadcasted_iota(jnp.int32, value.shape, 0)
    return jnp.sum(jnp.where(row == 2 * s + c, value, 0.0), axis=0, keepdims=True)


def as_own_row(value, s, c):
    wide = jnp.broadcast_to(value, (8, value.shape[1]))
    row = lax.broadcasted_iota(jnp.int32, wide.shape, 0)
    return jnp.where(row == 2 * s + c, wide, 0.0)


def pull_own(values_in, gain_row, incoming, s, c):
    inverse = lax.rsqrt(jnp.mean(values_in * values_in, axis=-1, keepdims=True) + norm_eps)
    scaled = incoming * gain_row
    inner = jnp.mean(scaled * values_in, axis=-1, keepdims=True)
    grad = inverse * scaled - values_in * (inverse * inverse * inverse * inner)
    return grad, own_row(incoming * values_in * inverse, s, c)


def put_blocks(ref, s, c, terms, size):
    for z, term in enumerate(terms):
        ref[s, c, z] = jnp.zeros(ref.shape[3:], f32)
        ref[s, c, z, :, :size] = term


def head_rows(width):
    lane = lax.broadcasted_iota(jnp.int32, (16, width), 1)
    row = lax.broadcasted_iota(jnp.int32, (16, width), 0)
    return (lane // HD) == row


def ffn_halves(parts):
    pieces = []
    for j in range(4):
        for c in range(2):
            pieces.append(parts[c][:, j * HALF : (j + 1) * HALF])
    return jnp.concatenate(pieces, axis=1)


class Decoder:
    (ROWS_IN, SELF_NORM, SELF_VALUES, ONE, CROSS_NORM, CROSS_ATT, FFN_NORM, TWO, TOP, QUERY) = range(10)
    INNER, PRE = 10, 14
    COUNT = 18

    def __init__(self, plane, st, gains, z_count):
        self.plane, self.st, self.gains, self.z_count = plane, st, gains, z_count
        self.s, self.c = plane.s, plane.c

    def gain(self, n):
        return self.gains[n : n + 1, :]

    def square_down(self, k, ref, value, wd, n):
        ref[self.s, self.c] = mm_down(value, lambda z: wd[n, z], self.s, self.z_count, ROWS)
        self.plane.start(k, ref)

    def square_sum(self, k, ref):
        self.plane.wait(k, ref)
        return jnp.concatenate(halves(ref), axis=1)

    def square_up(self, k, ref, value, wd, n):
        own = half_of(value, self.c).astype(bf16)
        put_blocks(
            ref, self.s, self.c, [mm_t(own, wd[n, z]) for z in range(self.z_count)], ROWS
        )
        self.plane.start(k, ref)

    def square_up_sum(self, k, ref):
        self.plane.wait(k, ref)
        return blocks_of(ref, ROWS, self.z_count)


def row_blocks(count, work):
    def body(i, carry):
        work(i, pl.ds(pl.multiple_of(i * BAND, BAND), BAND))
        return carry

    lax.fori_loop(0, count, body, 0)


def col_tiles(width, tile, work):
    def body(i, carry):
        work(pl.ds(pl.multiple_of(i * tile, tile), tile))
        return carry

    lax.fori_loop(0, width // tile, body, 0)


def wide(value):
    return value.reshape(value.shape[0] * value.shape[1] * value.shape[2], value.shape[3])


def softmax_keys(k_own, q_rows, band, block, span, live):
    scores = mm_t(k_own, q_rows) * (1.0 / math.sqrt(HD))
    count = span // BAND
    bias = [
        band[:, (block - n + count - 1) * BAND : (block - n + count) * BAND] for n in range(count)
    ]
    scores = jnp.where(live, scores + jnp.concatenate(bias, axis=0), neg_fill)
    raised = jnp.exp(scores - jnp.max(scores, axis=0, keepdims=True))
    return raised * (1.0 / jnp.sum(raised, axis=0, keepdims=True))


def own_lanes(value, t):
    lane = lax.broadcasted_iota(jnp.int32, value.shape, 1)
    return jnp.where((lane // HD) == t, value, jnp.zeros_like(value))


def attend_pair_fwd(pair, length, table_ref, q_ref, k_ref, v_ref, o_ref):
    span = k_ref.shape[0]
    at = pl.ds(pl.multiple_of(pair * 2 * HD, 2 * HD), 2 * HD)
    live = lax.broadcasted_iota(jnp.int32, (span, BAND), 0) < length
    k_all = k_ref[:, at]
    v_turned = v_ref[:, at].T
    keys = [own_lanes(k_all, t) for t in range(2)]
    bands = [bias_band(table_ref[2 * pair + t], span) for t in range(2)]
    row = lax.broadcasted_iota(jnp.int32, (2 * HD, BAND), 0)
    for block in range(span // BAND):
        rows = slice(block * BAND, (block + 1) * BAND)
        q_rows = q_ref[rows, at]
        parts = []
        for t in range(2):
            probs = softmax_keys(keys[t], q_rows, bands[t], block, span, live)
            parts.append(matmul(v_turned, probs.astype(bf16)))
        o_ref[rows, at] = jnp.where(row < HD, parts[0], parts[1]).T.astype(bf16)


def attend_pair_bwd(
    pair, length, table_ref, q_ref, k_ref, v_ref, do_ref, dq_ref, dk_ref, dv_ref, dt_ref, sums
):
    span = k_ref.shape[0]
    count = span // BAND
    scale = 1.0 / math.sqrt(HD)
    at = pl.ds(pl.multiple_of(pair * 2 * HD, 2 * HD), 2 * HD)
    live = lax.broadcasted_iota(jnp.int32, (span, BAND), 0) < length
    lane = lax.broadcasted_iota(jnp.int32, (1, 2 * HD), 1)
    row = lax.broadcasted_iota(jnp.int32, (2 * HD, BAND), 0)
    k_all = k_ref[:, at]
    k_turned = k_all.T
    v_all = v_ref[:, at]
    dks, dvs = [], []
    dqs = [[None, None] for _ in range(count)]
    for t in range(2):
        k_own = own_lanes(k_all, t)
        v_own = own_lanes(v_all, t)
        band = bias_band(table_ref[2 * pair + t], span)
        dk = jnp.zeros((span, 2 * HD), f32)
        dv = jnp.zeros((span, 2 * HD), f32)
        sums[...] = jnp.zeros_like(sums)
        for block in range(count):
            rows = slice(block * BAND, (block + 1) * BAND)
            q_rows = q_ref[rows, at]
            do_rows = do_ref[rows, at]
            probs = softmax_keys(k_own, q_rows, band, block, span, live)
            dprobs = mm_t(v_own, do_rows)
            dscore = probs * (dprobs - jnp.sum(dprobs * probs, axis=0, keepdims=True))
            for n in range(count):
                start = (block - n + count - 1) * BAND
                sums[:, start : start + BAND] += dscore[n * BAND : (n + 1) * BAND]
            dscore_b = dscore.astype(bf16)
            dv = dv + matmul(probs.astype(bf16), do_rows)
            dk = dk + matmul(dscore_b, q_rows)
            dqs[block][t] = matmul(k_turned, dscore_b)
        dks.append(dk)
        dvs.append(dv)
        dt_ref[2 * pair + t] = band_sums(sums[...], span)
    dk_ref[:, at] = (jnp.where(lane < HD, dks[0], dks[1]) * scale).astype(bf16)
    dv_ref[:, at] = jnp.where(lane < HD, dvs[0], dvs[1]).astype(bf16)
    for block in range(count):
        rows = slice(block * BAND, (block + 1) * BAND)
        value = jnp.where(row < HD, dqs[block][0], dqs[block][1]).T
        dq_ref[rows, at] = (value * scale).astype(bf16)


def forward_kernel(units, lines, z_count, *refs):
    (
        len_ref, bias_ref, bucket_ref, sq_ref, in_ref, out_ref, gains_ref, dec_ref, cot_ref, x_ref,
        in_o, out_o, x_o, q_o, k_o, v_o, att_o, hid_o, pre_o, hid2_o, enc_o, gck_o, gcv_o, wd_o,
        sq_o0, sq_o1, sq_o2, sq_o3, sq_o4, sq_o5, gain_o, st_o, gg_o, dec_o, table_ref,
        sq_w, in_w, out_w, gain_w, sq_r, in_r, out_r, gain_r,
        x_s, n_s, q_s, k_s, v_s, att_s, hid_s, pre_s, inner_s, hid2_s, enc_s, ck_s, cv_s, gains,
        gain_ref, wd, wdi, wdo, st, e_rows, e_sq, e_att, e_pre, e_out, e_inner, e_up, e_half,
        send, recv, first_send, first_recv, x_send, x_recv, d_send, d_recv, p_send, p_recv, local,
    ) = refs
    z, s, c = place()[:3]
    sibling = (z, s, 1 - c)
    sq_o = (sq_o0, sq_o1, sq_o2, sq_o3, sq_o4, sq_o5)
    n_sq, n_ff = sq_ref.shape[0], in_ref.shape[0]
    blocks = x_s.shape[0] * x_s.shape[1] // BAND
    greet_plane(z, s, c, z_count)
    plane = Plane(p_send, p_recv)
    dec = Decoder(plane, st, gains, z_count)
    length = len_ref[s]
    for n, ref in enumerate((dec_ref, cot_ref)):
        e_rows[s, c, n] = as_own_row(ref[0].astype(f32), s, c)
    row = lax.broadcasted_iota(jnp.int32, (gains_ref.shape[0], 128), 0)
    lane = lax.broadcasted_iota(jnp.int32, (gains_ref.shape[0], 128), 1)
    gain_ref[...] = lax.dot_general(
        gains_ref[...],
        jnp.where(row == lane, 1.0, 0.0),
        (((0,), (0,)), ((), ())),
        precision=highest_precision,
        preferred_element_type=f32,
    )
    plane.start(0, e_rows)

    first = []

    def to_sibling(src, dst):
        copy = remote(src, dst, first_send.at[len(first)], first_recv.at[len(first)], sibling)
        copy.start()
        first.append(copy)

    to_sibling(gain_ref, gain_r)
    to_sibling(sq_ref.at[:, :, cols(1 - c)], sq_r)
    x_copies = []
    for d in range(1, 4):
        peer = (s + d) % 4
        copy = remote(
            x_ref.at[peer], x_s.at[s], x_send.at[d - 1], x_recv.at[d - 1], (z, peer, c)
        )
        copy.start()
        x_copies.append(copy)
    mine = pltpu.make_async_copy(x_ref.at[s], x_s.at[s], local.at[0])
    mine.start()
    for n in range(n_ff):
        for j in range(4):
            to_sibling(in_ref.at[n, :, cols(1 - c, 2 * HALF * j)], in_r.at[n, j])
        to_sibling(out_ref.at[n, :, cols(1 - c)], out_r.at[n])

    def joined(own, other):
        top = jnp.where(c == 0, own, other)
        bottom = jnp.where(c == 0, other, own)
        return jnp.concatenate([top, bottom], axis=0).astype(bf16)

    gather = Gather(
        units,
        {
            "square": sq_w,
            "cols": in_w,
            "rows": out_w,
            "gain": gain_w,
            "line square": wd,
            "line cols": wdi,
            "line rows": wdo,
        },
        send,
        recv,
        z_count,
    )
    lined = Gather(lines, gather.refs, d_send, d_recv, z_count)
    first[0].wait_recv()
    gain_w[z, s] = joined(gain_ref[...], gain_r[...])
    first[1].wait_recv()
    for i, n in enumerate(ENC):
        sq_w[i, z, s, :, cols(c)] = joined(sq_ref[n, :, cols(c)], sq_r[n])
    drains = []

    def drain(src, dst):
        copy = pltpu.make_async_copy(src, dst, local.at[1 + len(drains)])
        copy.start()
        drains.append(copy)

    def done(u):
        kind, n = units[u]
        if kind == "square":
            drain(sq_w.at[n], sq_o[n])
        elif kind == "cols" and n % 4 == 3:
            drain(in_w.at[n // 4], in_o)
        elif kind == "rows" and n % 4 == 3:
            drain(out_w.at[n // 4], out_o)

    def normed(src, gain_row, dst):
        def work(i, at):
            dst[at, :] = rms_gain(src(i, at), gains[gain_row : gain_row + 1, :]).astype(bf16)

        row_blocks(blocks, work)

    def x_rows(i, at):
        return x_s[i].astype(f32)

    def start_piece():
        hot = bucket_hot(bucket_ref, bias_ref.shape[1])
        table = lax.dot_general(
            bias_ref[...],
            hot,
            (((1,), (0,)), ((), ())),
            precision=highest_precision,
            preferred_element_type=f32,
        )
        for h in range(table_ref.shape[0]):
            table_ref[h] = table[h : h + 1]
        for copy in x_copies:
            copy.wait_recv()
        mine.wait()
        drain(x_s, x_o)
        gains[...] = wide(gain_w[...]).astype(f32).T[:8]
        gain_o[...] = gains[...]
        normed(x_rows, 0, n_s)

    def square_dot(left, n, tile=256):
        def weight(at):
            return wide(sq_w[n, :, :, :, at])

        return lambda at: matmul(left[...], weight(at))

    def project(n, left, dst, out):
        dot = square_dot(left, n)

        def work(at):
            dst[:, at] = dot(at).astype(bf16)

        col_tiles(2 * HALF, 256, work)
        if out is not None:
            drain(dst, out)

    def attention(pairs):
        def body(pair, carry):
            attend_pair_fwd(pair, length, table_ref, q_s, k_s, v_s, att_s)
            return carry

        lax.fori_loop(pairs[0], pairs[1], body, 0)

    def hidden_piece():
        drain(att_s, att_o)
        dot = square_dot(att_s, 3)

        def work(at):
            hid_s[:, at] = dot(at)

        col_tiles(2 * HALF, 256, work)

        def add(i, at):
            total = hid_s[at, :] + x_rows(i, at)
            hid_s[at, :] = total
            n_s[at, :] = rms_gain(total, gains[1:2, :]).astype(bf16)

        row_blocks(blocks, add)
        drain(hid_s, hid_o)

    def ffn_piece(j):
        def work(i, carry):
            at = pl.ds(pl.multiple_of(j * 2 * HALF + i * 256, 256), 256)
            pre = matmul(n_s[...], wide(in_w[0, :, :, :, at]))
            pre_s[:, at] = pre
            inner_s[:, at] = gelu_tanh(pre).astype(bf16)
            return carry

        lax.fori_loop(0, 3, work, 0)

    def hidden_two_piece():
        drain(pre_s, pre_o)

        def work(at):
            hid2_s[:, at] = hid_s[:, at] + matmul(inner_s[...], wide(out_w[0, :, :, :, at]))

        col_tiles(2 * HALF, 256, work)
        normed(lambda i, at: hid2_s[at, :], 2, enc_s)
        drain(hid2_s, hid2_o)
        drain(enc_s, enc_o)

    def dec_start():
        plane.wait(0, e_rows)
        for n, to in ((0, Decoder.ROWS_IN), (1, Decoder.TOP)):
            total = e_rows[0, 0, n]
            for p in range(1, 8):
                total = total + e_rows[p // 2, p % 2, n]
            st[to] = total
        value = rounded(rms_gain(st[Decoder.ROWS_IN], dec.gain(3)))
        st[Decoder.SELF_NORM] = value
        drain(wd, wd_o)
        dec.square_down(1, e_sq.at[0], value, wd, 0)

    def dec_self_values():
        value = rounded(dec.square_sum(1, e_sq.at[0]))
        st[Decoder.SELF_VALUES] = value
        dec.square_down(2, e_sq.at[1], value, wd, 1)

    def dec_self_out():
        value = st[Decoder.ROWS_IN] + dec.square_sum(2, e_sq.at[1])
        st[Decoder.ONE] = value
        value = rounded(rms_gain(value, dec.gain(4)))
        st[Decoder.CROSS_NORM] = value
        dec.square_down(3, e_sq.at[2], value, wd, 2)

    def dec_query():
        st[Decoder.QUERY] = rounded(dec.square_sum(3, e_sq.at[2]))

    def dec_inner():
        own = half_of(st[Decoder.TOP], c).astype(bf16)
        put_blocks(e_inner, s, c, [mm_t(own, wdo[n]) for n in range(z_count)], 4 * ROWS)
        plane.start(7, e_inner)

    def dec_inner_end():
        plane.wait(7, e_inner)
        total = blocks_of(e_inner, 4 * ROWS, z_count)
        for j in range(4):
            st[Decoder.PRE + j] = total[:, j * 2 * HALF : (j + 1) * 2 * HALF]

    def dec_main():
        width = 2 * HALF
        scale = 1.0 / math.sqrt(HD)
        mask = head_rows(width)
        valid = lax.broadcasted_iota(jnp.int32, (1, x_s.shape[0] * BAND), 1) < length
        query = own_row(st[Decoder.QUERY], s, c)
        q_heads = jnp.where(mask, query, 0.0).astype(bf16)
        scores = jnp.where(valid, mm_t(q_heads, ck_s[...]) * scale, neg_fill)
        raised = jnp.exp(scores - jnp.max(scores, axis=-1, keepdims=True))
        probs = raised / jnp.sum(raised, axis=-1, keepdims=True)
        probs_b = probs.astype(bf16)
        att = jnp.where(mask, matmul(probs_b, cv_s[...]), 0.0)
        e_att[s, c] = rounded(jnp.sum(att, axis=0, keepdims=True))
        plane.start(4, e_att)
        plane.wait(4, e_att)
        value = jnp.concatenate([e_att[p // 2, p % 2] for p in range(8)], axis=0)
        st[Decoder.CROSS_ATT] = value
        dec.square_down(5, e_sq.at[3], value, wd, 3)
        two = st[Decoder.ONE] + dec.square_sum(5, e_sq.at[3])
        value = rounded(rms_gain(two, dec.gain(5)))
        st[Decoder.FFN_NORM] = value
        e_pre[s, c] = mm_down(value, lambda n: wdi[n], s, z_count, ROWS)
        plane.start(6, e_pre, SAME_CORE)
        plane.wait(6, e_pre, SAME_CORE)
        inner, slope = gelu_both(e_pre[0, c] + e_pre[1, c] + e_pre[2, c] + e_pre[3, c])
        g_inner = jnp.concatenate([half_of(st[Decoder.PRE + j], c) for j in range(4)], axis=1)
        g_pre = rounded(g_inner * slope)
        own = g_pre.astype(bf16)
        put_blocks(e_up.at[0], s, c, [mm_t(own, wdi[n]) for n in range(z_count)], ROWS)
        plane.start(9, e_up.at[0])
        e_half[c, 0] = rounded(inner)
        e_half[c, 1] = g_pre
        mine = e_half.at[c]
        swap = remote(mine, mine, p_send.at[11, 0], p_recv.at[11, 0], sibling)
        swap.start()
        g_norm = dec.square_up_sum(9, e_up.at[0])
        grad, gain = pull_own(two, dec.gain(5), g_norm, s, c)
        gg_o[...] = jnp.zeros_like(gg_o)
        gg_o[5:6, :] = gain
        g_two = st[Decoder.TOP] + grad
        st[Decoder.TWO] = g_two
        dec.square_up(10, e_up.at[1], g_two, wd, 3)
        other = e_half.at[1 - c]
        remote(other, other, p_send.at[11, 0], p_recv.at[11, 0], sibling).wait_recv()
        inner = ffn_halves([e_half[0, 0], e_half[1, 0]])
        g_pre = ffn_halves([e_half[0, 1], e_half[1, 1]])
        for j in range(4):
            st[Decoder.INNER + j] = inner[:, j * width : (j + 1) * width]
            st[Decoder.PRE + j] = g_pre[:, j * width : (j + 1) * width]
        e_out[s, c] = mm_down(inner, lambda n: wdo[n], s, z_count, 4 * ROWS)
        g_att = own_row(rounded(dec.square_up_sum(10, e_up.at[1])), s, c)
        plane.start(8, e_out)
        g_heads = jnp.where(mask, g_att, 0.0).astype(bf16)
        g_probs = mm_t(g_heads, cv_s[...])
        g_scores = probs * (g_probs - jnp.sum(g_probs * probs, axis=-1, keepdims=True))
        row = lax.broadcasted_iota(jnp.int32, g_scores.shape, 0)
        g_scores_b = jnp.where(row < H, g_scores, 0.0).astype(bf16)
        g_query = jnp.where(mask, matmul(g_scores_b, ck_s[...]), 0.0)
        g_query = jnp.sum(g_query, axis=0, keepdims=True) * scale
        st[Decoder.QUERY] = as_own_row(rounded(g_query), s, c)
        live_b = jnp.where(row < H, probs_b.astype(f32), 0.0).astype(bf16)
        n_s[...] = (mm_outer(g_scores_b, q_heads) * scale).astype(bf16)
        drain(n_s, gck_o)
        cv_s[...] = mm_outer(live_b, g_heads).astype(bf16)
        drain(cv_s, gcv_o)
        st_o[...] = st[...]
        plane.wait(8, e_out)
        out = two + jnp.concatenate(halves(e_out), axis=1)
        dec_o[...] = jnp.broadcast_to(own_row(out, s, c), dec_o.shape)
        swap.wait_send()

    pieces = {
        ("gain", 0): [start_piece],
        ("square", 0): [lambda: project(0, n_s, q_s, q_o)],
        ("square", 1): [lambda: project(1, n_s, k_s, k_o)],
        ("square", 2): [lambda: project(2, n_s, v_s, v_o), dec_start, lambda: attention((0, 2))],
        ("square", 3): [lambda: attention((2, 4)), dec_self_values],
        ("cols", 0): [lambda: attention((4, 6)), dec_self_out],
        ("cols", 1): [hidden_piece, lambda: ffn_piece(0), dec_query],
        ("cols", 2): [lambda: ffn_piece(1), lambda: ffn_piece(2)],
        ("cols", 3): [lambda: ffn_piece(3)],
        ("rows", 0): [dec_inner],
        ("rows", 2): [dec_inner_end],
        ("rows", 3): [hidden_two_piece],
        ("square", 4): [lambda: project(4, enc_s, ck_s, None)],
        ("square", 5): [lambda: project(5, enc_s, cv_s, None), dec_main],
    }
    k = 2
    there, early = gather.lag(z_count + 2), gather.lag(z_count + 1)
    for t in range(len(units) + there):
        gather.tick(t, done)
        if t >= 2:
            lined.tick(t - 2, done)
        if t == 1:
            for i, n in enumerate(DEC):
                wd[i, z] = joined(sq_ref[n, :, cols(c)], sq_r[n])
            for n in range(n_ff):
                for j in range(4):
                    first[k].wait_recv()
                    k += 1
                    at = cols(c, 2 * HALF * j)
                    value = joined(in_ref[n, :, at], in_r[n, j])
                    if n == 0:
                        in_w[n, z, s, :, at] = value
                    else:
                        wdi[z, :, j * HALF : (j + 1) * HALF] = value
                first[k].wait_recv()
                k += 1
                value = joined(out_ref[n, :, cols(c)], out_r[n])
                if n == 0:
                    out_w[n, z, s, :, cols(c)] = value
                else:
                    wdo[z] = value
        ready = 0 if t == early else t - there
        if ready > 0 or t == early:
            for piece in pieces.get(units[ready], ()):
                piece()
    gather.finish()
    lined.finish()
    plane.finish()
    for copy in first:
        copy.wait_send()
    for copy in x_copies:
        copy.wait_send()
    for copy in drains:
        copy.wait()


def bucket_hot(bucket_ref, count):
    row = lax.broadcasted_iota(jnp.int32, (count, bucket_ref.shape[1]), 0)
    return jnp.where(bucket_ref[...] == row, 1.0, 0.0)


def greet_plane(z, s, c, z_count):
    barrier = pltpu.get_barrier_semaphore()
    for d in range(1, z_count):
        peer = ((z + d) % z_count, s, c)
        pl.semaphore_signal(barrier, 1, device_id=peer, device_id_type=MESH_ID)
    for peer, _ in plane_peers(z, s, c):
        pl.semaphore_signal(barrier, 1, device_id=peer, device_id_type=MESH_ID)
    pl.semaphore_wait(barrier, z_count - 1 + 7)


def forward(
    lengths, rel_bias, buckets, square, ffn_in, ffn_out, gains, dec_in, cotangent, x, z_count
):
    n_sq, n_ff = square.shape[0], ffn_in.shape[0]
    order = [("gain", 0)]
    order += [("square", n) for n in (0, 1, 2)]
    lines = [("line square", n) for n in range(4)]
    lines += [("line cols", n) for n in range(4)] + [("line rows", n) for n in range(4)]
    plain = [("square", 3)] + [("cols", n) for n in range(4)] + [("rows", n) for n in range(4)]
    plain += [("square", n) for n in (4, 5)]
    order = order + plain
    blocks, band, width = x.shape
    span = blocks * band
    hidden_units = 8 * HALF
    sq_s = (len(ENC), z_count, 4, ROWS, width)
    in_s = (1, z_count, 4, ROWS, hidden_units)
    out_s = (1, z_count, 4, 4 * ROWS, width)
    gain_s = (z_count, 4, ROWS, 128)
    wd_s = (len(DEC), z_count, ROWS, HALF)
    firsts = 2 + 5 * n_ff
    slots = 2 * (z_count - 1) + 4
    vmem = pl.BlockSpec(memory_space=pltpu.VMEM)
    hbm = pl.BlockSpec(memory_space=pltpu.HBM)
    token = ((span, width), bf16)
    token_f = ((span, width), f32)
    st_s = ((Decoder.COUNT, 8, width), f32)
    outs = [(in_s[1:], bf16), (out_s[1:], bf16)]
    outs += [(x.shape, bf16), token, token, token, token, token_f]
    outs += [((span, hidden_units), f32), token_f, token, token, token, (wd_s, bf16)]
    outs += [(sq_s[1:], bf16)] * len(ENC)
    small = [((8, width), f32), st_s, ((8, width), f32), ((8, width), f32)]
    small += [((rel_bias.shape[0], 1, 2 * span), f32)]
    scratch = [(sq_s, bf16), (in_s, bf16), (out_s, bf16), (gain_s, bf16)]
    scratch += [((n_sq, ROWS // 2, HALF), f32), ((n_ff, 4, ROWS // 2, HALF), f32)]
    scratch += [((n_ff, 2 * ROWS, HALF), f32), ((ROWS // 2, 128), f32)]
    scratch += [(x.shape, bf16), token, token, token, token, token, token_f]
    scratch += [((span, hidden_units), f32), ((span, hidden_units), bf16), token_f]
    scratch += [token, token, token, ((8, width), f32)]
    scratch += [((gains.shape[1], 128), f32)]
    scratch += [(wd_s, bf16), ((z_count, ROWS, 4 * HALF), bf16), ((z_count, 4 * ROWS, HALF), bf16)]
    scratch += [st_s, ((4, 2, 2, 8, width), f32), ((4, 4, 2, 8, HALF), f32)]
    scratch += [((4, 2, 1, width), f32), ((4, 2, 8, 4 * HALF), f32), ((4, 2, 8, HALF), f32)]
    scratch += [((4, 2, z_count, 8, 256), f32), ((2, 4, 2, z_count, 8, 128), f32)]
    scratch += [((2, 2, 8, 4 * HALF), f32)]
    dma = pltpu.SemaphoreType.DMA
    return pl.pallas_call(
        functools.partial(forward_kernel, order, lines, z_count),
        out_shape=[jax.ShapeDtypeStruct(*o) for o in outs + small],
        in_specs=[pl.BlockSpec(memory_space=pltpu.SMEM)] + [vmem] * 8 + [hbm],
        out_specs=[hbm] * len(outs) + [vmem] * len(small),
        scratch_shapes=[pltpu.VMEM(*o) for o in scratch]
        + [dma((len(order), slots)), dma((len(order), slots)), dma((firsts,)), dma((firsts,))]
        + [dma((3,)), dma((3,)), dma((len(lines), slots)), dma((len(lines), slots))]
        + [dma((12, 7)), dma((12, 7)), dma((40,))],
        compiler_params=pltpu.CompilerParams(
            collective_id=0, has_side_effects=True, vmem_limit_bytes=62 * MIB
        ),
        name="forward",
    )(lengths, rel_bias, buckets, square, ffn_in, ffn_out, gains, dec_in, cotangent, x)


class Scatter:
    def __init__(self, units, sources, bufs, sems, z_count, put):
        self.units, self.sources, self.z_count, self.put = units, sources, z_count, put
        self.r0, self.r1, self.r2, self.r3, self.fin, self.sib = bufs
        self.send, self.recv = sems
        self.where = place()
        self.started = []
        self.lent = {}
        self.at = [0] * 6

    def go(self, u, slot, src, dst, peer):
        copy = remote(src, dst, self.send.at[u, slot], self.recv.at[u, slot], peer)
        copy.start()
        return copy

    def got(self, u, slot, ref):
        z, s, c = self.where[:3]
        remote(ref, ref, self.send.at[u, slot], self.recv.at[u, slot], (z, s, 1 - c)).wait_recv()

    def view(self, u, c, z=slice(None), s=slice(None)):
        kind, n = self.sources[u]
        if kind == "rows":
            return unit_view(kind, n, self.refs[kind], z, s, c)
        return self.refs["slots"].at[n, z, s, :, cols(c)]

    def c_start(self, u):
        z, s, c = self.where[:3]
        self.lent[u] = self.go(u, 0, self.view(u, 1 - c), self.r0.at[u], (z, s, 1 - c))

    def b_start(self, u):
        z, s, c, first, second, both = self.where
        self.got(u, 0, self.r0.at[u])

        def body(i, carry):
            n, m = i // 4, i % 4
            own = self.view(u, c, n, m)[...]
            total = own.astype(f32) + self.r0[u, n, m].astype(f32)
            self.r0[u, n, m] = total.astype(bf16)
            return carry

        lax.fori_loop(0, 4 * self.z_count, body, 0, unroll=4)
        self.started.append(self.go(u, 1, self.r0.at[u, :, second], self.r1.at[u, 0], (z, second, c)))
        self.started.append(self.go(u, 2, self.r0.at[u, :, both], self.r1.at[u, 1], (z, second, c)))
        self.lent.pop(u).wait_send()

    def a_start(self, u):
        z, s, c, first, second, both = self.where
        self.got(u, 2, self.r1.at[u, 1])
        for n in range(self.z_count):
            total = self.r0[u, n, first].astype(f32) + self.r1[u, 1, n].astype(f32)
            self.r1[u, 1, n] = total.astype(bf16)
        self.started.append(self.go(u, 3, self.r1.at[u, 1], self.r2.at[u], (z, first, c)))
        self.got(u, 1, self.r1.at[u, 0])
        for n in range(self.z_count):
            total = self.r0[u, n, s].astype(f32) + self.r1[u, 0, n].astype(f32)
            self.r1[u, 0, n] = total.astype(bf16)

    def z_start(self, u):
        z, s, c = self.where[:3]
        self.got(u, 3, self.r2.at[u])
        for n in range(self.z_count):
            total = self.r1[u, 0, n].astype(f32) + self.r2[u, n].astype(f32)
            self.r2[u, n] = total.astype(bf16)
        for d in range(1, self.z_count):
            to = (z + d) % self.z_count
            self.started.append(
                self.go(u, 3 + d, self.r2.at[u, to], self.r3.at[u, d - 1], (to, s, c))
            )

    def f_start(self, u):
        z, s, c = self.where[:3]
        total = self.r2[u, z].astype(f32)
        for d in range(1, self.z_count):
            self.got(u, 3 + d, self.r3.at[u, d - 1])
            total = total + self.r3[u, d - 1].astype(f32)
        self.fin[u] = total
        self.count(total)
        kind, n = self.units[u]
        if kind == "rows":
            if n % 2 == 1:
                @pl.when(c != n // 2)
                def _():
                    pair = pl.ds(u - 1, 2)
                    self.go(u, 7, self.fin.at[pair], self.sib.at[pair], (z, s, 1 - c))
        else:
            rows = pl.ds(pl.multiple_of((1 - c) * (ROWS // 2), 8), ROWS // 2)
            self.started.append(
                self.go(
                    u, 7, self.fin.at[u, rows], self.sib.at[u, pl.ds(0, ROWS // 2)], (z, s, 1 - c)
                )
            )

    def finish_unit(self, u):
        z, s, c = self.where[:3]
        kind, n = self.units[u]
        if kind == "rows":
            if n % 2 == 1:

                @pl.when(c == n // 2)
                def _():
                    self.got(u, 7, self.sib.at[pl.ds(u - 1, 2)])
                    for k in range(2):
                        self.put(kind, k, c, self.fin[u - 1 + k])
                        self.put(kind, k, 1 - c, self.sib[u - 1 + k])

                @pl.when(c != n // 2)
                def _():
                    pair = self.fin.at[pl.ds(u - 1, 2)]
                    remote(
                        pair, pair, self.send.at[u, 7], self.recv.at[u, 7], (z, s, 1 - c)
                    ).wait_send()
        else:
            self.got(u, 7, self.sib.at[u, pl.ds(0, ROWS // 2)])
            rows = pl.ds(pl.multiple_of(c * (ROWS // 2), 8), ROWS // 2)
            self.put(kind, n, c, self.fin[u, rows])
            self.put(kind, n, 1 - c, self.sib[u, : ROWS // 2])

    def reach(self, limits):
        steps = (self.c_start, self.b_start, self.a_start, self.z_start, self.f_start)
        for n, step in enumerate(steps + (self.finish_unit,)):
            while self.at[n] <= min(limits[n], len(self.units) - 1):
                step(self.at[n])
                self.at[n] += 1

    def tick(self, t):
        self.reach([t - lag for lag in (0, 1, 3, 5, 7, 8)])

    def flush(self):
        self.reach([len(self.units) - 1] + [n - 1 for n in self.at[:-1]])

    def finish(self):
        for copy in self.started:
            copy.wait_send()


def pull_rows(values_in, gain_row, incoming):
    inverse = lax.rsqrt(jnp.mean(values_in * values_in, axis=-1, keepdims=True) + norm_eps)
    scaled = incoming * gain_row
    inner = jnp.mean(scaled * values_in, axis=-1, keepdims=True)
    grad = inverse * scaled - values_in * (inverse * inverse * inverse * inner)
    return grad, jnp.sum(incoming * values_in * inverse, axis=0, keepdims=True)


def gelu_both(values_in):
    square = values_in * values_in
    slope = 0.7978845608028654
    bend = jnp.tanh(slope * values_in * (1.0 + 0.044715 * square))
    value = 0.5 * values_in * (1.0 + bend)
    grad = 0.5 * (1.0 + bend) + 0.5 * values_in * (1.0 - bend * bend) * slope * (
        1.0 + 3.0 * 0.044715 * square
    )
    return value, grad


def backward_kernel(z_count, *refs):
    (
        len_ref, table_ref, gain_ref, bucket_ref, w0, w1, w2, w3, w7, w8, win, wout,
        x_i, q_i, k_i, v_i, att_i, hid_i, pre_i, hid2_i, enc_i, gck_i, gcv_i, wd_i, st, gg_i,
        sq_o, in_o, out_o, x_o, own_o, bias_o, norm_o,
        slots, d_out, r0, r1, r2, r3, fin, sib,
        wbuf, x_s, q_s, k_s, v_s, att_s, enc_s, gck_s, gcv_s, hid_s, hid2_s, pre_s,
        gh, gh_b, acc, inner_s, gpre_s, turned, gatt, gq, gk, gv, gx, gx_r,
        wd, e_q, e_up, left_w, left_r, right_r, acc_one,
        sums, dt_o, gg_o, ss, e_small, z_small, e_sq, z_sq,
        send, recv, w_sem, p_sem, a_sem, x_send, x_recv, o_sem, p_send, p_recv, z_send, z_recv, t_send, t_recv,
    ) = refs
    z, s, c = place()[:3]
    blocks = x_s.shape[0]
    width = 2 * HALF

    loads = {}
    for n, (src, dst) in enumerate(
        (
            (enc_i, enc_s), (gck_i, gck_s), (gcv_i, gcv_s), (hid2_i, hid2_s), (hid_i, hid_s),
            (att_i, att_s), (q_i, q_s), (k_i, k_s), (v_i, v_s), (x_i, x_s), (wd_i, wd),
        )
    ):
        copy = pltpu.make_async_copy(src, dst, a_sem.at[n])
        copy.start()
        loads[n] = copy
    tiles = [w7, w8]
    for j in range(4):
        tiles.append(wout.at[pl.ds(j * width, width)])
        tiles.append(win.at[:, pl.ds(j * width, width)])
    tiles += [w3, w0, w1, w2]
    w_loads = {}

    def fetch(n):
        if n < len(tiles):
            copy = pltpu.make_async_copy(tiles[n], wbuf.at[n % 4], w_sem.at[n])
            copy.start()
            w_loads[n] = copy

    p_loads = {}

    def fetch_pre(j):
        if j < 4:
            copy = pltpu.make_async_copy(
                pre_i.at[:, pl.ds(j * width, width)], pre_s.at[j % 2], p_sem.at[j]
            )
            copy.start()
            p_loads[j] = copy

    for n in range(4):
        fetch(n)
    fetch_pre(0)
    fetch_pre(1)
    greet_plane(z, s, c, z_count)
    plane = Plane(p_send, p_recv)
    dec = Decoder(plane, st, gain_ref, z_count)
    e_q[s, c] = st[Decoder.QUERY]
    plane.start(0, e_q)
    z_copies = []

    def dec_query():
        plane.wait(0, e_q)
        value = e_q[0, 0]
        for p in range(1, 8):
            value = value + e_q[p // 2, p % 2]
        acc_one[1] = value
        loads[10].wait()
        dec.square_up(1, e_up.at[0], value, wd, 2)

    def dec_one():
        grad, gain = pull_own(st[Decoder.ONE], dec.gain(4), dec.square_up_sum(1, e_up.at[0]), s, c)
        gg_o[4:5, :] += gain
        value = rounded(st[Decoder.TWO] + grad)
        acc_one[0] = value
        dec.square_up(2, e_up.at[1], value, wd, 1)

    def dec_self():
        value = rounded(dec.square_up_sum(2, e_up.at[1]))
        dec.square_up(3, e_up.at[2], value, wd, 0)
        rights = [value, acc_one[0], acc_one[1], rounded(st[Decoder.TWO])]
        rights += [st[Decoder.PRE + j] for j in range(4)] + [st[Decoder.TOP], jnp.zeros_like(value)]
        right_r[z] = jnp.concatenate(rights, axis=0).astype(bf16)
        lefts = [st[n] for n in range(Decoder.SELF_NORM, Decoder.SELF_VALUES + 1)]
        lefts += [st[n] for n in range(Decoder.CROSS_NORM, Decoder.FFN_NORM + 1)]
        lefts = jnp.concatenate(lefts + [jnp.zeros_like(value)], axis=0).astype(bf16)
        row = lax.broadcasted_iota(jnp.int32, (width, 128), 0)
        lane = lax.broadcasted_iota(jnp.int32, (width, 128), 1)
        share = ROWS // 2
        hidden_at = (2 * s + c) * 4 * share
        hidden_pick = jnp.where((row == hidden_at + lane) & (lane < 4 * share), 1.0, 0.0)
        for to in range(z_count):
            at = (to * 8 + 2 * s + c) * share
            chosen = jnp.where((row == at + lane) & (lane < share), 1.0, 0.0).astype(bf16)
            inner = jnp.concatenate([st[Decoder.INNER + to], jnp.zeros_like(value)], axis=0)
            left_w[to] = jnp.concatenate(
                [
                    matmul(lefts, chosen).astype(bf16),
                    matmul(inner.astype(bf16), hidden_pick.astype(bf16)).astype(bf16),
                ],
                axis=0,
            )
        k = 0
        for d in range(1, z_count):
            to = (z + d) % z_count
            for src, dst in ((right_r.at[z], right_r.at[z]), (left_w.at[to], left_r.at[z])):
                copy = remote(src, dst, z_send.at[k], z_recv.at[k], (to, s, c))
                copy.start()
                z_copies.append(copy)
                k += 1
        left_r[z] = left_w[z]

    def dec_last():
        _, gain = pull_own(
            st[Decoder.ROWS_IN], dec.gain(3), dec.square_up_sum(3, e_up.at[2]), s, c
        )
        gg_o[3:4, :] += gain

    def dec_grads():
        for copy in z_copies:
            copy.wait()
        lefts = [left_r[n].astype(f32) for n in range(z_count)]
        rights = [right_r[n].astype(f32) for n in range(z_count)]

        def gathered(parts, n):
            return jnp.concatenate([p[8 * n : 8 * n + 8] for p in parts], axis=0).astype(bf16)

        share = ROWS // 2
        for n in range(4):
            value = mm_outer(gathered(lefts, n), gathered(rights, n))[:share]
            count(value)
            sq_o[DEC[n]] = value
        for j in range(4):
            value = mm_outer(gathered(lefts, 4), gathered(rights, 4 + j))[:share]
            count(value)
            in_o[1, :, j * width : (j + 1) * width] = value
        value = mm_outer(gathered(lefts, 6), gathered(rights, 8))[: 4 * share]
        count(value)
        out_o[1] = value

    z_started = []

    def line_start(k, ref):
        for d in range(1, z_count):
            mine = ref.at[z]
            copy = remote(
                mine, mine, t_send.at[k, d - 1], t_recv.at[k, d - 1], ((z + d) % z_count, s, c)
            )
            copy.start()
            z_started.append(copy)

    def line_sum(k, ref):
        for d in range(1, z_count):
            slot = ref.at[(z + z_count - d) % z_count]
            remote(slot, slot, t_send.at[k, d - 1], t_recv.at[k, d - 1], (z, s, 1 - c)).wait_recv()
        total = ref[0]
        for n in range(1, z_count):
            total = total + ref[n]
        return total

    def plane_sum(k, ref):
        plane.wait(k, ref)
        total = ref[0, 0]
        for p in range(1, 8):
            total = total + ref[p // 2, p % 2]
        return total

    def small_start():
        offsets = dt_o[...].reshape(dt_o.shape[0], dt_o.shape[2])
        hot = bucket_hot(bucket_ref, 128)
        row = lax.broadcasted_iota(jnp.int32, (16, dt_o.shape[0]), 0)
        lane = lax.broadcasted_iota(jnp.int32, (16, dt_o.shape[0]), 1)
        padded = lax.dot_general(
            jnp.where(row == lane, 1.0, 0.0),
            offsets,
            (((1,), (0,)), ((), ())),
            precision=highest_precision,
            preferred_element_type=f32,
        )
        totals = lax.dot_general(
            padded,
            hot,
            (((1,), (1,)), ((), ())),
            precision=highest_precision,
            preferred_element_type=f32,
        )
        pieces = [gg_o[...]] + [totals[8 * n : 8 * n + 8] for n in range(2)]
        e_small[s, c] = jnp.concatenate(pieces, axis=1)
        plane.start(4, e_small)

    def small_line():
        z_small[z] = plane_sum(4, e_small)
        line_start(0, z_small)

    def small_end():
        total = line_sum(0, z_small)
        gg_o[...] = total[:, :width]
        own_o[...] = pltpu.roll(total[:, :width], width - (z * 8 + 2 * s + c) * (ROWS // 2), 1)[
            :, :128
        ]
        parts = [total[:, width + 128 * n : width + 128 * (n + 1)] for n in range(2)]
        bias_o[...] = jnp.concatenate(parts, axis=0)

    def norm_start():
        e_sq[s, c] = ss[:, :128] + ss[:, 128:256] + ss[:, 256:]
        plane.start(5, e_sq)

    def norm_end():
        z_sq[z] = plane_sum(5, e_sq)
        line_start(1, z_sq)
        rest = jnp.sum(gg_o[...] * gg_o[...]) + jnp.sum(bias_o[...] * bias_o[...])
        total = jnp.sum(line_sum(1, z_sq)) + rest
        norm_o[0, 0] = jnp.max(jnp.sqrt(jnp.full((8, 128), total, f32)))

    units = [("square", 7), ("square", 8)] + [("cols", j) for j in range(4)] + [("square", 3)]
    units += [("rows", n) for n in range(4)] + [("heads", m) for m in range(3)]
    sources, held = [], 0
    for kind, n in units:
        if kind == "rows":
            sources.append((kind, n))
        else:
            sources.append(("slot", held % 3))
            held += 1

    def count(value):
        squares = value * value
        total = squares[:8]
        for n in range(8, value.shape[0], 8):
            total = total + squares[n : n + 8]
        for n in range(0, value.shape[1], HALF):
            ss[...] += total[:, n : n + HALF]

    def put(kind, n, side, value):
        if kind == "square":
            sq_o[n, :, cols(side)] = value
        elif kind == "cols":
            in_o[0, :, cols(side, n * width)] = value
        elif kind == "rows":
            out_o[0, n * ROWS : (n + 1) * ROWS, cols(side)] = value
        else:
            at = pl.ds(pl.multiple_of((2 * n + side) * 128, 128), 128)
            for t in range(3):
                sq_o[t, :, at] = value[:, t * 128 : (t + 1) * 128]

    scatter = Scatter(units, sources, (r0, r1, r2, r3, fin, sib), (send, recv), z_count, put)
    scatter.count = count
    scatter.refs = {"slots": slots, "rows": d_out}

    def turn(src):
        def body(i, carry):
            at = pl.ds(pl.multiple_of(i * 256, 256), 256)
            turned[at, :] = src[:, at].T
            return carry

        lax.fori_loop(0, 3, body, 0)

    def grad_to_slot(n, right):
        def work(at):
            value = matmul(turned[...], right[:, at]).astype(bf16)
            slots[n, :, :, :, at] = value.reshape(z_count, 4, ROWS, 256)

        col_tiles(width, 256, work)

    def back(left, n, dst, add):
        w_loads[n].wait()

        def work(at):
            value = mm_t(left[...], wbuf[n % 4, at, :])
            if add:
                value = value + dst[:, at]
            dst[:, at] = value

        col_tiles(width, 256, work)
        fetch(n + 4)

    gg_o[...] = gg_i[...]
    ss[...] = jnp.zeros_like(ss)
    loads[0].wait()
    loads[1].wait()
    turn(enc_s)
    grad_to_slot(0, gck_s)
    scatter.tick(0)
    dec_query()
    loads[2].wait()
    grad_to_slot(1, gcv_s)
    scatter.tick(1)
    back(gck_s, 0, acc, False)
    back(gcv_s, 1, acc, True)
    loads[3].wait()
    loads[4].wait()

    def pull_hid2(i, at):
        grad, gain = pull_rows(hid2_s[at, :], gain_ref[2:3, :], acc[at, :])
        gh[at, :] = grad
        gh_b[at, :] = grad.astype(bf16)
        gg_o[2:3, :] += gain
        enc_s[at, :] = rms_gain(hid_s[at, :], gain_ref[1:2, :]).astype(bf16)

    dec_one()
    row_blocks(blocks, pull_hid2)
    turn(enc_s)

    for j in range(4):
        p_loads[j].wait()
        w_loads[2 + 2 * j].wait()

        def hidden_tile(at):
            value, slope = gelu_both(pre_s[j % 2, :, at])
            inner_s[:, at] = value.astype(bf16)
            grad = mm_t(gh_b[...], wbuf[(2 + 2 * j) % 4, at, :])
            gpre_s[:, at] = (grad * slope).astype(bf16)

        col_tiles(width, 256, hidden_tile)
        fetch(6 + 2 * j)
        fetch_pre(j + 2)
        grad_to_slot((2 + j) % 3, gpre_s)
        scatter.tick(2 + j)

        def out_rows(i, carry):
            at = pl.ds(pl.multiple_of(i * HALF, HALF), HALF)
            value = mm_outer(inner_s[:, at], gh_b[...]).astype(bf16)
            d_out[0, j, pl.ds(2 * i, 2)] = value.reshape(2, 4 * ROWS, width)
            return carry

        lax.fori_loop(0, 2, out_rows, 0)
        back(gpre_s, 3 + 2 * j, acc, j > 0)
        if j < 2:
            (dec_self, dec_last)[j]()

    loads[5].wait()

    def pull_hid(i, at):
        grad, gain = pull_rows(hid_s[at, :], gain_ref[1:2, :], acc[at, :])
        total = gh[at, :] + grad
        gh[at, :] = total
        gh_b[at, :] = total.astype(bf16)
        gg_o[1:2, :] += gain

    row_blocks(blocks, pull_hid)
    turn(att_s)
    grad_to_slot(0, gh_b)
    scatter.tick(6)
    w_loads[10].wait()

    def attended_grad(at):
        gatt[:, at] = mm_t(gh_b[...], wbuf[10 % 4, at, :]).astype(bf16)

    col_tiles(width, 256, attended_grad)
    for n in (6, 7, 8, 9):
        loads[n].wait()

    def x_norm(i, at):
        enc_s[at, :] = rms_gain(x_s[i].astype(f32), gain_ref[0:1, :]).astype(bf16)

    row_blocks(blocks, x_norm)
    turn(enc_s)
    scatter.tick(7)

    def pair_grads(pairs):
        def body(pair, carry):
            attend_pair_bwd(
                pair, len_ref[s], table_ref, q_s, k_s, v_s, gatt, gq, gk, gv, dt_o, sums
            )
            return carry

        lax.fori_loop(pairs[0], pairs[1], body, 0)

    def heads_to_slot(m, n):
        for t, right in enumerate((gq, gk, gv)):
            value = matmul(turned[...], right[:, m * 256 : (m + 1) * 256]).astype(bf16)
            value = value.reshape(z_count, 4, ROWS, 256)
            slots[n, :, :, :, t * 128 : (t + 1) * 128] = value[..., :128]
            slots[n, :, :, :, HALF + t * 128 : HALF + (t + 1) * 128] = value[..., 128:]

    pair_grads((0, 1))
    scatter.tick(8)
    pair_grads((1, 2))
    heads_to_slot(0, 1)
    scatter.tick(9)
    pair_grads((2, 3))
    scatter.tick(10)
    pair_grads((3, 4))
    heads_to_slot(1, 2)
    scatter.tick(11)
    pair_grads((4, 5))
    scatter.tick(12)
    pair_grads((5, 6))
    heads_to_slot(2, 0)
    scatter.tick(13)
    back(gq, 11, acc, False)
    scatter.flush()
    back(gk, 12, acc, True)
    back(gv, 13, acc, True)

    def pull_x(i, at):
        grad, gain = pull_rows(x_s[i].astype(f32), gain_ref[0:1, :], acc[at, :])
        gx[i] = (gh[at, :] + grad).astype(bf16)
        gg_o[0:1, :] += gain

    row_blocks(blocks, pull_x)
    small_start()
    scatter.flush()
    x_copies = []
    for d in range(1, 4):
        peer = (s + d) % 4
        copy = remote(
            gx.at[peer], gx_r.at[s], x_send.at[d - 1], x_recv.at[d - 1], (z, peer, c)
        )
        copy.start()
        x_copies.append(copy)
    dec_grads()
    small_line()
    scatter.flush()
    gx_r[s] = gx[s]
    scatter.flush()
    small_end()
    norm_start()
    scatter.flush()
    norm_end()
    for copy in x_copies:
        copy.wait()

    copy = pltpu.make_async_copy(gx_r, x_o, o_sem.at[0])
    copy.start()
    scatter.finish()
    plane.finish()
    for sent in z_started:
        sent.wait_send()
    copy.wait()


def backward(lengths, table, gain, buckets, weights, win, wout, acts, small, z_count):
    x = acts[0]
    blocks, band, width = x.shape
    span = blocks * band
    vmem = pl.BlockSpec(memory_space=pltpu.VMEM)
    hbm = pl.BlockSpec(memory_space=pltpu.HBM)
    n = 14
    token = ((span, width), bf16)
    token_f = ((span, width), f32)
    scratch = [((3, z_count, 4, ROWS, width), bf16), ((1, z_count, 4, 4 * ROWS, width), bf16)]
    scratch += [((n, z_count, 4, ROWS, HALF), bf16), ((n, 2, z_count, ROWS, HALF), bf16)]
    scratch += [((n, z_count, ROWS, HALF), bf16), ((n, z_count - 1, ROWS, HALF), bf16)]
    scratch += [((n, ROWS, HALF), f32), ((n, ROWS, HALF), f32)]
    scratch += [((4, width, width), bf16), (x.shape, bf16)] + [token] * 7 + [token_f] * 2
    scratch += [((2, span, width), f32), token_f, token, token_f, token, token]
    scratch += [((width, span), bf16)] + [token] * 4 + [(x.shape, bf16)] * 2
    scratch += [((len(DEC), z_count, ROWS, HALF), bf16), ((4, 2, 8, width), f32)]
    scratch += [((3, 4, 2, z_count, 8, 128), f32), ((z_count, 64, 128), bf16)]
    scratch += [((z_count, 64, 128), bf16), ((z_count, 80, width), bf16), ((2, 8, width), f32)]
    scratch += [((BAND, 2 * span), f32), (table.shape, f32), ((8, width), f32), ((8, HALF), f32)]
    scratch += [((4, 2, 8, width + 256), f32), ((z_count, 8, width + 256), f32)]
    scratch += [((4, 2, 8, 128), f32), ((z_count, 8, 128), f32)]
    dma = pltpu.SemaphoreType.DMA
    return pl.pallas_call(
        functools.partial(backward_kernel, z_count),
        out_shape=[
            jax.ShapeDtypeStruct((10, ROWS // 2, width), f32),
            jax.ShapeDtypeStruct((2, ROWS // 2, 4 * width), f32),
            jax.ShapeDtypeStruct((2, 2 * ROWS, width), f32),
            jax.ShapeDtypeStruct(x.shape, bf16),
            jax.ShapeDtypeStruct((8, 128), f32),
            jax.ShapeDtypeStruct((16, 128), f32),
            jax.ShapeDtypeStruct((1, 1), f32),
        ],
        in_specs=[pl.BlockSpec(memory_space=pltpu.SMEM)] + [vmem] * 3 + [hbm] * 20 + [vmem] * 2,
        out_specs=[vmem] * 3 + [hbm] + [vmem] * 2 + [pl.BlockSpec(memory_space=pltpu.SMEM)],
        scratch_shapes=[pltpu.VMEM(*o) for o in scratch]
        + [dma((n, 8)), dma((n, 8)), dma((n,)), dma((4,)), dma((11,)), dma((3,)), dma((3,))]
        + [dma((1,)), dma((6, 7)), dma((6, 7)), dma((6,)), dma((6,)), dma((2, 3)), dma((2, 3))],
        compiler_params=pltpu.CompilerParams(
            collective_id=1, has_side_effects=True, vmem_limit_bytes=62 * MIB
        ),
        name="backward",
    )(lengths, table, gain, buckets, *weights, win, wout, *acts, *small)


def update_kernel(big, small, *refs):
    norm_ref, refs = refs[0], refs[1:]
    n_big, n_small = len(big), len(small)
    big_in, refs = refs[: 4 * n_big], refs[4 * n_big :]
    small_in, refs = refs[: 4 * n_small], refs[4 * n_small :]
    (grad_i, dec_i), refs = refs[:2], refs[2:]
    big_out, refs = refs[: 3 * n_big], refs[3 * n_big :]
    small_out, refs = refs[: 3 * n_small], refs[3 * n_small :]
    (grad_o, dec_o), refs = refs[:2], refs[2:]
    held, (grad_s, wide_s, in_sem, out_sem) = refs[: 4 * n_big], refs[4 * n_big :]
    loads, stores = [], []
    for n, (src, dst) in enumerate(zip((grad_i,) + big_in, (grad_s,) + held)):
        copy = pltpu.make_async_copy(src, dst, in_sem.at[n])
        copy.start()
        loads.append(copy)
    factor = 1.0 / jnp.maximum(jnp.full((1, 1), norm_ref[0, 0], f32), clip_bound)

    def store(src, dst):
        copy = pltpu.make_async_copy(src, dst, out_sem.at[len(stores)])
        copy.start()
        stores.append(copy)

    dec_o[0] = dec_i[:1].astype(bf16)
    for n, (rate, decay) in enumerate(small):
        w, m, v, g = small_in[4 * n : 4 * n + 4]
        rows, lanes = w.shape
        news = adam_step(w[...], m[...], v[...], g[:rows, :lanes], factor, rate, decay)
        for ref, value in zip(small_out[3 * n : 3 * n + 3], news):
            ref[...] = value
    loads[0].wait()

    def widen(i, carry):
        wide_s[i] = grad_s[i].astype(f32)
        return carry

    lax.fori_loop(0, wide_s.shape[0], widen, 0)
    store(wide_s, grad_o)
    for n, (rate, decay) in enumerate(big):
        w, m, v, g = held[4 * n : 4 * n + 4]
        for load in loads[1 + 4 * n : 5 + 4 * n]:
            load.wait()

        def step(i, carry):
            news = adam_step(w[i], m[i], v[i], g[i], factor, rate, decay)
            for ref, value in zip((w, m, v), news):
                ref[i] = value
            return carry

        lax.fori_loop(0, w.shape[0], step, 0)
        for ref, out in zip((w, m, v), big_out[3 * n : 3 * n + 3]):
            store(ref, out)
    for copy in stores:
        copy.wait()


def update(norm, big, small, grad, dec_out, grad_shape, dec_shape):
    vmem = pl.BlockSpec(memory_space=pltpu.VMEM)
    hbm = pl.BlockSpec(memory_space=pltpu.HBM)
    big_in = [a for item in big for a in item[:4]]
    small_in = [a for item in small for a in item[:4]]
    like = [jax.ShapeDtypeStruct(item[0].shape, f32) for item in big for _ in range(3)]
    like_small = [jax.ShapeDtypeStruct(item[0].shape, f32) for item in small for _ in range(3)]
    last = [jax.ShapeDtypeStruct(grad_shape, f32), jax.ShapeDtypeStruct(dec_shape, bf16)]
    dma = pltpu.SemaphoreType.DMA
    return pl.pallas_call(
        functools.partial(
            update_kernel, [item[4:] for item in big], [item[4:] for item in small]
        ),
        out_shape=like + like_small + last,
        in_specs=[pl.BlockSpec(memory_space=pltpu.SMEM)]
        + [hbm] * len(big_in)
        + [vmem] * len(small_in)
        + [hbm, vmem],
        out_specs=[hbm] * len(like) + [vmem] * len(like_small) + [hbm, vmem],
        scratch_shapes=[pltpu.VMEM(a.shape, f32) for a in big_in]
        + [pltpu.VMEM(grad_shape, bf16), pltpu.VMEM(grad_shape, f32)]
        + [dma((1 + len(big_in),)), dma((1 + len(like),))],
        compiler_params=pltpu.CompilerParams(vmem_limit_bytes=60 * MIB),
        name="update",
    )(norm, *big_in, *small_in, grad, dec_out)


def on_device(
    inputs,
    dec_in,
    cotangent,
    lengths,
    bucket_table,
    square,
    square_m,
    square_v,
    ffn_in,
    ffn_in_m,
    ffn_in_v,
    ffn_out,
    ffn_out_m,
    ffn_out_v,
    gains,
    gains_m,
    gains_v,
    rel_bias,
    rel_bias_m,
    rel_bias_v,
):
    z_count = lax.axis_size("dp")
    width = inputs.shape[2]
    direct = lax.axis_size("seq") == 4 and width == 2 * HALF and width == 4 * z_count * ROWS
    direct = direct and inputs.shape[:2] == (4, BAND)
    w = {}
    seq_pos = lax.axis_index("seq")
    local_len = inputs.shape[1]
    span = local_len * lax.axis_size("seq")
    bucket_count = rel_bias.shape[0]
    scale = 1.0 / math.sqrt(HD)
    length = lax.dynamic_slice_in_dim(lengths, seq_pos, 1, 0)
    key_valid = jnp.arange(span)[None, :] < length[:, None]
    one_hot = (
        jnp.pad(bucket_table, (0, 1), constant_values=-1)[:, None]
        == jnp.arange(bucket_count)[None, :]
    ).astype(f32)
    table = jnp.einsum("ob,bh->ho", one_hot, rel_bias, precision=highest_precision)[:, None, :]

    me = (
        lax.axis_index("dp") * lax.axis_size("seq") + seq_pos
    ) * lax.axis_size("head") + lax.axis_index("head")
    if direct:
        buckets = jnp.pad(bucket_table[::-1], (0, 1), constant_values=-1)[None]
        outs = forward(
            lengths,
            rel_bias.T,
            buckets,
            square,
            ffn_in,
            ffn_out,
            gains,
            dec_in,
            cotangent,
            inputs,
            z_count,
        )
        weights = [o.reshape(width, width) for o in outs[14:20]]
        gain_f, state, g_high, dec_out, table = outs[20:]
        summed_sq, summed_in, summed_out, input_grad, summed_gain, g_bias, norm = backward(
            lengths,
            table,
            gain_f,
            buckets,
            weights,
            outs[0].reshape(width, -1),
            outs[1].reshape(-1, width),
            outs[2:14],
            (state, g_high),
            z_count,
        )
        news = update(
            norm,
            (
                (square, square_m, square_v, summed_sq, rate_matrix, decay_rate),
                (ffn_in, ffn_in_m, ffn_in_v, summed_in, rate_matrix, decay_rate),
                (ffn_out, ffn_out_m, ffn_out_v, summed_out, rate_matrix, decay_rate),
            ),
            (
                (gains, gains_m, gains_v, summed_gain, rate_small, 0.0),
                (rel_bias.T, rel_bias_m.T, rel_bias_v.T, g_bias, rate_small, 0.0),
            ),
            input_grad,
            dec_out,
            inputs.shape,
            dec_in.shape,
        )
        bias_new = [o.T for o in news[12:15]]
        return (news[16], news[15], norm[0, 0], *news[:12], *bias_new)
    else:

        def gather_rows(x):
            return lax.all_gather(x.astype(bf16), AXES, axis=x.ndim - 2, tiled=True)

        sq_a = gather_rows(square[:4])
        w_in_e = gather_rows(ffn_in[0])
        w_out_e = gather_rows(ffn_out[0])
        sq_b = gather_rows(square[4:])
        w_in_d = gather_rows(ffn_in[1])
        w_out_d = gather_rows(ffn_out[1])
        gain_f = lax.all_gather(gains.astype(bf16), AXES, axis=1, tiled=True).astype(f32)
        for i in range(square.shape[0]):
            w[i] = sq_a[i] if i < 4 else sq_b[i - 4]
        x_b = lax.all_to_all(inputs, "seq", split_axis=0, concat_axis=1, tiled=True)[0]
        x_f = x_b.astype(f32)
        normed = rms_gain(x_f, gain_f[0]).astype(bf16)
        q = matmul(normed, w[0]).astype(bf16)
        k = matmul(normed, w[1]).astype(bf16)
        v = matmul(normed, w[2]).astype(bf16)
        attended = attend_fwd(length, table, q, k, v)
        hidden = x_f + matmul(attended, w[3])
        normed_two = rms_gain(hidden, gain_f[1]).astype(bf16)
        pre_act = matmul(normed_two, w_in_e)
        inner_act = gelu_tanh(pre_act).astype(bf16)
        hidden_two = hidden + matmul(inner_act, w_out_e)
        encoded = rms_gain(hidden_two, gain_f[2]).astype(bf16)
        cross_k = matmul(encoded, w[7]).astype(bf16)
        cross_v = matmul(encoded, w[8]).astype(bf16)

        dec_row = dec_in.reshape(1, width).astype(f32)
        self_norm = rms_gain(dec_row, gain_f[3]).astype(bf16)
        self_values = matmul(self_norm, w[4]).astype(bf16)
        dec_one = dec_row + matmul(self_values, w[5])
        cross_norm = rms_gain(dec_one, gain_f[4]).astype(bf16)
        cross_q = matmul(cross_norm, w[6]).astype(bf16)
        head_of = (jnp.arange(width)[None, :] // HD == jnp.arange(H)[:, None]).astype(bf16)
        q_heads = head_of * cross_q
        cross_scores = jnp.where(key_valid, mm_t(q_heads, cross_k) * scale, neg_fill)
        cross_probs = jax.nn.softmax(cross_scores, axis=-1)
        cross_probs_b = cross_probs.astype(bf16)
        cross_att = jnp.sum(
            matmul(cross_probs_b, cross_v) * head_of.astype(f32), axis=0, keepdims=True
        ).astype(bf16)
        dec_two = dec_one + matmul(cross_att, w[9])
        ffn_norm = rms_gain(dec_two, gain_f[5]).astype(bf16)
        pre_dec = matmul(ffn_norm, w_in_d)
        inner_dec = gelu_tanh(pre_dec).astype(bf16)
        dec_out = dec_two + matmul(inner_dec, w_out_d)

        g_top_b = cotangent.reshape(1, width)
        g_top = g_top_b.astype(f32)
        g_pre_dec = gelu_pull(pre_dec, mm_t(g_top_b, w_out_d)).astype(bf16)
        g_two_norm, g_gain_five = rms_pull(dec_two, gain_f[5], mm_t(g_pre_dec, w_in_d))
        g_two = g_top + g_two_norm
        g_two_b = g_two.astype(bf16)
        g_att = mm_t(g_two_b, w[9]).astype(bf16)
        g_att_heads = head_of * g_att
        g_probs = mm_t(g_att_heads, cross_v)
        g_cross_v = mm_outer(cross_probs_b, g_att_heads).astype(bf16)
        g_scores = cross_probs * (g_probs - jnp.sum(g_probs * cross_probs, axis=-1, keepdims=True))
        g_scores_b = g_scores.astype(bf16)
        g_cross_q = (
            jnp.sum(matmul(g_scores_b, cross_k) * head_of.astype(f32), axis=0, keepdims=True) * scale
        ).astype(bf16)
        g_cross_k = (mm_outer(g_scores_b, q_heads) * scale).astype(bf16)
        g_one_norm, g_gain_four = rms_pull(dec_one, gain_f[4], mm_t(g_cross_q, w[6]))
        g_one_b = (g_two + g_one_norm).astype(bf16)
        g_self_values = mm_t(g_one_b, w[5]).astype(bf16)
        g_gain_three = rms_pull(dec_row, gain_f[3], mm_t(g_self_values, w[4]))[1]

        lefts = (self_norm, self_values, cross_norm, cross_att, ffn_norm, inner_dec)
        rights = (g_self_values, g_one_b, g_cross_q, g_two_b, g_pre_dec, g_top_b)
        packed = lax.all_gather(jnp.concatenate(lefts + rights, axis=1), AXES, axis=0, tiled=True)
        devices = packed.shape[0]
        cuts = [0]
        for piece in lefts + rights:
            cuts.append(cuts[-1] + piece.shape[1])
        dec_grads = []
        for n in range(6):
            share = lefts[n].shape[1] // devices
            left = lax.dynamic_slice_in_dim(packed, cuts[n] + me * share, share, 1)
            right = packed[:, cuts[6 + n] : cuts[7 + n]]
            dec_grads.append(mm_outer(left, right))
        g_w7 = mm_outer(encoded, g_cross_k)
        g_w8 = mm_outer(encoded, g_cross_v)
        g_encoded = mm_t(g_cross_k, w[7]) + mm_t(g_cross_v, w[8])
        g_hidden_two, g_gain_two = rms_pull(hidden_two, gain_f[2], g_encoded)
        g_hidden_two_b = g_hidden_two.astype(bf16)
        g_out_e = mm_outer(inner_act, g_hidden_two_b)
        g_pre = gelu_pull(pre_act, mm_t(g_hidden_two_b, w_out_e)).astype(bf16)
        g_in_e = mm_outer(normed_two, g_pre)
        g_hidden_norm, g_gain_one = rms_pull(hidden, gain_f[1], mm_t(g_pre, w_in_e))
        g_hidden = g_hidden_two + g_hidden_norm
        g_hidden_b = g_hidden.astype(bf16)
        g_w3 = mm_outer(attended, g_hidden_b)
        g_attended = mm_t(g_hidden_b, w[3]).astype(bf16)
        gq, gk, gv, g_table = attend_bwd(length, table, q, k, v, g_attended)
        g_bias_here = jnp.einsum("ob,ho->bh", one_hot, g_table[:, 0, :], precision=highest_precision)
        g_w0 = mm_outer(normed, gq)
        g_w1 = mm_outer(normed, gk)
        g_w2 = mm_outer(normed, gv)
        g_normed = mm_t(gq, w[0]) + mm_t(gk, w[1]) + mm_t(gv, w[2])
        g_input_norm, g_gain_zero = rms_pull(x_f, gain_f[0], g_normed)
        g_x = (g_hidden + g_input_norm).astype(bf16)
        input_grad = lax.all_to_all(
            g_x[None], "seq", split_axis=1, concat_axis=0, tiled=True
        ).astype(f32)

        def scatter_rows(x):
            return lax.psum_scatter(
                x.astype(bf16), AXES, scatter_dimension=x.ndim - 2, tiled=True
            ).astype(f32)

        s_78 = scatter_rows(jnp.stack((g_w7, g_w8)))
        s_out = scatter_rows(g_out_e)
        s_in = scatter_rows(g_in_e)
        s_0123 = scatter_rows(jnp.stack((g_w0, g_w1, g_w2, g_w3)))
        g_gains = jnp.stack(
            (g_gain_zero, g_gain_one, g_gain_two, g_gain_three, g_gain_four, g_gain_five)
        )
        summed_sq = jnp.stack(
            (
                s_0123[0],
                s_0123[1],
                s_0123[2],
                s_0123[3],
                dec_grads[0],
                dec_grads[1],
                dec_grads[2],
                s_78[0],
                s_78[1],
                dec_grads[3],
            )
        )
        summed_in = jnp.stack((s_in, dec_grads[4]))
        summed_out = jnp.stack((s_out, dec_grads[5]))
        gain_share = gains.shape[1]
        local_squares = (
            jnp.sum(summed_sq * summed_sq)
            + jnp.sum(summed_in * summed_in)
            + jnp.sum(summed_out * summed_out)
        )
        g_gains, g_bias, shard_squares = lax.psum((g_gains, g_bias_here, local_squares), AXES)
        summed_gain = lax.dynamic_slice_in_dim(g_gains, me * gain_share, gain_share, 1)
        grad_norm = jnp.sqrt(shard_squares + jnp.sum(g_gains * g_gains) + jnp.sum(g_bias * g_bias))
        g_bias = g_bias.T
    factor = clip_bound / jnp.maximum(grad_norm, clip_bound)
    bias_new = adam_step(rel_bias.T, rel_bias_m.T, rel_bias_v.T, g_bias, factor, rate_small, 0.0)
    return (
        dec_out.astype(bf16).reshape(dec_in.shape),
        input_grad,
        grad_norm,
        *adam_step(square, square_m, square_v, summed_sq, factor, rate_matrix, decay_rate),
        *adam_step(ffn_in, ffn_in_m, ffn_in_v, summed_in, factor, rate_matrix, decay_rate),
        *adam_step(ffn_out, ffn_out_m, ffn_out_v, summed_out, factor, rate_matrix, decay_rate),
        *adam_step(gains, gains_m, gains_v, summed_gain, factor, rate_small, 0.0),
        *(o.T for o in bias_new),
    )


def solution(mesh):
    rows = P(("dp", "head"), "seq", None)
    shard = P(None, AXES, None)
    small = P(None, AXES)
    return jax.shard_map(
        on_device,
        mesh=mesh,
        in_specs=(rows, rows, rows, P(("dp", "head")), P())
        + (shard,) * 9
        + (small,) * 3
        + (P(),) * 3,
        out_specs=(rows, rows, P()) + (shard,) * 9 + (small,) * 3 + (P(),) * 3,
        check_vma=False,
    )
```

```python
import functools
import math

import jax
import jax.numpy as jnp
from jax import lax
from jax.experimental import pallas as pl
from jax.experimental.pallas import tpu as pltpu
from jax.sharding import PartitionSpec as P

H = 12
HD = 64
STEP = 5
AXES = ("dp", "seq", "head")

norm_eps = 1e-06
neg_fill = -1e30
beta_one = 0.9
beta_two = 0.999
adam_eps = 1e-08
decay_rate = 0.01
rate_matrix = 0.05
rate_small = 0.5
clip_bound = 1.0
highest_precision = lax.Precision.HIGHEST
bf16 = jnp.bfloat16
f32 = jnp.float32
BAND = 128


def rms_gain(values_in, gain_row):
    return (
        values_in
        * lax.rsqrt(jnp.mean(values_in * values_in, axis=-1, keepdims=True) + norm_eps)
        * gain_row
    )


def gelu_tanh(values_in):
    return jax.nn.gelu(values_in, approximate=True)


def matmul(left, right):
    return jnp.dot(left, right, preferred_element_type=f32)


def mm_t(left, right):
    return lax.dot_general(left, right, (((1,), (1,)), ((), ())), preferred_element_type=f32)


def mm_outer(left, right):
    return lax.dot_general(left, right, (((0,), (0,)), ((), ())), preferred_element_type=f32)


def rms_pull(values_in, gain_row, incoming):
    _, pull = jax.vjp(rms_gain, values_in, gain_row)
    return pull(incoming)


def gelu_pull(values_in, incoming):
    _, pull = jax.vjp(gelu_tanh, values_in)
    return pull(incoming)[0]


def adam_step(weight, first, second, grad, factor, rate, decay):
    grad = grad * factor
    first = beta_one * first + (1.0 - beta_one) * grad
    second = beta_two * second + (1.0 - beta_two) * grad * grad
    first_hat = first / (1.0 - beta_one**STEP)
    second_hat = second / (1.0 - beta_two**STEP)
    weight = weight - rate * (first_hat / (jnp.sqrt(second_hat) + adam_eps) + decay * weight)
    return (weight, first, second)


def bias_band(table_row, span):
    wide = jnp.broadcast_to(table_row, (BAND, 2 * span))
    shift = (2 * span - (BAND - 1)) % (2 * span)
    return pltpu.roll(wide, shift, 1, stride=1, stride_axis=0)


def band_sums(band, span):
    wide = 2 * span
    rows = BAND
    while rows > 8:
        rows //= 2
        band = band[:rows] + pltpu.roll(band[rows:], wide - rows, 1)
    row = lax.broadcasted_iota(jnp.int32, band.shape, 0)
    for step in (4, 2, 1):
        band = jnp.where((row // step) % 2 == 1, pltpu.roll(band, wide - step, 1), band)
    return pltpu.roll(jnp.sum(band, axis=0, keepdims=True), BAND - 1, 1)


def softmax_rows(q_rows, k_all, band, block, span, valid):
    start = span - BAND * (block + 1)
    scores = mm_t(q_rows, k_all) * (1.0 / math.sqrt(HD)) + band[:, start : start + span]
    scores = jnp.where(valid, scores, neg_fill)
    peak = jnp.max(scores, axis=-1, keepdims=True)
    raised = jnp.exp(scores - peak)
    return raised / jnp.sum(raised, axis=-1, keepdims=True)


def attend_fwd_kernel(len_ref, table_ref, q_ref, k_ref, v_ref, o_ref):
    span = k_ref.shape[0]
    valid = lax.broadcasted_iota(jnp.int32, (1, span), 1) < len_ref[0]
    lane = lax.broadcasted_iota(jnp.int32, (1, 2 * HD), 1)
    k_all = k_ref[...]
    v_all = v_ref[...]
    bands = [bias_band(table_ref[t], span) for t in range(2)]
    for block in range(span // BAND):
        rows = slice(block * BAND, (block + 1) * BAND)
        q_rows = q_ref[rows, :]
        parts = []
        for t in range(2):
            own = (lane // HD) == t
            probs = softmax_rows(
                jnp.where(own, q_rows, jnp.zeros_like(q_rows)), k_all, bands[t], block, span, valid
            )
            parts.append(matmul(probs.astype(bf16), v_all))
        o_ref[rows, :] = jnp.where(lane < HD, parts[0], parts[1]).astype(bf16)


def attend_bwd_kernel(
    len_ref, table_ref, q_ref, k_ref, v_ref, do_ref, dq_ref, dk_ref, dv_ref, dt_ref
):
    span = k_ref.shape[0]
    scale = 1.0 / math.sqrt(HD)
    valid = lax.broadcasted_iota(jnp.int32, (1, span), 1) < len_ref[0]
    lane = lax.broadcasted_iota(jnp.int32, (1, 2 * HD), 1)
    k_all = k_ref[...]
    v_all = v_ref[...]
    count = span // BAND
    dks, dvs = [], []
    dqs = [[None, None] for _ in range(count)]
    for t in range(2):
        own = (lane // HD) == t
        band = bias_band(table_ref[t], span)
        dk = jnp.zeros((span, 2 * HD), f32)
        dv = jnp.zeros((span, 2 * HD), f32)
        dband = jnp.zeros((BAND, 2 * span), f32)
        for block in range(count):
            rows = slice(block * BAND, (block + 1) * BAND)
            q_rows = q_ref[rows, :]
            do_rows = do_ref[rows, :]
            zero = jnp.zeros_like(q_rows)
            probs = softmax_rows(
                jnp.where(own, q_rows, zero), k_all, band, block, span, valid
            )
            dprobs = mm_t(jnp.where(own, do_rows, zero), v_all)
            dscore = probs * (dprobs - jnp.sum(dprobs * probs, axis=-1, keepdims=True))
            start = span - BAND * (block + 1)
            pieces = []
            if start:
                pieces.append(jnp.zeros((BAND, start), f32))
            pieces.append(dscore)
            if span - start:
                pieces.append(jnp.zeros((BAND, span - start), f32))
            dband = dband + jnp.concatenate(pieces, axis=1)
            dscore_b = dscore.astype(bf16)
            dv = dv + mm_outer(probs.astype(bf16), do_rows)
            dk = dk + mm_outer(dscore_b, q_rows)
            dqs[block][t] = matmul(dscore_b, k_all)
        dks.append(dk)
        dvs.append(dv)
        dt_ref[t] = band_sums(dband, span)
    dk_ref[...] = (jnp.where(lane < HD, dks[0], dks[1]) * scale).astype(bf16)
    dv_ref[...] = jnp.where(lane < HD, dvs[0], dvs[1]).astype(bf16)
    for block in range(count):
        rows = slice(block * BAND, (block + 1) * BAND)
        dq_ref[rows, :] = (jnp.where(lane < HD, dqs[block][0], dqs[block][1]) * scale).astype(bf16)


def head_specs(span, width, n):
    return [pl.BlockSpec((span, 2 * HD), lambda i: (0, i)) for _ in range(n)]


def attend_fwd(length, table, q, k, v):
    span, width = q.shape
    return pl.pallas_call(
        attend_fwd_kernel,
        grid=(width // (2 * HD),),
        out_shape=jax.ShapeDtypeStruct((span, width), bf16),
        in_specs=[
            pl.BlockSpec(memory_space=pltpu.SMEM),
            pl.BlockSpec((2, 1, 2 * span), lambda i: (i, 0, 0)),
            *head_specs(span, width, 3),
        ],
        out_specs=head_specs(span, width, 1)[0],
        compiler_params=pltpu.CompilerParams(vmem_limit_bytes=48 * 1024 * 1024),
        name="attend_fwd",
    )(length, table, q, k, v)


def attend_bwd(length, table, q, k, v, do):
    span, width = q.shape
    like = jax.ShapeDtypeStruct((span, width), bf16)
    return pl.pallas_call(
        attend_bwd_kernel,
        grid=(width // (2 * HD),),
        out_shape=(like, like, like, jax.ShapeDtypeStruct(table.shape, f32)),
        in_specs=[
            pl.BlockSpec(memory_space=pltpu.SMEM),
            pl.BlockSpec((2, 1, 2 * span), lambda i: (i, 0, 0)),
            *head_specs(span, width, 4),
        ],
        out_specs=(
            *head_specs(span, width, 3),
            pl.BlockSpec((2, 1, 2 * span), lambda i: (i, 0, 0)),
        ),
        compiler_params=pltpu.CompilerParams(vmem_limit_bytes=48 * 1024 * 1024),
        name="attend_bwd",
    )(length, table, q, k, v, do)


MESH_ID = pl.DeviceIdType.MESH
HALF = 384
ROWS = 48
MIB = 1024 * 1024


def place():
    z, s, c = lax.axis_index("dp"), lax.axis_index("seq"), lax.axis_index("head")
    near = s + 1 - 2 * (s % 2)
    far = (s + 2) % 4
    first = near + c * (far - near)
    second = far + c * (near - far)
    return z, s, c, first, second, 3 - s


def greet(z, s, c, z_count):
    barrier = pltpu.get_barrier_semaphore()
    for d in range(1, z_count):
        peer = ((z + d) % z_count, s, c)
        pl.semaphore_signal(barrier, 1, device_id=peer, device_id_type=MESH_ID)
    for d in range(1, 4):
        peer = (z, (s + d) % 4, c)
        pl.semaphore_signal(barrier, 1, device_id=peer, device_id_type=MESH_ID)
    pl.semaphore_signal(barrier, 1, device_id=(z, s, 1 - c), device_id_type=MESH_ID)
    pl.semaphore_wait(barrier, z_count + 3)


def remote(src, dst, send, recv, peer):
    return pltpu.make_async_remote_copy(
        src, dst, send, recv, device_id=peer, device_id_type=MESH_ID
    )


def cols(c, base=0):
    return pl.ds(pl.multiple_of(base + c * HALF, 128), HALF)


def unit_view(kind, n, ref, z, s, c):
    if kind == "square":
        return ref.at[n, z, s, :, cols(c)]
    if kind == "cols":
        return ref.at[n // 4, z, s, :, cols(c, (n % 4) * 2 * HALF)]
    if kind == "rows":
        return ref.at[n // 4, z, s, pl.ds((n % 4) * ROWS, ROWS), cols(c)]
    if kind == "line square":
        return ref.at[n, z]
    if kind == "line cols":
        return ref.at[z, :, pl.ds(n * HALF, HALF)]
    if kind == "line rows":
        return ref.at[z, pl.ds(n * ROWS, ROWS)]
    return ref.at[z, s]


class Gather:
    def __init__(self, units, refs, send, recv, z_count):
        self.units, self.refs, self.send, self.recv = units, refs, send, recv
        self.z_count = z_count
        self.where = place()
        self.started = []
        self.base = 2 * (z_count - 1)

    def view(self, u, z, s, c):
        kind, n = self.units[u]
        return unit_view(kind, n, self.refs[kind], z, s, c)

    def go(self, u, slot, ref, peer):
        copy = remote(ref, ref, self.send.at[u, slot], self.recv.at[u, slot], peer)
        copy.start()
        self.started.append(copy)

    def got(self, u, slot, ref):
        z, s, c = self.where[:3]
        remote(ref, ref, self.send.at[u, slot], self.recv.at[u, slot], (z, s, 1 - c)).wait_recv()

    def z_sends(self, u, i):
        z, s, c = self.where[:3]
        top = self.z_count - 1
        for slot, near, block, live in (
            (i, z + 1, z - i, (z >= i) & (z < top)),
            (top + i, z - 1, z + i, (z + i <= top) & (z > 0)),
        ):
            ref = self.view(u, block, s, c)
            copy = remote(
                ref, ref, self.send.at[u, slot], self.recv.at[u, slot], (near, s, c)
            )
            yield copy, live

    def z_send(self, u, i):
        for copy, live in self.z_sends(u, i):

            @pl.when(live)
            def _():
                copy.start()

    def z_got(self, u, i):
        z, s, c = self.where[:3]
        top = self.z_count - 1
        for slot, block, live in (
            (i, z - 1 - i, z - 1 - i >= 0),
            (top + i, z + 1 + i, z + 1 + i <= top),
        ):

            @pl.when(live)
            def _():
                self.got(u, slot, self.view(u, block, s, c))

    def a_start(self, u):
        z, s, c, first, second, both = self.where
        self.go(u, self.base, self.view(u, slice(None), s, c), (z, first, c))

    def a_wait(self, u):
        z, s, c, first, second, both = self.where
        self.got(u, self.base, self.view(u, slice(None), first, c))

    def b_start(self, u):
        z, s, c, first, second, both = self.where
        self.go(u, self.base + 1, self.view(u, slice(None), s, c), (z, second, c))
        self.go(u, self.base + 2, self.view(u, slice(None), first, c), (z, second, c))

    def b_wait(self, u):
        z, s, c, first, second, both = self.where
        self.got(u, self.base + 1, self.view(u, slice(None), second, c))
        self.got(u, self.base + 2, self.view(u, slice(None), both, c))

    def s_start(self, u):
        z, s, c = self.where[:3]
        if self.units[u][0] != "gain":
            self.go(u, self.base + 3, self.view(u, slice(None), slice(None), c), (z, s, 1 - c))

    def s_wait(self, u):
        z, s, c = self.where[:3]
        if self.units[u][0] != "gain":
            self.got(u, self.base + 3, self.view(u, slice(None), slice(None), 1 - c))

    def line(self, u, i):
        if i:
            self.z_got(u, i - 1)
        if i < self.z_count - 1:
            self.z_send(u, i)

    def lag(self, stage):
        return stage if stage < self.z_count else self.z_count - 1 + (0, 2, 4, 5)[stage - self.z_count + 1]

    def tick(self, t, done):
        lines = self.z_count
        for n in range(lines + 3):
            u = t - self.lag(n)
            if not 0 <= u < len(self.units):
                continue
            if n < lines:
                self.line(u, n)
            plain = not self.units[u][0].startswith("line")
            if plain and n == lines - 1:
                self.a_start(u)
            if plain and n == lines:
                self.a_wait(u)
                self.b_start(u)
            if plain and n == lines + 1:
                self.b_wait(u)
                self.s_start(u)
            if plain and n == lines + 2:
                self.s_wait(u)
                done(u)

    def finish(self):
        for copy in self.started:
            copy.wait_send()
        for u in range(len(self.units)):
            for i in range(self.z_count - 1):
                for copy, live in self.z_sends(u, i):

                    @pl.when(live)
                    def _():
                        copy.wait_send()


ENC = (0, 1, 2, 3, 7, 8)
DEC = (4, 5, 6, 9)
SAME_CORE = (1, 3, 5)


def plane_peers(z, s, c):
    peers = []
    for ds in range(4):
        for dc in range(2):
            if ds or dc:
                peers.append(((z, (s + ds) % 4, (c + dc) % 2), ((s + 4 - ds) % 4, (c + dc) % 2)))
    return peers


class Plane:
    def __init__(self, send, recv):
        self.send, self.recv = send, recv
        self.z, self.s, self.c = place()[:3]
        self.peers = plane_peers(self.z, self.s, self.c)
        self.started = []

    def start(self, k, ref, only=range(7)):
        for i in only:
            peer = self.peers[i][0]
            mine = ref.at[self.s, self.c]
            copy = remote(mine, mine, self.send.at[k, i], self.recv.at[k, i], peer)
            copy.start()
            self.started.append(copy)

    def wait(self, k, ref, only=range(7)):
        for i in only:
            s, c = self.peers[i][1]
            slot = ref.at[s, c]
            remote(
                slot, slot, self.send.at[k, i], self.recv.at[k, i], (self.z, self.s, 1 - self.c)
            ).wait_recv()

    def finish(self):
        for copy in self.started:
            copy.wait_send()


def rounded(value):
    return value.astype(bf16).astype(f32)


def pick(value, start, size):
    full = value.shape[1]
    return pltpu.roll(value, full - start, 1)[:, :size].astype(bf16)


def halves(ref):
    parts = []
    for c in range(2):
        parts.append(ref[0, c] + ref[1, c] + ref[2, c] + ref[3, c])
    return parts


def blocks_of(ref, size, z_count):
    group = HALF // size
    lanes = ref.shape[-1]
    pieces = []
    for n in range(4 * z_count // group):
        total = None
        for m in range(group):
            z, s = (n * group + m) // 4, (n * group + m) % 4
            piece = ref[s, 0, z] + ref[s, 1, z]
            piece = jnp.concatenate([piece, jnp.zeros((8, HALF - lanes), f32)], axis=1)
            if m:
                piece = pltpu.roll(piece, m * size, 1)
            total = piece if total is None else total + piece
        pieces.append(total)
    return jnp.concatenate(pieces, axis=1)


def half_of(value, c):
    return jnp.where(c == 0, value[:, :HALF], value[:, HALF : 2 * HALF])


def mm_down(value, weight, s, z_count, size):
    total = None
    for z in range(z_count):
        term = matmul(pick(value, (4 * z + s) * size, size), weight(z))
        total = term if total is None else total + term
    return total


def own_row(value, s, c):
    row = lax.broadcasted_iota(jnp.int32, value.shape, 0)
    return jnp.sum(jnp.where(row == 2 * s + c, value, 0.0), axis=0, keepdims=True)


def as_own_row(value, s, c):
    wide = jnp.broadcast_to(value, (8, value.shape[1]))
    row = lax.broadcasted_iota(jnp.int32, wide.shape, 0)
    return jnp.where(row == 2 * s + c, wide, 0.0)


def pull_own(values_in, gain_row, incoming, s, c):
    inverse = lax.rsqrt(jnp.mean(values_in * values_in, axis=-1, keepdims=True) + norm_eps)
    scaled = incoming * gain_row
    inner = jnp.mean(scaled * values_in, axis=-1, keepdims=True)
    grad = inverse * scaled - values_in * (inverse * inverse * inverse * inner)
    return grad, own_row(incoming * values_in * inverse, s, c)


def put_blocks(ref, s, c, terms, size):
    for z, term in enumerate(terms):
        ref[s, c, z] = jnp.zeros(ref.shape[3:], f32)
        ref[s, c, z, :, :size] = term


def head_rows(width):
    lane = lax.broadcasted_iota(jnp.int32, (16, width), 1)
    row = lax.broadcasted_iota(jnp.int32, (16, width), 0)
    return (lane // HD) == row


def ffn_halves(parts):
    pieces = []
    for j in range(4):
        for c in range(2):
            pieces.append(parts[c][:, j * HALF : (j + 1) * HALF])
    return jnp.concatenate(pieces, axis=1)


class Decoder:
    (ROWS_IN, SELF_NORM, SELF_VALUES, ONE, CROSS_NORM, CROSS_ATT, FFN_NORM, TWO, TOP, QUERY) = range(10)
    INNER, PRE = 10, 14
    COUNT = 18

    def __init__(self, plane, st, gains, z_count):
        self.plane, self.st, self.gains, self.z_count = plane, st, gains, z_count
        self.s, self.c = plane.s, plane.c

    def gain(self, n):
        return self.gains[n : n + 1, :]

    def square_down(self, k, ref, value, wd, n):
        ref[self.s, self.c] = mm_down(value, lambda z: wd[n, z], self.s, self.z_count, ROWS)
        self.plane.start(k, ref)

    def square_sum(self, k, ref):
        self.plane.wait(k, ref)
        return jnp.concatenate(halves(ref), axis=1)

    def square_up(self, k, ref, value, wd, n):
        own = half_of(value, self.c).astype(bf16)
        put_blocks(
            ref, self.s, self.c, [mm_t(own, wd[n, z]) for z in range(self.z_count)], ROWS
        )
        self.plane.start(k, ref)

    def square_up_sum(self, k, ref):
        self.plane.wait(k, ref)
        return blocks_of(ref, ROWS, self.z_count)


def row_blocks(count, work):
    def body(i, carry):
        work(i, pl.ds(pl.multiple_of(i * BAND, BAND), BAND))
        return carry

    lax.fori_loop(0, count, body, 0)


def col_tiles(width, tile, work):
    def body(i, carry):
        work(pl.ds(pl.multiple_of(i * tile, tile), tile))
        return carry

    lax.fori_loop(0, width // tile, body, 0)


def wide(value):
    return value.reshape(value.shape[0] * value.shape[1] * value.shape[2], value.shape[3])


def softmax_keys(k_own, q_rows, band, block, span, live):
    scores = mm_t(k_own, q_rows) * (1.0 / math.sqrt(HD))
    count = span // BAND
    bias = [
        band[:, (block - n + count - 1) * BAND : (block - n + count) * BAND] for n in range(count)
    ]
    scores = jnp.where(live, scores + jnp.concatenate(bias, axis=0), neg_fill)
    raised = jnp.exp(scores - jnp.max(scores, axis=0, keepdims=True))
    return raised * (1.0 / jnp.sum(raised, axis=0, keepdims=True))


def own_lanes(value, t):
    lane = lax.broadcasted_iota(jnp.int32, value.shape, 1)
    return jnp.where((lane // HD) == t, value, jnp.zeros_like(value))


def attend_pair_fwd(pair, length, table_ref, q_ref, k_ref, v_ref, o_ref):
    span = k_ref.shape[0]
    at = pl.ds(pl.multiple_of(pair * 2 * HD, 2 * HD), 2 * HD)
    live = lax.broadcasted_iota(jnp.int32, (span, BAND), 0) < length
    k_all = k_ref[:, at]
    v_turned = v_ref[:, at].T
    keys = [own_lanes(k_all, t) for t in range(2)]
    bands = [bias_band(table_ref[2 * pair + t], span) for t in range(2)]
    row = lax.broadcasted_iota(jnp.int32, (2 * HD, BAND), 0)
    for block in range(span // BAND):
        rows = slice(block * BAND, (block + 1) * BAND)
        q_rows = q_ref[rows, at]
        parts = []
        for t in range(2):
            probs = softmax_keys(keys[t], q_rows, bands[t], block, span, live)
            parts.append(matmul(v_turned, probs.astype(bf16)))
        o_ref[rows, at] = jnp.where(row < HD, parts[0], parts[1]).T.astype(bf16)


def attend_pair_bwd(
    pair, length, table_ref, q_ref, k_ref, v_ref, do_ref, dq_ref, dk_ref, dv_ref, dt_ref, sums
):
    span = k_ref.shape[0]
    count = span // BAND
    scale = 1.0 / math.sqrt(HD)
    at = pl.ds(pl.multiple_of(pair * 2 * HD, 2 * HD), 2 * HD)
    live = lax.broadcasted_iota(jnp.int32, (span, BAND), 0) < length
    lane = lax.broadcasted_iota(jnp.int32, (1, 2 * HD), 1)
    row = lax.broadcasted_iota(jnp.int32, (2 * HD, BAND), 0)
    k_all = k_ref[:, at]
    k_turned = k_all.T
    v_all = v_ref[:, at]
    dks, dvs = [], []
    dqs = [[None, None] for _ in range(count)]
    for t in range(2):
        k_own = own_lanes(k_all, t)
        v_own = own_lanes(v_all, t)
        band = bias_band(table_ref[2 * pair + t], span)
        dk = jnp.zeros((span, 2 * HD), f32)
        dv = jnp.zeros((span, 2 * HD), f32)
        sums[...] = jnp.zeros_like(sums)
        for block in range(count):
            rows = slice(block * BAND, (block + 1) * BAND)
            q_rows = q_ref[rows, at]
            do_rows = do_ref[rows, at]
            probs = softmax_keys(k_own, q_rows, band, block, span, live)
            dprobs = mm_t(v_own, do_rows)
            dscore = probs * (dprobs - jnp.sum(dprobs * probs, axis=0, keepdims=True))
            for n in range(count):
                start = (block - n + count - 1) * BAND
                sums[:, start : start + BAND] += dscore[n * BAND : (n + 1) * BAND]
            dscore_b = dscore.astype(bf16)
            dv = dv + matmul(probs.astype(bf16), do_rows)
            dk = dk + matmul(dscore_b, q_rows)
            dqs[block][t] = matmul(k_turned, dscore_b)
        dks.append(dk)
        dvs.append(dv)
        dt_ref[2 * pair + t] = band_sums(sums[...], span)
    dk_ref[:, at] = (jnp.where(lane < HD, dks[0], dks[1]) * scale).astype(bf16)
    dv_ref[:, at] = jnp.where(lane < HD, dvs[0], dvs[1]).astype(bf16)
    for block in range(count):
        rows = slice(block * BAND, (block + 1) * BAND)
        value = jnp.where(row < HD, dqs[block][0], dqs[block][1]).T
        dq_ref[rows, at] = (value * scale).astype(bf16)


def forward_kernel(units, lines, z_count, *refs):
    (
        len_ref, bias_ref, bucket_ref, sq_ref, in_ref, out_ref, gains_ref, dec_ref, cot_ref, x_ref,
        in_o, out_o, x_o, q_o, k_o, v_o, att_o, hid_o, pre_o, hid2_o, enc_o, gck_o, gcv_o, wd_o,
        sq_o0, sq_o1, sq_o2, sq_o3, sq_o4, sq_o5, gain_o, st_o, gg_o, dec_o, table_ref,
        sq_w, in_w, out_w, gain_w, sq_r, in_r, out_r, gain_r,
        x_s, n_s, q_s, k_s, v_s, att_s, hid_s, pre_s, inner_s, hid2_s, enc_s, ck_s, cv_s, gains,
        gain_ref, wd, wdi, wdo, st, e_rows, e_sq, e_att, e_pre, e_out, e_inner, e_up, e_half,
        send, recv, first_send, first_recv, x_send, x_recv, d_send, d_recv, p_send, p_recv, local,
    ) = refs
    z, s, c = place()[:3]
    sibling = (z, s, 1 - c)
    sq_o = (sq_o0, sq_o1, sq_o2, sq_o3, sq_o4, sq_o5)
    n_sq, n_ff = sq_ref.shape[0], in_ref.shape[0]
    blocks = x_s.shape[0] * x_s.shape[1] // BAND
    greet_plane(z, s, c, z_count)
    plane = Plane(p_send, p_recv)
    dec = Decoder(plane, st, gains, z_count)
    length = len_ref[s]
    for n, ref in enumerate((dec_ref, cot_ref)):
        e_rows[s, c, n] = as_own_row(ref[0].astype(f32), s, c)
    row = lax.broadcasted_iota(jnp.int32, (gains_ref.shape[0], 128), 0)
    lane = lax.broadcasted_iota(jnp.int32, (gains_ref.shape[0], 128), 1)
    gain_ref[...] = lax.dot_general(
        gains_ref[...],
        jnp.where(row == lane, 1.0, 0.0),
        (((0,), (0,)), ((), ())),
        precision=highest_precision,
        preferred_element_type=f32,
    )
    plane.start(0, e_rows)

    first = []

    def to_sibling(src, dst):
        copy = remote(src, dst, first_send.at[len(first)], first_recv.at[len(first)], sibling)
        copy.start()
        first.append(copy)

    to_sibling(gain_ref, gain_r)
    to_sibling(sq_ref.at[:, :, cols(1 - c)], sq_r)
    x_copies = []
    for d in range(1, 4):
        peer = (s + d) % 4
        copy = remote(
            x_ref.at[peer], x_s.at[s], x_send.at[d - 1], x_recv.at[d - 1], (z, peer, c)
        )
        copy.start()
        x_copies.append(copy)
    mine = pltpu.make_async_copy(x_ref.at[s], x_s.at[s], local.at[0])
    mine.start()
    for n in range(n_ff):
        for j in range(4):
            to_sibling(in_ref.at[n, :, cols(1 - c, 2 * HALF * j)], in_r.at[n, j])
        to_sibling(out_ref.at[n, :, cols(1 - c)], out_r.at[n])

    def joined(own, other):
        top = jnp.where(c == 0, own, other)
        bottom = jnp.where(c == 0, other, own)
        return jnp.concatenate([top, bottom], axis=0).astype(bf16)

    gather = Gather(
        units,
        {
            "square": sq_w,
            "cols": in_w,
            "rows": out_w,
            "gain": gain_w,
            "line square": wd,
            "line cols": wdi,
            "line rows": wdo,
        },
        send,
        recv,
        z_count,
    )
    lined = Gather(lines, gather.refs, d_send, d_recv, z_count)
    first[0].wait_recv()
    gain_w[z, s] = joined(gain_ref[...], gain_r[...])
    first[1].wait_recv()
    for i, n in enumerate(ENC):
        sq_w[i, z, s, :, cols(c)] = joined(sq_ref[n, :, cols(c)], sq_r[n])
    drains = []

    def drain(src, dst):
        copy = pltpu.make_async_copy(src, dst, local.at[1 + len(drains)])
        copy.start()
        drains.append(copy)

    def done(u):
        kind, n = units[u]
        if kind == "square":
            drain(sq_w.at[n], sq_o[n])
        elif kind == "cols" and n % 4 == 3:
            drain(in_w.at[n // 4], in_o)
        elif kind == "rows" and n % 4 == 3:
            drain(out_w.at[n // 4], out_o)

    def normed(src, gain_row, dst):
        def work(i, at):
            dst[at, :] = rms_gain(src(i, at), gains[gain_row : gain_row + 1, :]).astype(bf16)

        row_blocks(blocks, work)

    def x_rows(i, at):
        return x_s[i].astype(f32)

    def start_piece():
        hot = bucket_hot(bucket_ref, bias_ref.shape[1])
        table = lax.dot_general(
            bias_ref[...],
            hot,
            (((1,), (0,)), ((), ())),
            precision=highest_precision,
            preferred_element_type=f32,
        )
        for h in range(table_ref.shape[0]):
            table_ref[h] = table[h : h + 1]
        for copy in x_copies:
            copy.wait_recv()
        mine.wait()
        drain(x_s, x_o)
        gains[...] = wide(gain_w[...]).astype(f32).T[:8]
        gain_o[...] = gains[...]
        normed(x_rows, 0, n_s)

    def square_dot(left, n, tile=256):
        def weight(at):
            return wide(sq_w[n, :, :, :, at])

        return lambda at: matmul(left[...], weight(at))

    def project(n, left, dst, out):
        dot = square_dot(left, n)

        def work(at):
            dst[:, at] = dot(at).astype(bf16)

        col_tiles(2 * HALF, 256, work)
        if out is not None:
            drain(dst, out)

    def attention(pairs):
        def body(pair, carry):
            attend_pair_fwd(pair, length, table_ref, q_s, k_s, v_s, att_s)
            return carry

        lax.fori_loop(pairs[0], pairs[1], body, 0)

    def hidden_piece():
        drain(att_s, att_o)
        dot = square_dot(att_s, 3)

        def work(at):
            hid_s[:, at] = dot(at)

        col_tiles(2 * HALF, 256, work)

        def add(i, at):
            total = hid_s[at, :] + x_rows(i, at)
            hid_s[at, :] = total
            n_s[at, :] = rms_gain(total, gains[1:2, :]).astype(bf16)

        row_blocks(blocks, add)
        drain(hid_s, hid_o)

    def ffn_piece(j):
        def work(i, carry):
            at = pl.ds(pl.multiple_of(j * 2 * HALF + i * 256, 256), 256)
            pre = matmul(n_s[...], wide(in_w[0, :, :, :, at]))
            pre_s[:, at] = pre
            inner_s[:, at] = gelu_tanh(pre).astype(bf16)
            return carry

        lax.fori_loop(0, 3, work, 0)

    def hidden_two_piece():
        drain(pre_s, pre_o)

        def work(at):
            hid2_s[:, at] = hid_s[:, at] + matmul(inner_s[...], wide(out_w[0, :, :, :, at]))

        col_tiles(2 * HALF, 256, work)
        normed(lambda i, at: hid2_s[at, :], 2, enc_s)
        drain(hid2_s, hid2_o)
        drain(enc_s, enc_o)

    def dec_start():
        plane.wait(0, e_rows)
        for n, to in ((0, Decoder.ROWS_IN), (1, Decoder.TOP)):
            total = e_rows[0, 0, n]
            for p in range(1, 8):
                total = total + e_rows[p // 2, p % 2, n]
            st[to] = total
        value = rounded(rms_gain(st[Decoder.ROWS_IN], dec.gain(3)))
        st[Decoder.SELF_NORM] = value
        drain(wd, wd_o)
        dec.square_down(1, e_sq.at[0], value, wd, 0)

    def dec_self_values():
        value = rounded(dec.square_sum(1, e_sq.at[0]))
        st[Decoder.SELF_VALUES] = value
        dec.square_down(2, e_sq.at[1], value, wd, 1)

    def dec_self_out():
        value = st[Decoder.ROWS_IN] + dec.square_sum(2, e_sq.at[1])
        st[Decoder.ONE] = value
        value = rounded(rms_gain(value, dec.gain(4)))
        st[Decoder.CROSS_NORM] = value
        dec.square_down(3, e_sq.at[2], value, wd, 2)

    def dec_query():
        st[Decoder.QUERY] = rounded(dec.square_sum(3, e_sq.at[2]))

    def dec_inner():
        own = half_of(st[Decoder.TOP], c).astype(bf16)
        put_blocks(e_inner, s, c, [mm_t(own, wdo[n]) for n in range(z_count)], 4 * ROWS)
        plane.start(7, e_inner)

    def dec_inner_end():
        plane.wait(7, e_inner)
        total = blocks_of(e_inner, 4 * ROWS, z_count)
        for j in range(4):
            st[Decoder.PRE + j] = total[:, j * 2 * HALF : (j + 1) * 2 * HALF]

    def dec_main():
        width = 2 * HALF
        scale = 1.0 / math.sqrt(HD)
        mask = head_rows(width)
        valid = lax.broadcasted_iota(jnp.int32, (1, x_s.shape[0] * BAND), 1) < length
        query = own_row(st[Decoder.QUERY], s, c)
        q_heads = jnp.where(mask, query, 0.0).astype(bf16)
        scores = jnp.where(valid, mm_t(q_heads, ck_s[...]) * scale, neg_fill)
        raised = jnp.exp(scores - jnp.max(scores, axis=-1, keepdims=True))
        probs = raised / jnp.sum(raised, axis=-1, keepdims=True)
        probs_b = probs.astype(bf16)
        att = jnp.where(mask, matmul(probs_b, cv_s[...]), 0.0)
        e_att[s, c] = rounded(jnp.sum(att, axis=0, keepdims=True))
        plane.start(4, e_att)
        plane.wait(4, e_att)
        value = jnp.concatenate([e_att[p // 2, p % 2] for p in range(8)], axis=0)
        st[Decoder.CROSS_ATT] = value
        dec.square_down(5, e_sq.at[3], value, wd, 3)
        two = st[Decoder.ONE] + dec.square_sum(5, e_sq.at[3])
        value = rounded(rms_gain(two, dec.gain(5)))
        st[Decoder.FFN_NORM] = value
        e_pre[s, c] = mm_down(value, lambda n: wdi[n], s, z_count, ROWS)
        plane.start(6, e_pre, SAME_CORE)
        plane.wait(6, e_pre, SAME_CORE)
        inner, slope = gelu_both(e_pre[0, c] + e_pre[1, c] + e_pre[2, c] + e_pre[3, c])
        g_inner = jnp.concatenate([half_of(st[Decoder.PRE + j], c) for j in range(4)], axis=1)
        g_pre = rounded(g_inner * slope)
        own = g_pre.astype(bf16)
        put_blocks(e_up.at[0], s, c, [mm_t(own, wdi[n]) for n in range(z_count)], ROWS)
        plane.start(9, e_up.at[0])
        e_half[c, 0] = rounded(inner)
        e_half[c, 1] = g_pre
        mine = e_half.at[c]
        swap = remote(mine, mine, p_send.at[11, 0], p_recv.at[11, 0], sibling)
        swap.start()
        g_norm = dec.square_up_sum(9, e_up.at[0])
        grad, gain = pull_own(two, dec.gain(5), g_norm, s, c)
        gg_o[...] = jnp.zeros_like(gg_o)
        gg_o[5:6, :] = gain
        g_two = st[Decoder.TOP] + grad
        st[Decoder.TWO] = g_two
        dec.square_up(10, e_up.at[1], g_two, wd, 3)
        other = e_half.at[1 - c]
        remote(other, other, p_send.at[11, 0], p_recv.at[11, 0], sibling).wait_recv()
        inner = ffn_halves([e_half[0, 0], e_half[1, 0]])
        g_pre = ffn_halves([e_half[0, 1], e_half[1, 1]])
        for j in range(4):
            st[Decoder.INNER + j] = inner[:, j * width : (j + 1) * width]
            st[Decoder.PRE + j] = g_pre[:, j * width : (j + 1) * width]
        e_out[s, c] = mm_down(inner, lambda n: wdo[n], s, z_count, 4 * ROWS)
        g_att = own_row(rounded(dec.square_up_sum(10, e_up.at[1])), s, c)
        plane.start(8, e_out)
        g_heads = jnp.where(mask, g_att, 0.0).astype(bf16)
        g_probs = mm_t(g_heads, cv_s[...])
        g_scores = probs * (g_probs - jnp.sum(g_probs * probs, axis=-1, keepdims=True))
        row = lax.broadcasted_iota(jnp.int32, g_scores.shape, 0)
        g_scores_b = jnp.where(row < H, g_scores, 0.0).astype(bf16)
        g_query = jnp.where(mask, matmul(g_scores_b, ck_s[...]), 0.0)
        g_query = jnp.sum(g_query, axis=0, keepdims=True) * scale
        st[Decoder.QUERY] = as_own_row(rounded(g_query), s, c)
        live_b = jnp.where(row < H, probs_b.astype(f32), 0.0).astype(bf16)
        n_s[...] = (mm_outer(g_scores_b, q_heads) * scale).astype(bf16)
        drain(n_s, gck_o)
        cv_s[...] = mm_outer(live_b, g_heads).astype(bf16)
        drain(cv_s, gcv_o)
        st_o[...] = st[...]
        plane.wait(8, e_out)
        out = two + jnp.concatenate(halves(e_out), axis=1)
        dec_o[...] = jnp.broadcast_to(own_row(out, s, c), dec_o.shape)
        swap.wait_send()

    pieces = {
        ("gain", 0): [start_piece],
        ("square", 0): [lambda: project(0, n_s, q_s, q_o)],
        ("square", 1): [lambda: project(1, n_s, k_s, k_o)],
        ("square", 2): [lambda: project(2, n_s, v_s, v_o), dec_start, lambda: attention((0, 2))],
        ("square", 3): [lambda: attention((2, 4)), dec_self_values],
        ("cols", 0): [lambda: attention((4, 6)), dec_self_out],
        ("cols", 1): [hidden_piece, lambda: ffn_piece(0), dec_query],
        ("cols", 2): [lambda: ffn_piece(1), lambda: ffn_piece(2)],
        ("cols", 3): [lambda: ffn_piece(3)],
        ("rows", 1): [dec_inner],
        ("rows", 2): [dec_inner_end],
        ("rows", 3): [hidden_two_piece],
        ("square", 4): [lambda: project(4, enc_s, ck_s, None)],
        ("square", 5): [lambda: project(5, enc_s, cv_s, None), dec_main],
    }
    k = 2
    there, early = gather.lag(z_count + 2), gather.lag(z_count + 1)
    for t in range(len(units) + there):
        gather.tick(t, done)
        if t >= 4:
            lined.tick(t - 4, done)
        if t == 1:
            for i, n in enumerate(DEC):
                wd[i, z] = joined(sq_ref[n, :, cols(c)], sq_r[n])
            for n in range(n_ff):
                for j in range(4):
                    first[k].wait_recv()
                    k += 1
                    at = cols(c, 2 * HALF * j)
                    value = joined(in_ref[n, :, at], in_r[n, j])
                    if n == 0:
                        in_w[n, z, s, :, at] = value
                    else:
                        wdi[z, :, j * HALF : (j + 1) * HALF] = value
                first[k].wait_recv()
                k += 1
                value = joined(out_ref[n, :, cols(c)], out_r[n])
                if n == 0:
                    out_w[n, z, s, :, cols(c)] = value
                else:
                    wdo[z] = value
        ready = 0 if t == early else t - there
        if ready > 0 or t == early:
            for piece in pieces.get(units[ready], ()):
                piece()
    gather.finish()
    lined.finish()
    plane.finish()
    for copy in first:
        copy.wait_send()
    for copy in x_copies:
        copy.wait_send()
    for copy in drains:
        copy.wait()


def bucket_hot(bucket_ref, count):
    row = lax.broadcasted_iota(jnp.int32, (count, bucket_ref.shape[1]), 0)
    return jnp.where(bucket_ref[...] == row, 1.0, 0.0)


def greet_plane(z, s, c, z_count):
    barrier = pltpu.get_barrier_semaphore()
    for d in range(1, z_count):
        peer = ((z + d) % z_count, s, c)
        pl.semaphore_signal(barrier, 1, device_id=peer, device_id_type=MESH_ID)
    for peer, _ in plane_peers(z, s, c):
        pl.semaphore_signal(barrier, 1, device_id=peer, device_id_type=MESH_ID)
    pl.semaphore_wait(barrier, z_count - 1 + 7)


def forward(
    lengths, rel_bias, buckets, square, ffn_in, ffn_out, gains, dec_in, cotangent, x, z_count
):
    n_sq, n_ff = square.shape[0], ffn_in.shape[0]
    order = [("gain", 0)]
    order += [("square", n) for n in (0, 1, 2)]
    lines = [("line square", n) for n in range(4)]
    lines += [("line cols", n) for n in range(4)] + [("line rows", n) for n in range(4)]
    plain = [("square", 3)] + [("cols", n) for n in range(4)] + [("rows", n) for n in range(4)]
    plain += [("square", n) for n in (4, 5)]
    order = order + plain
    blocks, band, width = x.shape
    span = blocks * band
    hidden_units = 8 * HALF
    sq_s = (len(ENC), z_count, 4, ROWS, width)
    in_s = (1, z_count, 4, ROWS, hidden_units)
    out_s = (1, z_count, 4, 4 * ROWS, width)
    gain_s = (z_count, 4, ROWS, 128)
    wd_s = (len(DEC), z_count, ROWS, HALF)
    firsts = 2 + 5 * n_ff
    slots = 2 * (z_count - 1) + 4
    vmem = pl.BlockSpec(memory_space=pltpu.VMEM)
    hbm = pl.BlockSpec(memory_space=pltpu.HBM)
    token = ((span, width), bf16)
    token_f = ((span, width), f32)
    st_s = ((Decoder.COUNT, 8, width), f32)
    outs = [(in_s[1:], bf16), (out_s[1:], bf16)]
    outs += [(x.shape, bf16), token, token, token, token, token_f]
    outs += [((span, hidden_units), f32), token_f, token, token, token, (wd_s, bf16)]
    outs += [(sq_s[1:], bf16)] * len(ENC)
    small = [((8, width), f32), st_s, ((8, width), f32), ((8, width), f32)]
    small += [((rel_bias.shape[0], 1, 2 * span), f32)]
    scratch = [(sq_s, bf16), (in_s, bf16), (out_s, bf16), (gain_s, bf16)]
    scratch += [((n_sq, ROWS // 2, HALF), f32), ((n_ff, 4, ROWS // 2, HALF), f32)]
    scratch += [((n_ff, 2 * ROWS, HALF), f32), ((ROWS // 2, 128), f32)]
    scratch += [(x.shape, bf16), token, token, token, token, token, token_f]
    scratch += [((span, hidden_units), f32), ((span, hidden_units), bf16), token_f]
    scratch += [token, token, token, ((8, width), f32)]
    scratch += [((gains.shape[1], 128), f32)]
    scratch += [(wd_s, bf16), ((z_count, ROWS, 4 * HALF), bf16), ((z_count, 4 * ROWS, HALF), bf16)]
    scratch += [st_s, ((4, 2, 2, 8, width), f32), ((4, 4, 2, 8, HALF), f32)]
    scratch += [((4, 2, 1, width), f32), ((4, 2, 8, 4 * HALF), f32), ((4, 2, 8, HALF), f32)]
    scratch += [((4, 2, z_count, 8, 256), f32), ((2, 4, 2, z_count, 8, 128), f32)]
    scratch += [((2, 2, 8, 4 * HALF), f32)]
    dma = pltpu.SemaphoreType.DMA
    return pl.pallas_call(
        functools.partial(forward_kernel, order, lines, z_count),
        out_shape=[jax.ShapeDtypeStruct(*o) for o in outs + small],
        in_specs=[pl.BlockSpec(memory_space=pltpu.SMEM)] + [vmem] * 8 + [hbm],
        out_specs=[hbm] * len(outs) + [vmem] * len(small),
        scratch_shapes=[pltpu.VMEM(*o) for o in scratch]
        + [dma((len(order), slots)), dma((len(order), slots)), dma((firsts,)), dma((firsts,))]
        + [dma((3,)), dma((3,)), dma((len(lines), slots)), dma((len(lines), slots))]
        + [dma((12, 7)), dma((12, 7)), dma((40,))],
        compiler_params=pltpu.CompilerParams(
            collective_id=0, has_side_effects=True, vmem_limit_bytes=62 * MIB
        ),
        name="forward",
    )(lengths, rel_bias, buckets, square, ffn_in, ffn_out, gains, dec_in, cotangent, x)


class Scatter:
    def __init__(self, units, sources, bufs, sems, z_count, put):
        self.units, self.sources, self.z_count, self.put = units, sources, z_count, put
        self.r0, self.r1, self.r2, self.r3, self.fin, self.sib = bufs
        self.send, self.recv = sems
        self.where = place()
        self.started = []
        self.lent = {}
        self.at = [0] * 6

    def go(self, u, slot, src, dst, peer):
        copy = remote(src, dst, self.send.at[u, slot], self.recv.at[u, slot], peer)
        copy.start()
        return copy

    def got(self, u, slot, ref):
        z, s, c = self.where[:3]
        remote(ref, ref, self.send.at[u, slot], self.recv.at[u, slot], (z, s, 1 - c)).wait_recv()

    def view(self, u, c, z=slice(None), s=slice(None)):
        kind, n = self.sources[u]
        if kind == "rows":
            return unit_view(kind, n, self.refs[kind], z, s, c)
        return self.refs["slots"].at[n, z, s, :, cols(c)]

    def c_start(self, u):
        z, s, c = self.where[:3]
        self.lent[u] = self.go(u, 0, self.view(u, 1 - c), self.r0.at[u], (z, s, 1 - c))

    def b_start(self, u):
        z, s, c, first, second, both = self.where
        self.got(u, 0, self.r0.at[u])

        def body(i, carry):
            n, m = i // 4, i % 4
            own = self.view(u, c, n, m)[...]
            total = own.astype(f32) + self.r0[u, n, m].astype(f32)
            self.r0[u, n, m] = total.astype(bf16)
            return carry

        lax.fori_loop(0, 4 * self.z_count, body, 0, unroll=4)
        self.started.append(self.go(u, 1, self.r0.at[u, :, second], self.r1.at[u, 0], (z, second, c)))
        self.started.append(self.go(u, 2, self.r0.at[u, :, both], self.r1.at[u, 1], (z, second, c)))
        self.lent.pop(u).wait_send()

    def a_start(self, u):
        z, s, c, first, second, both = self.where
        self.got(u, 2, self.r1.at[u, 1])
        for n in range(self.z_count):
            total = self.r0[u, n, first].astype(f32) + self.r1[u, 1, n].astype(f32)
            self.r1[u, 1, n] = total.astype(bf16)
        self.started.append(self.go(u, 3, self.r1.at[u, 1], self.r2.at[u], (z, first, c)))
        self.got(u, 1, self.r1.at[u, 0])
        for n in range(self.z_count):
            total = self.r0[u, n, s].astype(f32) + self.r1[u, 0, n].astype(f32)
            self.r1[u, 0, n] = total.astype(bf16)

    def z_start(self, u):
        z, s, c = self.where[:3]
        self.got(u, 3, self.r2.at[u])
        for n in range(self.z_count):
            total = self.r1[u, 0, n].astype(f32) + self.r2[u, n].astype(f32)
            self.r2[u, n] = total.astype(bf16)
        for d in range(1, self.z_count):
            to = (z + d) % self.z_count
            self.started.append(
                self.go(u, 3 + d, self.r2.at[u, to], self.r3.at[u, d - 1], (to, s, c))
            )

    def f_start(self, u):
        z, s, c = self.where[:3]
        total = self.r2[u, z].astype(f32)
        for d in range(1, self.z_count):
            self.got(u, 3 + d, self.r3.at[u, d - 1])
            total = total + self.r3[u, d - 1].astype(f32)
        self.fin[u] = total
        self.count(total)
        kind, n = self.units[u]
        if kind == "rows":
            if n % 2 == 1:
                @pl.when(c != n // 2)
                def _():
                    pair = pl.ds(u - 1, 2)
                    self.go(u, 7, self.fin.at[pair], self.sib.at[pair], (z, s, 1 - c))
        else:
            rows = pl.ds(pl.multiple_of((1 - c) * (ROWS // 2), 8), ROWS // 2)
            self.started.append(
                self.go(
                    u, 7, self.fin.at[u, rows], self.sib.at[u, pl.ds(0, ROWS // 2)], (z, s, 1 - c)
                )
            )

    def finish_unit(self, u):
        z, s, c = self.where[:3]
        kind, n = self.units[u]
        if kind == "rows":
            if n % 2 == 1:

                @pl.when(c == n // 2)
                def _():
                    self.got(u, 7, self.sib.at[pl.ds(u - 1, 2)])
                    for k in range(2):
                        self.put(kind, k, c, self.fin[u - 1 + k])
                        self.put(kind, k, 1 - c, self.sib[u - 1 + k])

                @pl.when(c != n // 2)
                def _():
                    pair = self.fin.at[pl.ds(u - 1, 2)]
                    remote(
                        pair, pair, self.send.at[u, 7], self.recv.at[u, 7], (z, s, 1 - c)
                    ).wait_send()
        else:
            self.got(u, 7, self.sib.at[u, pl.ds(0, ROWS // 2)])
            rows = pl.ds(pl.multiple_of(c * (ROWS // 2), 8), ROWS // 2)
            self.put(kind, n, c, self.fin[u, rows])
            self.put(kind, n, 1 - c, self.sib[u, : ROWS // 2])

    def reach(self, limits):
        steps = (self.c_start, self.b_start, self.a_start, self.z_start, self.f_start)
        for n, step in enumerate(steps + (self.finish_unit,)):
            while self.at[n] <= min(limits[n], len(self.units) - 1):
                step(self.at[n])
                self.at[n] += 1

    def tick(self, t):
        self.reach([t - lag for lag in (0, 1, 3, 5, 7, 8)])

    def flush(self):
        self.reach([len(self.units) - 1] + [n - 1 for n in self.at[:-1]])

    def finish(self):
        for copy in self.started:
            copy.wait_send()


def pull_rows(values_in, gain_row, incoming):
    inverse = lax.rsqrt(jnp.mean(values_in * values_in, axis=-1, keepdims=True) + norm_eps)
    scaled = incoming * gain_row
    inner = jnp.mean(scaled * values_in, axis=-1, keepdims=True)
    grad = inverse * scaled - values_in * (inverse * inverse * inverse * inner)
    return grad, jnp.sum(incoming * values_in * inverse, axis=0, keepdims=True)


def gelu_both(values_in):
    square = values_in * values_in
    slope = 0.7978845608028654
    bend = jnp.tanh(slope * values_in * (1.0 + 0.044715 * square))
    value = 0.5 * values_in * (1.0 + bend)
    grad = 0.5 * (1.0 + bend) + 0.5 * values_in * (1.0 - bend * bend) * slope * (
        1.0 + 3.0 * 0.044715 * square
    )
    return value, grad


def backward_kernel(z_count, *refs):
    (
        len_ref, table_ref, gain_ref, bucket_ref, w0, w1, w2, w3, w7, w8, win, wout,
        x_i, q_i, k_i, v_i, att_i, hid_i, pre_i, hid2_i, enc_i, gck_i, gcv_i, wd_i, st, gg_i,
        sq_o, in_o, out_o, x_o, own_o, bias_o, norm_o,
        slots, d_out, r0, r1, r2, r3, fin, sib,
        wbuf, x_s, q_s, k_s, v_s, att_s, enc_s, gck_s, gcv_s, hid_s, hid2_s, pre_s,
        gh, gh_b, acc, inner_s, gpre_s, turned, gatt, gq, gk, gv, gx, gx_r,
        wd, e_q, e_up, left_w, left_r, right_r, acc_one,
        sums, dt_o, gg_o, ss, e_small, z_small, e_sq, z_sq,
        send, recv, w_sem, p_sem, a_sem, x_send, x_recv, o_sem, p_send, p_recv, z_send, z_recv, t_send, t_recv,
    ) = refs
    z, s, c = place()[:3]
    blocks = x_s.shape[0]
    width = 2 * HALF

    loads = {}
    for n, (src, dst) in enumerate(
        (
            (enc_i, enc_s), (gck_i, gck_s), (gcv_i, gcv_s), (hid2_i, hid2_s), (hid_i, hid_s),
            (att_i, att_s), (q_i, q_s), (k_i, k_s), (v_i, v_s), (x_i, x_s), (wd_i, wd),
        )
    ):
        copy = pltpu.make_async_copy(src, dst, a_sem.at[n])
        copy.start()
        loads[n] = copy
    tiles = [w7, w8]
    for j in range(4):
        tiles.append(wout.at[pl.ds(j * width, width)])
        tiles.append(win.at[:, pl.ds(j * width, width)])
    tiles += [w3, w0, w1, w2]
    w_loads = {}

    def fetch(n):
        if n < len(tiles):
            copy = pltpu.make_async_copy(tiles[n], wbuf.at[n % 4], w_sem.at[n])
            copy.start()
            w_loads[n] = copy

    p_loads = {}

    def fetch_pre(j):
        if j < 4:
            copy = pltpu.make_async_copy(
                pre_i.at[:, pl.ds(j * width, width)], pre_s.at[j % 2], p_sem.at[j]
            )
            copy.start()
            p_loads[j] = copy

    for n in range(4):
        fetch(n)
    fetch_pre(0)
    fetch_pre(1)
    greet_plane(z, s, c, z_count)
    plane = Plane(p_send, p_recv)
    dec = Decoder(plane, st, gain_ref, z_count)
    e_q[s, c] = st[Decoder.QUERY]
    plane.start(0, e_q)
    z_copies = []

    def dec_query():
        plane.wait(0, e_q)
        value = e_q[0, 0]
        for p in range(1, 8):
            value = value + e_q[p // 2, p % 2]
        acc_one[1] = value
        loads[10].wait()
        dec.square_up(1, e_up.at[0], value, wd, 2)

    def dec_one():
        grad, gain = pull_own(st[Decoder.ONE], dec.gain(4), dec.square_up_sum(1, e_up.at[0]), s, c)
        gg_o[4:5, :] += gain
        value = rounded(st[Decoder.TWO] + grad)
        acc_one[0] = value
        dec.square_up(2, e_up.at[1], value, wd, 1)

    def dec_self():
        value = rounded(dec.square_up_sum(2, e_up.at[1]))
        dec.square_up(3, e_up.at[2], value, wd, 0)
        rights = [value, acc_one[0], acc_one[1], rounded(st[Decoder.TWO])]
        rights += [st[Decoder.PRE + j] for j in range(4)] + [st[Decoder.TOP], jnp.zeros_like(value)]
        right_r[z] = jnp.concatenate(rights, axis=0).astype(bf16)
        lefts = [st[n] for n in range(Decoder.SELF_NORM, Decoder.SELF_VALUES + 1)]
        lefts += [st[n] for n in range(Decoder.CROSS_NORM, Decoder.FFN_NORM + 1)]
        lefts = jnp.concatenate(lefts + [jnp.zeros_like(value)], axis=0).astype(bf16)
        row = lax.broadcasted_iota(jnp.int32, (width, 128), 0)
        lane = lax.broadcasted_iota(jnp.int32, (width, 128), 1)
        share = ROWS // 2
        hidden_at = (2 * s + c) * 4 * share
        hidden_pick = jnp.where((row == hidden_at + lane) & (lane < 4 * share), 1.0, 0.0)
        for to in range(z_count):
            at = (to * 8 + 2 * s + c) * share
            chosen = jnp.where((row == at + lane) & (lane < share), 1.0, 0.0).astype(bf16)
            inner = jnp.concatenate([st[Decoder.INNER + to], jnp.zeros_like(value)], axis=0)
            left_w[to] = jnp.concatenate(
                [
                    matmul(lefts, chosen).astype(bf16),
                    matmul(inner.astype(bf16), hidden_pick.astype(bf16)).astype(bf16),
                ],
                axis=0,
            )
        k = 0
        for d in range(1, z_count):
            to = (z + d) % z_count
            for src, dst in ((right_r.at[z], right_r.at[z]), (left_w.at[to], left_r.at[z])):
                copy = remote(src, dst, z_send.at[k], z_recv.at[k], (to, s, c))
                copy.start()
                z_copies.append(copy)
                k += 1
        left_r[z] = left_w[z]

    def dec_last():
        _, gain = pull_own(
            st[Decoder.ROWS_IN], dec.gain(3), dec.square_up_sum(3, e_up.at[2]), s, c
        )
        gg_o[3:4, :] += gain

    def dec_grads():
        for copy in z_copies:
            copy.wait()
        lefts = [left_r[n].astype(f32) for n in range(z_count)]
        rights = [right_r[n].astype(f32) for n in range(z_count)]

        def gathered(parts, n):
            return jnp.concatenate([p[8 * n : 8 * n + 8] for p in parts], axis=0).astype(bf16)

        share = ROWS // 2
        for n in range(4):
            value = mm_outer(gathered(lefts, n), gathered(rights, n))[:share]
            count(value)
            sq_o[DEC[n]] = value
        for j in range(4):
            value = mm_outer(gathered(lefts, 4), gathered(rights, 4 + j))[:share]
            count(value)
            in_o[1, :, j * width : (j + 1) * width] = value
        value = mm_outer(gathered(lefts, 6), gathered(rights, 8))[: 4 * share]
        count(value)
        out_o[1] = value

    z_started = []

    def line_start(k, ref):
        for d in range(1, z_count):
            mine = ref.at[z]
            copy = remote(
                mine, mine, t_send.at[k, d - 1], t_recv.at[k, d - 1], ((z + d) % z_count, s, c)
            )
            copy.start()
            z_started.append(copy)

    def line_sum(k, ref):
        for d in range(1, z_count):
            slot = ref.at[(z + z_count - d) % z_count]
            remote(slot, slot, t_send.at[k, d - 1], t_recv.at[k, d - 1], (z, s, 1 - c)).wait_recv()
        total = ref[0]
        for n in range(1, z_count):
            total = total + ref[n]
        return total

    def plane_sum(k, ref):
        plane.wait(k, ref)
        total = ref[0, 0]
        for p in range(1, 8):
            total = total + ref[p // 2, p % 2]
        return total

    def small_start():
        offsets = dt_o[...].reshape(dt_o.shape[0], dt_o.shape[2])
        hot = bucket_hot(bucket_ref, 128)
        row = lax.broadcasted_iota(jnp.int32, (16, dt_o.shape[0]), 0)
        lane = lax.broadcasted_iota(jnp.int32, (16, dt_o.shape[0]), 1)
        padded = lax.dot_general(
            jnp.where(row == lane, 1.0, 0.0),
            offsets,
            (((1,), (0,)), ((), ())),
            precision=highest_precision,
            preferred_element_type=f32,
        )
        totals = lax.dot_general(
            padded,
            hot,
            (((1,), (1,)), ((), ())),
            precision=highest_precision,
            preferred_element_type=f32,
        )
        pieces = [gg_o[...]] + [totals[8 * n : 8 * n + 8] for n in range(2)]
        e_small[s, c] = jnp.concatenate(pieces, axis=1)
        plane.start(4, e_small)

    def small_line():
        z_small[z] = plane_sum(4, e_small)
        line_start(0, z_small)

    def small_end():
        total = line_sum(0, z_small)
        gg_o[...] = total[:, :width]
        own_o[...] = pltpu.roll(total[:, :width], width - (z * 8 + 2 * s + c) * (ROWS // 2), 1)[
            :, :128
        ]
        parts = [total[:, width + 128 * n : width + 128 * (n + 1)] for n in range(2)]
        bias_o[...] = jnp.concatenate(parts, axis=0)

    def norm_start():
        e_sq[s, c] = ss[:, :128] + ss[:, 128:256] + ss[:, 256:]
        plane.start(5, e_sq)

    def norm_end():
        z_sq[z] = plane_sum(5, e_sq)
        line_start(1, z_sq)
        rest = jnp.sum(gg_o[...] * gg_o[...]) + jnp.sum(bias_o[...] * bias_o[...])
        total = jnp.sum(line_sum(1, z_sq)) + rest
        norm_o[0, 0] = jnp.max(jnp.sqrt(jnp.full((8, 128), total, f32)))

    units = [("square", 7), ("square", 8)] + [("cols", j) for j in range(4)] + [("square", 3)]
    units += [("rows", n) for n in range(4)] + [("heads", m) for m in range(3)]
    sources, held = [], 0
    for kind, n in units:
        if kind == "rows":
            sources.append((kind, n))
        else:
            sources.append(("slot", held % 3))
            held += 1

    def count(value):
        squares = value * value
        total = squares[:8]
        for n in range(8, value.shape[0], 8):
            total = total + squares[n : n + 8]
        for n in range(0, value.shape[1], HALF):
            ss[...] += total[:, n : n + HALF]

    def put(kind, n, side, value):
        if kind == "square":
            sq_o[n, :, cols(side)] = value
        elif kind == "cols":
            in_o[0, :, cols(side, n * width)] = value
        elif kind == "rows":
            out_o[0, n * ROWS : (n + 1) * ROWS, cols(side)] = value
        else:
            at = pl.ds(pl.multiple_of((2 * n + side) * 128, 128), 128)
            for t in range(3):
                sq_o[t, :, at] = value[:, t * 128 : (t + 1) * 128]

    scatter = Scatter(units, sources, (r0, r1, r2, r3, fin, sib), (send, recv), z_count, put)
    scatter.count = count
    scatter.refs = {"slots": slots, "rows": d_out}

    def turn(src):
        def body(i, carry):
            at = pl.ds(pl.multiple_of(i * 256, 256), 256)
            turned[at, :] = src[:, at].T
            return carry

        lax.fori_loop(0, 3, body, 0)

    def grad_to_slot(n, right):
        def work(at):
            value = matmul(turned[...], right[:, at]).astype(bf16)
            slots[n, :, :, :, at] = value.reshape(z_count, 4, ROWS, 256)

        col_tiles(width, 256, work)

    def back(left, n, dst, add):
        w_loads[n].wait()

        def work(at):
            value = mm_t(left[...], wbuf[n % 4, at, :])
            if add:
                value = value + dst[:, at]
            dst[:, at] = value

        col_tiles(width, 256, work)
        fetch(n + 4)

    gg_o[...] = gg_i[...]
    ss[...] = jnp.zeros_like(ss)
    loads[0].wait()
    loads[1].wait()
    turn(enc_s)
    grad_to_slot(0, gck_s)
    scatter.tick(0)
    dec_query()
    loads[2].wait()
    grad_to_slot(1, gcv_s)
    scatter.tick(1)
    back(gck_s, 0, acc, False)
    back(gcv_s, 1, acc, True)
    loads[3].wait()
    loads[4].wait()

    def pull_hid2(i, at):
        grad, gain = pull_rows(hid2_s[at, :], gain_ref[2:3, :], acc[at, :])
        gh[at, :] = grad
        gh_b[at, :] = grad.astype(bf16)
        gg_o[2:3, :] += gain
        enc_s[at, :] = rms_gain(hid_s[at, :], gain_ref[1:2, :]).astype(bf16)

    dec_one()
    row_blocks(blocks, pull_hid2)
    turn(enc_s)

    for j in range(4):
        p_loads[j].wait()
        w_loads[2 + 2 * j].wait()

        def hidden_tile(at):
            value, slope = gelu_both(pre_s[j % 2, :, at])
            inner_s[:, at] = value.astype(bf16)
            grad = mm_t(gh_b[...], wbuf[(2 + 2 * j) % 4, at, :])
            gpre_s[:, at] = (grad * slope).astype(bf16)

        col_tiles(width, 256, hidden_tile)
        fetch(6 + 2 * j)
        fetch_pre(j + 2)
        grad_to_slot((2 + j) % 3, gpre_s)
        scatter.tick(2 + j)

        def out_rows(i, carry):
            at = pl.ds(pl.multiple_of(i * HALF, HALF), HALF)
            value = mm_outer(inner_s[:, at], gh_b[...]).astype(bf16)
            d_out[0, j, pl.ds(2 * i, 2)] = value.reshape(2, 4 * ROWS, width)
            return carry

        lax.fori_loop(0, 2, out_rows, 0)
        back(gpre_s, 3 + 2 * j, acc, j > 0)
        if j < 2:
            (dec_self, dec_last)[j]()

    loads[5].wait()

    def pull_hid(i, at):
        grad, gain = pull_rows(hid_s[at, :], gain_ref[1:2, :], acc[at, :])
        total = gh[at, :] + grad
        gh[at, :] = total
        gh_b[at, :] = total.astype(bf16)
        gg_o[1:2, :] += gain

    row_blocks(blocks, pull_hid)
    turn(att_s)
    grad_to_slot(0, gh_b)
    scatter.tick(6)
    w_loads[10].wait()

    def attended_grad(at):
        gatt[:, at] = mm_t(gh_b[...], wbuf[10 % 4, at, :]).astype(bf16)

    col_tiles(width, 256, attended_grad)
    for n in (6, 7, 8, 9):
        loads[n].wait()

    def x_norm(i, at):
        enc_s[at, :] = rms_gain(x_s[i].astype(f32), gain_ref[0:1, :]).astype(bf16)

    row_blocks(blocks, x_norm)
    turn(enc_s)
    scatter.tick(7)

    def pair_grads(pairs):
        def body(pair, carry):
            attend_pair_bwd(
                pair, len_ref[s], table_ref, q_s, k_s, v_s, gatt, gq, gk, gv, dt_o, sums
            )
            return carry

        lax.fori_loop(pairs[0], pairs[1], body, 0)

    def heads_to_slot(m, n):
        for t, right in enumerate((gq, gk, gv)):
            value = matmul(turned[...], right[:, m * 256 : (m + 1) * 256]).astype(bf16)
            value = value.reshape(z_count, 4, ROWS, 256)
            slots[n, :, :, :, t * 128 : (t + 1) * 128] = value[..., :128]
            slots[n, :, :, :, HALF + t * 128 : HALF + (t + 1) * 128] = value[..., 128:]

    pair_grads((0, 1))
    scatter.tick(8)
    pair_grads((1, 2))
    heads_to_slot(0, 1)
    scatter.tick(9)
    pair_grads((2, 3))
    scatter.tick(10)
    pair_grads((3, 4))
    heads_to_slot(1, 2)
    scatter.tick(11)
    pair_grads((4, 5))
    scatter.tick(12)
    pair_grads((5, 6))
    heads_to_slot(2, 0)
    scatter.tick(13)
    back(gq, 11, acc, False)
    scatter.flush()
    back(gk, 12, acc, True)
    back(gv, 13, acc, True)

    def pull_x(i, at):
        grad, gain = pull_rows(x_s[i].astype(f32), gain_ref[0:1, :], acc[at, :])
        gx[i] = (gh[at, :] + grad).astype(bf16)
        gg_o[0:1, :] += gain

    row_blocks(blocks, pull_x)
    small_start()
    scatter.flush()
    x_copies = []
    for d in range(1, 4):
        peer = (s + d) % 4
        copy = remote(
            gx.at[peer], gx_r.at[s], x_send.at[d - 1], x_recv.at[d - 1], (z, peer, c)
        )
        copy.start()
        x_copies.append(copy)
    dec_grads()
    small_line()
    scatter.flush()
    gx_r[s] = gx[s]
    scatter.flush()
    small_end()
    norm_start()
    scatter.flush()
    norm_end()
    for copy in x_copies:
        copy.wait()

    copy = pltpu.make_async_copy(gx_r, x_o, o_sem.at[0])
    copy.start()
    scatter.finish()
    plane.finish()
    for sent in z_started:
        sent.wait_send()
    copy.wait()


def backward(lengths, table, gain, buckets, weights, win, wout, acts, small, z_count):
    x = acts[0]
    blocks, band, width = x.shape
    span = blocks * band
    vmem = pl.BlockSpec(memory_space=pltpu.VMEM)
    hbm = pl.BlockSpec(memory_space=pltpu.HBM)
    n = 14
    token = ((span, width), bf16)
    token_f = ((span, width), f32)
    scratch = [((3, z_count, 4, ROWS, width), bf16), ((1, z_count, 4, 4 * ROWS, width), bf16)]
    scratch += [((n, z_count, 4, ROWS, HALF), bf16), ((n, 2, z_count, ROWS, HALF), bf16)]
    scratch += [((n, z_count, ROWS, HALF), bf16), ((n, z_count - 1, ROWS, HALF), bf16)]
    scratch += [((n, ROWS, HALF), f32), ((n, ROWS, HALF), f32)]
    scratch += [((4, width, width), bf16), (x.shape, bf16)] + [token] * 7 + [token_f] * 2
    scratch += [((2, span, width), f32), token_f, token, token_f, token, token]
    scratch += [((width, span), bf16)] + [token] * 4 + [(x.shape, bf16)] * 2
    scratch += [((len(DEC), z_count, ROWS, HALF), bf16), ((4, 2, 8, width), f32)]
    scratch += [((3, 4, 2, z_count, 8, 128), f32), ((z_count, 64, 128), bf16)]
    scratch += [((z_count, 64, 128), bf16), ((z_count, 80, width), bf16), ((2, 8, width), f32)]
    scratch += [((BAND, 2 * span), f32), (table.shape, f32), ((8, width), f32), ((8, HALF), f32)]
    scratch += [((4, 2, 8, width + 256), f32), ((z_count, 8, width + 256), f32)]
    scratch += [((4, 2, 8, 128), f32), ((z_count, 8, 128), f32)]
    dma = pltpu.SemaphoreType.DMA
    return pl.pallas_call(
        functools.partial(backward_kernel, z_count),
        out_shape=[
            jax.ShapeDtypeStruct((10, ROWS // 2, width), f32),
            jax.ShapeDtypeStruct((2, ROWS // 2, 4 * width), f32),
            jax.ShapeDtypeStruct((2, 2 * ROWS, width), f32),
            jax.ShapeDtypeStruct(x.shape, bf16),
            jax.ShapeDtypeStruct((8, 128), f32),
            jax.ShapeDtypeStruct((16, 128), f32),
            jax.ShapeDtypeStruct((1, 1), f32),
        ],
        in_specs=[pl.BlockSpec(memory_space=pltpu.SMEM)] + [vmem] * 3 + [hbm] * 20 + [vmem] * 2,
        out_specs=[vmem] * 3 + [hbm] + [vmem] * 2 + [pl.BlockSpec(memory_space=pltpu.SMEM)],
        scratch_shapes=[pltpu.VMEM(*o) for o in scratch]
        + [dma((n, 8)), dma((n, 8)), dma((n,)), dma((4,)), dma((11,)), dma((3,)), dma((3,))]
        + [dma((1,)), dma((6, 7)), dma((6, 7)), dma((6,)), dma((6,)), dma((2, 3)), dma((2, 3))],
        compiler_params=pltpu.CompilerParams(
            collective_id=1, has_side_effects=True, vmem_limit_bytes=62 * MIB
        ),
        name="backward",
    )(lengths, table, gain, buckets, *weights, win, wout, *acts, *small)


def update_kernel(big, small, *refs):
    norm_ref, refs = refs[0], refs[1:]
    n_big, n_small = len(big), len(small)
    big_in, refs = refs[: 4 * n_big], refs[4 * n_big :]
    small_in, refs = refs[: 4 * n_small], refs[4 * n_small :]
    (grad_i, dec_i), refs = refs[:2], refs[2:]
    big_out, refs = refs[: 3 * n_big], refs[3 * n_big :]
    small_out, refs = refs[: 3 * n_small], refs[3 * n_small :]
    (grad_o, dec_o), refs = refs[:2], refs[2:]
    held, (grad_s, wide_s, in_sem, out_sem) = refs[: 4 * n_big], refs[4 * n_big :]
    loads, stores = [], []
    for n, (src, dst) in enumerate(zip((grad_i,) + big_in, (grad_s,) + held)):
        copy = pltpu.make_async_copy(src, dst, in_sem.at[n])
        copy.start()
        loads.append(copy)
    factor = 1.0 / jnp.maximum(jnp.full((1, 1), norm_ref[0, 0], f32), clip_bound)

    def store(src, dst):
        copy = pltpu.make_async_copy(src, dst, out_sem.at[len(stores)])
        copy.start()
        stores.append(copy)

    dec_o[0] = dec_i[:1].astype(bf16)
    for n, (rate, decay) in enumerate(small):
        w, m, v, g = small_in[4 * n : 4 * n + 4]
        rows, lanes = w.shape
        news = adam_step(w[...], m[...], v[...], g[:rows, :lanes], factor, rate, decay)
        for ref, value in zip(small_out[3 * n : 3 * n + 3], news):
            ref[...] = value
    loads[0].wait()

    def widen(i, carry):
        wide_s[i] = grad_s[i].astype(f32)
        return carry

    lax.fori_loop(0, wide_s.shape[0], widen, 0)
    store(wide_s, grad_o)
    for n, (rate, decay) in enumerate(big):
        w, m, v, g = held[4 * n : 4 * n + 4]
        for load in loads[1 + 4 * n : 5 + 4 * n]:
            load.wait()

        def step(i, carry):
            news = adam_step(w[i], m[i], v[i], g[i], factor, rate, decay)
            for ref, value in zip((w, m, v), news):
                ref[i] = value
            return carry

        lax.fori_loop(0, w.shape[0], step, 0)
        for ref, out in zip((w, m, v), big_out[3 * n : 3 * n + 3]):
            store(ref, out)
    for copy in stores:
        copy.wait()


def update(norm, big, small, grad, dec_out, grad_shape, dec_shape):
    vmem = pl.BlockSpec(memory_space=pltpu.VMEM)
    hbm = pl.BlockSpec(memory_space=pltpu.HBM)
    big_in = [a for item in big for a in item[:4]]
    small_in = [a for item in small for a in item[:4]]
    like = [jax.ShapeDtypeStruct(item[0].shape, f32) for item in big for _ in range(3)]
    like_small = [jax.ShapeDtypeStruct(item[0].shape, f32) for item in small for _ in range(3)]
    last = [jax.ShapeDtypeStruct(grad_shape, f32), jax.ShapeDtypeStruct(dec_shape, bf16)]
    dma = pltpu.SemaphoreType.DMA
    return pl.pallas_call(
        functools.partial(
            update_kernel, [item[4:] for item in big], [item[4:] for item in small]
        ),
        out_shape=like + like_small + last,
        in_specs=[pl.BlockSpec(memory_space=pltpu.SMEM)]
        + [hbm] * len(big_in)
        + [vmem] * len(small_in)
        + [hbm, vmem],
        out_specs=[hbm] * len(like) + [vmem] * len(like_small) + [hbm, vmem],
        scratch_shapes=[pltpu.VMEM(a.shape, f32) for a in big_in]
        + [pltpu.VMEM(grad_shape, bf16), pltpu.VMEM(grad_shape, f32)]
        + [dma((1 + len(big_in),)), dma((1 + len(like),))],
        compiler_params=pltpu.CompilerParams(vmem_limit_bytes=60 * MIB),
        name="update",
    )(norm, *big_in, *small_in, grad, dec_out)


def on_device(
    inputs,
    dec_in,
    cotangent,
    lengths,
    bucket_table,
    square,
    square_m,
    square_v,
    ffn_in,
    ffn_in_m,
    ffn_in_v,
    ffn_out,
    ffn_out_m,
    ffn_out_v,
    gains,
    gains_m,
    gains_v,
    rel_bias,
    rel_bias_m,
    rel_bias_v,
):
    z_count = lax.axis_size("dp")
    width = inputs.shape[2]
    direct = lax.axis_size("seq") == 4 and width == 2 * HALF and width == 4 * z_count * ROWS
    direct = direct and inputs.shape[:2] == (4, BAND)
    w = {}
    seq_pos = lax.axis_index("seq")
    local_len = inputs.shape[1]
    span = local_len * lax.axis_size("seq")
    bucket_count = rel_bias.shape[0]
    scale = 1.0 / math.sqrt(HD)
    length = lax.dynamic_slice_in_dim(lengths, seq_pos, 1, 0)
    key_valid = jnp.arange(span)[None, :] < length[:, None]
    one_hot = (
        jnp.pad(bucket_table, (0, 1), constant_values=-1)[:, None]
        == jnp.arange(bucket_count)[None, :]
    ).astype(f32)
    table = jnp.einsum("ob,bh->ho", one_hot, rel_bias, precision=highest_precision)[:, None, :]

    me = (
        lax.axis_index("dp") * lax.axis_size("seq") + seq_pos
    ) * lax.axis_size("head") + lax.axis_index("head")
    if direct:
        buckets = jnp.pad(bucket_table[::-1], (0, 1), constant_values=-1)[None]
        outs = forward(
            lengths,
            rel_bias.T,
            buckets,
            square,
            ffn_in,
            ffn_out,
            gains,
            dec_in,
            cotangent,
            inputs,
            z_count,
        )
        weights = [o.reshape(width, width) for o in outs[14:20]]
        gain_f, state, g_high, dec_out, table = outs[20:]
        summed_sq, summed_in, summed_out, input_grad, summed_gain, g_bias, norm = backward(
            lengths,
            table,
            gain_f,
            buckets,
            weights,
            outs[0].reshape(width, -1),
            outs[1].reshape(-1, width),
            outs[2:14],
            (state, g_high),
            z_count,
        )
        news = update(
            norm,
            (
                (square, square_m, square_v, summed_sq, rate_matrix, decay_rate),
                (ffn_in, ffn_in_m, ffn_in_v, summed_in, rate_matrix, decay_rate),
                (ffn_out, ffn_out_m, ffn_out_v, summed_out, rate_matrix, decay_rate),
            ),
            (
                (gains, gains_m, gains_v, summed_gain, rate_small, 0.0),
                (rel_bias.T, rel_bias_m.T, rel_bias_v.T, g_bias, rate_small, 0.0),
            ),
            input_grad,
            dec_out,
            inputs.shape,
            dec_in.shape,
        )
        bias_new = [o.T for o in news[12:15]]
        return (news[16], news[15], norm[0, 0], *news[:12], *bias_new)
    else:

        def gather_rows(x):
            return lax.all_gather(x.astype(bf16), AXES, axis=x.ndim - 2, tiled=True)

        sq_a = gather_rows(square[:4])
        w_in_e = gather_rows(ffn_in[0])
        w_out_e = gather_rows(ffn_out[0])
        sq_b = gather_rows(square[4:])
        w_in_d = gather_rows(ffn_in[1])
        w_out_d = gather_rows(ffn_out[1])
        gain_f = lax.all_gather(gains.astype(bf16), AXES, axis=1, tiled=True).astype(f32)
        for i in range(square.shape[0]):
            w[i] = sq_a[i] if i < 4 else sq_b[i - 4]
        x_b = lax.all_to_all(inputs, "seq", split_axis=0, concat_axis=1, tiled=True)[0]
        x_f = x_b.astype(f32)
        normed = rms_gain(x_f, gain_f[0]).astype(bf16)
        q = matmul(normed, w[0]).astype(bf16)
        k = matmul(normed, w[1]).astype(bf16)
        v = matmul(normed, w[2]).astype(bf16)
        attended = attend_fwd(length, table, q, k, v)
        hidden = x_f + matmul(attended, w[3])
        normed_two = rms_gain(hidden, gain_f[1]).astype(bf16)
        pre_act = matmul(normed_two, w_in_e)
        inner_act = gelu_tanh(pre_act).astype(bf16)
        hidden_two = hidden + matmul(inner_act, w_out_e)
        encoded = rms_gain(hidden_two, gain_f[2]).astype(bf16)
        cross_k = matmul(encoded, w[7]).astype(bf16)
        cross_v = matmul(encoded, w[8]).astype(bf16)

        dec_row = dec_in.reshape(1, width).astype(f32)
        self_norm = rms_gain(dec_row, gain_f[3]).astype(bf16)
        self_values = matmul(self_norm, w[4]).astype(bf16)
        dec_one = dec_row + matmul(self_values, w[5])
        cross_norm = rms_gain(dec_one, gain_f[4]).astype(bf16)
        cross_q = matmul(cross_norm, w[6]).astype(bf16)
        head_of = (jnp.arange(width)[None, :] // HD == jnp.arange(H)[:, None]).astype(bf16)
        q_heads = head_of * cross_q
        cross_scores = jnp.where(key_valid, mm_t(q_heads, cross_k) * scale, neg_fill)
        cross_probs = jax.nn.softmax(cross_scores, axis=-1)
        cross_probs_b = cross_probs.astype(bf16)
        cross_att = jnp.sum(
            matmul(cross_probs_b, cross_v) * head_of.astype(f32), axis=0, keepdims=True
        ).astype(bf16)
        dec_two = dec_one + matmul(cross_att, w[9])
        ffn_norm = rms_gain(dec_two, gain_f[5]).astype(bf16)
        pre_dec = matmul(ffn_norm, w_in_d)
        inner_dec = gelu_tanh(pre_dec).astype(bf16)
        dec_out = dec_two + matmul(inner_dec, w_out_d)

        g_top_b = cotangent.reshape(1, width)
        g_top = g_top_b.astype(f32)
        g_pre_dec = gelu_pull(pre_dec, mm_t(g_top_b, w_out_d)).astype(bf16)
        g_two_norm, g_gain_five = rms_pull(dec_two, gain_f[5], mm_t(g_pre_dec, w_in_d))
        g_two = g_top + g_two_norm
        g_two_b = g_two.astype(bf16)
        g_att = mm_t(g_two_b, w[9]).astype(bf16)
        g_att_heads = head_of * g_att
        g_probs = mm_t(g_att_heads, cross_v)
        g_cross_v = mm_outer(cross_probs_b, g_att_heads).astype(bf16)
        g_scores = cross_probs * (g_probs - jnp.sum(g_probs * cross_probs, axis=-1, keepdims=True))
        g_scores_b = g_scores.astype(bf16)
        g_cross_q = (
            jnp.sum(matmul(g_scores_b, cross_k) * head_of.astype(f32), axis=0, keepdims=True) * scale
        ).astype(bf16)
        g_cross_k = (mm_outer(g_scores_b, q_heads) * scale).astype(bf16)
        g_one_norm, g_gain_four = rms_pull(dec_one, gain_f[4], mm_t(g_cross_q, w[6]))
        g_one_b = (g_two + g_one_norm).astype(bf16)
        g_self_values = mm_t(g_one_b, w[5]).astype(bf16)
        g_gain_three = rms_pull(dec_row, gain_f[3], mm_t(g_self_values, w[4]))[1]

        lefts = (self_norm, self_values, cross_norm, cross_att, ffn_norm, inner_dec)
        rights = (g_self_values, g_one_b, g_cross_q, g_two_b, g_pre_dec, g_top_b)
        packed = lax.all_gather(jnp.concatenate(lefts + rights, axis=1), AXES, axis=0, tiled=True)
        devices = packed.shape[0]
        cuts = [0]
        for piece in lefts + rights:
            cuts.append(cuts[-1] + piece.shape[1])
        dec_grads = []
        for n in range(6):
            share = lefts[n].shape[1] // devices
            left = lax.dynamic_slice_in_dim(packed, cuts[n] + me * share, share, 1)
            right = packed[:, cuts[6 + n] : cuts[7 + n]]
            dec_grads.append(mm_outer(left, right))
        g_w7 = mm_outer(encoded, g_cross_k)
        g_w8 = mm_outer(encoded, g_cross_v)
        g_encoded = mm_t(g_cross_k, w[7]) + mm_t(g_cross_v, w[8])
        g_hidden_two, g_gain_two = rms_pull(hidden_two, gain_f[2], g_encoded)
        g_hidden_two_b = g_hidden_two.astype(bf16)
        g_out_e = mm_outer(inner_act, g_hidden_two_b)
        g_pre = gelu_pull(pre_act, mm_t(g_hidden_two_b, w_out_e)).astype(bf16)
        g_in_e = mm_outer(normed_two, g_pre)
        g_hidden_norm, g_gain_one = rms_pull(hidden, gain_f[1], mm_t(g_pre, w_in_e))
        g_hidden = g_hidden_two + g_hidden_norm
        g_hidden_b = g_hidden.astype(bf16)
        g_w3 = mm_outer(attended, g_hidden_b)
        g_attended = mm_t(g_hidden_b, w[3]).astype(bf16)
        gq, gk, gv, g_table = attend_bwd(length, table, q, k, v, g_attended)
        g_bias_here = jnp.einsum("ob,ho->bh", one_hot, g_table[:, 0, :], precision=highest_precision)
        g_w0 = mm_outer(normed, gq)
        g_w1 = mm_outer(normed, gk)
        g_w2 = mm_outer(normed, gv)
        g_normed = mm_t(gq, w[0]) + mm_t(gk, w[1]) + mm_t(gv, w[2])
        g_input_norm, g_gain_zero = rms_pull(x_f, gain_f[0], g_normed)
        g_x = (g_hidden + g_input_norm).astype(bf16)
        input_grad = lax.all_to_all(
            g_x[None], "seq", split_axis=1, concat_axis=0, tiled=True
        ).astype(f32)

        def scatter_rows(x):
            return lax.psum_scatter(
                x.astype(bf16), AXES, scatter_dimension=x.ndim - 2, tiled=True
            ).astype(f32)

        s_78 = scatter_rows(jnp.stack((g_w7, g_w8)))
        s_out = scatter_rows(g_out_e)
        s_in = scatter_rows(g_in_e)
        s_0123 = scatter_rows(jnp.stack((g_w0, g_w1, g_w2, g_w3)))
        g_gains = jnp.stack(
            (g_gain_zero, g_gain_one, g_gain_two, g_gain_three, g_gain_four, g_gain_five)
        )
        summed_sq = jnp.stack(
            (
                s_0123[0],
                s_0123[1],
                s_0123[2],
                s_0123[3],
                dec_grads[0],
                dec_grads[1],
                dec_grads[2],
                s_78[0],
                s_78[1],
                dec_grads[3],
            )
        )
        summed_in = jnp.stack((s_in, dec_grads[4]))
        summed_out = jnp.stack((s_out, dec_grads[5]))
        gain_share = gains.shape[1]
        local_squares = (
            jnp.sum(summed_sq * summed_sq)
            + jnp.sum(summed_in * summed_in)
            + jnp.sum(summed_out * summed_out)
        )
        g_gains, g_bias, shard_squares = lax.psum((g_gains, g_bias_here, local_squares), AXES)
        summed_gain = lax.dynamic_slice_in_dim(g_gains, me * gain_share, gain_share, 1)
        grad_norm = jnp.sqrt(shard_squares + jnp.sum(g_gains * g_gains) + jnp.sum(g_bias * g_bias))
        g_bias = g_bias.T
    factor = clip_bound / jnp.maximum(grad_norm, clip_bound)
    bias_new = adam_step(rel_bias.T, rel_bias_m.T, rel_bias_v.T, g_bias, factor, rate_small, 0.0)
    return (
        dec_out.astype(bf16).reshape(dec_in.shape),
        input_grad,
        grad_norm,
        *adam_step(square, square_m, square_v, summed_sq, factor, rate_matrix, decay_rate),
        *adam_step(ffn_in, ffn_in_m, ffn_in_v, summed_in, factor, rate_matrix, decay_rate),
        *adam_step(ffn_out, ffn_out_m, ffn_out_v, summed_out, factor, rate_matrix, decay_rate),
        *adam_step(gains, gains_m, gains_v, summed_gain, factor, rate_small, 0.0),
        *(o.T for o in bias_new),
    )


def solution(mesh):
    rows = P(("dp", "head"), "seq", None)
    shard = P(None, AXES, None)
    small = P(None, AXES)
    return jax.shard_map(
        on_device,
        mesh=mesh,
        in_specs=(rows, rows, rows, P(("dp", "head")), P())
        + (shard,) * 9
        + (small,) * 3
        + (P(),) * 3,
        out_specs=(rows, rows, P()) + (shard,) * 9 + (small,) * 3 + (P(),) * 3,
        check_vma=False,
    )
```
